32 devices in a mesh: dev: 32 (over z, y, x, core).
Axes of the slice: x: 2, y: 2, z: 4, core: 2. Of those that a mesh axis runs over, the one named last changes fastest.
Arguments:
- moles: float32 [18, 2048, 1024], P(None, 'dev'), may hold values from 0.1 to 1
- old_content: float32 [18, 2048, 1024], P(None, 'dev'), may hold values from 0 to 1
- pressure: float32 [2048, 1024], P('dev'), may hold values from 0.5 to 1
- perm: float32 [2048, 1024], P('dev'), may hold values from 0.1 to 10
- labels: int32 [2048, 1024], P('dev'), may hold values from 0 to 1
- roots: int32 [2048, 1024], P('dev'), may hold values from 0 to 1
- counts: int32 [32], P('dev'), may hold values from 1 to 128, 2048 in all
- block_ids: int32 [4096], P('dev'), may hold values from 0 to 511, as said below
- wilson: float32 [18], replicated, may hold values from -1.5 to 1.5
- attraction: float32 [18, 18], replicated, may hold values from 0.3 to 0.9
- covolume: float32 [18], replicated, may hold values from 0.03 to 0.08
Outputs:
- residual: float32 [18, 2048, 1024], P(None, 'dev')
- pressure_step: float32 [2048, 1024], P('dev')
- vapour_fraction: float32 [2048, 1024], P('dev')
The draws below stay inside these ranges and needn't reach their ends.
Inputs may be any that keep to these rules, and one draw needn't show every extreme that they name: counts sum to 2048; each device holds at least one two-phase block and at most 128, exactly 128 on some device. `block_ids`: each device's 128 entries are distinct block numbers of that device.
All inputs are finite; a program needn't handle non-finite values.
Results may differ from the reference program's by a relative error of at most 0.0003.
Values sent between devices are 32-bit elements; how exact they have to be, the bound alone decides.
No kernel may reach another device: no remote copies, remote signals or barrier semaphores. Data moves between devices by JAX's collectives and lax.ppermute only.
A program may use at most 128 MiB of HBM per device.

```python
import math
import jax
import jax.numpy as jnp
import numpy as np
from jax import lax

NC = 18
BLK = 128
LX = 64
SS_ITERS = 3
RR_ITERS = 3
Z_ITERS = 5
FACE = 1024
NBLK = 512
MEANB = 64
MOST = 128
NX = 2048
N_DEV = 32


def draw_block_ids(key, part):
    key = jax.random.fold_in(key, 7)
    device_keys = jax.random.split(key, N_DEV)

    def one_device(device_key):
        return jax.random.permutation(device_key, NBLK)[:MOST].astype(jnp.int32)
    return jax.vmap(one_device)(device_keys).reshape(N_DEV * MOST).astype(jnp.int32)


def with_ends(entries, key, least, top_value):
    longest = entries.shape.index(max(entries.shape))
    spots = []
    for shift in (0, 1):
        where = [jax.random.randint(jax.random.fold_in(key, axis), (), 0, length) for axis, length in enumerate(entries.shape)]
        where[longest] = (where[longest] + shift) % entries.shape[longest]
        spots.append(tuple(where))
    return entries.at[spots[0]].set(least).at[spots[1]].set(top_value)


def shard_levels(rng, dims, cuts, least, top_value):
    factor_of = 1.0
    for dim, blocks in cuts:
        heights = jax.random.uniform(jax.random.fold_in(jax.random.fold_in(rng, 6), dim), (blocks,), jnp.float32, least / len(cuts), top_value / len(cuts))
        factor_of = factor_of * jnp.repeat(jnp.exp(heights), dims[dim] // blocks).reshape((-1,) + (1,) * (len(dims) - 1 - dim))
    return factor_of


def profile(count, total, reach, lean):
    loads = [(1 << 20) // math.isqrt(rank ** lean) + 1 for rank in range(2, count + 1)]
    rest, holding = total - reach - (count - 1), [1] * (count - 1)
    while rest > 0:
        free = [i for i in range(count - 1) if holding[i] < reach]
        whole, remaining = sum([loads[i] for i in free]), rest
        for i in free:
            addition = min(reach - holding[i], max(1, remaining * loads[i] // whole), rest)
            holding[i] = holding[i] + addition
            rest = rest - addition
    return np.array([reach] + holding)


def uneven(stream_key, number_of, total, limit, slope):
    if number_of == 2:
        one = jax.random.randint(stream_key, (), max(1, total - limit), min(limit, total - 1) + 1)
        return jnp.stack([one, total - one])
    lengths = jnp.asarray(profile(number_of, total, limit, slope), jnp.int32)
    pairs = (number_of - 1) // 2
    giver, receiver = lengths[1:1 + 2 * pairs:2], lengths[2:2 + 2 * pairs:2]
    slack = jnp.minimum(giver - 1, limit - receiver)
    passed = jax.random.randint(jax.random.fold_in(stream_key, 1), (pairs,), 0, 1 << 20) % (slack + 1)
    lengths = lengths.at[1:1 + 2 * pairs:2].set(giver - passed).at[2:2 + 2 * pairs:2].set(receiver + passed)
    return lengths[jax.random.permutation(jax.random.fold_in(stream_key, 2), number_of)]


def setup_inputs(seed: int = 0) -> dict:
    keys = jax.random.split(jax.random.key(seed), 12)
    moles = jnp.clip(jnp.exp(math.log(1.0) - 2.3025851 * jax.random.uniform(keys[0], (NC, NX, FACE), jnp.float32) ** shard_levels(keys[0], (NC, NX, FACE), ((1, 32),), -0.2, 0.2)), 0.1, 1.0)
    old_content = jnp.clip(1.0 * jax.random.uniform(keys[1], (NC, NX, FACE), jnp.float32) ** shard_levels(keys[1], (NC, NX, FACE), ((1, 32),), -0.2, 0.2), 0.0, 1.0)
    pressure = jnp.clip(0.5 + 0.5 * jax.random.uniform(keys[2], (NX, FACE), jnp.float32) ** shard_levels(keys[2], (NX, FACE), ((0, 32),), -0.2, 0.2), 0.5, 1.0)
    perm = jnp.clip(jnp.exp(math.log(10.0) - 4.6051702 * jax.random.uniform(keys[3], (NX, FACE), jnp.float32) ** shard_levels(keys[3], (NX, FACE), ((0, 32),), -0.2, 0.2)), 0.1, 10.0)
    labels = with_ends(jax.random.randint(keys[4], (NX, FACE), 0, 2), jax.random.fold_in(keys[4], 1), 0, 1).astype(jnp.int32)
    roots = with_ends(jax.random.randint(keys[5], (NX, FACE), 0, 2), jax.random.fold_in(keys[5], 1), 0, 1).astype(jnp.int32)
    counts = uneven(keys[6], N_DEV, MEANB * N_DEV, MOST, 2).astype(jnp.int32)
    block_ids = draw_block_ids(jax.random.fold_in(keys[11], 71), 0)
    wilson = jnp.clip(jax.random.uniform(keys[8], (NC,), jnp.float32, -1.5, 1.5), -1.5, 1.5)
    attraction = jnp.clip(jax.random.uniform(keys[9], (NC, NC), jnp.float32, 0.3, 0.9), 0.3, 0.9)
    covolume = jnp.clip(jax.random.uniform(keys[10], (NC,), jnp.float32, 0.03, 0.08), 0.03, 0.08)
    return {"moles": moles, "old_content": old_content, "pressure": pressure, "perm": perm, "labels": labels, "roots": roots, "counts": counts, "block_ids": block_ids, "wilson": wilson, "attraction": attraction, "covolume": covolume}


SQRT_TWO = math.sqrt(2.0)
TIME_STEP = 0.5
RELAX = 0.7
STEP_SCALE = 10.0

def mixture(fraction, pressure, attract, co_volume):
    attract_sum = jnp.dot(attract, fraction, precision=lax.Precision.HIGHEST)
    a_mixture = lax.optimization_barrier(jnp.sum(fraction * attract_sum, 0))
    b_mixture = lax.optimization_barrier(jnp.sum(co_volume[:, None] * fraction, 0))
    return (attract_sum, a_mixture, b_mixture, pressure * a_mixture, pressure * b_mixture)

def cubic_root(big_a, big_b, largest):
    z_factor = jnp.where(largest, jnp.ones_like(big_b), 2.0 * big_b)
    for sweep_index in range(Z_ITERS):
        spread = z_factor * z_factor + 2.0 * big_b * z_factor - big_b * big_b
        vapour_map = 1.0 + big_b - big_a * (z_factor - big_b) / spread
        liquid_map = big_b + spread * (1.0 + big_b - z_factor) / big_a
        z_factor = jnp.clip(0.5 * z_factor + 0.5 * jnp.where(largest, vapour_map, liquid_map), big_b + 0.01, 2.0)
    return z_factor

def fugacity(attract_sum, a_mixture, b_mixture, big_a, big_b, z_factor, co_volume):
    b_ratio = co_volume[:, None] / b_mixture
    log_arg = (z_factor + (1.0 + SQRT_TWO) * big_b) / (z_factor + (1.0 - SQRT_TWO) * big_b)
    return b_ratio * (z_factor - 1.0) - jnp.log(z_factor - big_b) - big_a / (2.0 * SQRT_TWO * big_b) * (2.0 * attract_sum / a_mixture - b_ratio) * jnp.log(log_arg)

def flash_cells(fraction, pressure, wilson, attract, co_volume):
    log_k = wilson[:, None] - jnp.log(pressure)[None, :]
    no_flag = jnp.zeros(pressure.shape, jnp.bool_)
    yes_flag = jnp.ones(pressure.shape, jnp.bool_)
    for sweep_index in range(SS_ITERS):
        kvalue = jnp.exp(log_k)
        excess = kvalue - 1.0
        vapour = jnp.full(pressure.shape, 0.5, jnp.float32)
        for newton_step in range(RR_ITERS):
            denominator = 1.0 + vapour * excess
            rr_value = lax.optimization_barrier(jnp.sum(fraction * excess / denominator, 0))
            rr_slope = lax.optimization_barrier(jnp.sum(fraction * excess * excess / (denominator * denominator), 0))
            vapour = jnp.clip(vapour + rr_value / (rr_slope + 0.05), 0.0, 1.0)
        liquid = fraction / (1.0 + vapour * excess)
        vapour_comp = kvalue * liquid
        vapour_comp = vapour_comp / lax.optimization_barrier(jnp.sum(vapour_comp, 0))
        liquid = liquid / lax.optimization_barrier(jnp.sum(liquid, 0))
        mix_liquid = mixture(liquid, pressure, attract, co_volume)
        mix_vapour = mixture(vapour_comp, pressure, attract, co_volume)
        z_liquid = cubic_root(mix_liquid[3], mix_liquid[4], no_flag)
        z_vapour = cubic_root(mix_vapour[3], mix_vapour[4], yes_flag)
        if sweep_index + 1 < SS_ITERS:
            log_k = jnp.clip(fugacity(*mix_liquid, z_liquid, co_volume) - fugacity(*mix_vapour, z_vapour, co_volume), -3.0, 3.0)
    return (vapour, liquid, vapour_comp, z_liquid, z_vapour)

def phase_totals(vapour, liquid, vapour_comp, z_liquid, z_vapour, pressure, amount):
    rho_liquid = pressure / z_liquid
    rho_vapour = pressure / z_vapour
    lam_liquid = (1.0 - vapour) * (1.0 - vapour)
    lam_vapour = 4.0 * vapour * vapour
    mobile = amount * (lam_liquid * rho_liquid * liquid + lam_vapour * rho_vapour * vapour_comp)
    content = amount * ((1.0 - vapour) * rho_liquid * liquid + vapour * rho_vapour * vapour_comp)
    return jnp.concatenate([mobile, content, vapour[None]], 0)

def two_phase(moles, pressure, wilson, attract, co_volume):
    amount = lax.optimization_barrier(jnp.sum(moles, 0))
    fraction = moles / amount
    vapour, liquid, vapour_comp, z_liquid, z_vapour = flash_cells(fraction, pressure, wilson, attract, co_volume)
    return phase_totals(vapour, liquid, vapour_comp, z_liquid, z_vapour, pressure, amount)

def one_phase(moles, pressure, labels, roots, attract, co_volume):
    amount = lax.optimization_barrier(jnp.sum(moles, 0))
    fraction = moles / amount
    mix_single = mixture(fraction, pressure, attract, co_volume)
    z_single = cubic_root(mix_single[3], mix_single[4], roots == 1)
    vapour = labels.astype(jnp.float32)
    return phase_totals(vapour, fraction, fraction, z_single, z_single, pressure, amount)

def neighbours(padded):
    return (padded[..., :-2, 1:-1], padded[..., 2:, 1:-1], padded[..., 1:-1, :-2], padded[..., 1:-1, 2:])

def assemble(mobile_pad, pressure_pad, perm_pad):
    mobile = mobile_pad[:, 1:-1, 1:-1]
    pressure = pressure_pad[1:-1, 1:-1]
    perm = perm_pad[1:-1, 1:-1]
    lam_total = lax.optimization_barrier(jnp.sum(mobile, 0))
    flux_sum = jnp.zeros_like(mobile)
    couplings = []
    for mob_near, pres_near, perm_near in zip(neighbours(mobile_pad), neighbours(pressure_pad), neighbours(perm_pad)):
        transmiss = 2.0 * perm * perm_near / (perm + perm_near)
        flux_sum = flux_sum + transmiss * 0.5 * (mobile + mob_near) * (pressure - pres_near)
        couplings.append(transmiss * 0.5 * (lam_total + lax.optimization_barrier(jnp.sum(mob_near, 0))))
    return (flux_sum, couplings)

def first_step(content, old_content, flux_sum, couplings, pressure):
    residual = content - old_content + TIME_STEP * flux_sum
    pressure_row = lax.optimization_barrier(jnp.sum(residual, 0))
    diagonal = TIME_STEP * (couplings[0] + couplings[1] + couplings[2] + couplings[3]) + lax.optimization_barrier(jnp.sum(content, 0)) / pressure
    return (residual, diagonal, -pressure_row / diagonal)

def second_step(first, first_pad, couplings, diagonal):
    near = neighbours(first_pad)
    off_sum = couplings[0] * near[0] + couplings[1] * near[1] + couplings[2] * near[2] + couplings[3] * near[3]
    return STEP_SCALE * (first + RELAX * TIME_STEP * off_sum / diagonal)

def reference(moles, old_content, pressure, perm, labels, roots, counts, block_ids, wilson, attraction, covolume):
    attract = 0.5 * (attraction + attraction.T)
    block_table = block_ids.reshape(N_DEV, MOST)
    live_slot = jnp.arange(MOST, dtype=jnp.int32)[None, :] < counts[:, None]
    block_hit = (block_table[:, :, None] == jnp.arange(NBLK, dtype=jnp.int32)[None, None, :]) & live_slot[:, :, None]
    two_blocks = jnp.any(block_hit, 1)
    cell_count = LX * FACE
    two_cells = jnp.repeat(two_blocks, BLK, axis=1)
    moles_dev = moles.reshape(NC, N_DEV, cell_count).transpose(1, 0, 2)
    pres_dev = pressure.reshape(N_DEV, cell_count)
    label_dev = labels.reshape(N_DEV, cell_count)
    root_dev = roots.reshape(N_DEV, cell_count)

    def per_device(device_item):
        dev_moles, dev_pres, dev_label, dev_root, dev_two = device_item
        single = one_phase(dev_moles, dev_pres, dev_label, dev_root, attract, covolume)
        double_phase = two_phase(dev_moles, dev_pres, wilson, attract, covolume)
        return jnp.where(dev_two[None, :], double_phase, single)
    properties = lax.map(per_device, (moles_dev, pres_dev, label_dev, root_dev, two_cells))
    properties = properties.transpose(1, 0, 2).reshape(2 * NC + 1, NX, FACE)
    mobile = properties[:NC]
    content = properties[NC:2 * NC]
    vapour = properties[2 * NC]
    mobile_pad = jnp.pad(mobile, ((0, 0), (1, 1), (1, 1)))
    pressure_pad = jnp.pad(pressure, ((1, 1), (1, 1)))
    perm_pad = jnp.pad(perm, ((1, 1), (1, 1)))
    flux_sum, couplings = assemble(mobile_pad, pressure_pad, perm_pad)
    residual, diagonal, first = first_step(content, old_content, flux_sum, couplings, pressure)
    first_pad = jnp.pad(first, ((1, 1), (1, 1)))
    step_out = second_step(first, first_pad, couplings, diagonal)
    return (residual, step_out, vapour)
```

```python
import math

import jax
import jax.numpy as jnp
from jax import lax
from jax.experimental import pallas as pl
from jax.experimental.pallas import tpu as pltpu
from jax.sharding import PartitionSpec as P

BLK = 128
SUB = 8
SS_ITERS = 3
RR_ITERS = 3
Z_ITERS = 5
WIDE = 4

SQRT_TWO = math.sqrt(2.0)
TIME_STEP = 0.5
RELAX = 0.7
STEP_SCALE = 10.0
OFF_SCALE = RELAX * TIME_STEP

EDGE_PRES, EDGE_PERM, EDGE_ROW, EDGE_DIAG, EDGE_LAM = range(5)
EDGE_ROWS = 5
AUX_IN, AUX_LEFT, AUX_RIGHT, AUX_FIRST, AUX_GAIN, AUX_STEP = range(6)
AUX_ROWS = 6


def recip(value):
    return pltpu.reciprocal(value, approx=True)


def split_halves(value):
    high = value.astype(jnp.bfloat16)
    low = (value - high.astype(jnp.float32)).astype(jnp.bfloat16)
    return high, low


def widen(ref_high, ref_low, attraction, covolume, comps):
    cols = comps * SUB
    lane = lax.broadcasted_iota(jnp.int32, (SUB, cols), 1)
    row = lax.broadcasted_iota(jnp.int32, (SUB, cols), 0)
    group = lane // SUB
    diagonal = (lane - group * SUB) == row
    zero = jnp.zeros((SUB, cols), jnp.float32)

    def put(at, values):
        full = zero
        for j in range(comps):
            full = jnp.where(group == j, values[j], full)
        full = jnp.where(diagonal, full, zero)
        high, low = split_halves(full)
        ref_high[at * SUB : (at + 1) * SUB, :] = high.astype(jnp.float32)
        ref_low[at * SUB : (at + 1) * SUB, :] = low.astype(jnp.float32)

    for i in range(comps):
        put(i, [0.5 * (attraction[i, j] + attraction[j, i]) for j in range(comps)])
    put(comps, [covolume[j] for j in range(comps)])
    put(comps + 1, [jnp.float32(1.0)] * comps)


def cubic_pair(big_a, big_b, start, vapour_flag):
    two_b = 2.0 * big_b
    b_square = big_b * big_b
    one_b = 1.0 + big_b
    least = big_b + 0.01
    inv_a = None if vapour_flag is True else recip(big_a)
    z_factor = start
    for _ in range(Z_ITERS):
        spread = z_factor * (z_factor + two_b) - b_square
        if vapour_flag is not False:
            vap = one_b - big_a * (z_factor - big_b) * recip(spread)
        if vapour_flag is not True:
            liq = big_b + spread * (one_b - z_factor) * inv_a
        if vapour_flag is True:
            new = vap
        elif vapour_flag is False:
            new = liq
        else:
            new = jnp.where(vapour_flag, vap, liq)
        z_factor = jnp.minimum(jnp.maximum(0.5 * (z_factor + new), least), 2.0)
    return z_factor


def slab_kernel(
    counts,
    block_ids,
    wilson,
    attraction,
    covolume,
    moles_hbm,
    old_hbm,
    pres_hbm,
    perm_hbm,
    labels_hbm,
    roots_hbm,
    resid_hbm,
    step_hbm,
    vap_hbm,
    top_edge,
    low_edge,
    top_aux,
    low_aux,
    held,
    old,
    mobile,
    pres,
    perm,
    lam,
    first,
    vap,
    scale,
    csum,
    row_sum,
    diag,
    weights,
    pres_flat,
    perm_flat,
    labels,
    roots,
    step,
    w_high,
    w_low,
    w_high_f32,
    w_low_f32,
    x_high,
    x_low,
    sums,
    pack,
    pack_pres,
    excess,
    liquid,
    vapour,
    out_mobile,
    out_content,
    out_cell,
    in_sem,
    old_sem,
    cell_sem,
    out_sem,
):
    comps, layers, face = moles_hbm.shape
    strips = face // BLK
    groups = layers // SUB
    padded = layers + 2 * SUB
    inside = slice(SUB, SUB + layers)

    def lanes_of(k):
        return pl.ds(pl.multiple_of(k * BLK, BLK), BLK)

    def strip_in(source, target, sem, k):
        return pltpu.make_async_copy(source.at[:, :, lanes_of(k)], target.at[:, k], sem.at[k])

    def strip_out(k):
        return pltpu.make_async_copy(old.at[:, k], resid_hbm.at[:, :, lanes_of(k)], out_sem.at[k])

    cell_copies = [
        pltpu.make_async_copy(pres_hbm, pres_flat, cell_sem.at[0]),
        pltpu.make_async_copy(roots_hbm, roots, cell_sem.at[1]),
        pltpu.make_async_copy(labels_hbm, labels, cell_sem.at[2]),
        pltpu.make_async_copy(perm_hbm, perm_flat, cell_sem.at[3]),
    ]
    for copy in cell_copies:
        copy.start()
    for k in range(strips):
        strip_in(moles_hbm, held, in_sem, k).start()
    for k in range(strips):
        strip_in(old_hbm, old, old_sem, k).start()

    widen(w_high_f32, w_low_f32, attraction, covolume, comps)
    w_high[...] = w_high_f32[...].astype(jnp.bfloat16)
    w_low[...] = w_low_f32[...].astype(jnp.bfloat16)
    zero_tile = jnp.zeros((SUB, BLK), jnp.float32)
    zero_strip = jnp.zeros((padded, BLK), jnp.float32)

    def clear(ref, *at):
        for k in (0, strips + 1):
            ref[(*at, k)] = zero_strip
        for k in range(1, strips + 1):
            ref[(*at, k, slice(0, SUB))] = zero_tile
            ref[(*at, k, slice(SUB + layers, padded))] = zero_tile

    for ref in (pres, perm, lam, first):
        clear(ref)
    for i in range(comps):
        clear(mobile, i)
    pack[...] = jnp.ones_like(pack)
    pack_pres[...] = jnp.ones_like(pack_pres)

    def multiply(width):
        high = x_high[:, 0:width]
        sums[:, 0:width] = (
            jnp.dot(w_high[...], high, preferred_element_type=jnp.float32)
            + jnp.dot(w_high[...], x_low[:, 0:width], preferred_element_type=jnp.float32)
            + jnp.dot(w_low[...], high, preferred_element_type=jnp.float32)
        )

    def total(at, start, count):
        rows = slice(at * SUB, (at + 1) * SUB)
        return jnp.concatenate(
            [sums[rows, g * BLK : (g + 1) * BLK] for g in range(start, start + count)], 0
        )

    def put_halves(j, g, pair):
        high, low = split_halves(jnp.concatenate(pair, 0))
        rows = slice(2 * SUB * j, 2 * SUB * (j + 1))
        lanes = slice(g * BLK, (g + 1) * BLK)
        x_high[rows, lanes] = high
        x_low[rows, lanes] = low

    def rows_of(g):
        return slice(g * SUB, (g + 1) * SUB)

    for copy in cell_copies:
        copy.wait()
    for k in range(strips):
        pres[k + 1, inside, :] = pres_flat[:, k * BLK : (k + 1) * BLK]
        perm[k + 1, inside, :] = perm_flat[:, k * BLK : (k + 1) * BLK]

    def single(k, carry):
        strip_in(moles_hbm, held, in_sem, k).wait()
        for j in range(comps // 2):
            for g in range(groups):
                put_halves(j, g, [held[i, k, rows_of(g), :] for i in (2 * j, 2 * j + 1)])
        multiply(groups * BLK)
        quad = held[0, k] * total(0, 0, groups)
        for i in range(1, comps):
            quad = quad + held[i, k] * total(i, 0, groups)
        amount = total(comps + 1, 0, groups)
        pressure = pres[k + 1, inside, :]
        inv_amount = recip(amount)
        big_a = pressure * quad * inv_amount * inv_amount
        big_b = pressure * total(comps, 0, groups) * inv_amount
        is_vapour = roots[:, lanes_of(k)] == 1
        start = jnp.where(is_vapour, 1.0, 2.0 * big_b)
        z_factor = cubic_pair(big_a, big_b, start, is_vapour)
        rho = pressure * recip(z_factor)
        part = labels[:, lanes_of(k)].astype(jnp.float32)
        move = ((1.0 - part) * (1.0 - part) + 4.0 * part * part) * rho
        vap[k] = part
        scale[k] = rho
        csum[k] = amount * rho
        lam[k + 1, inside, :] = amount * move
        for i in range(comps):
            mobile[i, k + 1, inside, :] = held[i, k] * move
        return carry

    lax.fori_loop(0, strips, single, 0)

    batch = WIDE * SUB
    own_count = counts[0]
    held_rows = held.reshape(comps * strips * layers, BLK)
    mobile_rows = mobile.reshape(comps * (strips + 2) * padded, BLK)
    pack_rows = pack.reshape(comps * batch, BLK)
    out_mobile_rows = out_mobile.reshape(comps * batch, BLK)
    out_content_rows = out_content.reshape(comps * batch, BLK)

    def place(slot):
        block = block_ids[slot]
        layer = block // strips
        return block - layer * strips, layer

    def field_at(k, layer):
        return pl.ds(k * layers + layer, comps, stride=strips * layers)

    def mobile_at(k, layer):
        return pl.ds((k + 1) * padded + layer + SUB, comps, stride=(strips + 2) * padded)

    def flash(number, carry):
        base = number * batch
        live = jnp.minimum(own_count - base, batch)

        def gather(r, inner):
            k, layer = place(base + r)
            pack_rows[pl.ds(r, comps, stride=batch), :] = held_rows[field_at(k, layer), :]
            pack_pres[pl.ds(r, 1), :] = pres[k + 1, pl.ds(layer + SUB, 1), :]
            return inner

        lax.fori_loop(0, live, gather, 0)
        pressure = pack_pres[...]
        log_pres = jnp.log(pressure)
        amount = pack[0]
        for i in range(1, comps):
            amount = amount + pack[i]
        inv_amount = recip(amount)
        for i in range(comps):
            pack[i] = pack[i] * inv_amount
        for i in range(comps):
            excess[i] = jnp.exp(wilson[i] - log_pres) - 1.0
        for sweep in range(SS_ITERS):
            part = jnp.full((batch, BLK), 0.5, jnp.float32)
            for _ in range(RR_ITERS):
                value = jnp.zeros((batch, BLK), jnp.float32)
                slope = jnp.full((batch, BLK), 0.05, jnp.float32)
                for i in range(comps):
                    extra = excess[i]
                    ratio = extra * recip(1.0 + part * extra)
                    term = pack[i] * ratio
                    value = value + term
                    slope = slope + term * ratio
                part = jnp.minimum(jnp.maximum(part + value * recip(slope), 0.0), 1.0)
            for j in range(comps // 2):
                liq_two = []
                vap_two = []
                for i in (2 * j, 2 * j + 1):
                    extra = excess[i]
                    liq = pack[i] * recip(1.0 + part * extra)
                    gas = liq + extra * liq
                    liquid[i] = liq
                    vapour[i] = gas
                    liq_two.append(liq)
                    vap_two.append(gas)
                for g in range(WIDE):
                    put_halves(j, g, [value[rows_of(g)] for value in liq_two])
                    put_halves(j, WIDE + g, [value[rows_of(g)] for value in vap_two])
            multiply(2 * WIDE * BLK)
            phases = []
            for values, at, flag in ((liquid, 0, False), (vapour, WIDE, True)):
                quad = values[0] * total(0, at, WIDE)
                for i in range(1, comps):
                    quad = quad + values[i] * total(i, at, WIDE)
                whole = total(comps + 1, at, WIDE)
                inv_whole = recip(whole)
                b_mix = total(comps, at, WIDE) * inv_whole
                a_mix = quad * inv_whole * inv_whole
                big_a = pressure * a_mix
                big_b = pressure * b_mix
                start = jnp.ones_like(big_b) if flag else 2.0 * big_b
                z_factor = cubic_pair(big_a, big_b, start, flag)
                phases.append((quad, whole, inv_whole, a_mix, b_mix, big_b, z_factor))
            if sweep + 1 < SS_ITERS:
                parts = []
                for quad, whole, inv_whole, a_mix, b_mix, big_b, z_factor in phases:
                    log_arg = (z_factor + (1.0 + SQRT_TWO) * big_b) * recip(
                        z_factor + (1.0 - SQRT_TWO) * big_b
                    )
                    inv_b = recip(b_mix)
                    depart = a_mix * inv_b * (1.0 / (2.0 * SQRT_TWO)) * jnp.log(log_arg)
                    of_cov = (z_factor - 1.0 + depart) * inv_b
                    of_sum = 2.0 * depart * whole * recip(quad)
                    parts.append((of_cov, jnp.log(z_factor - big_b), of_sum))
                cov_gap = parts[0][0] - parts[1][0]
                log_gap = parts[0][1] - parts[1][1]
                for i in range(comps):
                    log_k = (
                        covolume[i] * cov_gap
                        - log_gap
                        - parts[0][2] * total(i, 0, WIDE)
                        + parts[1][2] * total(i, WIDE, WIDE)
                    )
                    excess[i] = jnp.exp(jnp.minimum(jnp.maximum(log_k, -3.0), 3.0)) - 1.0
        rho_liq = amount * pressure * recip(phases[0][6])
        rho_vap = amount * pressure * recip(phases[1][6])
        rest = 1.0 - part
        move_liq = rest * rest * rho_liq
        move_vap = 4.0 * part * part * rho_vap
        hold_liq = rest * rho_liq
        hold_vap = part * rho_vap
        out_cell[0] = part
        out_cell[1] = move_liq + move_vap
        out_cell[2] = hold_liq + hold_vap
        move_liq = move_liq * phases[0][2]
        move_vap = move_vap * phases[1][2]
        hold_liq = hold_liq * phases[0][2]
        hold_vap = hold_vap * phases[1][2]
        for i in range(comps):
            out_mobile[i] = move_liq * liquid[i] + move_vap * vapour[i]
            out_content[i] = hold_liq * liquid[i] + hold_vap * vapour[i]

        def scatter(r, inner):
            k, layer = place(base + r)
            of = pl.ds(r, comps, stride=batch)
            held_rows[field_at(k, layer), :] = out_content_rows[of, :]
            mobile_rows[mobile_at(k, layer), :] = out_mobile_rows[of, :]
            one = pl.ds(r, 1)
            row = pl.ds(layer, 1)
            vap[k, row, :] = out_cell[0, one, :]
            lam[k + 1, pl.ds(layer + SUB, 1), :] = out_cell[1, one, :]
            csum[k, row, :] = out_cell[2, one, :]
            scale[k, row, :] = jnp.ones((1, BLK), jnp.float32)
            return inner

        lax.fori_loop(0, live, scatter, 0)
        return carry

    lax.fori_loop(0, (own_count + batch - 1) // batch, flash, 0)
    for k in range(strips):
        pres_flat[:, k * BLK : (k + 1) * BLK] = vap[k]
    vap_copy = pltpu.make_async_copy(pres_flat, vap_hbm, cell_sem.at[0])
    vap_copy.start()

    lane_index = lax.broadcasted_iota(jnp.int32, (SUB, BLK), 1)
    is_last_lane = lane_index == BLK - 1
    is_first_lane = lane_index == 0

    def around(load, k, g):
        at = SUB * (g + 1)
        here = load(k + 1, slice(at, at + SUB))
        up = load(k + 1, slice(at - 1, at + SUB - 1))
        down = load(k + 1, slice(at + 1, at + SUB + 1))
        before = load(k, slice(at, at + SUB))
        after = load(k + 2, slice(at, at + SUB))
        left = pltpu.roll(jnp.where(is_last_lane, before, here), 1, 1)
        right = pltpu.roll(jnp.where(is_first_lane, after, here), BLK - 1, 1)
        return here, (up, down, left, right)

    def fluxes(k, carry):
        strip_in(old_hbm, old, old_sem, k).wait()
        for g in range(groups):
            rows = rows_of(g)
            p_here, p_near = around(lambda s, r: pres[s, r, :], k, g)
            k_here, k_near = around(lambda s, r: perm[s, r, :], k, g)
            l_here, l_near = around(lambda s, r: lam[s, r, :], k, g)
            drives = []
            couplings = []
            for n in range(4):
                transmiss = k_here * k_near[n] * recip(k_here + k_near[n])
                drives.append((TIME_STEP * transmiss) * (p_here - p_near[n]))
                couplings.append(transmiss * (l_here + l_near[n]))
            drive_sum = (drives[0] + drives[1]) + (drives[2] + drives[3])
            content_scale = scale[k, rows, :]
            row_total = zero_tile
            for i in range(comps):
                m_here, m_near = around(lambda s, r, i=i: mobile[i, s, r, :], k, g)
                value = held[i, k, rows, :] * content_scale - old[i, k, rows, :]
                value = value + drive_sum * m_here
                value = value + (drives[0] * m_near[0] + drives[1] * m_near[1])
                value = value + (drives[2] * m_near[2] + drives[3] * m_near[3])
                old[i, k, rows, :] = value
                row_total = row_total + value
            diagonal = TIME_STEP * (
                (couplings[0] + couplings[1]) + (couplings[2] + couplings[3])
            ) + csum[k, rows, :] * recip(p_here)
            inv_diag = recip(diagonal)
            row_sum[k, rows, :] = row_total
            diag[k, rows, :] = diagonal
            first[k + 1, SUB * (g + 1) : SUB * (g + 2), :] = -row_total * inv_diag
            gain = (STEP_SCALE * OFF_SCALE) * inv_diag
            for n in range(4):
                weights[n, k, rows, :] = couplings[n] * gain
        strip_out(k).start()
        return carry

    lax.fori_loop(0, strips, fluxes, 0)

    def steps(k, carry):
        for g in range(groups):
            rows = rows_of(g)
            here, near = around(lambda s, r: first[s, r, :], k, g)
            step[rows, lanes_of(k)] = (
                STEP_SCALE * here
                + (weights[0, k, rows, :] * near[0] + weights[1, k, rows, :] * near[1])
                + (weights[2, k, rows, :] * near[2] + weights[3, k, rows, :] * near[3])
            )
        return carry

    lax.fori_loop(0, strips, steps, 0)
    step_copy = pltpu.make_async_copy(step, step_hbm, cell_sem.at[1])
    step_copy.start()

    old_rows = old.reshape(comps * strips * layers, BLK)
    for edge, aux, at, inner, toward, away in (
        (top_edge, top_aux, 0, 1, 0, 1),
        (low_edge, low_aux, layers - 1, layers - 2, 1, 0),
    ):
        for k in range(strips):
            lanes = slice(k * BLK, (k + 1) * BLK)
            here = slice(at, at + 1)
            pad_here = slice(SUB + at, SUB + at + 1)
            edge[0:comps, lanes] = mobile_rows[mobile_at(k, at), :]
            aux[0:comps, lanes] = old_rows[field_at(k, at), :]
            unscale = diag[k, here, :]
            edge_values = [None] * EDGE_ROWS
            edge_values[EDGE_PRES] = pres[k + 1, pad_here, :]
            edge_values[EDGE_PERM] = perm[k + 1, pad_here, :]
            edge_values[EDGE_ROW] = row_sum[k, here, :]
            edge_values[EDGE_DIAG] = unscale
            edge_values[EDGE_LAM] = lam[k + 1, pad_here, :]
            aux_values = [None] * AUX_ROWS
            aux_values[AUX_IN] = weights[away, k, here, :] * unscale
            aux_values[AUX_LEFT] = weights[2, k, here, :] * unscale
            aux_values[AUX_RIGHT] = weights[3, k, here, :] * unscale
            aux_values[AUX_FIRST] = first[k + 1, SUB + inner : SUB + inner + 1, :]
            aux_values[AUX_GAIN] = weights[toward, k, inner : inner + 1, :]
            aux_values[AUX_STEP] = step[inner : inner + 1, lanes]
            for n, value in enumerate(edge_values):
                edge[comps + n : comps + n + 1, lanes] = value
            for n, value in enumerate(aux_values):
                aux[comps + n : comps + n + 1, lanes] = value

    vap_copy.wait()
    step_copy.wait()
    for k in range(strips):
        strip_out(k).wait()


def edge_kernel(
    top_edge,
    low_edge,
    top_aux,
    low_aux,
    from_prev,
    from_next,
    resid_in,
    step_in,
    resid_hbm,
    step_hbm,
    resid,
    step,
    sem,
):
    comps, layers, face = resid_hbm.shape
    copies = []
    for n, (edge, aux, other, at, inner) in enumerate(
        (
            (top_edge, top_aux, from_prev, 0, 1),
            (low_edge, low_aux, from_next, layers - 1, layers - 2),
        )
    ):

        def own(index):
            return edge[comps + index : comps + index + 1, :]

        def far(index):
            return other[comps + index : comps + index + 1, :]

        def near(index):
            return aux[comps + index : comps + index + 1, :]

        perm, perm_far = own(EDGE_PERM), far(EDGE_PERM)
        transmiss = perm * perm_far / (perm + perm_far)
        drive = TIME_STEP * transmiss * (own(EDGE_PRES) - far(EDGE_PRES))
        lam_both = own(EDGE_LAM) + far(EDGE_LAM)
        coupling = transmiss * lam_both
        row = own(EDGE_ROW) + drive * lam_both
        row_far = far(EDGE_ROW) - drive * lam_both
        diag = own(EDGE_DIAG) + TIME_STEP * coupling
        diag_far = far(EDGE_DIAG) + TIME_STEP * coupling
        diag_far = jnp.where(diag_far == 0.0, 1.0, diag_far)
        first = -row / diag
        first_old = -own(EDGE_ROW) / own(EDGE_DIAG)
        first_far = -row_far / diag_far
        off = (
            (STEP_SCALE * OFF_SCALE) * coupling * first_far
            + near(AUX_IN) * near(AUX_FIRST)
            + near(AUX_LEFT) * pltpu.roll(first, 1, 1)
            + near(AUX_RIGHT) * pltpu.roll(first, face - 1, 1)
        )
        least = min(at, inner)
        step[n, at - least : at - least + 1, :] = STEP_SCALE * first + off / diag
        step[n, inner - least : inner - least + 1, :] = near(AUX_STEP) + near(AUX_GAIN) * (
            first - first_old
        )
        resid[n] = aux[0:comps, :] + drive * (edge[0:comps, :] + other[0:comps, :])
        for source, target in (
            (resid.at[n], resid_hbm.at[:, at, :]),
            (step.at[n, 0:2, :], step_hbm.at[least : least + 2, :]),
        ):
            copies.append(pltpu.make_async_copy(source, target, sem.at[len(copies)]))
            copies[-1].start()
    for copy in copies:
        copy.wait()


def on_device(
    moles,
    old_content,
    pressure,
    perm,
    labels,
    roots,
    counts,
    block_ids,
    wilson,
    attraction,
    covolume,
):
    comps, layers, face = moles.shape
    f32 = jnp.float32
    strips = face // BLK
    rows_sum = (comps + 2) * SUB
    rows_in = comps * SUB
    widest = max(layers // SUB, 2 * WIDE) * BLK
    smem = pl.BlockSpec(memory_space=pltpu.SMEM)
    vmem = pl.BlockSpec(memory_space=pltpu.VMEM)
    hbm = pl.BlockSpec(memory_space=pl.ANY)
    padded = layers + 2 * SUB
    flat = pltpu.VMEM((layers, face), f32)
    flat_int = pltpu.VMEM((layers, face), jnp.int32)
    cell = pltpu.VMEM((strips, layers, BLK), f32)
    cell_pad = pltpu.VMEM((strips + 2, padded, BLK), f32)
    field = pltpu.VMEM((comps, strips, layers, BLK), f32)
    field_pad = pltpu.VMEM((comps, strips + 2, padded, BLK), f32)
    packed = pltpu.VMEM((comps, WIDE * SUB, BLK), f32)
    edge_shape = jax.ShapeDtypeStruct((comps + EDGE_ROWS, face), f32)
    aux_shape = jax.ShapeDtypeStruct((comps + AUX_ROWS, face), f32)
    field_shape = jax.ShapeDtypeStruct((comps, layers, face), f32)
    cell_shape = jax.ShapeDtypeStruct((layers, face), f32)
    residual, step, vapour, top_edge, low_edge, top_aux, low_aux = pl.pallas_call(
        slab_kernel,
        out_shape=[field_shape, cell_shape, cell_shape]
        + [edge_shape, edge_shape, aux_shape, aux_shape],
        in_specs=[smem] * 5 + [hbm] * 6,
        out_specs=[hbm] * 3 + [vmem] * 4,
        scratch_shapes=[field, field, field_pad]
        + [cell_pad] * 4
        + [cell] * 5
        + [pltpu.VMEM((4, strips, layers, BLK), f32)]
        + [flat, flat, flat_int, flat_int, flat]
        + [pltpu.VMEM((rows_sum, rows_in), jnp.bfloat16)] * 2
        + [pltpu.VMEM((rows_sum, rows_in), f32)] * 2
        + [pltpu.VMEM((rows_in, widest), jnp.bfloat16)] * 2
        + [pltpu.VMEM((rows_sum, widest), f32)]
        + [packed, pltpu.VMEM((WIDE * SUB, BLK), f32)]
        + [packed] * 5
        + [pltpu.VMEM((3, WIDE * SUB, BLK), f32)]
        + [
            pltpu.SemaphoreType.DMA((strips,)),
            pltpu.SemaphoreType.DMA((strips,)),
            pltpu.SemaphoreType.DMA((4,)),
            pltpu.SemaphoreType.DMA((strips,)),
        ],
        compiler_params=pltpu.CompilerParams(vmem_limit_bytes=48 * 1024 * 1024),
        name="slab",
    )(
        counts,
        block_ids,
        wilson,
        attraction,
        covolume,
        moles,
        old_content,
        pressure,
        perm,
        labels,
        roots,
    )
    ends = lax.axis_size("dev") - 1
    from_prev = lax.ppermute(low_edge, "dev", [(i, i + 1) for i in range(ends)])
    from_next = lax.ppermute(top_edge, "dev", [(i + 1, i) for i in range(ends)])
    residual, step = pl.pallas_call(
        edge_kernel,
        out_shape=[field_shape, cell_shape],
        in_specs=[vmem] * 6 + [hbm] * 2,
        out_specs=[hbm] * 2,
        input_output_aliases={6: 0, 7: 1},
        scratch_shapes=[
            pltpu.VMEM((2, comps, face), f32),
            pltpu.VMEM((2, SUB, face), f32),
            pltpu.SemaphoreType.DMA((4,)),
        ],
        compiler_params=pltpu.CompilerParams(vmem_limit_bytes=16 * 1024 * 1024),
        name="edges",
    )(top_edge, low_edge, top_aux, low_aux, from_prev, from_next, residual, step)
    return (residual, step, vapour)


def solution(mesh):
    in_specs = (
        P(None, "dev", None),
        P(None, "dev", None),
        P("dev", None),
        P("dev", None),
        P("dev", None),
        P("dev", None),
        P("dev"),
        P("dev"),
        P(),
        P(),
        P(),
    )
    out_specs = (P(None, "dev", None), P("dev", None), P("dev", None))
    return jax.shard_map(
        on_device, mesh=mesh, in_specs=in_specs, out_specs=out_specs, check_vma=False
    )
```

```python
import math

import jax
import jax.numpy as jnp
from jax import lax
from jax.experimental import pallas as pl
from jax.experimental.pallas import tpu as pltpu
from jax.sharding import PartitionSpec as P

BLK = 128
SUB = 8
SS_ITERS = 3
RR_ITERS = 3
Z_ITERS = 5
WIDE = 8
TINY = 1e-30

SQRT_TWO = math.sqrt(2.0)
TIME_STEP = 0.5
RELAX = 0.7
STEP_SCALE = 10.0
OFF_SCALE = RELAX * TIME_STEP

EDGE_PRES, EDGE_PERM, EDGE_ROW, EDGE_DIAG, EDGE_LAM = range(5)
EDGE_ROWS = 5
AUX_IN, AUX_LEFT, AUX_RIGHT, AUX_FIRST, AUX_GAIN, AUX_STEP = range(6)
AUX_ROWS = 6


def recip(value):
    return pltpu.reciprocal(value, approx=True)


def split_halves(value):
    high = value.astype(jnp.bfloat16)
    low = (value - high.astype(jnp.float32)).astype(jnp.bfloat16)
    return high, low


def widen(stack, attraction, comps):
    cols = comps * SUB
    lane = lax.broadcasted_iota(jnp.int32, (SUB, cols), 1)
    row = lax.broadcasted_iota(jnp.int32, (SUB, cols), 0)
    group = lane // SUB
    diagonal = (lane - group * SUB) == row
    zero = jnp.zeros((SUB, cols), jnp.float32)
    for pair in range(comps // 2):
        rows = []
        for i in (2 * pair, 2 * pair + 1):
            full = zero
            for j in range(comps):
                full = jnp.where(group == j, 0.5 * (attraction[i, j] + attraction[j, i]), full)
            rows.append(jnp.where(diagonal, full, zero))
        high, low = split_halves(jnp.concatenate(rows, 0))
        at = 2 * SUB * pair
        stack[at : at + 2 * SUB, :] = high
        stack[cols + at : cols + at + 2 * SUB, :] = low


def cubic_pair(big_a, big_b, start, vapour_flag):
    two_b = 2.0 * big_b
    b_square = big_b * big_b
    one_b = 1.0 + big_b
    least = big_b + 0.01
    half_b = 0.5 * big_b
    half_one_b = 0.5 * one_b
    half_a = 0.5 * big_a
    half_inv_a = None if vapour_flag is True else 0.5 * recip(big_a)
    z_factor = start
    for _ in range(Z_ITERS):
        spread = z_factor * (z_factor + two_b) - b_square
        half_z = 0.5 * z_factor
        if vapour_flag is not False:
            vap = (half_z + half_one_b) - half_a * (z_factor - big_b) * recip(spread)
        if vapour_flag is not True:
            liq = (half_z + half_b) + spread * (one_b - z_factor) * half_inv_a
        if vapour_flag is True:
            new = vap
        elif vapour_flag is False:
            new = liq
        else:
            new = jnp.where(vapour_flag, vap, liq)
        z_factor = jnp.minimum(jnp.maximum(new, least), 2.0)
    return z_factor


def slab_kernel(
    counts_hbm,
    block_ids_hbm,
    wilson_hbm,
    attraction_hbm,
    covolume_hbm,
    moles_hbm,
    old_hbm,
    pres_hbm,
    perm_hbm,
    labels_hbm,
    roots_hbm,
    resid_hbm,
    step_hbm,
    vap_hbm,
    top_edge,
    low_edge,
    top_aux,
    low_aux,
    held,
    old,
    mobile,
    pres,
    perm,
    lam,
    first,
    vap,
    scale,
    csum,
    row_sum,
    diag,
    weights,
    pres_flat,
    perm_flat,
    labels,
    roots,
    step,
    w_stack,
    x_high,
    x_low,
    sums,
    pack,
    pack_pres,
    inv_excess,
    liquid,
    vapour,
    out_cell,
    counts,
    block_ids,
    wilson,
    attraction,
    covolume,
    in_sem,
    old_sem,
    cell_sem,
    table_sem,
    out_sem,
):
    comps, layers, face = moles_hbm.shape
    strips = face // BLK
    groups = layers // SUB
    padded = layers + 2 * SUB
    inside = slice(SUB, SUB + layers)

    def lanes_of(k):
        return pl.ds(pl.multiple_of(k * BLK, BLK), BLK)

    def strip_in(source, target, sem, k):
        return pltpu.make_async_copy(source.at[:, :, lanes_of(k)], target.at[:, k], sem.at[k])

    def strip_out(k):
        return pltpu.make_async_copy(old.at[:, k], resid_hbm.at[:, :, lanes_of(k)], out_sem.at[k])

    cell_copies = [
        pltpu.make_async_copy(pres_hbm, pres_flat, cell_sem.at[0]),
        pltpu.make_async_copy(roots_hbm, roots, cell_sem.at[1]),
        pltpu.make_async_copy(labels_hbm, labels, cell_sem.at[2]),
        pltpu.make_async_copy(perm_hbm, perm_flat, cell_sem.at[3]),
    ]
    table_copies = [
        pltpu.make_async_copy(source, target, table_sem.at[n])
        for n, (source, target) in enumerate(
            (
                (attraction_hbm, attraction),
                (covolume_hbm, covolume),
                (wilson_hbm, wilson),
                (counts_hbm, counts),
                (block_ids_hbm, block_ids),
            )
        )
    ]
    for copy in table_copies + cell_copies:
        copy.start()
    for k in range(strips):
        strip_in(moles_hbm, held, in_sem, k).start()
    for k in range(strips):
        strip_in(old_hbm, old, old_sem, k).start()

    zero_tile = jnp.zeros((SUB, BLK), jnp.float32)
    zero_strip = jnp.zeros((padded, BLK), jnp.float32)

    def clear(ref, *at):
        for k in (0, strips + 1):
            ref[(*at, k)] = zero_strip
        for k in range(1, strips + 1):
            ref[(*at, k, slice(0, SUB))] = zero_tile
            ref[(*at, k, slice(SUB + layers, padded))] = zero_tile

    for ref in (pres, perm, lam, first):
        clear(ref)
    for i in range(comps):
        clear(mobile, i)
    for copy in table_copies:
        copy.wait()
    widen(w_stack, attraction, comps)

    cols = comps * SUB

    def multiply(width, with_low):
        both = jnp.dot(w_stack[...], x_high[:, 0:width], preferred_element_type=jnp.float32)
        result = both[0:cols] + both[cols : 2 * cols]
        if with_low:
            result = result + jnp.dot(
                w_stack[0:cols, :], x_low[:, 0:width], preferred_element_type=jnp.float32
            )
        sums[:, 0:width] = result

    def total(at, start, count):
        rows = slice(at * SUB, (at + 1) * SUB)
        return jnp.concatenate(
            [sums[rows, g * BLK : (g + 1) * BLK] for g in range(start, start + count)], 0
        )

    def put_halves(j, g, pair, with_low):
        value = jnp.concatenate(pair, 0)
        rows = slice(2 * SUB * j, 2 * SUB * (j + 1))
        lanes = slice(g * BLK, (g + 1) * BLK)
        high = value.astype(jnp.bfloat16)
        x_high[rows, lanes] = high
        if with_low:
            x_low[rows, lanes] = (value - high.astype(jnp.float32)).astype(jnp.bfloat16)

    def quadratic(values, start, count, with_low):
        quad = None
        for i in range(comps):
            value = values(i)
            if not with_low:
                high = value.astype(jnp.bfloat16).astype(jnp.float32)
                value = value + (value - high)
            term = value * total(i, start, count)
            quad = term if quad is None else quad + term
        return quad

    def rows_of(g):
        return slice(g * SUB, (g + 1) * SUB)

    for copy in cell_copies:
        copy.wait()
    for k in range(strips):
        pres[k + 1, inside, :] = pres_flat[:, k * BLK : (k + 1) * BLK]
        perm[k + 1, inside, :] = perm_flat[:, k * BLK : (k + 1) * BLK]

    def single(k, carry):
        strip_in(moles_hbm, held, in_sem, k).wait()
        for j in range(comps // 2):
            for g in range(groups):
                pair = [held[i, k, rows_of(g), :] for i in (2 * j, 2 * j + 1)]
                put_halves(j, g, pair, False)
        multiply(groups * BLK, False)
        amount = held[0, k]
        b_sum = covolume[0] * amount
        for i in range(1, comps):
            value = held[i, k]
            amount = amount + value
            b_sum = b_sum + covolume[i] * value
        quad = quadratic(lambda i: held[i, k], 0, groups, False)
        pressure = pres[k + 1, inside, :]
        inv_amount = recip(amount)
        big_a = pressure * quad * inv_amount * inv_amount
        big_b = pressure * b_sum * inv_amount
        is_vapour = roots[:, lanes_of(k)] == 1
        start = jnp.where(is_vapour, 1.0, 2.0 * big_b)
        z_factor = cubic_pair(big_a, big_b, start, is_vapour)
        rho = pressure * recip(z_factor)
        part = labels[:, lanes_of(k)].astype(jnp.float32)
        move = ((1.0 - part) * (1.0 - part) + 4.0 * part * part) * rho
        vap[k] = part
        scale[k] = rho
        csum[k] = amount * rho
        lam[k + 1, inside, :] = amount * move
        for i in range(comps):
            mobile[i, k + 1, inside, :] = held[i, k] * move
        return carry

    lax.fori_loop(0, strips, single, 0)

    batch = WIDE * SUB
    own_count = counts[0]
    held_rows = held.reshape(comps * strips * layers, BLK)
    mobile_rows = mobile.reshape(comps * (strips + 2) * padded, BLK)
    pack_rows = pack.reshape(comps * batch, BLK)
    liquid_rows = liquid.reshape(comps * batch, BLK)
    vapour_rows = vapour.reshape(comps * batch, BLK)
    bits = strips.bit_length() - 1

    def place(slot):
        block = block_ids[jnp.minimum(slot, own_count - 1)]
        layer = lax.shift_right_logical(block, bits)
        return block - lax.shift_left(layer, bits), layer

    def field_at(k, layer):
        return pl.ds(k * layers + layer, comps, stride=strips * layers)

    def mobile_at(k, layer):
        return pl.ds((k + 1) * padded + layer + SUB, comps, stride=(strips + 2) * padded)

    def flash(number, carry):
        base = number * batch
        places = [place(base + r) for r in range(batch)]
        for r, (k, layer) in enumerate(places):
            pack_rows[pl.ds(r, comps, stride=batch), :] = held_rows[field_at(k, layer), :]
            pack_pres[r : r + 1, :] = pres[k + 1, pl.ds(layer + SUB, 1), :]
        pressure = pack_pres[...]
        log_pres = jnp.log(pressure)
        amount = pack[0]
        for i in range(1, comps):
            amount = amount + pack[i]
        inv_amount = recip(amount)
        for i in range(comps):
            pack[i] = pack[i] * inv_amount

        def keep_k(i, log_k):
            inv_excess[i] = recip((jnp.exp(log_k) - 1.0) + TINY)

        for i in range(comps):
            keep_k(i, wilson[i] - log_pres)
        for sweep in range(SS_ITERS):
            with_low = sweep + 1 < SS_ITERS
            part = jnp.full((batch, BLK), 0.5, jnp.float32)
            for _ in range(RR_ITERS):
                value = jnp.zeros((batch, BLK), jnp.float32)
                slope = jnp.full((batch, BLK), 0.05, jnp.float32)
                for i in range(comps):
                    ratio = recip(inv_excess[i] + part)
                    term = pack[i] * ratio
                    value = value + term
                    slope = slope + term * ratio
                part = jnp.minimum(jnp.maximum(part + value * recip(slope), 0.0), 1.0)
            sums_of = [[None, None], [None, None]]
            for j in range(comps // 2):
                liq_two = []
                vap_two = []
                for i in (2 * j, 2 * j + 1):
                    term = pack[i] * recip(inv_excess[i] + part)
                    liq = pack[i] - part * term
                    gas = liq + term
                    liquid[i] = liq
                    vapour[i] = gas
                    liq_two.append(liq)
                    vap_two.append(gas)
                    for acc, value in zip(sums_of, (liq, gas)):
                        scaled = covolume[i] * value
                        acc[0] = value if acc[0] is None else acc[0] + value
                        acc[1] = scaled if acc[1] is None else acc[1] + scaled
                for g in range(WIDE):
                    put_halves(j, g, [value[rows_of(g)] for value in liq_two], with_low)
                    put_halves(j, WIDE + g, [value[rows_of(g)] for value in vap_two], with_low)
            multiply(2 * WIDE * BLK, with_low)
            phases = []
            for values, at, flag, (whole, b_sum) in (
                (liquid, 0, False, sums_of[0]),
                (vapour, WIDE, True, sums_of[1]),
            ):
                quad = quadratic(lambda i: values[i], at, WIDE, with_low)
                inv_whole = recip(whole)
                b_mix = b_sum * inv_whole
                a_mix = quad * inv_whole * inv_whole
                big_a = pressure * a_mix
                big_b = pressure * b_mix
                start = jnp.ones_like(big_b) if flag else 2.0 * big_b
                z_factor = cubic_pair(big_a, big_b, start, flag)
                phases.append((quad, whole, inv_whole, a_mix, b_mix, big_b, z_factor))
            if sweep + 1 < SS_ITERS:
                parts = []
                for quad, whole, inv_whole, a_mix, b_mix, big_b, z_factor in phases:
                    log_arg = (z_factor + (1.0 + SQRT_TWO) * big_b) * recip(
                        z_factor + (1.0 - SQRT_TWO) * big_b
                    )
                    inv_b = recip(b_mix)
                    depart = a_mix * inv_b * (1.0 / (2.0 * SQRT_TWO)) * jnp.log(log_arg)
                    of_cov = (z_factor - 1.0 + depart) * inv_b
                    of_sum = 2.0 * depart * whole * recip(quad)
                    parts.append((of_cov, jnp.log(z_factor - big_b), of_sum))
                cov_gap = parts[0][0] - parts[1][0]
                log_gap = parts[0][1] - parts[1][1]
                for i in range(comps):
                    log_k = (
                        covolume[i] * cov_gap
                        - log_gap
                        - parts[0][2] * total(i, 0, WIDE)
                        + parts[1][2] * total(i, WIDE, WIDE)
                    )
                    keep_k(i, jnp.minimum(jnp.maximum(log_k, -3.0), 3.0))
        rho_liq = amount * pressure * recip(phases[0][6])
        rho_vap = amount * pressure * recip(phases[1][6])
        rest = 1.0 - part
        move_liq = rest * rest * rho_liq
        move_vap = 4.0 * part * part * rho_vap
        hold_liq = rest * rho_liq
        hold_vap = part * rho_vap
        out_cell[0] = part
        out_cell[1] = move_liq + move_vap
        out_cell[2] = hold_liq + hold_vap
        move_liq = move_liq * phases[0][2]
        move_vap = move_vap * phases[1][2]
        hold_liq = hold_liq * phases[0][2]
        hold_vap = hold_vap * phases[1][2]
        for i in range(comps):
            liq, gas = liquid[i], vapour[i]
            liquid[i] = move_liq * liq + move_vap * gas
            vapour[i] = hold_liq * liq + hold_vap * gas
        one_row = jnp.ones((1, BLK), jnp.float32)
        for r, (k, layer) in enumerate(places):
            of = pl.ds(r, comps, stride=batch)
            mobile_rows[mobile_at(k, layer), :] = liquid_rows[of, :]
            held_rows[field_at(k, layer), :] = vapour_rows[of, :]
            one = slice(r, r + 1)
            row = pl.ds(layer, 1)
            vap[k, row, :] = out_cell[0, one, :]
            lam[k + 1, pl.ds(layer + SUB, 1), :] = out_cell[1, one, :]
            csum[k, row, :] = out_cell[2, one, :]
            scale[k, row, :] = one_row
        return carry

    lax.fori_loop(0, (own_count + batch - 1) // batch, flash, 0)
    for k in range(strips):
        pres_flat[:, k * BLK : (k + 1) * BLK] = vap[k]
    vap_copy = pltpu.make_async_copy(pres_flat, vap_hbm, cell_sem.at[0])
    vap_copy.start()

    lane_index = lax.broadcasted_iota(jnp.int32, (SUB, BLK), 1)
    is_last_lane = lane_index == BLK - 1
    is_first_lane = lane_index == 0

    def around(load, k, g):
        at = SUB * (g + 1)
        here = load(k + 1, slice(at, at + SUB))
        up = load(k + 1, slice(at - 1, at + SUB - 1))
        down = load(k + 1, slice(at + 1, at + SUB + 1))
        before = load(k, slice(at, at + SUB))
        after = load(k + 2, slice(at, at + SUB))
        left = pltpu.roll(jnp.where(is_last_lane, before, here), 1, 1)
        right = pltpu.roll(jnp.where(is_first_lane, after, here), BLK - 1, 1)
        return here, (up, down, left, right)

    def fluxes(k, carry):
        strip_in(old_hbm, old, old_sem, k).wait()
        for g in range(groups):
            rows = rows_of(g)
            p_here, p_near = around(lambda s, r: pres[s, r, :], k, g)
            k_here, k_near = around(lambda s, r: perm[s, r, :], k, g)
            l_here, l_near = around(lambda s, r: lam[s, r, :], k, g)
            drives = []
            couplings = []
            for n in range(4):
                transmiss = k_here * k_near[n] * recip(k_here + k_near[n])
                drives.append((TIME_STEP * transmiss) * (p_here - p_near[n]))
                couplings.append(transmiss * (l_here + l_near[n]))
            drive_sum = (drives[0] + drives[1]) + (drives[2] + drives[3])
            content_scale = scale[k, rows, :]
            row_total = zero_tile
            for i in range(comps):
                m_here, m_near = around(lambda s, r, i=i: mobile[i, s, r, :], k, g)
                value = held[i, k, rows, :] * content_scale - old[i, k, rows, :]
                value = value + drive_sum * m_here
                value = value + (drives[0] * m_near[0] + drives[1] * m_near[1])
                value = value + (drives[2] * m_near[2] + drives[3] * m_near[3])
                old[i, k, rows, :] = value
                row_total = row_total + value
            diagonal = TIME_STEP * (
                (couplings[0] + couplings[1]) + (couplings[2] + couplings[3])
            ) + csum[k, rows, :] * recip(p_here)
            inv_diag = recip(diagonal)
            row_sum[k, rows, :] = row_total
            diag[k, rows, :] = diagonal
            first[k + 1, SUB * (g + 1) : SUB * (g + 2), :] = -row_total * inv_diag
            gain = (STEP_SCALE * OFF_SCALE) * inv_diag
            for n in range(4):
                weights[n, k, rows, :] = couplings[n] * gain
        strip_out(k).start()
        return carry

    lax.fori_loop(0, strips, fluxes, 0)

    def steps(k, carry):
        for g in range(groups):
            rows = rows_of(g)
            here, near = around(lambda s, r: first[s, r, :], k, g)
            step[rows, lanes_of(k)] = (
                STEP_SCALE * here
                + (weights[0, k, rows, :] * near[0] + weights[1, k, rows, :] * near[1])
                + (weights[2, k, rows, :] * near[2] + weights[3, k, rows, :] * near[3])
            )
        return carry

    lax.fori_loop(0, strips, steps, 0)
    step_copy = pltpu.make_async_copy(step, step_hbm, cell_sem.at[1])
    step_copy.start()

    old_rows = old.reshape(comps * strips * layers, BLK)
    for edge, aux, at, inner, toward, away in (
        (top_edge, top_aux, 0, 1, 0, 1),
        (low_edge, low_aux, layers - 1, layers - 2, 1, 0),
    ):
        for k in range(strips):
            lanes = slice(k * BLK, (k + 1) * BLK)
            here = slice(at, at + 1)
            pad_here = slice(SUB + at, SUB + at + 1)
            edge[0:comps, lanes] = mobile_rows[mobile_at(k, at), :]
            aux[0:comps, lanes] = old_rows[field_at(k, at), :]
            unscale = diag[k, here, :]
            edge_values = [None] * EDGE_ROWS
            edge_values[EDGE_PRES] = pres[k + 1, pad_here, :]
            edge_values[EDGE_PERM] = perm[k + 1, pad_here, :]
            edge_values[EDGE_ROW] = row_sum[k, here, :]
            edge_values[EDGE_DIAG] = unscale
            edge_values[EDGE_LAM] = lam[k + 1, pad_here, :]
            aux_values = [None] * AUX_ROWS
            aux_values[AUX_IN] = weights[away, k, here, :] * unscale
            aux_values[AUX_LEFT] = weights[2, k, here, :] * unscale
            aux_values[AUX_RIGHT] = weights[3, k, here, :] * unscale
            aux_values[AUX_FIRST] = first[k + 1, SUB + inner : SUB + inner + 1, :]
            aux_values[AUX_GAIN] = weights[toward, k, inner : inner + 1, :]
            aux_values[AUX_STEP] = step[inner : inner + 1, lanes]
            for n, value in enumerate(edge_values):
                edge[comps + n : comps + n + 1, lanes] = value
            for n, value in enumerate(aux_values):
                aux[comps + n : comps + n + 1, lanes] = value

    vap_copy.wait()
    step_copy.wait()
    for k in range(strips):
        strip_out(k).wait()


def edge_kernel(
    top_edge,
    low_edge,
    top_aux,
    low_aux,
    from_prev,
    from_next,
    resid_in,
    step_in,
    resid_hbm,
    step_hbm,
    resid,
    step,
    sem,
):
    comps, layers, face = resid_hbm.shape
    copies = []
    for n, (edge, aux, other, at, inner) in enumerate(
        (
            (top_edge, top_aux, from_prev, 0, 1),
            (low_edge, low_aux, from_next, layers - 1, layers - 2),
        )
    ):

        def own(index):
            return edge[comps + index : comps + index + 1, :]

        def far(index):
            return other[comps + index : comps + index + 1, :]

        def near(index):
            return aux[comps + index : comps + index + 1, :]

        perm, perm_far = own(EDGE_PERM), far(EDGE_PERM)
        transmiss = perm * perm_far / (perm + perm_far)
        drive = TIME_STEP * transmiss * (own(EDGE_PRES) - far(EDGE_PRES))
        lam_both = own(EDGE_LAM) + far(EDGE_LAM)
        coupling = transmiss * lam_both
        row = own(EDGE_ROW) + drive * lam_both
        row_far = far(EDGE_ROW) - drive * lam_both
        diag = own(EDGE_DIAG) + TIME_STEP * coupling
        diag_far = far(EDGE_DIAG) + TIME_STEP * coupling
        diag_far = jnp.where(diag_far == 0.0, 1.0, diag_far)
        first = -row / diag
        first_old = -own(EDGE_ROW) / own(EDGE_DIAG)
        first_far = -row_far / diag_far
        off = (
            (STEP_SCALE * OFF_SCALE) * coupling * first_far
            + near(AUX_IN) * near(AUX_FIRST)
            + near(AUX_LEFT) * pltpu.roll(first, 1, 1)
            + near(AUX_RIGHT) * pltpu.roll(first, face - 1, 1)
        )
        least = min(at, inner)
        step[n, at - least : at - least + 1, :] = STEP_SCALE * first + off / diag
        step[n, inner - least : inner - least + 1, :] = near(AUX_STEP) + near(AUX_GAIN) * (
            first - first_old
        )
        resid[n] = aux[0:comps, :] + drive * (edge[0:comps, :] + other[0:comps, :])
        for source, target in (
            (resid.at[n], resid_hbm.at[:, at, :]),
            (step.at[n, 0:2, :], step_hbm.at[least : least + 2, :]),
        ):
            copies.append(pltpu.make_async_copy(source, target, sem.at[len(copies)]))
            copies[-1].start()
    for copy in copies:
        copy.wait()


def on_device(
    moles,
    old_content,
    pressure,
    perm,
    labels,
    roots,
    counts,
    block_ids,
    wilson,
    attraction,
    covolume,
):
    comps, layers, face = moles.shape
    f32 = jnp.float32
    strips = face // BLK
    tables = (counts, block_ids, wilson, attraction, covolume)
    rows_in = comps * SUB
    widest = max(layers // SUB, 2 * WIDE) * BLK
    vmem = pl.BlockSpec(memory_space=pltpu.VMEM)
    hbm = pl.BlockSpec(memory_space=pltpu.HBM)
    padded = layers + 2 * SUB
    flat = pltpu.VMEM((layers, face), f32)
    flat_int = pltpu.VMEM((layers, face), jnp.int32)
    cell = pltpu.VMEM((strips, layers, BLK), f32)
    cell_pad = pltpu.VMEM((strips + 2, padded, BLK), f32)
    field = pltpu.VMEM((comps, strips, layers, BLK), f32)
    field_pad = pltpu.VMEM((comps, strips + 2, padded, BLK), f32)
    packed = pltpu.VMEM((comps, WIDE * SUB, BLK), f32)
    edge_shape = jax.ShapeDtypeStruct((comps + EDGE_ROWS, face), f32)
    aux_shape = jax.ShapeDtypeStruct((comps + AUX_ROWS, face), f32)
    field_shape = jax.ShapeDtypeStruct((comps, layers, face), f32)
    cell_shape = jax.ShapeDtypeStruct((layers, face), f32)
    residual, step, vapour, top_edge, low_edge, top_aux, low_aux = pl.pallas_call(
        slab_kernel,
        out_shape=[field_shape, cell_shape, cell_shape]
        + [edge_shape, edge_shape, aux_shape, aux_shape],
        in_specs=[hbm] * 11,
        out_specs=[hbm] * 3 + [vmem] * 4,
        scratch_shapes=[field, field, field_pad]
        + [cell_pad] * 4
        + [cell] * 5
        + [pltpu.VMEM((4, strips, layers, BLK), f32)]
        + [flat, flat, flat_int, flat_int, flat]
        + [pltpu.VMEM((2 * rows_in, rows_in), jnp.bfloat16)]
        + [pltpu.VMEM((rows_in, widest), jnp.bfloat16)] * 2
        + [pltpu.VMEM((rows_in, widest), f32)]
        + [packed, pltpu.VMEM((WIDE * SUB, BLK), f32)]
        + [packed] * 3
        + [pltpu.VMEM((3, WIDE * SUB, BLK), f32)]
        + [pltpu.SMEM(table.shape, table.dtype) for table in tables]
        + [
            pltpu.SemaphoreType.DMA((strips,)),
            pltpu.SemaphoreType.DMA((strips,)),
            pltpu.SemaphoreType.DMA((4,)),
            pltpu.SemaphoreType.DMA((len(tables),)),
            pltpu.SemaphoreType.DMA((strips,)),
        ],
        compiler_params=pltpu.CompilerParams(vmem_limit_bytes=63 * 1024 * 1024),
        name="slab",
    )(
        *tables,
        moles,
        old_content,
        pressure,
        perm,
        labels,
        roots,
    )
    ends = lax.axis_size("dev") - 1
    from_prev = lax.ppermute(low_edge, "dev", [(i, i + 1) for i in range(ends)])
    from_next = lax.ppermute(top_edge, "dev", [(i + 1, i) for i in range(ends)])
    residual, step = pl.pallas_call(
        edge_kernel,
        out_shape=[field_shape, cell_shape],
        in_specs=[vmem] * 6 + [hbm] * 2,
        out_specs=[hbm] * 2,
        input_output_aliases={6: 0, 7: 1},
        scratch_shapes=[
            pltpu.VMEM((2, comps, face), f32),
            pltpu.VMEM((2, SUB, face), f32),
            pltpu.SemaphoreType.DMA((4,)),
        ],
        compiler_params=pltpu.CompilerParams(vmem_limit_bytes=16 * 1024 * 1024),
        name="edges",
    )(top_edge, low_edge, top_aux, low_aux, from_prev, from_next, residual, step)
    return (residual, step, vapour)


def solution(mesh):
    in_specs = (
        P(None, "dev", None),
        P(None, "dev", None),
        P("dev", None),
        P("dev", None),
        P("dev", None),
        P("dev", None),
        P("dev"),
        P("dev"),
        P(),
        P(),
        P(),
    )
    out_specs = (P(None, "dev", None), P("dev", None), P("dev", None))
    return jax.shard_map(
        on_device, mesh=mesh, in_specs=in_specs, out_specs=out_specs, check_vma=False
    )
```

```python
import math

import jax
import jax.numpy as jnp
from jax import lax
from jax.experimental import pallas as pl
from jax.experimental.pallas import tpu as pltpu
from jax.sharding import PartitionSpec as P

BLK = 128
SUB = 8
SS_ITERS = 3
RR_ITERS = 3
Z_ITERS = 5
WIDE = 8
TINY = 1e-30
CELLS_VMEM = 32 * 1024 * 1024
FLUX_VMEM = 32 * 1024 * 1024

SQRT_TWO = math.sqrt(2.0)
TIME_STEP = 0.5
RELAX = 0.7
STEP_SCALE = 10.0
OFF_SCALE = RELAX * TIME_STEP

EDGE_PRES, EDGE_PERM, EDGE_LAM, EDGE_CSUM, EDGE_OSUM = range(5)
EDGE_PRES2, EDGE_PERM2, EDGE_LAM2 = range(5, 8)
EDGE_ROWS = 8
AUX_IN, AUX_LEFT, AUX_RIGHT, AUX_FIRST, AUX_GAIN, AUX_STEP, AUX_ROW, AUX_DIAG = range(8)
AUX_ROWS = 8


def keep_in(space, *arrays):
    return [pltpu.with_memory_space_constraint(x, space) for x in arrays]


def recip(value):
    return pltpu.reciprocal(value, approx=True)


def split_halves(value):
    high = value.astype(jnp.bfloat16)
    low = (value - high.astype(jnp.float32)).astype(jnp.bfloat16)
    return high, low


def widen(stack, attraction, comps):
    cols = comps * SUB
    lane = lax.broadcasted_iota(jnp.int32, (SUB, cols), 1)
    row = lax.broadcasted_iota(jnp.int32, (SUB, cols), 0)
    group = lane // SUB
    diagonal = (lane - group * SUB) == row
    zero = jnp.zeros((SUB, cols), jnp.float32)
    for pair in range(comps // 2):
        rows = []
        for i in (2 * pair, 2 * pair + 1):
            full = zero
            for j in range(comps):
                full = jnp.where(group == j, 0.5 * (attraction[i, j] + attraction[j, i]), full)
            rows.append(jnp.where(diagonal, full, zero))
        high, low = split_halves(jnp.concatenate(rows, 0))
        at = 2 * SUB * pair
        stack[at : at + 2 * SUB, :] = high
        stack[cols + at : cols + at + 2 * SUB, :] = low


def rows_of(g):
    return slice(g * SUB, (g + 1) * SUB)


def cubic_pair(big_a, big_b, start, vapour_flag):
    two_b = 2.0 * big_b
    b_square = big_b * big_b
    one_b = 1.0 + big_b
    least = big_b + 0.01
    half_b = 0.5 * big_b
    half_one_b = 0.5 * one_b
    half_a = 0.5 * big_a
    half_inv_a = None if vapour_flag is True else 0.5 * recip(big_a)
    z_factor = start
    for _ in range(Z_ITERS):
        spread = z_factor * (z_factor + two_b) - b_square
        half_z = 0.5 * z_factor
        if vapour_flag is not False:
            vap = (half_z + half_one_b) - half_a * (z_factor - big_b) * recip(spread)
        if vapour_flag is not True:
            liq = (half_z + half_b) + spread * (one_b - z_factor) * half_inv_a
        if vapour_flag is True:
            new = vap
        elif vapour_flag is False:
            new = liq
        else:
            new = jnp.where(vapour_flag, vap, liq)
        z_factor = jnp.minimum(jnp.maximum(new, least), 2.0)
    return z_factor


def cells_kernel(
    counts,
    block_ids_hbm,
    wilson_hbm,
    attraction_hbm,
    covolume_hbm,
    moles_hbm,
    old_hbm,
    pres_hbm,
    perm_hbm,
    labels_hbm,
    roots_hbm,
    vap_hbm,
    top_edge,
    low_edge,
    held,
    old,
    mobile,
    pres,
    perm,
    lam,
    scale,
    csum,
    vap,
    pres_flat,
    perm_flat,
    labels,
    roots,
    w_stack,
    x_high,
    x_low,
    sums,
    pack,
    pack_pres,
    inv_excess,
    liquid,
    vapour,
    out_cell,
    block_ids,
    wilson,
    attraction,
    covolume,
    in_sem,
    old_sem,
    cell_sem,
    table_sem,
):
    comps, layers, face = moles_hbm.shape
    strips = face // BLK
    groups = layers // SUB
    padded = layers + 2 * SUB
    inside = slice(SUB, SUB + layers)

    def lanes_of(k):
        return pl.ds(pl.multiple_of(k * BLK, BLK), BLK)

    def strip_in(source, target, sem, k):
        return pltpu.make_async_copy(source.at[:, :, lanes_of(k)], target.at[:, k], sem.at[k])

    cell_copies = [
        pltpu.make_async_copy(pres_hbm, pres_flat, cell_sem.at[0]),
        pltpu.make_async_copy(roots_hbm, roots, cell_sem.at[1]),
        pltpu.make_async_copy(labels_hbm, labels, cell_sem.at[2]),
        pltpu.make_async_copy(perm_hbm, perm_flat, cell_sem.at[3]),
    ]
    table_copies = [
        pltpu.make_async_copy(source, target, table_sem.at[n])
        for n, (source, target) in enumerate(
            (
                (attraction_hbm, attraction),
                (covolume_hbm, covolume),
                (wilson_hbm, wilson),
                (block_ids_hbm, block_ids),
            )
        )
    ]
    for copy in table_copies + cell_copies:
        copy.start()
    for k in range(strips):
        strip_in(moles_hbm, held, in_sem, k).start()
    for k in range(strips):
        strip_in(old_hbm, old, old_sem, k).start()

    zero_tile = jnp.zeros((SUB, BLK), jnp.float32)
    zero_strip = jnp.zeros((padded, BLK), jnp.float32)

    def clear(ref, *at):
        for k in (0, strips + 1):
            ref[(*at, k)] = zero_strip
        for k in range(1, strips + 1):
            ref[(*at, k, slice(0, SUB))] = zero_tile
            ref[(*at, k, slice(SUB + layers, padded))] = zero_tile

    for ref in (pres, perm, lam):
        clear(ref)
    for i in range(comps):
        clear(mobile, i)
    for copy in table_copies:
        copy.wait()
    widen(w_stack, attraction, comps)

    cols = comps * SUB

    def multiply(width, with_low):
        both = jnp.dot(w_stack[...], x_high[:, 0:width], preferred_element_type=jnp.float32)
        result = both[0:cols] + both[cols : 2 * cols]
        if with_low:
            result = result + jnp.dot(
                w_stack[0:cols, :], x_low[:, 0:width], preferred_element_type=jnp.float32
            )
        sums[:, 0:width] = result

    def total(at, start, count):
        rows = slice(at * SUB, (at + 1) * SUB)
        return jnp.concatenate(
            [sums[rows, g * BLK : (g + 1) * BLK] for g in range(start, start + count)], 0
        )

    def put_halves(j, g, pair, with_low):
        value = jnp.concatenate(pair, 0)
        rows = slice(2 * SUB * j, 2 * SUB * (j + 1))
        lanes = slice(g * BLK, (g + 1) * BLK)
        high = value.astype(jnp.bfloat16)
        x_high[rows, lanes] = high
        if with_low:
            x_low[rows, lanes] = (value - high.astype(jnp.float32)).astype(jnp.bfloat16)

    def quadratic(values, start, count, with_low):
        quad = None
        for i in range(comps):
            value = values(i)
            if not with_low:
                high = value.astype(jnp.bfloat16).astype(jnp.float32)
                value = value + (value - high)
            term = value * total(i, start, count)
            quad = term if quad is None else quad + term
        return quad

    for copy in cell_copies:
        copy.wait()
    for k in range(strips):
        pres[k + 1, inside, :] = pres_flat[:, k * BLK : (k + 1) * BLK]
        perm[k + 1, inside, :] = perm_flat[:, k * BLK : (k + 1) * BLK]

    def single(k, carry):
        strip_in(moles_hbm, held, in_sem, k).wait()
        for j in range(comps // 2):
            for g in range(groups):
                pair = [held[i, k, rows_of(g), :] for i in (2 * j, 2 * j + 1)]
                put_halves(j, g, pair, False)
        multiply(groups * BLK, False)
        amount = held[0, k]
        b_sum = covolume[0] * amount
        for i in range(1, comps):
            value = held[i, k]
            amount = amount + value
            b_sum = b_sum + covolume[i] * value
        quad = quadratic(lambda i: held[i, k], 0, groups, False)
        pressure = pres[k + 1, inside, :]
        inv_amount = recip(amount)
        big_a = pressure * quad * inv_amount * inv_amount
        big_b = pressure * b_sum * inv_amount
        is_vapour = roots[:, lanes_of(k)] == 1
        start = jnp.where(is_vapour, 1.0, 2.0 * big_b)
        z_factor = cubic_pair(big_a, big_b, start, is_vapour)
        rho = pressure * recip(z_factor)
        part = labels[:, lanes_of(k)].astype(jnp.float32)
        move = ((1.0 - part) * (1.0 - part) + 4.0 * part * part) * rho
        vap[k] = part
        scale[k] = rho
        csum[k] = amount * rho
        lam[k + 1, inside, :] = amount * move
        for i in range(comps):
            mobile[i, k + 1, inside, :] = held[i, k] * move
        return carry

    lax.fori_loop(0, strips, single, 0)

    batch = WIDE * SUB
    own_count = counts[0]
    held_rows = held.reshape(comps * strips * layers, BLK)
    mobile_rows = mobile.reshape(comps * (strips + 2) * padded, BLK)
    pack_rows = pack.reshape(comps * batch, BLK)
    liquid_rows = liquid.reshape(comps * batch, BLK)
    vapour_rows = vapour.reshape(comps * batch, BLK)
    bits = strips.bit_length() - 1

    def place(slot):
        block = block_ids[jnp.minimum(slot, own_count - 1)]
        layer = lax.shift_right_logical(block, bits)
        return block - lax.shift_left(layer, bits), layer

    def field_at(k, layer):
        return pl.ds(k * layers + layer, comps, stride=strips * layers)

    def mobile_at(k, layer):
        return pl.ds((k + 1) * padded + layer + SUB, comps, stride=(strips + 2) * padded)

    def flash(number, carry):
        base = number * batch
        places = [place(base + r) for r in range(batch)]
        for r, (k, layer) in enumerate(places):
            pack_rows[pl.ds(r, comps, stride=batch), :] = held_rows[field_at(k, layer), :]
            pack_pres[r : r + 1, :] = pres[k + 1, pl.ds(layer + SUB, 1), :]
        pressure = pack_pres[...]
        log_pres = jnp.log(pressure)
        amount = pack[0]
        for i in range(1, comps):
            amount = amount + pack[i]
        inv_amount = recip(amount)
        for i in range(comps):
            pack[i] = pack[i] * inv_amount

        def keep_k(i, log_k):
            inv_excess[i] = recip((jnp.exp(log_k) - 1.0) + TINY)

        for i in range(comps):
            keep_k(i, wilson[i] - log_pres)
        for sweep in range(SS_ITERS):
            with_low = sweep + 1 < SS_ITERS
            part = jnp.full((batch, BLK), 0.5, jnp.float32)
            for _ in range(RR_ITERS):
                value = jnp.zeros((batch, BLK), jnp.float32)
                slope = jnp.full((batch, BLK), 0.05, jnp.float32)
                for i in range(comps):
                    ratio = recip(inv_excess[i] + part)
                    term = pack[i] * ratio
                    value = value + term
                    slope = slope + term * ratio
                part = jnp.minimum(jnp.maximum(part + value * recip(slope), 0.0), 1.0)
            sums_of = [[None, None], [None, None]]
            for j in range(comps // 2):
                liq_two = []
                vap_two = []
                for i in (2 * j, 2 * j + 1):
                    term = pack[i] * recip(inv_excess[i] + part)
                    liq = pack[i] - part * term
                    gas = liq + term
                    liquid[i] = liq
                    vapour[i] = gas
                    liq_two.append(liq)
                    vap_two.append(gas)
                    for acc, value in zip(sums_of, (liq, gas)):
                        scaled = covolume[i] * value
                        acc[0] = value if acc[0] is None else acc[0] + value
                        acc[1] = scaled if acc[1] is None else acc[1] + scaled
                for g in range(WIDE):
                    put_halves(j, g, [value[rows_of(g)] for value in liq_two], with_low)
                    put_halves(j, WIDE + g, [value[rows_of(g)] for value in vap_two], with_low)
            multiply(2 * WIDE * BLK, with_low)
            phases = []
            for values, at, flag, (whole, b_sum) in (
                (liquid, 0, False, sums_of[0]),
                (vapour, WIDE, True, sums_of[1]),
            ):
                quad = quadratic(lambda i: values[i], at, WIDE, with_low)
                inv_whole = recip(whole)
                b_mix = b_sum * inv_whole
                a_mix = quad * inv_whole * inv_whole
                big_a = pressure * a_mix
                big_b = pressure * b_mix
                start = jnp.ones_like(big_b) if flag else 2.0 * big_b
                z_factor = cubic_pair(big_a, big_b, start, flag)
                phases.append((quad, whole, inv_whole, a_mix, b_mix, big_b, z_factor))
            if sweep + 1 < SS_ITERS:
                parts = []
                for quad, whole, inv_whole, a_mix, b_mix, big_b, z_factor in phases:
                    log_arg = (z_factor + (1.0 + SQRT_TWO) * big_b) * recip(
                        z_factor + (1.0 - SQRT_TWO) * big_b
                    )
                    inv_b = recip(b_mix)
                    depart = a_mix * inv_b * (1.0 / (2.0 * SQRT_TWO)) * jnp.log(log_arg)
                    of_cov = (z_factor - 1.0 + depart) * inv_b
                    of_sum = 2.0 * depart * whole * recip(quad)
                    parts.append((of_cov, jnp.log(z_factor - big_b), of_sum))
                cov_gap = parts[0][0] - parts[1][0]
                log_gap = parts[0][1] - parts[1][1]
                for i in range(comps):
                    log_k = (
                        covolume[i] * cov_gap
                        - log_gap
                        - parts[0][2] * total(i, 0, WIDE)
                        + parts[1][2] * total(i, WIDE, WIDE)
                    )
                    keep_k(i, jnp.minimum(jnp.maximum(log_k, -3.0), 3.0))
        rho_liq = amount * pressure * recip(phases[0][6])
        rho_vap = amount * pressure * recip(phases[1][6])
        rest = 1.0 - part
        move_liq = rest * rest * rho_liq
        move_vap = 4.0 * part * part * rho_vap
        hold_liq = rest * rho_liq
        hold_vap = part * rho_vap
        out_cell[0] = part
        out_cell[1] = move_liq + move_vap
        out_cell[2] = hold_liq + hold_vap
        move_liq = move_liq * phases[0][2]
        move_vap = move_vap * phases[1][2]
        hold_liq = hold_liq * phases[0][2]
        hold_vap = hold_vap * phases[1][2]
        for i in range(comps):
            liq, gas = liquid[i], vapour[i]
            liquid[i] = move_liq * liq + move_vap * gas
            vapour[i] = hold_liq * liq + hold_vap * gas
        one_row = jnp.ones((1, BLK), jnp.float32)
        for r, (k, layer) in enumerate(places):
            of = pl.ds(r, comps, stride=batch)
            mobile_rows[mobile_at(k, layer), :] = liquid_rows[of, :]
            held_rows[field_at(k, layer), :] = vapour_rows[of, :]
            one = slice(r, r + 1)
            row = pl.ds(layer, 1)
            vap[k, row, :] = out_cell[0, one, :]
            lam[k + 1, pl.ds(layer + SUB, 1), :] = out_cell[1, one, :]
            csum[k, row, :] = out_cell[2, one, :]
            scale[k, row, :] = one_row
        return carry

    lax.fori_loop(0, (own_count + batch - 1) // batch, flash, 0)
    for k in range(strips):
        pres_flat[:, k * BLK : (k + 1) * BLK] = vap[k]
    vap_copy = pltpu.make_async_copy(pres_flat, vap_hbm, cell_sem.at[0])
    vap_copy.start()

    for k in range(strips):
        strip_in(old_hbm, old, old_sem, k).wait()
    old_rows = old.reshape(comps * strips * layers, BLK)
    for edge, at, inner in ((top_edge, 0, 1), (low_edge, layers - 1, layers - 2)):
        for k in range(strips):
            lanes = slice(k * BLK, (k + 1) * BLK)
            here = slice(at, at + 1)
            pad_here = slice(SUB + at, SUB + at + 1)
            pad_inner = slice(SUB + inner, SUB + inner + 1)
            edge[0:comps, lanes] = mobile_rows[mobile_at(k, at), :]
            values = [None] * EDGE_ROWS
            values[EDGE_PRES] = pres[k + 1, pad_here, :]
            values[EDGE_PERM] = perm[k + 1, pad_here, :]
            values[EDGE_LAM] = lam[k + 1, pad_here, :]
            values[EDGE_CSUM] = csum[k, here, :]
            values[EDGE_OSUM] = jnp.sum(old_rows[field_at(k, at), :], 0, keepdims=True)
            values[EDGE_PRES2] = pres[k + 1, pad_inner, :]
            values[EDGE_PERM2] = perm[k + 1, pad_inner, :]
            values[EDGE_LAM2] = lam[k + 1, pad_inner, :]
            for n, value in enumerate(values):
                edge[comps + n : comps + n + 1, lanes] = value
    vap_copy.wait()


def flux_kernel(
    held,
    old,
    mobile,
    pres,
    perm,
    lam,
    scale,
    csum,
    resid_hbm,
    step_hbm,
    top_aux,
    low_aux,
    resid,
    first,
    row_sum,
    diag,
    weights,
    step,
    step_sem,
    out_sem,
):
    comps, strips, layers, _ = held.shape
    groups = layers // SUB

    def lanes_of(k):
        return pl.ds(pl.multiple_of(k * BLK, BLK), BLK)

    def strip_out(k):
        return pltpu.make_async_copy(resid.at[:, k], resid_hbm.at[:, :, lanes_of(k)], out_sem.at[k])

    zero_tile = jnp.zeros((SUB, BLK), jnp.float32)
    for k in range(strips + 2):
        for g in range(groups + 2):
            if k in (0, strips + 1) or g in (0, groups + 1):
                first[k, rows_of(g), :] = zero_tile

    lane_index = lax.broadcasted_iota(jnp.int32, (SUB, BLK), 1)
    is_last_lane = lane_index == BLK - 1
    is_first_lane = lane_index == 0

    def around(load, k, g):
        at = SUB * (g + 1)
        here = load(k + 1, slice(at, at + SUB))
        up = load(k + 1, slice(at - 1, at + SUB - 1))
        down = load(k + 1, slice(at + 1, at + SUB + 1))
        before = load(k, slice(at, at + SUB))
        after = load(k + 2, slice(at, at + SUB))
        left = pltpu.roll(jnp.where(is_last_lane, before, here), 1, 1)
        right = pltpu.roll(jnp.where(is_first_lane, after, here), BLK - 1, 1)
        return here, (up, down, left, right)

    def fluxes(k, carry):
        for g in range(groups):
            rows = rows_of(g)
            p_here, p_near = around(lambda s, r: pres[s, r, :], k, g)
            k_here, k_near = around(lambda s, r: perm[s, r, :], k, g)
            l_here, l_near = around(lambda s, r: lam[s, r, :], k, g)
            drives = []
            couplings = []
            for n in range(4):
                transmiss = k_here * k_near[n] * recip(k_here + k_near[n])
                drives.append((TIME_STEP * transmiss) * (p_here - p_near[n]))
                couplings.append(transmiss * (l_here + l_near[n]))
            drive_sum = (drives[0] + drives[1]) + (drives[2] + drives[3])
            content_scale = scale[k, rows, :]
            row_total = zero_tile
            for i in range(comps):
                m_here, m_near = around(lambda s, r, i=i: mobile[i, s, r, :], k, g)
                value = held[i, k, rows, :] * content_scale - old[i, k, rows, :]
                value = value + drive_sum * m_here
                value = value + (drives[0] * m_near[0] + drives[1] * m_near[1])
                value = value + (drives[2] * m_near[2] + drives[3] * m_near[3])
                resid[i, k, rows, :] = value
                row_total = row_total + value
            diagonal = TIME_STEP * (
                (couplings[0] + couplings[1]) + (couplings[2] + couplings[3])
            ) + csum[k, rows, :] * recip(p_here)
            inv_diag = recip(diagonal)
            row_sum[k, rows, :] = row_total
            diag[k, rows, :] = diagonal
            first[k + 1, SUB * (g + 1) : SUB * (g + 2), :] = -row_total * inv_diag
            gain = (STEP_SCALE * OFF_SCALE) * inv_diag
            for n in range(4):
                weights[n, k, rows, :] = couplings[n] * gain
        strip_out(k).start()
        return carry

    lax.fori_loop(0, strips, fluxes, 0)

    def steps(k, carry):
        for g in range(groups):
            rows = rows_of(g)
            here, near = around(lambda s, r: first[s, r, :], k, g)
            step[rows, lanes_of(k)] = (
                STEP_SCALE * here
                + (weights[0, k, rows, :] * near[0] + weights[1, k, rows, :] * near[1])
                + (weights[2, k, rows, :] * near[2] + weights[3, k, rows, :] * near[3])
            )
        return carry

    lax.fori_loop(0, strips, steps, 0)
    step_copy = pltpu.make_async_copy(step, step_hbm, step_sem)
    step_copy.start()

    resid_rows = resid.reshape(comps * strips * layers, BLK)
    for aux, at, inner, toward, away in (
        (top_aux, 0, 1, 0, 1),
        (low_aux, layers - 1, layers - 2, 1, 0),
    ):
        for k in range(strips):
            lanes = slice(k * BLK, (k + 1) * BLK)
            here = slice(at, at + 1)
            behind = slice(inner, inner + 1)
            from_row = pl.ds(k * layers + at, comps, stride=strips * layers)
            aux[0:comps, lanes] = resid_rows[from_row, :]
            unscale = diag[k, here, :]
            values = [None] * AUX_ROWS
            values[AUX_IN] = weights[away, k, here, :] * unscale
            values[AUX_LEFT] = weights[2, k, here, :] * unscale
            values[AUX_RIGHT] = weights[3, k, here, :] * unscale
            values[AUX_FIRST] = first[k + 1, SUB + inner : SUB + inner + 1, :]
            values[AUX_GAIN] = weights[toward, k, behind, :]
            values[AUX_STEP] = step[behind, lanes]
            values[AUX_ROW] = row_sum[k, here, :]
            values[AUX_DIAG] = unscale
            for n, value in enumerate(values):
                aux[comps + n : comps + n + 1, lanes] = value
    step_copy.wait()
    for k in range(strips):
        strip_out(k).wait()


def transmissibility(perm, perm_near):
    both = perm + perm_near
    return perm * perm_near / jnp.where(both == 0.0, 1.0, both)


def edge_kernel(
    top_edge,
    low_edge,
    top_aux,
    low_aux,
    from_prev,
    from_next,
    resid_in,
    step_in,
    resid_hbm,
    step_hbm,
    resid,
    step,
    sem,
):
    comps, layers, face = resid_hbm.shape
    copies = []
    for n, (edge, aux, other, at, inner) in enumerate(
        (
            (top_edge, top_aux, from_prev, 0, 1),
            (low_edge, low_aux, from_next, layers - 1, layers - 2),
        )
    ):

        def own(index):
            return edge[comps + index : comps + index + 1, :]

        def far(index):
            return other[comps + index : comps + index + 1, :]

        def near(index):
            return aux[comps + index : comps + index + 1, :]

        pres_far, perm_far, lam_far = far(EDGE_PRES), far(EDGE_PERM), far(EDGE_LAM)
        transmiss = transmissibility(own(EDGE_PERM), perm_far)
        drive = TIME_STEP * transmiss * (own(EDGE_PRES) - pres_far)
        lam_both = own(EDGE_LAM) + lam_far
        coupling = transmiss * lam_both
        row = near(AUX_ROW) + drive * lam_both
        diag = near(AUX_DIAG) + TIME_STEP * coupling
        first = -row / diag
        first_old = -near(AUX_ROW) / near(AUX_DIAG)
        row_far = far(EDGE_CSUM) - far(EDGE_OSUM) - drive * lam_both
        diag_far = coupling
        lane = lax.broadcasted_iota(jnp.int32, (1, face), 1)
        sides = [(far(EDGE_PRES2), far(EDGE_PERM2), far(EDGE_LAM2))]
        for shift, end in ((1, 0), (face - 1, face - 1)):
            pres_n, perm_n, lam_n = (pltpu.roll(x, shift, 1) for x in (pres_far, perm_far, lam_far))
            sides.append((pres_n, jnp.where(lane == end, 0.0, perm_n), lam_n))
        for pres_n, perm_n, lam_n in sides:
            joint = transmissibility(perm_far, perm_n) * (lam_far + lam_n)
            row_far = row_far + TIME_STEP * joint * (pres_far - pres_n)
            diag_far = diag_far + joint
        diag_far = TIME_STEP * diag_far + far(EDGE_CSUM) / jnp.where(pres_far == 0.0, 1.0, pres_far)
        first_far = -row_far / jnp.where(diag_far == 0.0, 1.0, diag_far)
        off = (
            (STEP_SCALE * OFF_SCALE) * coupling * first_far
            + near(AUX_IN) * near(AUX_FIRST)
            + near(AUX_LEFT) * pltpu.roll(first, 1, 1)
            + near(AUX_RIGHT) * pltpu.roll(first, face - 1, 1)
        )
        least = min(at, inner)
        step[n, at - least : at - least + 1, :] = STEP_SCALE * first + off / diag
        step[n, inner - least : inner - least + 1, :] = near(AUX_STEP) + near(AUX_GAIN) * (
            first - first_old
        )
        resid[n] = aux[0:comps, :] + drive * (edge[0:comps, :] + other[0:comps, :])
        for source, target in (
            (resid.at[n], resid_hbm.at[:, at, :]),
            (step.at[n, 0:2, :], step_hbm.at[least : least + 2, :]),
        ):
            copies.append(pltpu.make_async_copy(source, target, sem.at[len(copies)]))
            copies[-1].start()
    for copy in copies:
        copy.wait()


def on_device(
    moles,
    old_content,
    pressure,
    perm,
    labels,
    roots,
    counts,
    block_ids,
    wilson,
    attraction,
    covolume,
):
    comps, layers, face = moles.shape
    f32 = jnp.float32
    strips = face // BLK
    tables = (block_ids, wilson, attraction, covolume)
    rows_in = comps * SUB
    widest = max(layers // SUB, 2 * WIDE) * BLK
    vmem = pl.BlockSpec(memory_space=pltpu.VMEM)
    hbm = pl.BlockSpec(memory_space=pltpu.HBM)
    padded = layers + 2 * SUB
    flat = pltpu.VMEM((layers, face), f32)
    flat_int = pltpu.VMEM((layers, face), jnp.int32)
    cell = pltpu.VMEM((strips, layers, BLK), f32)
    cell_pad = pltpu.VMEM((strips + 2, padded, BLK), f32)
    field = pltpu.VMEM((comps, strips, layers, BLK), f32)
    field_pad = pltpu.VMEM((comps, strips + 2, padded, BLK), f32)
    packed = pltpu.VMEM((comps, WIDE * SUB, BLK), f32)
    edge_shape = pltpu.VMEM((comps + EDGE_ROWS, face), f32)
    aux_shape = pltpu.VMEM((comps + AUX_ROWS, face), f32)
    field_shape = jax.ShapeDtypeStruct((comps, layers, face), f32)
    cell_shape = jax.ShapeDtypeStruct((layers, face), f32)
    held_types = [field, field, field_pad] + [cell_pad] * 3 + [cell] * 2
    vapour, top_edge, low_edge, *state = pl.pallas_call(
        cells_kernel,
        out_shape=[cell_shape, edge_shape, edge_shape]
        + held_types,
        in_specs=[pl.BlockSpec(memory_space=pltpu.SMEM)] + [hbm] * 10,
        out_specs=[hbm] + [vmem] * (2 + len(held_types)),
        scratch_shapes=[cell, flat, flat, flat_int, flat_int]
        + [pltpu.VMEM((2 * rows_in, rows_in), jnp.bfloat16)]
        + [pltpu.VMEM((rows_in, widest), jnp.bfloat16)] * 2
        + [pltpu.VMEM((rows_in, widest), f32)]
        + [packed, pltpu.VMEM((WIDE * SUB, BLK), f32)]
        + [packed] * 3
        + [pltpu.VMEM((3, WIDE * SUB, BLK), f32)]
        + [pltpu.SMEM(table.shape, table.dtype) for table in tables]
        + [
            pltpu.SemaphoreType.DMA((strips,)),
            pltpu.SemaphoreType.DMA((strips,)),
            pltpu.SemaphoreType.DMA((4,)),
            pltpu.SemaphoreType.DMA((len(tables),)),
        ],
        compiler_params=pltpu.CompilerParams(vmem_limit_bytes=CELLS_VMEM),
        name="cells",
    )(counts, *keep_in(pltpu.HBM, *tables, moles, old_content, pressure, perm, labels, roots))
    ends = lax.axis_size("dev") - 1
    from_prev = lax.ppermute(low_edge, "dev", [(i, i + 1) for i in range(ends)])
    from_next = lax.ppermute(top_edge, "dev", [(i + 1, i) for i in range(ends)])
    residual, step, top_aux, low_aux = pl.pallas_call(
        flux_kernel,
        out_shape=[field_shape, cell_shape, aux_shape, aux_shape],
        in_specs=[vmem] * len(state),
        out_specs=[hbm] * 2 + [vmem] * 2,
        scratch_shapes=[field, cell_pad, cell, cell]
        + [pltpu.VMEM((4, strips, layers, BLK), f32), flat]
        + [pltpu.SemaphoreType.DMA(()), pltpu.SemaphoreType.DMA((strips,))],
        compiler_params=pltpu.CompilerParams(vmem_limit_bytes=FLUX_VMEM),
        name="flux",
    )(*keep_in(pltpu.VMEM, *state))
    residual, step = pl.pallas_call(
        edge_kernel,
        out_shape=[field_shape, cell_shape],
        in_specs=[vmem] * 6 + [hbm] * 2,
        out_specs=[hbm] * 2,
        input_output_aliases={6: 0, 7: 1},
        scratch_shapes=[
            pltpu.VMEM((2, comps, face), f32),
            pltpu.VMEM((2, SUB, face), f32),
            pltpu.SemaphoreType.DMA((4,)),
        ],
        compiler_params=pltpu.CompilerParams(vmem_limit_bytes=16 * 1024 * 1024),
        name="edges",
    )(top_edge, low_edge, top_aux, low_aux, from_prev, from_next, residual, step)
    return (residual, step, vapour)


def solution(mesh):
    in_specs = (
        P(None, "dev", None),
        P(None, "dev", None),
        P("dev", None),
        P("dev", None),
        P("dev", None),
        P("dev", None),
        P("dev"),
        P("dev"),
        P(),
        P(),
        P(),
    )
    out_specs = (P(None, "dev", None), P("dev", None), P("dev", None))
    return jax.shard_map(
        on_device, mesh=mesh, in_specs=in_specs, out_specs=out_specs, check_vma=False
    )
```

```python
import math

import jax
import jax.numpy as jnp
from jax import lax
from jax.experimental import pallas as pl
from jax.experimental.pallas import tpu as pltpu
from jax.sharding import PartitionSpec as P

BLK = 128
SUB = 8
SS_ITERS = 3
RR_ITERS = 3
Z_ITERS = 5
WIDE = 8
TINY = 1e-30
CELLS_VMEM = 32 * 1024 * 1024
FLUX_VMEM = 32 * 1024 * 1024

SQRT_TWO = math.sqrt(2.0)
TIME_STEP = 0.5
RELAX = 0.7
STEP_SCALE = 10.0
OFF_SCALE = RELAX * TIME_STEP

EDGE_PRES, EDGE_PERM, EDGE_LAM, EDGE_CSUM, EDGE_OSUM = range(5)
EDGE_PRES2, EDGE_PERM2, EDGE_LAM2 = range(5, 8)
EDGE_ROWS = 8
EDGE_SPAN = 32
AUX_IN, AUX_LEFT, AUX_RIGHT, AUX_FIRST, AUX_GAIN, AUX_STEP, AUX_ROW, AUX_DIAG = range(8)
AUX_ROWS = 8


def keep_in(space, *arrays):
    return [pltpu.with_memory_space_constraint(x, space) for x in arrays]


def recip(value):
    return pltpu.reciprocal(value, approx=True)


def split_halves(value):
    high = value.astype(jnp.bfloat16)
    low = (value - high.astype(jnp.float32)).astype(jnp.bfloat16)
    return high, low


def widen(stack, attraction, comps):
    cols = comps * SUB
    lane = lax.broadcasted_iota(jnp.int32, (SUB, cols), 1)
    row = lax.broadcasted_iota(jnp.int32, (SUB, cols), 0)
    group = lane // SUB
    diagonal = (lane - group * SUB) == row
    zero = jnp.zeros((SUB, cols), jnp.float32)
    for pair in range(comps // 2):
        rows = []
        for i in (2 * pair, 2 * pair + 1):
            full = zero
            for j in range(comps):
                full = jnp.where(group == j, 0.5 * (attraction[i, j] + attraction[j, i]), full)
            rows.append(jnp.where(diagonal, full, zero))
        high, low = split_halves(jnp.concatenate(rows, 0))
        at = 2 * SUB * pair
        stack[at : at + 2 * SUB, :] = high
        stack[cols + at : cols + at + 2 * SUB, :] = low


def rows_of(g):
    return slice(g * SUB, (g + 1) * SUB)


def cubic(big_a, big_b, start, vapour_flag):
    two_b = 2.0 * big_b
    b_square = big_b * big_b
    one_b = 1.0 + big_b
    least = big_b + 0.01
    half_b = 0.5 * big_b
    half_one_b = 0.5 * one_b
    half_a = 0.5 * big_a
    half_inv_a = None if vapour_flag is True else 0.5 * recip(big_a)

    def step(z_factor):
        spread = z_factor * (z_factor + two_b) - b_square
        half_z = 0.5 * z_factor
        if vapour_flag is not False:
            vap = (half_z + half_one_b) - half_a * (z_factor - big_b) * recip(spread)
        if vapour_flag is not True:
            liq = (half_z + half_b) + spread * (one_b - z_factor) * half_inv_a
        if vapour_flag is True:
            new = vap
        elif vapour_flag is False:
            new = liq
        else:
            new = jnp.where(vapour_flag, vap, liq)
        return jnp.minimum(jnp.maximum(new, least), 2.0)

    return start, step


def roots_of(*equations):
    found = [start for start, _ in equations]
    for _ in range(Z_ITERS):
        found = [step(z_factor) for z_factor, (_, step) in zip(found, equations)]
    return found


def cells_kernel(
    counts,
    block_ids_hbm,
    wilson_hbm,
    attraction_hbm,
    covolume_hbm,
    moles_hbm,
    old_hbm,
    pres_hbm,
    perm_hbm,
    labels_hbm,
    roots_hbm,
    vap_hbm,
    edges_hbm,
    top_edge,
    low_edge,
    held,
    old,
    mobile,
    pres,
    perm,
    lam,
    scale,
    csum,
    vap,
    pres_flat,
    perm_flat,
    labels,
    roots,
    w_stack,
    x_high,
    x_low,
    sums,
    pack,
    pack_pres,
    inv_excess,
    liquid,
    vapour,
    out_cell,
    block_ids,
    wilson,
    attraction,
    covolume,
    in_sem,
    old_sem,
    cell_sem,
    table_sem,
    edge_sem,
):
    comps, layers, face = moles_hbm.shape
    strips = face // BLK
    groups = layers // SUB
    padded = layers + 2 * SUB
    inside = slice(SUB, SUB + layers)

    def lanes_of(k):
        return pl.ds(pl.multiple_of(k * BLK, BLK), BLK)

    def strip_in(source, target, sem, k):
        return pltpu.make_async_copy(source.at[:, :, lanes_of(k)], target.at[:, k], sem.at[k])

    cell_copies = [
        pltpu.make_async_copy(pres_hbm, pres_flat, cell_sem.at[0]),
        pltpu.make_async_copy(roots_hbm, roots, cell_sem.at[1]),
        pltpu.make_async_copy(labels_hbm, labels, cell_sem.at[2]),
        pltpu.make_async_copy(perm_hbm, perm_flat, cell_sem.at[3]),
    ]
    table_copies = [
        pltpu.make_async_copy(source, target, table_sem.at[n])
        for n, (source, target) in enumerate(
            (
                (attraction_hbm, attraction),
                (covolume_hbm, covolume),
                (wilson_hbm, wilson),
                (block_ids_hbm, block_ids),
            )
        )
    ]
    for copy in table_copies + cell_copies:
        copy.start()
    for k in range(strips):
        strip_in(moles_hbm, held, in_sem, k).start()
    for k in range(strips):
        strip_in(old_hbm, old, old_sem, k).start()

    zero_tile = jnp.zeros((SUB, BLK), jnp.float32)
    zero_strip = jnp.zeros((padded, BLK), jnp.float32)

    def clear(ref, *at):
        for k in (0, strips + 1):
            ref[(*at, k)] = zero_strip
        for k in range(1, strips + 1):
            ref[(*at, k, slice(0, SUB))] = zero_tile
            ref[(*at, k, slice(SUB + layers, padded))] = zero_tile

    for ref in (pres, perm, lam):
        clear(ref)
    for i in range(comps):
        clear(mobile, i)
    for copy in table_copies:
        copy.wait()
    widen(w_stack, attraction, comps)

    cols = comps * SUB

    def multiply(n, width, with_low):
        lanes = slice(0, width)
        both = jnp.dot(w_stack[...], x_high[n, :, lanes], preferred_element_type=jnp.float32)
        result = both[0:cols] + both[cols : 2 * cols]
        if with_low:
            result = result + jnp.dot(
                w_stack[0:cols, :], x_low[n, :, lanes], preferred_element_type=jnp.float32
            )
        sums[n, :, lanes] = result

    def total(n, at, count):
        rows = slice(at * SUB, (at + 1) * SUB)
        return jnp.concatenate(
            [sums[n, rows, g * BLK : (g + 1) * BLK] for g in range(count)], 0
        )

    def put_halves(n, j, g, pair, with_low):
        value = jnp.concatenate(pair, 0)
        rows = slice(2 * SUB * j, 2 * SUB * (j + 1))
        lanes = slice(g * BLK, (g + 1) * BLK)
        high = value.astype(jnp.bfloat16)
        x_high[n, rows, lanes] = high
        if with_low:
            x_low[n, rows, lanes] = (value - high.astype(jnp.float32)).astype(jnp.bfloat16)

    def quadratic(values, n, count, with_low):
        quad = None
        for i in range(comps):
            value = values(i)
            if not with_low:
                high = value.astype(jnp.bfloat16).astype(jnp.float32)
                value = value + (value - high)
            term = value * total(n, i, count)
            quad = term if quad is None else quad + term
        return quad

    def added(values):
        whole = values(0)
        b_sum = covolume[0] * whole
        for i in range(1, comps):
            value = values(i)
            whole = whole + value
            b_sum = b_sum + covolume[i] * value
        return whole, b_sum

    for copy in cell_copies:
        copy.wait()
    for k in range(strips):
        pres[k + 1, inside, :] = pres_flat[:, k * BLK : (k + 1) * BLK]
        perm[k + 1, inside, :] = perm_flat[:, k * BLK : (k + 1) * BLK]

    def single(k, carry):
        strip_in(moles_hbm, held, in_sem, k).wait()
        for j in range(comps // 2):
            for g in range(groups):
                pair = [held[i, k, rows_of(g), :] for i in (2 * j, 2 * j + 1)]
                put_halves(0, j, g, pair, False)
        multiply(0, groups * BLK, False)
        amount, b_sum = added(lambda i: held[i, k])
        quad = quadratic(lambda i: held[i, k], 0, groups, False)
        pressure = pres[k + 1, inside, :]
        inv_amount = recip(amount)
        big_a = pressure * quad * inv_amount * inv_amount
        big_b = pressure * b_sum * inv_amount
        is_vapour = roots[:, lanes_of(k)] == 1
        start = jnp.where(is_vapour, 1.0, 2.0 * big_b)
        (z_factor,) = roots_of(cubic(big_a, big_b, start, is_vapour))
        rho = pressure * recip(z_factor)
        part = labels[:, lanes_of(k)].astype(jnp.float32)
        move = ((1.0 - part) * (1.0 - part) + 4.0 * part * part) * rho
        vap[k] = part
        scale[k] = rho
        csum[k] = amount * rho
        lam[k + 1, inside, :] = amount * move
        for i in range(comps):
            mobile[i, k + 1, inside, :] = held[i, k] * move
        return carry

    lax.fori_loop(0, strips, single, 0)

    half = WIDE * SUB
    halves = pack.shape[1] // half
    slots = halves * half
    own_count = counts[0]
    held_rows = held.reshape(comps * strips * layers, BLK)
    mobile_rows = mobile.reshape(comps * (strips + 2) * padded, BLK)
    pack_rows = pack.reshape(comps * slots, BLK)
    liquid_rows = liquid.reshape(comps * slots, BLK)
    vapour_rows = vapour.reshape(comps * slots, BLK)
    bits = strips.bit_length() - 1

    def place(slot):
        block = block_ids[jnp.minimum(slot, own_count - 1)]
        layer = lax.shift_right_logical(block, bits)
        return block - lax.shift_left(layer, bits), layer

    def field_at(k, layer):
        return pl.ds(k * layers + layer, comps, stride=strips * layers)

    def mobile_at(k, layer):
        return pl.ds((k + 1) * padded + layer + SUB, comps, stride=(strips + 2) * padded)

    places = [place(r) for r in range(slots)]
    for r, (k, layer) in enumerate(places):
        pack_rows[pl.ds(r, comps, stride=slots), :] = held_rows[field_at(k, layer), :]
        pack_pres[r : r + 1, :] = pres[k + 1, pl.ds(layer + SUB, 1), :]

    class Half:
        pass

    def prepare(h):
        it = Half()
        it.rows = slice(h * half, (h + 1) * half)
        it.buffers = (2 * h, 2 * h + 1)
        it.pressure = pack_pres[it.rows, :]
        it.amount = pack[0, it.rows, :]
        for i in range(1, comps):
            it.amount = it.amount + pack[i, it.rows, :]
        inv_amount = recip(it.amount)
        for i in range(comps):
            pack[i, it.rows, :] = pack[i, it.rows, :] * inv_amount
        log_pres = jnp.log(it.pressure)
        for i in range(comps):
            keep_k(it, i, wilson[i] - log_pres)
        return it

    def keep_k(it, i, log_k):
        inv_excess[i, it.rows, :] = recip((jnp.exp(log_k) - 1.0) + TINY)

    def split_phases(it, with_low):
        part = jnp.full((half, BLK), 0.5, jnp.float32)
        for _ in range(RR_ITERS):
            value = jnp.zeros((half, BLK), jnp.float32)
            slope = jnp.full((half, BLK), 0.05, jnp.float32)
            for i in range(comps):
                ratio = recip(inv_excess[i, it.rows, :] + part)
                term = pack[i, it.rows, :] * ratio
                value = value + term
                slope = slope + term * ratio
            part = jnp.minimum(jnp.maximum(part + value * recip(slope), 0.0), 1.0)
        it.part = part
        for j in range(comps // 2):
            pair = []
            for i in (2 * j, 2 * j + 1):
                fraction = pack[i, it.rows, :]
                term = fraction * recip(inv_excess[i, it.rows, :] + part)
                liq = fraction - part * term
                liquid[i, it.rows, :] = liq
                vapour[i, it.rows, :] = liq + term
                pair.append(liq)
            for g in range(WIDE):
                put_halves(it.buffers[0], j, g, [value[rows_of(g)] for value in pair], with_low)
        multiply(it.buffers[0], half * BLK // SUB, with_low)
        for j in range(comps // 2):
            pair = [vapour[i, it.rows, :] for i in (2 * j, 2 * j + 1)]
            for g in range(WIDE):
                put_halves(it.buffers[1], j, g, [value[rows_of(g)] for value in pair], with_low)
        multiply(it.buffers[1], half * BLK // SUB, with_low)
        it.sums = [added(lambda i: ref[i, it.rows, :]) for ref in (liquid, vapour)]

    def solve_phases(it, with_low):
        it.phases = []
        equations = []
        for ref, n, flag, (whole, b_sum) in zip(
            (liquid, vapour), it.buffers, (False, True), it.sums
        ):
            quad = quadratic(lambda i: ref[i, it.rows, :], n, WIDE, with_low)
            inv_whole = recip(whole)
            b_mix = b_sum * inv_whole
            a_mix = quad * inv_whole * inv_whole
            big_b = it.pressure * b_mix
            start = jnp.ones_like(big_b) if flag else 2.0 * big_b
            equations.append(cubic(it.pressure * a_mix, big_b, start, flag))
            it.phases.append((quad, whole, inv_whole, a_mix, b_mix, big_b))
        it.factors = roots_of(*equations)

    def renew_k(it):
        parts = []
        for (quad, whole, _, a_mix, b_mix, big_b), z_factor in zip(it.phases, it.factors):
            log_arg = (z_factor + (1.0 + SQRT_TWO) * big_b) * recip(
                z_factor + (1.0 - SQRT_TWO) * big_b
            )
            inv_b = recip(b_mix)
            depart = a_mix * inv_b * (1.0 / (2.0 * SQRT_TWO)) * jnp.log(log_arg)
            of_cov = (z_factor - 1.0 + depart) * inv_b
            of_sum = 2.0 * depart * whole * recip(quad)
            parts.append((of_cov, jnp.log(z_factor - big_b), of_sum))
        cov_gap = parts[0][0] - parts[1][0]
        log_gap = parts[0][1] - parts[1][1]
        for i in range(comps):
            log_k = (
                covolume[i] * cov_gap
                - log_gap
                - parts[0][2] * total(it.buffers[0], i, WIDE)
                + parts[1][2] * total(it.buffers[1], i, WIDE)
            )
            keep_k(it, i, jnp.minimum(jnp.maximum(log_k, -3.0), 3.0))

    def finish(it):
        part = it.part
        rho_liq = it.amount * it.pressure * recip(it.factors[0])
        rho_vap = it.amount * it.pressure * recip(it.factors[1])
        rest = 1.0 - part
        move_liq = rest * rest * rho_liq
        move_vap = 4.0 * part * part * rho_vap
        hold_liq = rest * rho_liq
        hold_vap = part * rho_vap
        out_cell[0, it.rows, :] = part
        out_cell[1, it.rows, :] = move_liq + move_vap
        out_cell[2, it.rows, :] = hold_liq + hold_vap
        inv_liq, inv_vap = it.phases[0][2], it.phases[1][2]
        move_liq = move_liq * inv_liq
        move_vap = move_vap * inv_vap
        hold_liq = hold_liq * inv_liq
        hold_vap = hold_vap * inv_vap
        for i in range(comps):
            liq, gas = liquid[i, it.rows, :], vapour[i, it.rows, :]
            liquid[i, it.rows, :] = move_liq * liq + move_vap * gas
            vapour[i, it.rows, :] = hold_liq * liq + hold_vap * gas

    items = [prepare(h) for h in range(halves)]
    for sweep in range(SS_ITERS):
        with_low = sweep + 1 < SS_ITERS
        for it in items:
            split_phases(it, with_low)
        for it in items:
            solve_phases(it, with_low)
            if with_low:
                renew_k(it)
            else:
                finish(it)

    one_row = jnp.ones((1, BLK), jnp.float32)
    for r, (k, layer) in enumerate(places):
        of = pl.ds(r, comps, stride=slots)
        mobile_rows[mobile_at(k, layer), :] = liquid_rows[of, :]
        held_rows[field_at(k, layer), :] = vapour_rows[of, :]
        one = slice(r, r + 1)
        row = pl.ds(layer, 1)
        vap[k, row, :] = out_cell[0, one, :]
        lam[k + 1, pl.ds(layer + SUB, 1), :] = out_cell[1, one, :]
        csum[k, row, :] = out_cell[2, one, :]
        scale[k, row, :] = one_row

    for k in range(strips):
        strip_in(old_hbm, old, old_sem, k).wait()
    old_rows = old.reshape(comps * strips * layers, BLK)
    for edge, at, inner in ((top_edge, 0, 1), (low_edge, layers - 1, layers - 2)):
        for k in range(strips):
            lanes = slice(k * BLK, (k + 1) * BLK)
            here = slice(at, at + 1)
            pad_here = slice(SUB + at, SUB + at + 1)
            pad_inner = slice(SUB + inner, SUB + inner + 1)
            edge[0:comps, lanes] = mobile_rows[mobile_at(k, at), :]
            values = [None] * EDGE_ROWS
            values[EDGE_PRES] = pres[k + 1, pad_here, :]
            values[EDGE_PERM] = perm[k + 1, pad_here, :]
            values[EDGE_LAM] = lam[k + 1, pad_here, :]
            values[EDGE_CSUM] = csum[k, here, :]
            values[EDGE_OSUM] = jnp.sum(old_rows[field_at(k, at), :], 0, keepdims=True)
            values[EDGE_PRES2] = pres[k + 1, pad_inner, :]
            values[EDGE_PERM2] = perm[k + 1, pad_inner, :]
            values[EDGE_LAM2] = lam[k + 1, pad_inner, :]
            for n, value in enumerate(values):
                edge[comps + n : comps + n + 1, lanes] = value
    edge_copies = [
        pltpu.make_async_copy(edge, edges_hbm.at[pl.ds(n * EDGE_SPAN, EDGE_SPAN), :], edge_sem.at[n])
        for n, edge in enumerate((top_edge, low_edge))
    ]
    for copy in edge_copies:
        copy.start()
    for k in range(strips):
        pres_flat[:, k * BLK : (k + 1) * BLK] = vap[k]
    vap_copy = pltpu.make_async_copy(pres_flat, vap_hbm, cell_sem.at[0])
    vap_copy.start()

    vap_copy.wait()
    for copy in edge_copies:
        copy.wait()


def flux_kernel(
    held,
    old,
    mobile,
    pres,
    perm,
    lam,
    scale,
    csum,
    resid_hbm,
    step_hbm,
    top_aux,
    low_aux,
    resid,
    first,
    row_sum,
    diag,
    weights,
    step,
    step_sem,
    out_sem,
):
    comps, strips, layers, _ = held.shape
    groups = layers // SUB

    def lanes_of(k):
        return pl.ds(pl.multiple_of(k * BLK, BLK), BLK)

    def strip_out(k):
        return pltpu.make_async_copy(resid.at[:, k], resid_hbm.at[:, :, lanes_of(k)], out_sem.at[k])

    zero_tile = jnp.zeros((SUB, BLK), jnp.float32)
    for k in range(strips + 2):
        for g in range(groups + 2):
            if k in (0, strips + 1) or g in (0, groups + 1):
                first[k, rows_of(g), :] = zero_tile

    lane_index = lax.broadcasted_iota(jnp.int32, (SUB, BLK), 1)
    is_last_lane = lane_index == BLK - 1
    is_first_lane = lane_index == 0

    def around(load, k, g):
        at = SUB * (g + 1)
        here = load(k + 1, slice(at, at + SUB))
        up = load(k + 1, slice(at - 1, at + SUB - 1))
        down = load(k + 1, slice(at + 1, at + SUB + 1))
        before = load(k, slice(at, at + SUB))
        after = load(k + 2, slice(at, at + SUB))
        left = pltpu.roll(jnp.where(is_last_lane, before, here), 1, 1)
        right = pltpu.roll(jnp.where(is_first_lane, after, here), BLK - 1, 1)
        return here, (up, down, left, right)

    def fluxes(k, carry):
        for g in range(groups):
            rows = rows_of(g)
            p_here, p_near = around(lambda s, r: pres[s, r, :], k, g)
            k_here, k_near = around(lambda s, r: perm[s, r, :], k, g)
            l_here, l_near = around(lambda s, r: lam[s, r, :], k, g)
            drives = []
            couplings = []
            for n in range(4):
                transmiss = k_here * k_near[n] * recip(k_here + k_near[n])
                drives.append((TIME_STEP * transmiss) * (p_here - p_near[n]))
                couplings.append(transmiss * (l_here + l_near[n]))
            drive_sum = (drives[0] + drives[1]) + (drives[2] + drives[3])
            content_scale = scale[k, rows, :]
            row_total = zero_tile
            for i in range(comps):
                m_here, m_near = around(lambda s, r, i=i: mobile[i, s, r, :], k, g)
                value = held[i, k, rows, :] * content_scale - old[i, k, rows, :]
                value = value + drive_sum * m_here
                value = value + (drives[0] * m_near[0] + drives[1] * m_near[1])
                value = value + (drives[2] * m_near[2] + drives[3] * m_near[3])
                resid[i, k, rows, :] = value
                row_total = row_total + value
            diagonal = TIME_STEP * (
                (couplings[0] + couplings[1]) + (couplings[2] + couplings[3])
            ) + csum[k, rows, :] * recip(p_here)
            inv_diag = recip(diagonal)
            row_sum[k, rows, :] = row_total
            diag[k, rows, :] = diagonal
            first[k + 1, SUB * (g + 1) : SUB * (g + 2), :] = -row_total * inv_diag
            gain = (STEP_SCALE * OFF_SCALE) * inv_diag
            for n in range(4):
                weights[n, k, rows, :] = couplings[n] * gain
        strip_out(k).start()
        return carry

    lax.fori_loop(0, strips, fluxes, 0)

    def steps(k, carry):
        for g in range(groups):
            rows = rows_of(g)
            here, near = around(lambda s, r: first[s, r, :], k, g)
            step[rows, lanes_of(k)] = (
                STEP_SCALE * here
                + (weights[0, k, rows, :] * near[0] + weights[1, k, rows, :] * near[1])
                + (weights[2, k, rows, :] * near[2] + weights[3, k, rows, :] * near[3])
            )
        return carry

    lax.fori_loop(0, strips, steps, 0)
    step_copy = pltpu.make_async_copy(step, step_hbm, step_sem)
    step_copy.start()

    resid_rows = resid.reshape(comps * strips * layers, BLK)
    for aux, at, inner, toward, away in (
        (top_aux, 0, 1, 0, 1),
        (low_aux, layers - 1, layers - 2, 1, 0),
    ):
        for k in range(strips):
            lanes = slice(k * BLK, (k + 1) * BLK)
            here = slice(at, at + 1)
            behind = slice(inner, inner + 1)
            from_row = pl.ds(k * layers + at, comps, stride=strips * layers)
            aux[0:comps, lanes] = resid_rows[from_row, :]
            unscale = diag[k, here, :]
            values = [None] * AUX_ROWS
            values[AUX_IN] = weights[away, k, here, :] * unscale
            values[AUX_LEFT] = weights[2, k, here, :] * unscale
            values[AUX_RIGHT] = weights[3, k, here, :] * unscale
            values[AUX_FIRST] = first[k + 1, SUB + inner : SUB + inner + 1, :]
            values[AUX_GAIN] = weights[toward, k, behind, :]
            values[AUX_STEP] = step[behind, lanes]
            values[AUX_ROW] = row_sum[k, here, :]
            values[AUX_DIAG] = unscale
            for n, value in enumerate(values):
                aux[comps + n : comps + n + 1, lanes] = value
    step_copy.wait()
    for k in range(strips):
        strip_out(k).wait()


def transmissibility(perm, perm_near):
    both = perm + perm_near
    return perm * perm_near / jnp.where(both == 0.0, 1.0, both)


def edge_kernel(
    top_edge,
    low_edge,
    top_aux,
    low_aux,
    in_even,
    in_odd,
    resid_in,
    step_in,
    resid_hbm,
    step_hbm,
    from_prev,
    from_next,
    resid,
    step,
    in_sem,
    sem,
):
    comps, layers, face = resid_hbm.shape
    me = lax.axis_index("dev")
    odd = lax.rem(me, 2) == 1

    def arrivals(prev_pair, next_pair):
        return [
            pltpu.make_async_copy(
                pair.at[pl.ds((n + 1) * EDGE_SPAN, EDGE_SPAN), :], target, in_sem.at[n]
            )
            for n, (pair, target) in enumerate(((prev_pair, from_prev), (next_pair, from_next)))
        ]

    @pl.when(odd)
    def _():
        for copy in arrivals(in_even, in_odd):
            copy.start()

    @pl.when(jnp.logical_not(odd))
    def _():
        for copy in arrivals(in_odd, in_even):
            copy.start()

    for copy in arrivals(in_even, in_odd):
        copy.wait()
    copies = []
    for n, (edge, aux, other, at, inner, linked) in enumerate(
        (
            (top_edge, top_aux, from_prev, 0, 1, me > 0),
            (low_edge, low_aux, from_next, layers - 1, layers - 2, me < lax.axis_size("dev") - 1),
        )
    ):

        def own(index):
            return edge[comps + index : comps + index + 1, :]

        def far(index):
            return other[comps + index : comps + index + 1, :]

        def near(index):
            return aux[comps + index : comps + index + 1, :]

        pres_far, lam_far = far(EDGE_PRES), far(EDGE_LAM)
        perm_far = jnp.where(linked, far(EDGE_PERM), 0.0)
        transmiss = transmissibility(own(EDGE_PERM), perm_far)
        drive = TIME_STEP * transmiss * (own(EDGE_PRES) - pres_far)
        lam_both = own(EDGE_LAM) + lam_far
        coupling = transmiss * lam_both
        row = near(AUX_ROW) + drive * lam_both
        diag = near(AUX_DIAG) + TIME_STEP * coupling
        first = -row / diag
        first_old = -near(AUX_ROW) / near(AUX_DIAG)
        row_far = far(EDGE_CSUM) - far(EDGE_OSUM) - drive * lam_both
        diag_far = coupling
        lane = lax.broadcasted_iota(jnp.int32, (1, face), 1)
        sides = [(far(EDGE_PRES2), far(EDGE_PERM2), far(EDGE_LAM2))]
        for shift, end in ((1, 0), (face - 1, face - 1)):
            pres_n, perm_n, lam_n = (pltpu.roll(x, shift, 1) for x in (pres_far, perm_far, lam_far))
            sides.append((pres_n, jnp.where(lane == end, 0.0, perm_n), lam_n))
        for pres_n, perm_n, lam_n in sides:
            joint = transmissibility(perm_far, perm_n) * (lam_far + lam_n)
            row_far = row_far + TIME_STEP * joint * (pres_far - pres_n)
            diag_far = diag_far + joint
        diag_far = TIME_STEP * diag_far + far(EDGE_CSUM) / jnp.where(pres_far == 0.0, 1.0, pres_far)
        first_far = -row_far / jnp.where(diag_far == 0.0, 1.0, diag_far)
        off = (
            (STEP_SCALE * OFF_SCALE) * coupling * first_far
            + near(AUX_IN) * near(AUX_FIRST)
            + near(AUX_LEFT) * pltpu.roll(first, 1, 1)
            + near(AUX_RIGHT) * pltpu.roll(first, face - 1, 1)
        )
        least = min(at, inner)
        step[n, at - least : at - least + 1, :] = STEP_SCALE * first + off / diag
        step[n, inner - least : inner - least + 1, :] = near(AUX_STEP) + near(AUX_GAIN) * (
            first - first_old
        )
        resid[n] = aux[0:comps, :] + drive * (edge[0:comps, :] + other[0:comps, :])
        for source, target in (
            (resid.at[n], resid_hbm.at[:, at, :]),
            (step.at[n, 0:2, :], step_hbm.at[least : least + 2, :]),
        ):
            copies.append(pltpu.make_async_copy(source, target, sem.at[len(copies)]))
            copies[-1].start()
    for copy in copies:
        copy.wait()


def on_device(
    moles,
    old_content,
    pressure,
    perm,
    labels,
    roots,
    counts,
    block_ids,
    wilson,
    attraction,
    covolume,
):
    comps, layers, face = moles.shape
    f32 = jnp.float32
    strips = face // BLK
    tables = (block_ids, wilson, attraction, covolume)
    rows_in = comps * SUB
    widest = max(layers // SUB, WIDE) * BLK
    half = WIDE * SUB
    halves = (block_ids.shape[0] + half - 1) // half
    slots = halves * half
    vmem = pl.BlockSpec(memory_space=pltpu.VMEM)
    hbm = pl.BlockSpec(memory_space=pltpu.HBM)
    padded = layers + 2 * SUB
    flat = pltpu.VMEM((layers, face), f32)
    flat_int = pltpu.VMEM((layers, face), jnp.int32)
    cell = pltpu.VMEM((strips, layers, BLK), f32)
    cell_pad = pltpu.VMEM((strips + 2, padded, BLK), f32)
    field = pltpu.VMEM((comps, strips, layers, BLK), f32)
    field_pad = pltpu.VMEM((comps, strips + 2, padded, BLK), f32)
    packed = pltpu.VMEM((comps, slots, BLK), f32)
    edge_shape = pltpu.VMEM((EDGE_SPAN, face), f32)
    edges_shape = jax.ShapeDtypeStruct((2 * EDGE_SPAN, face), f32)
    aux_shape = pltpu.VMEM((comps + AUX_ROWS, face), f32)
    field_shape = jax.ShapeDtypeStruct((comps, layers, face), f32)
    cell_shape = jax.ShapeDtypeStruct((layers, face), f32)
    held_types = [field, field, field_pad] + [cell_pad] * 3 + [cell] * 2
    vapour, edges, top_edge, low_edge, *state = pl.pallas_call(
        cells_kernel,
        out_shape=[cell_shape, edges_shape, edge_shape, edge_shape]
        + held_types,
        in_specs=[pl.BlockSpec(memory_space=pltpu.SMEM)] + [hbm] * 10,
        out_specs=[hbm] * 2 + [vmem] * (2 + len(held_types)),
        scratch_shapes=[cell, flat, flat, flat_int, flat_int]
        + [pltpu.VMEM((2 * rows_in, rows_in), jnp.bfloat16)]
        + [pltpu.VMEM((2 * halves, rows_in, widest), jnp.bfloat16)] * 2
        + [pltpu.VMEM((2 * halves, rows_in, widest), f32)]
        + [packed, pltpu.VMEM((slots, BLK), f32)]
        + [packed] * 3
        + [pltpu.VMEM((3, slots, BLK), f32)]
        + [pltpu.SMEM(table.shape, table.dtype) for table in tables]
        + [
            pltpu.SemaphoreType.DMA((strips,)),
            pltpu.SemaphoreType.DMA((strips,)),
            pltpu.SemaphoreType.DMA((4,)),
            pltpu.SemaphoreType.DMA((len(tables),)),
            pltpu.SemaphoreType.DMA((2,)),
        ],
        compiler_params=pltpu.CompilerParams(vmem_limit_bytes=CELLS_VMEM),
        name="cells",
    )(counts, *keep_in(pltpu.HBM, *tables, moles, old_content, pressure, perm, labels, roots))
    count = lax.axis_size("dev")
    pairs = [[[i, (i + 1) % count] for i in range(start, count, 2)] for start in (0, 1)]
    in_even, in_odd = (
        lax.all_gather(edges, "dev", axis_index_groups=groups, tiled=True) for groups in pairs
    )
    residual, step, top_aux, low_aux = pl.pallas_call(
        flux_kernel,
        out_shape=[field_shape, cell_shape, aux_shape, aux_shape],
        in_specs=[vmem] * len(state),
        out_specs=[hbm] * 2 + [vmem] * 2,
        scratch_shapes=[field, cell_pad, cell, cell]
        + [pltpu.VMEM((4, strips, layers, BLK), f32), flat]
        + [pltpu.SemaphoreType.DMA(()), pltpu.SemaphoreType.DMA((strips,))],
        compiler_params=pltpu.CompilerParams(vmem_limit_bytes=FLUX_VMEM),
        name="flux",
    )(*keep_in(pltpu.VMEM, *state))
    residual, step = pl.pallas_call(
        edge_kernel,
        out_shape=[field_shape, cell_shape],
        in_specs=[vmem] * 4 + [hbm] * 4,
        out_specs=[hbm] * 2,
        input_output_aliases={6: 0, 7: 1},
        scratch_shapes=[
            pltpu.VMEM((EDGE_SPAN, face), f32),
            pltpu.VMEM((EDGE_SPAN, face), f32),
            pltpu.VMEM((2, comps, face), f32),
            pltpu.VMEM((2, SUB, face), f32),
            pltpu.SemaphoreType.DMA((2,)),
            pltpu.SemaphoreType.DMA((4,)),
        ],
        compiler_params=pltpu.CompilerParams(vmem_limit_bytes=16 * 1024 * 1024),
        name="edges",
    )(
        *keep_in(pltpu.VMEM, top_edge, low_edge, top_aux, low_aux),
        *keep_in(pltpu.HBM, in_even, in_odd),
        residual,
        step,
    )
    return (residual, step, vapour)


def solution(mesh):
    in_specs = (
        P(None, "dev", None),
        P(None, "dev", None),
        P("dev", None),
        P("dev", None),
        P("dev", None),
        P("dev", None),
        P("dev"),
        P("dev"),
        P(),
        P(),
        P(),
    )
    out_specs = (P(None, "dev", None), P("dev", None), P("dev", None))
    return jax.shard_map(
        on_device, mesh=mesh, in_specs=in_specs, out_specs=out_specs, check_vma=False
    )
```

```python
import math

import jax
import jax.numpy as jnp
from jax import lax
from jax.experimental import pallas as pl
from jax.experimental.pallas import tpu as pltpu
from jax.sharding import PartitionSpec as P

BLK = 128
SUB = 8
SS_ITERS = 3
RR_ITERS = 3
Z_ITERS = 5
WIDE = 8
LOG2E = math.log2(math.e)
CELLS_VMEM = 32 * 1024 * 1024
FLUX_VMEM = 32 * 1024 * 1024

SQRT_TWO = math.sqrt(2.0)
TIME_STEP = 0.5
RELAX = 0.7
STEP_SCALE = 10.0
OFF_SCALE = RELAX * TIME_STEP

EDGE_PRES, EDGE_PERM, EDGE_LAM, EDGE_CSUM, EDGE_OSUM = range(5)
EDGE_PRES2, EDGE_PERM2, EDGE_LAM2 = range(5, 8)
EDGE_ROWS = 8
EDGE_SPAN = 32
AUX_IN, AUX_LEFT, AUX_RIGHT, AUX_FIRST, AUX_GAIN, AUX_STEP, AUX_ROW, AUX_DIAG = range(8)
AUX_ROWS = 8


def keep_in(space, *arrays):
    return [pltpu.with_memory_space_constraint(x, space) for x in arrays]


def recip(value):
    return pltpu.reciprocal(value, approx=True)


def odd_tiles(rows):
    return rows + SUB if (rows // SUB) % 2 == 0 else rows


def split_halves(value):
    high = value.astype(jnp.bfloat16)
    low = (value - high.astype(jnp.float32)).astype(jnp.bfloat16)
    return high, low


def widen(wide, attraction, covolume, comps):
    cols = comps * SUB
    lane = lax.broadcasted_iota(jnp.int32, (SUB, cols), 1)
    row = lax.broadcasted_iota(jnp.int32, (SUB, cols), 0)
    group = lane // SUB
    diagonal = (lane - group * SUB) == row
    zero = jnp.zeros((SUB, cols), jnp.float32)
    coefficients = [
        [0.5 * (attraction[i, j] + attraction[j, i]) for j in range(comps)] for i in range(comps)
    ]
    coefficients.append([covolume[j] for j in range(comps)])
    coefficients.append([1.0] * comps)
    for pair in range(len(coefficients) // 2):
        rows = []
        for i in (2 * pair, 2 * pair + 1):
            full = zero
            for j in range(comps):
                full = jnp.where(group == j, coefficients[i][j], full)
            rows.append(jnp.where(diagonal, full, zero))
        high, low = split_halves(jnp.concatenate(rows, 0))
        wide[2 * SUB * pair : 2 * SUB * (pair + 1), :] = jnp.concatenate([high, low, high], 1)


def rows_of(g):
    return slice(g * SUB, (g + 1) * SUB)


def cubic(big_a, big_b, start, vapour_flag):
    two_b = 2.0 * big_b
    b_square = big_b * big_b
    one_b = 1.0 + big_b
    least = big_b + 0.01
    half_b = 0.5 * big_b
    half_one_b = 0.5 * one_b
    half_a = 0.5 * big_a
    half_inv_a = None if vapour_flag is True else 0.5 * recip(big_a)

    def step(z_factor):
        spread = z_factor * (z_factor + two_b) - b_square
        half_z = 0.5 * z_factor
        if vapour_flag is not False:
            vap = (half_z + half_one_b) - half_a * (z_factor - big_b) * recip(spread)
        if vapour_flag is not True:
            liq = (half_z + half_b) + spread * (one_b - z_factor) * half_inv_a
        if vapour_flag is True:
            new = vap
        elif vapour_flag is False:
            new = liq
        else:
            new = jnp.where(vapour_flag, vap, liq)
        return jnp.minimum(jnp.maximum(new, least), 2.0)

    return start, step


def roots_of(*equations):
    found = [start for start, _ in equations]
    for _ in range(Z_ITERS):
        found = [step(z_factor) for z_factor, (_, step) in zip(found, equations)]
    return found


def cells_kernel(
    counts,
    block_ids_hbm,
    wilson_hbm,
    attraction_hbm,
    covolume_hbm,
    moles_hbm,
    old_hbm,
    pres_hbm,
    perm_hbm,
    labels_hbm,
    roots_hbm,
    vap_hbm,
    edges,
    held,
    old,
    mobile,
    pres,
    perm,
    lam,
    scale,
    csum,
    vap,
    pres_flat,
    perm_flat,
    labels,
    roots,
    w_wide,
    x_wide,
    sums,
    pack,
    pack_pres,
    inv_excess,
    liquid,
    vapour,
    out_cell,
    block_ids,
    wilson,
    attraction,
    covolume,
    in_sem,
    old_sem,
    cell_sem,
    table_sem,
):
    comps, layers, face = moles_hbm.shape
    strips = face // BLK
    groups = layers // SUB
    padded = layers + 2 * SUB
    inside = slice(SUB, SUB + layers)

    def lanes_of(k):
        return pl.ds(pl.multiple_of(k * BLK, BLK), BLK)

    def strip_of(k):
        return pl.ds(pl.multiple_of(k * layers, SUB), layers)

    def strip_in(source, target, sem, k):
        return pltpu.make_async_copy(
            source.at[:, :, lanes_of(k)], target.at[:, strip_of(k), :], sem.at[k]
        )

    cell_copies = [
        pltpu.make_async_copy(pres_hbm, pres_flat, cell_sem.at[0]),
        pltpu.make_async_copy(roots_hbm, roots, cell_sem.at[1]),
        pltpu.make_async_copy(labels_hbm, labels, cell_sem.at[2]),
        pltpu.make_async_copy(perm_hbm, perm_flat, cell_sem.at[3]),
    ]
    table_copies = [
        pltpu.make_async_copy(source, target, table_sem.at[n])
        for n, (source, target) in enumerate(
            (
                (attraction_hbm, attraction),
                (covolume_hbm, covolume),
                (wilson_hbm, wilson),
                (block_ids_hbm, block_ids),
            )
        )
    ]
    for copy in table_copies + cell_copies:
        copy.start()
    for k in range(strips):
        strip_in(moles_hbm, held, in_sem, k).start()
    for k in range(strips):
        strip_in(old_hbm, old, old_sem, k).start()

    zero_tile = jnp.zeros((SUB, BLK), jnp.float32)
    zero_strip = jnp.zeros((padded, BLK), jnp.float32)

    for ref in (pres, perm, lam):
        for k in (0, strips + 1):
            ref[k] = zero_strip
        for k in range(1, strips + 1):
            ref[k, 0:SUB] = zero_tile
            ref[k, SUB + layers : padded] = zero_tile
    for i in range(comps):
        for k in (0, strips + 1):
            mobile[i, k * padded : (k + 1) * padded, :] = zero_strip
        for k in range(1, strips + 1):
            mobile[i, k * padded : k * padded + SUB, :] = zero_tile
            mobile[i, (k + 1) * padded - SUB : (k + 1) * padded, :] = zero_tile
    for copy in table_copies:
        copy.wait()
    widen(w_wide, attraction, covolume, comps)

    cols = comps * SUB

    def multiply(width):
        lanes = slice(0, width)
        sums[:, lanes] = jnp.dot(
            w_wide[...], x_wide[:, lanes], preferred_element_type=jnp.float32
        )

    def total(at, start, count):
        rows = slice(at * SUB, (at + 1) * SUB)
        return jnp.concatenate(
            [sums[rows, g * BLK : (g + 1) * BLK] for g in range(start, start + count)], 0
        )

    def put_halves(j, g, pair):
        high, low = split_halves(jnp.concatenate(pair, 0))
        lanes = slice(g * BLK, (g + 1) * BLK)
        for n, value in enumerate((high, high, low)):
            at = n * cols + 2 * SUB * j
            x_wide[at : at + 2 * SUB, lanes] = value

    def mixture(values, start, count):
        quad = values(0) * total(0, start, count)
        for i in range(1, comps):
            quad = quad + values(i) * total(i, start, count)
        return total(comps + 1, start, count), total(comps, start, count), quad

    for copy in cell_copies:
        copy.wait()
    for k in range(strips):
        pres[k + 1, inside, :] = pres_flat[:, k * BLK : (k + 1) * BLK]
        perm[k + 1, inside, :] = perm_flat[:, k * BLK : (k + 1) * BLK]

    def padded_of(k):
        return pl.ds(pl.multiple_of((k + 1) * padded + SUB, SUB), layers)

    def single(k, carry):
        strip_in(moles_hbm, held, in_sem, k).wait()
        for j in range(comps // 2):
            for g in range(groups):
                rows = pl.ds(pl.multiple_of(k * layers + g * SUB, SUB), SUB)
                put_halves(j, g, [held[i, rows, :] for i in (2 * j, 2 * j + 1)])
        multiply(groups * BLK)
        amount, b_sum, quad = mixture(lambda i: held[i, strip_of(k), :], 0, groups)
        pressure = pres[k + 1, inside, :]
        inv_amount = recip(amount)
        big_a = pressure * quad * inv_amount * inv_amount
        big_b = pressure * b_sum * inv_amount
        is_vapour = roots[:, lanes_of(k)] == 1
        start = jnp.where(is_vapour, 1.0, 2.0 * big_b)
        (z_factor,) = roots_of(cubic(big_a, big_b, start, is_vapour))
        rho = pressure * recip(z_factor)
        part = labels[:, lanes_of(k)].astype(jnp.float32)
        move = ((1.0 - part) * (1.0 - part) + 4.0 * part * part) * rho
        vap[k] = part
        scale[k] = rho
        csum[k] = amount * rho
        lam[k + 1, inside, :] = amount * move
        for i in range(comps):
            mobile[i, padded_of(k), :] = held[i, strip_of(k), :] * move
        return carry

    lax.fori_loop(0, strips, single, 0)

    batch = WIDE * SUB
    own_count = counts[0]
    held_stride, mobile_stride, pack_stride = (ref.shape[1] for ref in (held, mobile, pack))
    held_rows = held.reshape(comps * held_stride, BLK)
    mobile_rows = mobile.reshape(comps * mobile_stride, BLK)
    pack_rows = pack.reshape(comps * pack_stride, BLK)
    liquid_rows = liquid.reshape(comps * pack_stride, BLK)
    vapour_rows = vapour.reshape(comps * pack_stride, BLK)
    bits = strips.bit_length() - 1

    def place(slot):
        block = block_ids[jnp.minimum(slot, own_count - 1)]
        layer = lax.shift_right_logical(block, bits)
        return block - lax.shift_left(layer, bits), layer

    def field_at(k, layer):
        return pl.ds(k * layers + layer, comps, stride=held_stride)

    def mobile_at(k, layer):
        return pl.ds((k + 1) * padded + layer + SUB, comps, stride=mobile_stride)

    def flash(number, carry):
        base = number * batch
        places = [place(base + r) for r in range(batch)]
        for r, (k, layer) in enumerate(places):
            pack_rows[pl.ds(r, comps, stride=pack_stride), :] = held_rows[field_at(k, layer), :]
            pack_pres[r : r + 1, :] = pres[k + 1, pl.ds(layer + SUB, 1), :]
        slots = slice(0, batch)
        pressure = pack_pres[...]
        amount = pack[0, slots, :]
        for i in range(1, comps):
            amount = amount + pack[i, slots, :]
        inv_amount = recip(amount)
        for i in range(comps):
            pack[i, slots, :] = pack[i, slots, :] * inv_amount

        def keep_k(i, log2_k):
            inv_excess[i, slots, :] = recip(jnp.exp2(log2_k) - 1.0)

        log2_pres = jnp.log(pressure) * LOG2E
        for i in range(comps):
            keep_k(i, wilson[i] * LOG2E - log2_pres)
        for sweep in range(SS_ITERS):
            part = jnp.full((batch, BLK), 0.5, jnp.float32)
            for _ in range(RR_ITERS):
                value = jnp.zeros((batch, BLK), jnp.float32)
                slope = jnp.full((batch, BLK), 0.05, jnp.float32)
                for i in range(comps):
                    ratio = recip(inv_excess[i, slots, :] + part)
                    term = pack[i, slots, :] * ratio
                    value = value + term
                    slope = slope + term * ratio
                part = jnp.minimum(jnp.maximum(part + value * recip(slope), 0.0), 1.0)
            for j in range(comps // 2):
                pairs = ([], [])
                for i in (2 * j, 2 * j + 1):
                    fraction = pack[i, slots, :]
                    term = fraction * recip(inv_excess[i, slots, :] + part)
                    liq = fraction - part * term
                    gas = liq + term
                    liquid[i, slots, :] = liq
                    vapour[i, slots, :] = gas
                    pairs[0].append(liq)
                    pairs[1].append(gas)
                for n, pair in enumerate(pairs):
                    for g in range(WIDE):
                        put_halves(j, n * WIDE + g, [value[rows_of(g)] for value in pair])
            multiply(2 * WIDE * BLK)
            phases = []
            equations = []
            for n, (ref, flag) in enumerate(((liquid, False), (vapour, True))):
                whole, b_sum, quad = mixture(lambda i: ref[i, slots, :], n * WIDE, WIDE)
                inv_whole = recip(whole)
                b_mix = b_sum * inv_whole
                a_mix = quad * inv_whole * inv_whole
                big_b = pressure * b_mix
                start = jnp.ones_like(big_b) if flag else 2.0 * big_b
                equations.append(cubic(pressure * a_mix, big_b, start, flag))
                phases.append((quad, whole, inv_whole, a_mix, b_mix, big_b))
            factors = roots_of(*equations)
            if sweep + 1 < SS_ITERS:
                parts = []
                for (quad, whole, _, a_mix, b_mix, big_b), z_factor in zip(phases, factors):
                    log_arg = (z_factor + (1.0 + SQRT_TWO) * big_b) * recip(
                        z_factor + (1.0 - SQRT_TWO) * big_b
                    )
                    inv_b = recip(b_mix)
                    depart = a_mix * inv_b * (1.0 / (2.0 * SQRT_TWO)) * jnp.log(log_arg)
                    of_cov = (LOG2E * inv_b) * (z_factor - 1.0 + depart)
                    of_sum = (2.0 * LOG2E) * depart * whole * recip(quad)
                    parts.append((of_cov, LOG2E * jnp.log(z_factor - big_b), of_sum))
                cov_gap = parts[0][0] - parts[1][0]
                log_gap = parts[0][1] - parts[1][1]
                for i in range(comps):
                    log2_k = (covolume[i] * cov_gap - log_gap) - (
                        parts[0][2] * total(i, 0, WIDE) - parts[1][2] * total(i, WIDE, WIDE)
                    )
                    keep_k(i, jnp.minimum(jnp.maximum(log2_k, -3.0 * LOG2E), 3.0 * LOG2E))
        rho_liq = amount * pressure * recip(factors[0])
        rho_vap = amount * pressure * recip(factors[1])
        rest = 1.0 - part
        move_liq = rest * rest * rho_liq
        move_vap = 4.0 * part * part * rho_vap
        hold_liq = rest * rho_liq
        hold_vap = part * rho_vap
        out_cell[0] = part
        out_cell[1] = move_liq + move_vap
        out_cell[2] = hold_liq + hold_vap
        move_liq = move_liq * phases[0][2]
        move_vap = move_vap * phases[1][2]
        hold_liq = hold_liq * phases[0][2]
        hold_vap = hold_vap * phases[1][2]
        for i in range(comps):
            liq, gas = liquid[i, slots, :], vapour[i, slots, :]
            liquid[i, slots, :] = move_liq * liq + move_vap * gas
            vapour[i, slots, :] = hold_liq * liq + hold_vap * gas
        one_row = jnp.ones((1, BLK), jnp.float32)
        for r, (k, layer) in enumerate(places):
            of = pl.ds(r, comps, stride=pack_stride)
            mobile_rows[mobile_at(k, layer), :] = liquid_rows[of, :]
            held_rows[field_at(k, layer), :] = vapour_rows[of, :]
            one = slice(r, r + 1)
            row = pl.ds(layer, 1)
            vap[k, row, :] = out_cell[0, one, :]
            lam[k + 1, pl.ds(layer + SUB, 1), :] = out_cell[1, one, :]
            csum[k, row, :] = out_cell[2, one, :]
            scale[k, row, :] = one_row
        return carry

    lax.fori_loop(0, (own_count + batch - 1) // batch, flash, 0)
    for k in range(strips):
        pres_flat[:, k * BLK : (k + 1) * BLK] = vap[k]
    vap_copy = pltpu.make_async_copy(pres_flat, vap_hbm, cell_sem.at[0])
    vap_copy.start()

    for k in range(strips):
        strip_in(old_hbm, old, old_sem, k).wait()
    old_rows = old.reshape(comps * old.shape[1], BLK)
    for n, (at, inner) in enumerate(((0, 1), (layers - 1, layers - 2))):
        base = n * EDGE_SPAN
        for k in range(strips):
            lanes = slice(k * BLK, (k + 1) * BLK)
            here = slice(at, at + 1)
            pad_here = slice(SUB + at, SUB + at + 1)
            pad_inner = slice(SUB + inner, SUB + inner + 1)
            edges[base : base + comps, lanes] = mobile_rows[mobile_at(k, at), :]
            values = [None] * EDGE_ROWS
            values[EDGE_PRES] = pres[k + 1, pad_here, :]
            values[EDGE_PERM] = perm[k + 1, pad_here, :]
            values[EDGE_LAM] = lam[k + 1, pad_here, :]
            values[EDGE_CSUM] = csum[k, here, :]
            values[EDGE_OSUM] = jnp.sum(old_rows[field_at(k, at), :], 0, keepdims=True)
            values[EDGE_PRES2] = pres[k + 1, pad_inner, :]
            values[EDGE_PERM2] = perm[k + 1, pad_inner, :]
            values[EDGE_LAM2] = lam[k + 1, pad_inner, :]
            for m, value in enumerate(values):
                edges[base + comps + m : base + comps + m + 1, lanes] = value
    vap_copy.wait()


def flux_kernel(
    held,
    old,
    mobile,
    pres,
    perm,
    lam,
    scale,
    csum,
    resid_hbm,
    step_hbm,
    top_aux,
    low_aux,
    resid,
    first,
    row_sum,
    diag,
    weights,
    step,
    step_sem,
    out_sem,
):
    comps = held.shape[0]
    strips, layers, _ = scale.shape
    groups = layers // SUB
    padded = layers + 2 * SUB

    def lanes_of(k):
        return pl.ds(pl.multiple_of(k * BLK, BLK), BLK)

    def strip_out(k):
        return pltpu.make_async_copy(resid.at[:, k], resid_hbm.at[:, :, lanes_of(k)], out_sem.at[k])

    zero_tile = jnp.zeros((SUB, BLK), jnp.float32)
    for k in range(strips + 2):
        for g in range(groups + 2):
            if k in (0, strips + 1) or g in (0, groups + 1):
                first[k, rows_of(g), :] = zero_tile

    lane_index = lax.broadcasted_iota(jnp.int32, (SUB, BLK), 1)
    is_last_lane = lane_index == BLK - 1
    is_first_lane = lane_index == 0

    def around(load, k, g):
        at = SUB * (g + 1)
        here = load(k + 1, slice(at, at + SUB))
        up = load(k + 1, slice(at - 1, at + SUB - 1))
        down = load(k + 1, slice(at + 1, at + SUB + 1))
        before = load(k, slice(at, at + SUB))
        after = load(k + 2, slice(at, at + SUB))
        left = pltpu.roll(jnp.where(is_last_lane, before, here), 1, 1)
        right = pltpu.roll(jnp.where(is_first_lane, after, here), BLK - 1, 1)
        return here, (up, down, left, right)

    def fluxes(k, carry):
        for g in range(groups):
            rows = rows_of(g)
            p_here, p_near = around(lambda s, r: pres[s, r, :], k, g)
            k_here, k_near = around(lambda s, r: perm[s, r, :], k, g)
            l_here, l_near = around(lambda s, r: lam[s, r, :], k, g)
            drives = []
            couplings = []
            for n in range(4):
                transmiss = k_here * k_near[n] * recip(k_here + k_near[n])
                drives.append((TIME_STEP * transmiss) * (p_here - p_near[n]))
                couplings.append(transmiss * (l_here + l_near[n]))
            drive_sum = (drives[0] + drives[1]) + (drives[2] + drives[3])
            content_scale = scale[k, rows, :]
            flat_rows = pl.ds(pl.multiple_of(k * layers + g * SUB, SUB), SUB)
            row_total = zero_tile
            for i in range(comps):
                m_here, m_near = around(
                    lambda s, r, i=i: mobile[i, pl.ds(s * padded + r.start, SUB), :], k, g
                )
                value = held[i, flat_rows, :] * content_scale - old[i, flat_rows, :]
                value = value + drive_sum * m_here
                value = value + (drives[0] * m_near[0] + drives[1] * m_near[1])
                value = value + (drives[2] * m_near[2] + drives[3] * m_near[3])
                resid[i, k, rows, :] = value
                row_total = row_total + value
            diagonal = TIME_STEP * (
                (couplings[0] + couplings[1]) + (couplings[2] + couplings[3])
            ) + csum[k, rows, :] * recip(p_here)
            inv_diag = recip(diagonal)
            row_sum[k, rows, :] = row_total
            diag[k, rows, :] = diagonal
            first[k + 1, SUB * (g + 1) : SUB * (g + 2), :] = -row_total * inv_diag
            gain = (STEP_SCALE * OFF_SCALE) * inv_diag
            for n in range(4):
                weights[n, k, rows, :] = couplings[n] * gain
        strip_out(k).start()
        return carry

    lax.fori_loop(0, strips, fluxes, 0)

    def steps(k, carry):
        for g in range(groups):
            rows = rows_of(g)
            here, near = around(lambda s, r: first[s, r, :], k, g)
            step[rows, lanes_of(k)] = (
                STEP_SCALE * here
                + (weights[0, k, rows, :] * near[0] + weights[1, k, rows, :] * near[1])
                + (weights[2, k, rows, :] * near[2] + weights[3, k, rows, :] * near[3])
            )
        return carry

    lax.fori_loop(0, strips, steps, 0)
    step_copy = pltpu.make_async_copy(step, step_hbm, step_sem)
    step_copy.start()

    resid_rows = resid.reshape(comps * strips * layers, BLK)
    for aux, at, inner, toward, away in (
        (top_aux, 0, 1, 0, 1),
        (low_aux, layers - 1, layers - 2, 1, 0),
    ):
        for k in range(strips):
            lanes = slice(k * BLK, (k + 1) * BLK)
            here = slice(at, at + 1)
            behind = slice(inner, inner + 1)
            from_row = pl.ds(k * layers + at, comps, stride=strips * layers)
            aux[0:comps, lanes] = resid_rows[from_row, :]
            unscale = diag[k, here, :]
            values = [None] * AUX_ROWS
            values[AUX_IN] = weights[away, k, here, :] * unscale
            values[AUX_LEFT] = weights[2, k, here, :] * unscale
            values[AUX_RIGHT] = weights[3, k, here, :] * unscale
            values[AUX_FIRST] = first[k + 1, SUB + inner : SUB + inner + 1, :]
            values[AUX_GAIN] = weights[toward, k, behind, :]
            values[AUX_STEP] = step[behind, lanes]
            values[AUX_ROW] = row_sum[k, here, :]
            values[AUX_DIAG] = unscale
            for n, value in enumerate(values):
                aux[comps + n : comps + n + 1, lanes] = value
    step_copy.wait()
    for k in range(strips):
        strip_out(k).wait()


def transmissibility(perm, perm_near):
    both = perm + perm_near
    return perm * perm_near / jnp.where(both == 0.0, 1.0, both)


def edge_kernel(
    edges,
    top_aux,
    low_aux,
    in_even,
    in_odd,
    resid_in,
    step_in,
    resid_hbm,
    step_hbm,
    resid,
    step,
    sem,
):
    comps, layers, face = resid_hbm.shape
    odd = lax.rem(lax.axis_index("dev"), 2) == 1
    top, low = slice(0, EDGE_SPAN), slice(EDGE_SPAN, 2 * EDGE_SPAN)
    from_prev = jnp.where(odd, in_even[low, :], in_odd[low, :])
    from_next = jnp.where(odd, in_odd[top, :], in_even[top, :])
    copies = []
    for n, (edge, aux, other, at, inner) in enumerate(
        (
            (edges[top, :], top_aux, from_prev, 0, 1),
            (edges[low, :], low_aux, from_next, layers - 1, layers - 2),
        )
    ):

        def own(index):
            return edge[comps + index : comps + index + 1, :]

        def far(index):
            return other[comps + index : comps + index + 1, :]

        def near(index):
            return aux[comps + index : comps + index + 1, :]

        pres_far, perm_far, lam_far = far(EDGE_PRES), far(EDGE_PERM), far(EDGE_LAM)
        transmiss = transmissibility(own(EDGE_PERM), perm_far)
        drive = TIME_STEP * transmiss * (own(EDGE_PRES) - pres_far)
        lam_both = own(EDGE_LAM) + lam_far
        coupling = transmiss * lam_both
        row = near(AUX_ROW) + drive * lam_both
        diag = near(AUX_DIAG) + TIME_STEP * coupling
        first = -row / diag
        first_old = -near(AUX_ROW) / near(AUX_DIAG)
        row_far = far(EDGE_CSUM) - far(EDGE_OSUM) - drive * lam_both
        diag_far = coupling
        lane = lax.broadcasted_iota(jnp.int32, (1, face), 1)
        sides = [(far(EDGE_PRES2), far(EDGE_PERM2), far(EDGE_LAM2))]
        for shift, end in ((1, 0), (face - 1, face - 1)):
            pres_n, perm_n, lam_n = (pltpu.roll(x, shift, 1) for x in (pres_far, perm_far, lam_far))
            sides.append((pres_n, jnp.where(lane == end, 0.0, perm_n), lam_n))
        for pres_n, perm_n, lam_n in sides:
            joint = transmissibility(perm_far, perm_n) * (lam_far + lam_n)
            row_far = row_far + TIME_STEP * joint * (pres_far - pres_n)
            diag_far = diag_far + joint
        diag_far = TIME_STEP * diag_far + far(EDGE_CSUM) / jnp.where(pres_far == 0.0, 1.0, pres_far)
        first_far = -row_far / jnp.where(diag_far == 0.0, 1.0, diag_far)
        off = (
            (STEP_SCALE * OFF_SCALE) * coupling * first_far
            + near(AUX_IN) * near(AUX_FIRST)
            + near(AUX_LEFT) * pltpu.roll(first, 1, 1)
            + near(AUX_RIGHT) * pltpu.roll(first, face - 1, 1)
        )
        least = min(at, inner)
        step[n, at - least : at - least + 1, :] = STEP_SCALE * first + off / diag
        step[n, inner - least : inner - least + 1, :] = near(AUX_STEP) + near(AUX_GAIN) * (
            first - first_old
        )
        resid[n] = aux[0:comps, :] + drive * (edge[0:comps, :] + other[0:comps, :])
        for source, target in (
            (resid.at[n], resid_hbm.at[:, at, :]),
            (step.at[n, 0:2, :], step_hbm.at[least : least + 2, :]),
        ):
            copies.append(pltpu.make_async_copy(source, target, sem.at[len(copies)]))
            copies[-1].start()
    for copy in copies:
        copy.wait()


def on_device(
    moles,
    old_content,
    pressure,
    perm,
    labels,
    roots,
    counts,
    block_ids,
    wilson,
    attraction,
    covolume,
):
    comps, layers, face = moles.shape
    f32 = jnp.float32
    strips = face // BLK
    tables = (block_ids, wilson, attraction, covolume)
    rows_in = comps * SUB
    widest = max(layers // SUB, 2 * WIDE) * BLK
    vmem = pl.BlockSpec(memory_space=pltpu.VMEM)
    hbm = pl.BlockSpec(memory_space=pltpu.HBM)
    padded = layers + 2 * SUB
    flat = pltpu.VMEM((layers, face), f32)
    flat_int = pltpu.VMEM((layers, face), jnp.int32)
    cell = pltpu.VMEM((strips, layers, BLK), f32)
    cell_pad = pltpu.VMEM((strips + 2, padded, BLK), f32)
    field = pltpu.VMEM((comps, odd_tiles(strips * layers), BLK), f32)
    field_pad = pltpu.VMEM((comps, odd_tiles((strips + 2) * padded), BLK), f32)
    packed = pltpu.VMEM((comps, odd_tiles(WIDE * SUB), BLK), f32)
    edges_shape = pltpu.VMEM((2 * EDGE_SPAN, face), f32)
    aux_shape = pltpu.VMEM((comps + AUX_ROWS, face), f32)
    field_shape = jax.ShapeDtypeStruct((comps, layers, face), f32)
    cell_shape = jax.ShapeDtypeStruct((layers, face), f32)
    field_out = pltpu.VMEM((comps, strips, layers, BLK), f32)
    held_types = [field, field, field_pad] + [cell_pad] * 3 + [cell] * 2
    vapour, edges, *state = pl.pallas_call(
        cells_kernel,
        out_shape=[cell_shape, edges_shape]
        + held_types,
        in_specs=[pl.BlockSpec(memory_space=pltpu.SMEM)] + [hbm] * 10,
        out_specs=[hbm] + [vmem] * (1 + len(held_types)),
        scratch_shapes=[cell, flat, flat, flat_int, flat_int]
        + [pltpu.VMEM((rows_in + 2 * SUB, 3 * rows_in), jnp.bfloat16)]
        + [pltpu.VMEM((3 * rows_in, widest), jnp.bfloat16)]
        + [pltpu.VMEM((rows_in + 2 * SUB, widest), f32)]
        + [packed, pltpu.VMEM((WIDE * SUB, BLK), f32)]
        + [packed] * 3
        + [pltpu.VMEM((3, WIDE * SUB, BLK), f32)]
        + [pltpu.SMEM(table.shape, table.dtype) for table in tables]
        + [
            pltpu.SemaphoreType.DMA((strips,)),
            pltpu.SemaphoreType.DMA((strips,)),
            pltpu.SemaphoreType.DMA((4,)),
            pltpu.SemaphoreType.DMA((len(tables),)),
        ],
        compiler_params=pltpu.CompilerParams(vmem_limit_bytes=CELLS_VMEM),
        name="cells",
    )(counts, *keep_in(pltpu.HBM, *tables, moles, old_content, pressure, perm, labels, roots))
    count = lax.axis_size("dev")
    arrived = []
    for start in (0, 1):
        pairs = [(i, i + 1) for i in range(start, count - 1, 2)]
        arrived.append(lax.ppermute(edges, "dev", pairs + [pair[::-1] for pair in pairs]))
    residual, step, top_aux, low_aux = pl.pallas_call(
        flux_kernel,
        out_shape=[field_shape, cell_shape, aux_shape, aux_shape],
        in_specs=[vmem] * len(state),
        out_specs=[hbm] * 2 + [vmem] * 2,
        scratch_shapes=[field_out, cell_pad, cell, cell]
        + [pltpu.VMEM((4, strips, layers, BLK), f32), flat]
        + [pltpu.SemaphoreType.DMA(()), pltpu.SemaphoreType.DMA((strips,))],
        compiler_params=pltpu.CompilerParams(vmem_limit_bytes=FLUX_VMEM),
        name="flux",
    )(*keep_in(pltpu.VMEM, *state))
    residual, step = pl.pallas_call(
        edge_kernel,
        out_shape=[field_shape, cell_shape],
        in_specs=[vmem] * 5 + [hbm] * 2,
        out_specs=[hbm] * 2,
        input_output_aliases={5: 0, 6: 1},
        scratch_shapes=[
            pltpu.VMEM((2, comps, face), f32),
            pltpu.VMEM((2, SUB, face), f32),
            pltpu.SemaphoreType.DMA((4,)),
        ],
        compiler_params=pltpu.CompilerParams(vmem_limit_bytes=16 * 1024 * 1024),
        name="edges",
    )(edges, top_aux, low_aux, *arrived, residual, step)
    return (residual, step, vapour)


def solution(mesh):
    in_specs = (
        P(None, "dev", None),
        P(None, "dev", None),
        P("dev", None),
        P("dev", None),
        P("dev", None),
        P("dev", None),
        P("dev"),
        P("dev"),
        P(),
        P(),
        P(),
    )
    out_specs = (P(None, "dev", None), P("dev", None), P("dev", None))
    return jax.shard_map(
        on_device, mesh=mesh, in_specs=in_specs, out_specs=out_specs, check_vma=False
    )
```

```python
import math

import jax
import jax.numpy as jnp
from jax import lax
from jax.experimental import pallas as pl
from jax.experimental.pallas import tpu as pltpu
from jax.sharding import PartitionSpec as P

BLK = 128
SUB = 8
SS_ITERS = 3
RR_ITERS = 3
Z_ITERS = 5
WIDE = 8
LOG2E = math.log2(math.e)
CELLS_VMEM = 32 * 1024 * 1024
FLUX_VMEM = 32 * 1024 * 1024

SQRT_TWO = math.sqrt(2.0)
TIME_STEP = 0.5
RELAX = 0.7
STEP_SCALE = 10.0
OFF_SCALE = RELAX * TIME_STEP

EDGE_PRES, EDGE_PERM, EDGE_LAM, EDGE_CSUM, EDGE_OSUM = range(5)
EDGE_PRES2, EDGE_PERM2, EDGE_LAM2 = range(5, 8)
EDGE_ROWS = 8
EDGE_SPAN = 32
AUX_IN, AUX_LEFT, AUX_RIGHT, AUX_FIRST, AUX_GAIN, AUX_STEP, AUX_ROW, AUX_DIAG = range(8)
AUX_ROWS = 8


def keep_in(space, *arrays):
    return [pltpu.with_memory_space_constraint(x, space) for x in arrays]


def recip(value):
    return pltpu.reciprocal(value, approx=True)


def odd_tiles(rows):
    return rows + SUB if (rows // SUB) % 2 == 0 else rows


def split_halves(value):
    high = value.astype(jnp.bfloat16)
    low = (value - high.astype(jnp.float32)).astype(jnp.bfloat16)
    return high, low


def widen(wide, attraction, covolume, comps):
    cols = comps * SUB
    lane = lax.broadcasted_iota(jnp.int32, (SUB, cols), 1)
    row = lax.broadcasted_iota(jnp.int32, (SUB, cols), 0)
    group = lane // SUB
    diagonal = (lane - group * SUB) == row
    zero = jnp.zeros((SUB, cols), jnp.float32)
    coefficients = [
        [0.5 * (attraction[i, j] + attraction[j, i]) for j in range(comps)] for i in range(comps)
    ]
    coefficients.append([covolume[j] for j in range(comps)])
    coefficients.append([1.0] * comps)
    for pair in range(len(coefficients) // 2):
        rows = []
        for i in (2 * pair, 2 * pair + 1):
            full = zero
            for j in range(comps):
                full = jnp.where(group == j, coefficients[i][j], full)
            rows.append(jnp.where(diagonal, full, zero))
        high, low = split_halves(jnp.concatenate(rows, 0))
        wide[2 * SUB * pair : 2 * SUB * (pair + 1), :] = jnp.concatenate([high, low, high], 1)


def rows_of(g):
    return slice(g * SUB, (g + 1) * SUB)


def cubic(big_a, big_b, start, vapour_flag):
    two_b = 2.0 * big_b
    b_square = big_b * big_b
    one_b = 1.0 + big_b
    least = big_b + 0.01
    half_b = 0.5 * big_b
    half_one_b = 0.5 * one_b
    half_a = 0.5 * big_a
    half_inv_a = None if vapour_flag is True else 0.5 * recip(big_a)

    def step(z_factor):
        spread = z_factor * (z_factor + two_b) - b_square
        half_z = 0.5 * z_factor
        if vapour_flag is not False:
            vap = (half_z + half_one_b) - half_a * (z_factor - big_b) * recip(spread)
        if vapour_flag is not True:
            liq = (half_z + half_b) + spread * (one_b - z_factor) * half_inv_a
        if vapour_flag is True:
            new = vap
        elif vapour_flag is False:
            new = liq
        else:
            new = jnp.where(vapour_flag, vap, liq)
        return jnp.minimum(jnp.maximum(new, least), 2.0)

    return start, step


def roots_of(*equations):
    found = [start for start, _ in equations]
    for _ in range(Z_ITERS):
        found = [step(z_factor) for z_factor, (_, step) in zip(found, equations)]
    return found


def cells_kernel(
    counts,
    block_ids_hbm,
    wilson_hbm,
    attraction_hbm,
    covolume_hbm,
    moles_hbm,
    old_hbm,
    pres_hbm,
    perm_hbm,
    labels_hbm,
    roots_hbm,
    edge_a,
    edge_b,
    held,
    old,
    mobile,
    pres,
    perm,
    lam,
    scale,
    csum,
    vap,
    pres_flat,
    perm_flat,
    labels,
    roots,
    w_wide,
    x_wide,
    sums,
    pack,
    pack_pres,
    inv_excess,
    liquid,
    vapour,
    out_cell,
    found,
    block_ids,
    wilson,
    attraction,
    covolume,
    in_sem,
    old_sem,
    cell_sem,
    table_sem,
):
    comps, layers, face = moles_hbm.shape
    strips = face // BLK
    groups = layers // SUB
    padded = layers + 2 * SUB
    inside = slice(SUB, SUB + layers)

    def lanes_of(k):
        return pl.ds(pl.multiple_of(k * BLK, BLK), BLK)

    def strip_of(k):
        return pl.ds(pl.multiple_of(k * layers, SUB), layers)

    def strip_in(source, target, sem, k):
        return pltpu.make_async_copy(
            source.at[:, :, lanes_of(k)], target.at[:, strip_of(k), :], sem.at[k]
        )

    cell_copies = [
        pltpu.make_async_copy(pres_hbm, pres_flat, cell_sem.at[0]),
        pltpu.make_async_copy(roots_hbm, roots, cell_sem.at[1]),
        pltpu.make_async_copy(labels_hbm, labels, cell_sem.at[2]),
        pltpu.make_async_copy(perm_hbm, perm_flat, cell_sem.at[3]),
    ]
    table_copies = [
        pltpu.make_async_copy(source, target, table_sem.at[n])
        for n, (source, target) in enumerate(
            (
                (attraction_hbm, attraction),
                (covolume_hbm, covolume),
                (wilson_hbm, wilson),
                (block_ids_hbm, block_ids),
            )
        )
    ]
    for copy in table_copies + cell_copies:
        copy.start()
    for k in range(strips):
        strip_in(moles_hbm, held, in_sem, k).start()

    zero_tile = jnp.zeros((SUB, BLK), jnp.float32)
    zero_strip = jnp.zeros((padded, BLK), jnp.float32)

    for ref in (pres, perm, lam):
        for k in (0, strips + 1):
            ref[k] = zero_strip
        for k in range(1, strips + 1):
            ref[k, 0:SUB] = zero_tile
            ref[k, SUB + layers : padded] = zero_tile

    def clear(i, carry):
        for k in (0, strips + 1):
            mobile[i, k * padded : (k + 1) * padded, :] = zero_strip
        for k in range(1, strips + 1):
            mobile[i, k * padded : k * padded + SUB, :] = zero_tile
            mobile[i, (k + 1) * padded - SUB : (k + 1) * padded, :] = zero_tile
        return carry

    lax.fori_loop(0, comps, clear, 0)
    for copy in table_copies:
        copy.wait()
    widen(w_wide, attraction, covolume, comps)

    cols = comps * SUB

    def multiply(width):
        lanes = slice(0, width)
        sums[:, lanes] = jnp.dot(
            w_wide[...], x_wide[:, lanes], preferred_element_type=jnp.float32
        )

    def total(at, start, count):
        rows = slice(at * SUB, (at + 1) * SUB)
        return jnp.concatenate(
            [sums[rows, g * BLK : (g + 1) * BLK] for g in range(start, start + count)], 0
        )

    def put_halves(j, g, pair):
        high, low = split_halves(jnp.concatenate(pair, 0))
        lanes = slice(g * BLK, (g + 1) * BLK)
        for n, value in enumerate((high, high, low)):
            at = n * cols + 2 * SUB * j
            x_wide[at : at + 2 * SUB, lanes] = value

    def mixture(values, start, count):
        quad = values(0) * total(0, start, count)
        for i in range(1, comps):
            quad = quad + values(i) * total(i, start, count)
        return total(comps + 1, start, count), total(comps, start, count), quad

    for copy in cell_copies:
        copy.wait()
    for k in range(strips):
        pres[k + 1, inside, :] = pres_flat[:, k * BLK : (k + 1) * BLK]
        perm[k + 1, inside, :] = perm_flat[:, k * BLK : (k + 1) * BLK]

    def padded_of(k):
        return pl.ds(pl.multiple_of((k + 1) * padded + SUB, SUB), layers)

    def single(k, carry):
        strip_in(moles_hbm, held, in_sem, k).wait()
        strip_in(old_hbm, old, old_sem, k).start()
        for j in range(comps // 2):
            for g in range(groups):
                rows = pl.ds(pl.multiple_of(k * layers + g * SUB, SUB), SUB)
                put_halves(j, g, [held[i, rows, :] for i in (2 * j, 2 * j + 1)])
        multiply(groups * BLK)
        amount, b_sum, quad = mixture(lambda i: held[i, strip_of(k), :], 0, groups)
        pressure = pres[k + 1, inside, :]
        inv_amount = recip(amount)
        big_a = pressure * quad * inv_amount * inv_amount
        big_b = pressure * b_sum * inv_amount
        is_vapour = roots[:, lanes_of(k)] == 1
        start = jnp.where(is_vapour, 1.0, 2.0 * big_b)
        (z_factor,) = roots_of(cubic(big_a, big_b, start, is_vapour))
        rho = pressure * recip(z_factor)
        part = labels[:, lanes_of(k)].astype(jnp.float32)
        move = ((1.0 - part) * (1.0 - part) + 4.0 * part * part) * rho
        vap[k] = part
        scale[k] = rho
        csum[k] = amount * rho
        lam[k + 1, inside, :] = amount * move
        for i in range(comps):
            mobile[i, padded_of(k), :] = held[i, strip_of(k), :] * move
        return carry

    lax.fori_loop(0, strips, single, 0)

    batch = WIDE * SUB
    own_count = counts[0]
    held_stride, mobile_stride, pack_stride = (ref.shape[1] for ref in (held, mobile, pack))
    held_rows = held.reshape(comps * held_stride, BLK)
    mobile_rows = mobile.reshape(comps * mobile_stride, BLK)
    pack_rows = pack.reshape(comps * pack_stride, BLK)
    liquid_rows = liquid.reshape(comps * pack_stride, BLK)
    vapour_rows = vapour.reshape(comps * pack_stride, BLK)
    bits = strips.bit_length() - 1

    def place(slot):
        block = block_ids[jnp.minimum(slot, own_count - 1)]
        layer = lax.shift_right_logical(block, bits)
        return block - lax.shift_left(layer, bits), layer

    def field_at(k, layer):
        return pl.ds(k * layers + layer, comps, stride=held_stride)

    def mobile_at(k, layer):
        return pl.ds((k + 1) * padded + layer + SUB, comps, stride=mobile_stride)

    def flash(number, carry):
        base = number * batch

        def gather(group, inner):
            for n in range(SUB):
                r = group * SUB + n
                k, layer = place(base + r)
                pack_rows[pl.ds(r, comps, stride=pack_stride), :] = held_rows[field_at(k, layer), :]
                pack_pres[pl.ds(r, 1), :] = pres[k + 1, pl.ds(layer + SUB, 1), :]
            return inner

        lax.fori_loop(0, WIDE, gather, 0)
        slots = slice(0, batch)
        pressure = pack_pres[...]
        amount = pack[0, slots, :]
        for i in range(1, comps):
            amount = amount + pack[i, slots, :]
        inv_amount = recip(amount)
        for i in range(comps):
            pack[i, slots, :] = pack[i, slots, :] * inv_amount

        def keep_k(i, log2_k):
            inv_excess[i, slots, :] = recip(jnp.exp2(log2_k) - 1.0)

        log2_pres = jnp.log(pressure) * LOG2E
        for i in range(comps):
            keep_k(i, wilson[i] * LOG2E - log2_pres)

        def newton(_, part):
            value = jnp.zeros((batch, BLK), jnp.float32)
            slope = jnp.full((batch, BLK), 0.05, jnp.float32)
            for i in range(comps):
                ratio = recip(inv_excess[i, slots, :] + part)
                term = pack[i, slots, :] * ratio
                value = value + term
                slope = slope + term * ratio
            return jnp.minimum(jnp.maximum(part + value * recip(slope), 0.0), 1.0)

        def sweep(number_of_sweep, inner):
            half = jnp.full((batch, BLK), 0.5, jnp.float32)
            part = lax.fori_loop(0, RR_ITERS, newton, half)
            for j in range(comps // 2):
                pairs = ([], [])
                for i in (2 * j, 2 * j + 1):
                    fraction = pack[i, slots, :]
                    term = fraction * recip(inv_excess[i, slots, :] + part)
                    liq = fraction - part * term
                    gas = liq + term
                    liquid[i, slots, :] = liq
                    vapour[i, slots, :] = gas
                    pairs[0].append(liq)
                    pairs[1].append(gas)
                for n, pair in enumerate(pairs):
                    for g in range(WIDE):
                        put_halves(j, n * WIDE + g, [value[rows_of(g)] for value in pair])
            multiply(2 * WIDE * BLK)
            phases = []
            equations = []
            for n, (ref, flag) in enumerate(((liquid, False), (vapour, True))):
                whole, b_sum, quad = mixture(lambda i: ref[i, slots, :], n * WIDE, WIDE)
                inv_whole = recip(whole)
                b_mix = b_sum * inv_whole
                a_mix = quad * inv_whole * inv_whole
                big_b = pressure * b_mix
                start = jnp.ones_like(big_b) if flag else 2.0 * big_b
                equations.append(cubic(pressure * a_mix, big_b, start, flag))
                phases.append((quad, whole, inv_whole, a_mix, b_mix, big_b))
            factors = roots_of(*equations)
            found[0] = part
            for n in range(2):
                found[1 + n] = factors[n]
                found[3 + n] = phases[n][2]

            @pl.when(number_of_sweep + 1 < SS_ITERS)
            def _():
                parts = []
                for (quad, whole, _, a_mix, b_mix, big_b), z_factor in zip(phases, factors):
                    log_arg = (z_factor + (1.0 + SQRT_TWO) * big_b) * recip(
                        z_factor + (1.0 - SQRT_TWO) * big_b
                    )
                    inv_b = recip(b_mix)
                    depart = a_mix * inv_b * (1.0 / (2.0 * SQRT_TWO)) * jnp.log(log_arg)
                    of_cov = (LOG2E * inv_b) * (z_factor - 1.0 + depart)
                    of_sum = (2.0 * LOG2E) * depart * whole * recip(quad)
                    parts.append((of_cov, LOG2E * jnp.log(z_factor - big_b), of_sum))
                cov_gap = parts[0][0] - parts[1][0]
                log_gap = parts[0][1] - parts[1][1]
                for i in range(comps):
                    log2_k = (covolume[i] * cov_gap - log_gap) - (
                        parts[0][2] * total(i, 0, WIDE) - parts[1][2] * total(i, WIDE, WIDE)
                    )
                    keep_k(i, jnp.minimum(jnp.maximum(log2_k, -3.0 * LOG2E), 3.0 * LOG2E))
            return inner

        lax.fori_loop(0, SS_ITERS, sweep, 0)
        part = found[0]
        rho_liq = amount * pressure * recip(found[1])
        rho_vap = amount * pressure * recip(found[2])
        rest = 1.0 - part
        move_liq = rest * rest * rho_liq
        move_vap = 4.0 * part * part * rho_vap
        hold_liq = rest * rho_liq
        hold_vap = part * rho_vap
        out_cell[0] = part
        out_cell[1] = move_liq + move_vap
        out_cell[2] = hold_liq + hold_vap
        inv_liq, inv_vap = found[3], found[4]
        move_liq = move_liq * inv_liq
        move_vap = move_vap * inv_vap
        hold_liq = hold_liq * inv_liq
        hold_vap = hold_vap * inv_vap
        for i in range(comps):
            liq, gas = liquid[i, slots, :], vapour[i, slots, :]
            liquid[i, slots, :] = move_liq * liq + move_vap * gas
            vapour[i, slots, :] = hold_liq * liq + hold_vap * gas
        one_row = jnp.ones((1, BLK), jnp.float32)

        def scatter(group, inner):
            for n in range(SUB):
                r = group * SUB + n
                k, layer = place(base + r)
                of = pl.ds(r, comps, stride=pack_stride)
                mobile_rows[mobile_at(k, layer), :] = liquid_rows[of, :]
                held_rows[field_at(k, layer), :] = vapour_rows[of, :]
                one = pl.ds(r, 1)
                row = pl.ds(layer, 1)
                vap[k, row, :] = out_cell[0, one, :]
                lam[k + 1, pl.ds(layer + SUB, 1), :] = out_cell[1, one, :]
                csum[k, row, :] = out_cell[2, one, :]
                scale[k, row, :] = one_row
            return inner

        lax.fori_loop(0, WIDE, scatter, 0)
        return carry

    lax.fori_loop(0, (own_count + batch - 1) // batch, flash, 0)
    for k in range(strips):
        strip_in(old_hbm, old, old_sem, k).wait()
    old_rows = old.reshape(comps * old.shape[1], BLK)

    def edge_values(k, at, inner):
        here = slice(at, at + 1)
        pad_here = slice(SUB + at, SUB + at + 1)
        pad_inner = slice(SUB + inner, SUB + inner + 1)
        values = [None] * EDGE_ROWS
        values[EDGE_PRES] = pres[k + 1, pad_here, :]
        values[EDGE_PERM] = perm[k + 1, pad_here, :]
        values[EDGE_LAM] = lam[k + 1, pad_here, :]
        values[EDGE_CSUM] = csum[k, here, :]
        values[EDGE_OSUM] = jnp.sum(old_rows[field_at(k, at), :], 0, keepdims=True)
        values[EDGE_PRES2] = pres[k + 1, pad_inner, :]
        values[EDGE_PERM2] = perm[k + 1, pad_inner, :]
        values[EDGE_LAM2] = lam[k + 1, pad_inner, :]
        return [mobile_rows[mobile_at(k, at), :]] + values

    odd = lax.rem(lax.axis_index("dev"), 2) == 1
    for k in range(strips):
        lanes = slice(k * BLK, (k + 1) * BLK)
        tops = edge_values(k, 0, 1)
        lows = edge_values(k, layers - 1, layers - 2)
        row = 0
        for top, low in zip(tops, lows):
            rows = slice(row, row + top.shape[0])
            edge_a[rows, lanes] = jnp.where(odd, top, low)
            edge_b[rows, lanes] = jnp.where(odd, low, top)
            row = rows.stop


def flux_kernel(
    held,
    old,
    mobile,
    pres,
    perm,
    lam,
    scale,
    csum,
    vap,
    resid_hbm,
    step_hbm,
    vap_hbm,
    top_aux,
    low_aux,
    resid,
    first,
    row_sum,
    diag,
    weights,
    step,
    vap_flat,
    step_sem,
    vap_sem,
    out_sem,
):
    comps = held.shape[0]
    strips, layers, _ = scale.shape
    groups = layers // SUB
    padded = layers + 2 * SUB

    def lanes_of(k):
        return pl.ds(pl.multiple_of(k * BLK, BLK), BLK)

    def strip_out(k):
        return pltpu.make_async_copy(resid.at[:, k], resid_hbm.at[:, :, lanes_of(k)], out_sem.at[k])

    for k in range(strips):
        vap_flat[:, k * BLK : (k + 1) * BLK] = vap[k]
    vap_copy = pltpu.make_async_copy(vap_flat, vap_hbm, vap_sem)
    vap_copy.start()
    zero_tile = jnp.zeros((SUB, BLK), jnp.float32)
    for k in range(strips + 2):
        for g in range(groups + 2):
            if k in (0, strips + 1) or g in (0, groups + 1):
                first[k, rows_of(g), :] = zero_tile

    lane_index = lax.broadcasted_iota(jnp.int32, (SUB, BLK), 1)
    is_last_lane = lane_index == BLK - 1
    is_first_lane = lane_index == 0

    def around(load, k, g):
        at = SUB * (g + 1)
        here = load(k + 1, slice(at, at + SUB))
        up = load(k + 1, slice(at - 1, at + SUB - 1))
        down = load(k + 1, slice(at + 1, at + SUB + 1))
        before = load(k, slice(at, at + SUB))
        after = load(k + 2, slice(at, at + SUB))
        left = pltpu.roll(jnp.where(is_last_lane, before, here), 1, 1)
        right = pltpu.roll(jnp.where(is_first_lane, after, here), BLK - 1, 1)
        return here, (up, down, left, right)

    def fluxes(k, carry):
        for g in range(groups):
            rows = rows_of(g)
            p_here, p_near = around(lambda s, r: pres[s, r, :], k, g)
            k_here, k_near = around(lambda s, r: perm[s, r, :], k, g)
            l_here, l_near = around(lambda s, r: lam[s, r, :], k, g)
            drives = []
            couplings = []
            for n in range(4):
                transmiss = k_here * k_near[n] * recip(k_here + k_near[n])
                drives.append((TIME_STEP * transmiss) * (p_here - p_near[n]))
                couplings.append(transmiss * (l_here + l_near[n]))
            drive_sum = (drives[0] + drives[1]) + (drives[2] + drives[3])
            content_scale = scale[k, rows, :]
            flat_rows = pl.ds(pl.multiple_of(k * layers + g * SUB, SUB), SUB)
            row_total = zero_tile
            for i in range(comps):
                m_here, m_near = around(
                    lambda s, r, i=i: mobile[i, pl.ds(s * padded + r.start, SUB), :], k, g
                )
                value = held[i, flat_rows, :] * content_scale - old[i, flat_rows, :]
                value = value + drive_sum * m_here
                value = value + (drives[0] * m_near[0] + drives[1] * m_near[1])
                value = value + (drives[2] * m_near[2] + drives[3] * m_near[3])
                resid[i, k, rows, :] = value
                row_total = row_total + value
            diagonal = TIME_STEP * (
                (couplings[0] + couplings[1]) + (couplings[2] + couplings[3])
            ) + csum[k, rows, :] * recip(p_here)
            inv_diag = recip(diagonal)
            row_sum[k, rows, :] = row_total
            diag[k, rows, :] = diagonal
            first[k + 1, SUB * (g + 1) : SUB * (g + 2), :] = -row_total * inv_diag
            gain = (STEP_SCALE * OFF_SCALE) * inv_diag
            for n in range(4):
                weights[n, k, rows, :] = couplings[n] * gain
        strip_out(k).start()
        return carry

    lax.fori_loop(0, strips, fluxes, 0)

    def steps(k, carry):
        for g in range(groups):
            rows = rows_of(g)
            here, near = around(lambda s, r: first[s, r, :], k, g)
            step[rows, lanes_of(k)] = (
                STEP_SCALE * here
                + (weights[0, k, rows, :] * near[0] + weights[1, k, rows, :] * near[1])
                + (weights[2, k, rows, :] * near[2] + weights[3, k, rows, :] * near[3])
            )
        return carry

    lax.fori_loop(0, strips, steps, 0)
    step_copy = pltpu.make_async_copy(step, step_hbm, step_sem)
    step_copy.start()

    resid_rows = resid.reshape(comps * strips * layers, BLK)
    for aux, at, inner, toward, away in (
        (top_aux, 0, 1, 0, 1),
        (low_aux, layers - 1, layers - 2, 1, 0),
    ):
        for k in range(strips):
            lanes = slice(k * BLK, (k + 1) * BLK)
            here = slice(at, at + 1)
            behind = slice(inner, inner + 1)
            from_row = pl.ds(k * layers + at, comps, stride=strips * layers)
            aux[0:comps, lanes] = resid_rows[from_row, :]
            unscale = diag[k, here, :]
            values = [None] * AUX_ROWS
            values[AUX_IN] = weights[away, k, here, :] * unscale
            values[AUX_LEFT] = weights[2, k, here, :] * unscale
            values[AUX_RIGHT] = weights[3, k, here, :] * unscale
            values[AUX_FIRST] = first[k + 1, SUB + inner : SUB + inner + 1, :]
            values[AUX_GAIN] = weights[toward, k, behind, :]
            values[AUX_STEP] = step[behind, lanes]
            values[AUX_ROW] = row_sum[k, here, :]
            values[AUX_DIAG] = unscale
            for n, value in enumerate(values):
                aux[comps + n : comps + n + 1, lanes] = value
    vap_copy.wait()
    step_copy.wait()
    for k in range(strips):
        strip_out(k).wait()


def transmissibility(perm, perm_near):
    both = perm + perm_near
    return perm * perm_near / jnp.where(both == 0.0, 1.0, both)


def edge_kernel(
    edge_a,
    edge_b,
    top_aux,
    low_aux,
    in_even,
    in_odd,
    resid_in,
    step_in,
    resid_hbm,
    step_hbm,
    resid,
    step,
    sem,
):
    comps, layers, face = resid_hbm.shape
    odd = lax.rem(lax.axis_index("dev"), 2) == 1
    top_edge = jnp.where(odd, edge_a[...], edge_b[...])
    low_edge = jnp.where(odd, edge_b[...], edge_a[...])
    from_prev = jnp.where(odd, in_even[...], in_odd[...])
    from_next = jnp.where(odd, in_odd[...], in_even[...])
    copies = []
    for n, (edge, aux, other, at, inner) in enumerate(
        (
            (top_edge, top_aux, from_prev, 0, 1),
            (low_edge, low_aux, from_next, layers - 1, layers - 2),
        )
    ):

        def own(index):
            return edge[comps + index : comps + index + 1, :]

        def far(index):
            return other[comps + index : comps + index + 1, :]

        def near(index):
            return aux[comps + index : comps + index + 1, :]

        pres_far, perm_far, lam_far = far(EDGE_PRES), far(EDGE_PERM), far(EDGE_LAM)
        transmiss = transmissibility(own(EDGE_PERM), perm_far)
        drive = TIME_STEP * transmiss * (own(EDGE_PRES) - pres_far)
        lam_both = own(EDGE_LAM) + lam_far
        coupling = transmiss * lam_both
        row = near(AUX_ROW) + drive * lam_both
        diag = near(AUX_DIAG) + TIME_STEP * coupling
        first = -row / diag
        first_old = -near(AUX_ROW) / near(AUX_DIAG)
        row_far = far(EDGE_CSUM) - far(EDGE_OSUM) - drive * lam_both
        diag_far = coupling
        lane = lax.broadcasted_iota(jnp.int32, (1, face), 1)
        sides = [(far(EDGE_PRES2), far(EDGE_PERM2), far(EDGE_LAM2))]
        for shift, end in ((1, 0), (face - 1, face - 1)):
            pres_n, perm_n, lam_n = (pltpu.roll(x, shift, 1) for x in (pres_far, perm_far, lam_far))
            sides.append((pres_n, jnp.where(lane == end, 0.0, perm_n), lam_n))
        for pres_n, perm_n, lam_n in sides:
            joint = transmissibility(perm_far, perm_n) * (lam_far + lam_n)
            row_far = row_far + TIME_STEP * joint * (pres_far - pres_n)
            diag_far = diag_far + joint
        diag_far = TIME_STEP * diag_far + far(EDGE_CSUM) / jnp.where(pres_far == 0.0, 1.0, pres_far)
        first_far = -row_far / jnp.where(diag_far == 0.0, 1.0, diag_far)
        off = (
            (STEP_SCALE * OFF_SCALE) * coupling * first_far
            + near(AUX_IN) * near(AUX_FIRST)
            + near(AUX_LEFT) * pltpu.roll(first, 1, 1)
            + near(AUX_RIGHT) * pltpu.roll(first, face - 1, 1)
        )
        least = min(at, inner)
        step[n, at - least : at - least + 1, :] = STEP_SCALE * first + off / diag
        step[n, inner - least : inner - least + 1, :] = near(AUX_STEP) + near(AUX_GAIN) * (
            first - first_old
        )
        resid[n] = aux[0:comps, :] + drive * (edge[0:comps, :] + other[0:comps, :])
        for source, target in (
            (resid.at[n], resid_hbm.at[:, at, :]),
            (step.at[n, 0:2, :], step_hbm.at[least : least + 2, :]),
        ):
            copies.append(pltpu.make_async_copy(source, target, sem.at[len(copies)]))
            copies[-1].start()
    for copy in copies:
        copy.wait()


def on_device(
    moles,
    old_content,
    pressure,
    perm,
    labels,
    roots,
    counts,
    block_ids,
    wilson,
    attraction,
    covolume,
):
    comps, layers, face = moles.shape
    f32 = jnp.float32
    strips = face // BLK
    tables = (block_ids, wilson, attraction, covolume)
    rows_in = comps * SUB
    widest = max(layers // SUB, 2 * WIDE) * BLK
    vmem = pl.BlockSpec(memory_space=pltpu.VMEM)
    hbm = pl.BlockSpec(memory_space=pltpu.HBM)
    padded = layers + 2 * SUB
    flat = pltpu.VMEM((layers, face), f32)
    flat_int = pltpu.VMEM((layers, face), jnp.int32)
    cell = pltpu.VMEM((strips, layers, BLK), f32)
    cell_pad = pltpu.VMEM((strips + 2, padded, BLK), f32)
    field = pltpu.VMEM((comps, odd_tiles(strips * layers), BLK), f32)
    field_pad = pltpu.VMEM((comps, odd_tiles((strips + 2) * padded), BLK), f32)
    packed = pltpu.VMEM((comps, odd_tiles(WIDE * SUB), BLK), f32)
    edge_shape = pltpu.VMEM((EDGE_SPAN, face), f32)
    aux_shape = pltpu.VMEM((comps + AUX_ROWS, face), f32)
    field_shape = jax.ShapeDtypeStruct((comps, layers, face), f32)
    cell_shape = jax.ShapeDtypeStruct((layers, face), f32)
    field_out = pltpu.VMEM((comps, strips, layers, BLK), f32)
    held_types = [field, field, field_pad] + [cell_pad] * 3 + [cell] * 3
    edge_a, edge_b, *state = pl.pallas_call(
        cells_kernel,
        out_shape=[edge_shape, edge_shape]
        + held_types,
        in_specs=[pl.BlockSpec(memory_space=pltpu.SMEM)] + [hbm] * 10,
        out_specs=[vmem] * (2 + len(held_types)),
        scratch_shapes=[flat, flat, flat_int, flat_int]
        + [pltpu.VMEM((rows_in + 2 * SUB, 3 * rows_in), jnp.bfloat16)]
        + [pltpu.VMEM((3 * rows_in, widest), jnp.bfloat16)]
        + [pltpu.VMEM((rows_in + 2 * SUB, widest), f32)]
        + [packed, pltpu.VMEM((WIDE * SUB, BLK), f32)]
        + [packed] * 3
        + [pltpu.VMEM((3, WIDE * SUB, BLK), f32), pltpu.VMEM((5, WIDE * SUB, BLK), f32)]
        + [pltpu.SMEM(table.shape, table.dtype) for table in tables]
        + [
            pltpu.SemaphoreType.DMA((strips,)),
            pltpu.SemaphoreType.DMA((strips,)),
            pltpu.SemaphoreType.DMA((4,)),
            pltpu.SemaphoreType.DMA((len(tables),)),
        ],
        compiler_params=pltpu.CompilerParams(vmem_limit_bytes=CELLS_VMEM),
        name="cells",
    )(counts, *keep_in(pltpu.HBM, *tables, moles, old_content, pressure, perm, labels, roots))
    count = lax.axis_size("dev")
    arrived = []
    for start, edge in ((0, edge_a), (1, edge_b)):
        pairs = [(i, i + 1) for i in range(start, count - 1, 2)]
        arrived.append(lax.ppermute(edge, "dev", pairs + [pair[::-1] for pair in pairs]))
    residual, step, vapour, top_aux, low_aux = pl.pallas_call(
        flux_kernel,
        out_shape=[field_shape, cell_shape, cell_shape, aux_shape, aux_shape],
        in_specs=[vmem] * len(state),
        out_specs=[hbm] * 3 + [vmem] * 2,
        scratch_shapes=[field_out, cell_pad, cell, cell]
        + [pltpu.VMEM((4, strips, layers, BLK), f32), flat, flat]
        + [pltpu.SemaphoreType.DMA(())] * 2
        + [pltpu.SemaphoreType.DMA((strips,))],
        compiler_params=pltpu.CompilerParams(vmem_limit_bytes=FLUX_VMEM),
        name="flux",
    )(*keep_in(pltpu.VMEM, *state))
    residual, step = pl.pallas_call(
        edge_kernel,
        out_shape=[field_shape, cell_shape],
        in_specs=[vmem] * 6 + [hbm] * 2,
        out_specs=[hbm] * 2,
        input_output_aliases={6: 0, 7: 1},
        scratch_shapes=[
            pltpu.VMEM((2, comps, face), f32),
            pltpu.VMEM((2, SUB, face), f32),
            pltpu.SemaphoreType.DMA((4,)),
        ],
        compiler_params=pltpu.CompilerParams(vmem_limit_bytes=16 * 1024 * 1024),
        name="edges",
    )(edge_a, edge_b, top_aux, low_aux, *arrived, residual, step)
    return (residual, step, vapour)


def solution(mesh):
    in_specs = (
        P(None, "dev", None),
        P(None, "dev", None),
        P("dev", None),
        P("dev", None),
        P("dev", None),
        P("dev", None),
        P("dev"),
        P("dev"),
        P(),
        P(),
        P(),
    )
    out_specs = (P(None, "dev", None), P("dev", None), P("dev", None))
    return jax.shard_map(
        on_device, mesh=mesh, in_specs=in_specs, out_specs=out_specs, check_vma=False
    )
```

```python
import math

import jax
import jax.numpy as jnp
from jax import lax
from jax.experimental import pallas as pl
from jax.experimental.pallas import tpu as pltpu
from jax.sharding import PartitionSpec as P

BLK = 128
SUB = 8
SS_ITERS = 3
RR_ITERS = 3
Z_ITERS = 5
WIDE = 8
LOG2E = math.log2(math.e)
CELLS_VMEM = 32 * 1024 * 1024
FLUX_VMEM = 32 * 1024 * 1024

SQRT_TWO = math.sqrt(2.0)
TIME_STEP = 0.5
RELAX = 0.7
STEP_SCALE = 10.0
OFF_SCALE = RELAX * TIME_STEP

EDGE_PRES, EDGE_PERM, EDGE_LAM, EDGE_CSUM, EDGE_OSUM = range(5)
EDGE_PRES2, EDGE_PERM2, EDGE_LAM2 = range(5, 8)
EDGE_ROWS = 8
EDGE_SPAN = 32
AUX_IN, AUX_LEFT, AUX_RIGHT, AUX_FIRST, AUX_GAIN, AUX_STEP, AUX_ROW, AUX_DIAG = range(8)
AUX_ROWS = 8


def keep_in(space, *arrays):
    return [pltpu.with_memory_space_constraint(x, space) for x in arrays]


def recip(value):
    return pltpu.reciprocal(value, approx=True)


def odd_tiles(rows):
    return rows + SUB if (rows // SUB) % 2 == 0 else rows


def split_halves(value):
    high = value.astype(jnp.bfloat16)
    low = (value - high.astype(jnp.float32)).astype(jnp.bfloat16)
    return high, low


def widen(wide, attraction, covolume, comps):
    cols = comps * SUB
    group = lax.broadcasted_iota(jnp.int32, (comps, cols), 1) // SUB
    spread = jnp.where(group == lax.broadcasted_iota(jnp.int32, (comps, cols), 0), 1.0, 0.0)
    table = attraction[...]
    coefficients = 0.5 * (
        lax.dot_general(table, spread, (((1,), (0,)), ((), ())), precision=lax.Precision.HIGHEST)
        + lax.dot_general(table, spread, (((0,), (0,)), ((), ())), precision=lax.Precision.HIGHEST)
    )
    lane = lax.broadcasted_iota(jnp.int32, (SUB, cols), 1)
    row = lax.broadcasted_iota(jnp.int32, (SUB, cols), 0)
    diagonal = lane - (lane // SUB) * SUB == row
    zero = jnp.zeros((SUB, cols), jnp.float32)
    of_cov = zero
    for j in range(comps):
        of_cov = jnp.where(lane // SUB == j, covolume[j], of_cov)
    blocks = [coefficients[i : i + 1, :] for i in range(comps)] + [of_cov, zero + 1.0]
    for pair in range(len(blocks) // 2):
        rows = [jnp.where(diagonal, blocks[i], zero) for i in (2 * pair, 2 * pair + 1)]
        high, low = split_halves(jnp.concatenate(rows, 0))
        wide[2 * SUB * pair : 2 * SUB * (pair + 1), :] = jnp.concatenate([high, low, high], 1)


def rows_of(g):
    return slice(g * SUB, (g + 1) * SUB)


def cubic(big_a, big_b, vapour_flag):
    two_b = 2.0 * big_b
    two_b_square = two_b * big_b
    least = two_b + 0.01
    most = big_b + 2.0
    if vapour_flag is True:
        start, shift, factor = 1.0 + big_b, big_b + 0.5, -0.5 * big_a
    elif vapour_flag is False:
        start, shift, factor = 3.0 * big_b, big_b, 0.5 * recip(big_a)
    else:
        start = jnp.where(vapour_flag, 1.0 + big_b, 3.0 * big_b)
        shift = jnp.where(vapour_flag, big_b + 0.5, big_b)
        factor = jnp.where(vapour_flag, -0.5 * big_a, -0.5 * recip(big_a))
        base = jnp.where(vapour_flag, two_b, 1.0 + two_b)

    def step(w):
        spread = w * w - two_b_square
        if vapour_flag is True:
            part = factor * (w - two_b) * recip(spread)
        elif vapour_flag is False:
            part = spread * ((1.0 + two_b) - w) * factor
        else:
            part = factor * (w - base) * jnp.where(vapour_flag, recip(spread), spread)
        return jnp.minimum(jnp.maximum((0.5 * w + shift) + part, least), most)

    return start, step


def roots_of(*equations):
    steps = [cubic(*equation) for equation in equations]
    found = [start for start, _ in steps]
    for _ in range(Z_ITERS):
        found = [step(w) for w, (_, step) in zip(found, steps)]
    return [w - big_b for w, (_, big_b, _) in zip(found, equations)]


def cells_kernel(
    counts,
    block_ids_hbm,
    wilson_hbm,
    covolume_hbm,
    attraction_hbm,
    moles_hbm,
    old_hbm,
    pres_hbm,
    perm_hbm,
    labels_hbm,
    roots_hbm,
    edge_a,
    edge_b,
    held,
    old,
    mobile,
    pres,
    perm,
    lam,
    scale,
    csum,
    vap,
    pres_flat,
    perm_flat,
    labels,
    roots,
    w_wide,
    sums,
    pack,
    pack_pres,
    inv_excess,
    liquid,
    vapour,
    out_cell,
    found,
    block_ids,
    wilson,
    covolume,
    attraction,
    in_sem,
    old_sem,
    cell_sem,
    table_sem,
):
    comps, layers, face = moles_hbm.shape
    strips = face // BLK
    groups = layers // SUB
    padded = layers + 2 * SUB
    inside = slice(SUB, SUB + layers)

    def lanes_of(k):
        return pl.ds(pl.multiple_of(k * BLK, BLK), BLK)

    def strip_of(k):
        return pl.ds(pl.multiple_of(k * layers, SUB), layers)

    def strip_in(source, target, sem, k):
        return pltpu.make_async_copy(
            source.at[:, :, lanes_of(k)], target.at[:, strip_of(k), :], sem.at[k]
        )

    cell_copies = [
        pltpu.make_async_copy(pres_hbm, pres_flat, cell_sem.at[0]),
        pltpu.make_async_copy(roots_hbm, roots, cell_sem.at[1]),
        pltpu.make_async_copy(labels_hbm, labels, cell_sem.at[2]),
        pltpu.make_async_copy(perm_hbm, perm_flat, cell_sem.at[3]),
    ]
    table_copies = [
        pltpu.make_async_copy(source, target, table_sem.at[n])
        for n, (source, target) in enumerate(
            (
                (attraction_hbm, attraction),
                (covolume_hbm, covolume),
                (wilson_hbm, wilson),
                (block_ids_hbm, block_ids),
            )
        )
    ]
    for copy in table_copies + cell_copies:
        copy.start()
    for k in range(strips):
        strip_in(moles_hbm, held, in_sem, k).start()

    zero_tile = jnp.zeros((SUB, BLK), jnp.float32)
    zero_strip = jnp.zeros((padded, BLK), jnp.float32)

    for ref in (pres, perm, lam):
        for k in (0, strips + 1):
            ref[k] = zero_strip
        for k in range(1, strips + 1):
            ref[k, 0:SUB] = zero_tile
            ref[k, SUB + layers : padded] = zero_tile

    def clear(i, carry):
        for k in (0, strips + 1):
            mobile[i, k * padded : (k + 1) * padded, :] = zero_strip
        for k in range(1, strips + 1):
            mobile[i, k * padded : k * padded + SUB, :] = zero_tile
            mobile[i, (k + 1) * padded - SUB : (k + 1) * padded, :] = zero_tile
        return carry

    lax.fori_loop(0, comps, clear, 0)
    for copy in table_copies:
        copy.wait()
    widen(w_wide, attraction, covolume, comps)

    cols = comps * SUB

    def mixture(tile, count, keep=None):
        parts = ([], [], [])
        for g in range(0, count, 2):
            highs, lows = [], []
            for j in range(comps // 2):
                both = [
                    jnp.concatenate([tile(2 * j, at), tile(2 * j + 1, at)], 0) for at in (g, g + 1)
                ]
                high, low = split_halves(jnp.concatenate(both, 1))
                highs.append(high)
                lows.append(low)
            result = jnp.dot(
                w_wide[...],
                jnp.concatenate(highs + highs + lows, 0),
                preferred_element_type=jnp.float32,
            )
            if keep is not None:
                sums[:, (keep + g) * BLK : (keep + g + 2) * BLK] = result[0:cols]
            for n, at in enumerate((g, g + 1)):
                lanes = slice(n * BLK, (n + 1) * BLK)
                quad = tile(0, at) * result[0:SUB, lanes]
                for i in range(1, comps):
                    quad = quad + tile(i, at) * result[i * SUB : (i + 1) * SUB, lanes]
                parts[0].append(result[cols + SUB : cols + 2 * SUB, lanes])
                parts[1].append(result[cols : cols + SUB, lanes])
                parts[2].append(quad)
        return [jnp.concatenate(part, 0) for part in parts]

    def total(at, start, count):
        rows = slice(at * SUB, (at + 1) * SUB)
        return jnp.concatenate(
            [sums[rows, g * BLK : (g + 1) * BLK] for g in range(start, start + count)], 0
        )

    for copy in cell_copies:
        copy.wait()
    for k in range(strips):
        pres[k + 1, inside, :] = pres_flat[:, k * BLK : (k + 1) * BLK]
        perm[k + 1, inside, :] = perm_flat[:, k * BLK : (k + 1) * BLK]

    def padded_of(k):
        return pl.ds(pl.multiple_of((k + 1) * padded + SUB, SUB), layers)

    def single(k, carry):
        strip_in(moles_hbm, held, in_sem, k).wait()
        strip_in(old_hbm, old, old_sem, k).start()
        amount, b_sum, quad = mixture(
            lambda i, g: held[i, pl.ds(pl.multiple_of(k * layers + g * SUB, SUB), SUB), :], groups
        )
        pressure = pres[k + 1, inside, :]
        inv_amount = recip(amount)
        big_a = pressure * quad * inv_amount * inv_amount
        big_b = pressure * b_sum * inv_amount
        is_vapour = roots[:, lanes_of(k)] == 1
        (z_factor,) = roots_of((big_a, big_b, is_vapour))
        rho = pressure * recip(z_factor)
        part = labels[:, lanes_of(k)].astype(jnp.float32)
        move = ((1.0 - part) * (1.0 - part) + 4.0 * part * part) * rho
        vap[k] = part
        scale[k] = rho
        csum[k] = amount * rho
        lam[k + 1, inside, :] = amount * move
        for i in range(comps):
            mobile[i, padded_of(k), :] = held[i, strip_of(k), :] * move
        return carry

    lax.fori_loop(0, strips, single, 0)

    batch = WIDE * SUB
    own_count = counts[0]
    held_stride, mobile_stride, pack_stride = (ref.shape[1] for ref in (held, mobile, pack))
    held_rows = held.reshape(comps * held_stride, BLK)
    mobile_rows = mobile.reshape(comps * mobile_stride, BLK)
    pack_rows = pack.reshape(comps * pack_stride, BLK)
    liquid_rows = liquid.reshape(comps * pack_stride, BLK)
    vapour_rows = vapour.reshape(comps * pack_stride, BLK)
    bits = strips.bit_length() - 1

    def place(slot):
        block = block_ids[jnp.minimum(slot, own_count - 1)]
        layer = lax.shift_right_logical(block, bits)
        return block - lax.shift_left(layer, bits), layer

    def field_at(k, layer):
        return pl.ds(k * layers + layer, comps, stride=held_stride)

    def mobile_at(k, layer):
        return pl.ds((k + 1) * padded + layer + SUB, comps, stride=mobile_stride)

    def flash(number, carry):
        base = number * batch

        def gather(group, inner):
            for n in range(SUB):
                r = group * SUB + n
                k, layer = place(base + r)
                pack_rows[pl.ds(r, comps, stride=pack_stride), :] = held_rows[field_at(k, layer), :]
                pack_pres[pl.ds(r, 1), :] = pres[k + 1, pl.ds(layer + SUB, 1), :]
            return inner

        lax.fori_loop(0, WIDE, gather, 0)
        slots = slice(0, batch)
        pressure = pack_pres[...]
        amount = pack[0, slots, :]
        for i in range(1, comps):
            amount = amount + pack[i, slots, :]
        inv_amount = recip(amount)
        for i in range(comps):
            pack[i, slots, :] = pack[i, slots, :] * inv_amount

        def keep_k(i, log2_k):
            inv_excess[i, slots, :] = recip(jnp.exp2(log2_k) - 1.0)

        log2_pres = jnp.log(pressure) * LOG2E
        for i in range(comps):
            keep_k(i, wilson[i] * LOG2E - log2_pres)

        def newton(_, part):
            value = jnp.zeros((batch, BLK), jnp.float32)
            slope = jnp.full((batch, BLK), 0.05, jnp.float32)
            for i in range(comps):
                ratio = recip(inv_excess[i, slots, :] + part)
                term = pack[i, slots, :] * ratio
                value = value + term
                slope = slope + term * ratio
            return jnp.minimum(jnp.maximum(part + value * recip(slope), 0.0), 1.0)

        def sweep(number_of_sweep, inner):
            half = jnp.full((batch, BLK), 0.5, jnp.float32)
            part = lax.fori_loop(0, RR_ITERS, newton, half)
            for i in range(comps):
                fraction = pack[i, slots, :]
                term = fraction * recip(inv_excess[i, slots, :] + part)
                liq = fraction - part * term
                liquid[i, slots, :] = liq
                vapour[i, slots, :] = liq + term
            phases = []
            equations = []
            for n, (ref, flag) in enumerate(((liquid, False), (vapour, True))):
                whole, b_sum, quad = mixture(lambda i, g: ref[i, rows_of(g), :], WIDE, n * WIDE)
                inv_whole = recip(whole)
                b_mix = b_sum * inv_whole
                a_mix = quad * inv_whole * inv_whole
                big_b = pressure * b_mix
                equations.append((pressure * a_mix, big_b, flag))
                phases.append((quad, whole, inv_whole, a_mix, b_mix, big_b))
            factors = roots_of(*equations)
            found[0] = part
            for n in range(2):
                found[1 + n] = factors[n]
                found[3 + n] = phases[n][2]

            @pl.when(number_of_sweep + 1 < SS_ITERS)
            def _():
                parts = []
                for (quad, whole, _, a_mix, b_mix, big_b), z_factor in zip(phases, factors):
                    log_arg = (z_factor + (1.0 + SQRT_TWO) * big_b) * recip(
                        z_factor + (1.0 - SQRT_TWO) * big_b
                    )
                    inv_b = recip(b_mix)
                    depart = a_mix * inv_b * (1.0 / (2.0 * SQRT_TWO)) * jnp.log(log_arg)
                    of_cov = (LOG2E * inv_b) * (z_factor - 1.0 + depart)
                    of_sum = (2.0 * LOG2E) * depart * whole * recip(quad)
                    parts.append((of_cov, LOG2E * jnp.log(z_factor - big_b), of_sum))
                cov_gap = parts[0][0] - parts[1][0]
                log_gap = parts[0][1] - parts[1][1]
                for i in range(comps):
                    log2_k = (covolume[i] * cov_gap - log_gap) - (
                        parts[0][2] * total(i, 0, WIDE) - parts[1][2] * total(i, WIDE, WIDE)
                    )
                    keep_k(i, jnp.minimum(jnp.maximum(log2_k, -3.0 * LOG2E), 3.0 * LOG2E))
            return inner

        lax.fori_loop(0, SS_ITERS, sweep, 0)
        part = found[0]
        rho_liq = amount * pressure * recip(found[1])
        rho_vap = amount * pressure * recip(found[2])
        rest = 1.0 - part
        move_liq = rest * rest * rho_liq
        move_vap = 4.0 * part * part * rho_vap
        hold_liq = rest * rho_liq
        hold_vap = part * rho_vap
        out_cell[0] = part
        out_cell[1] = move_liq + move_vap
        out_cell[2] = hold_liq + hold_vap
        inv_liq, inv_vap = found[3], found[4]
        move_liq = move_liq * inv_liq
        move_vap = move_vap * inv_vap
        hold_liq = hold_liq * inv_liq
        hold_vap = hold_vap * inv_vap
        for i in range(comps):
            liq, gas = liquid[i, slots, :], vapour[i, slots, :]
            liquid[i, slots, :] = move_liq * liq + move_vap * gas
            vapour[i, slots, :] = hold_liq * liq + hold_vap * gas
        one_row = jnp.ones((1, BLK), jnp.float32)

        def scatter(group, inner):
            for n in range(SUB):
                r = group * SUB + n
                k, layer = place(base + r)
                of = pl.ds(r, comps, stride=pack_stride)
                mobile_rows[mobile_at(k, layer), :] = liquid_rows[of, :]
                held_rows[field_at(k, layer), :] = vapour_rows[of, :]
                one = pl.ds(r, 1)
                row = pl.ds(layer, 1)
                vap[k, row, :] = out_cell[0, one, :]
                lam[k + 1, pl.ds(layer + SUB, 1), :] = out_cell[1, one, :]
                csum[k, row, :] = out_cell[2, one, :]
                scale[k, row, :] = one_row
            return inner

        lax.fori_loop(0, WIDE, scatter, 0)
        return carry

    lax.fori_loop(0, (own_count + batch - 1) // batch, flash, 0)
    for k in range(strips):
        strip_in(old_hbm, old, old_sem, k).wait()
    old_rows = old.reshape(comps * old.shape[1], BLK)

    def edge_values(k, at, inner):
        here = slice(at, at + 1)
        pad_here = slice(SUB + at, SUB + at + 1)
        pad_inner = slice(SUB + inner, SUB + inner + 1)
        values = [None] * EDGE_ROWS
        values[EDGE_PRES] = pres[k + 1, pad_here, :]
        values[EDGE_PERM] = perm[k + 1, pad_here, :]
        values[EDGE_LAM] = lam[k + 1, pad_here, :]
        values[EDGE_CSUM] = csum[k, here, :]
        values[EDGE_OSUM] = jnp.sum(old_rows[field_at(k, at), :], 0, keepdims=True)
        values[EDGE_PRES2] = pres[k + 1, pad_inner, :]
        values[EDGE_PERM2] = perm[k + 1, pad_inner, :]
        values[EDGE_LAM2] = lam[k + 1, pad_inner, :]
        return [mobile_rows[mobile_at(k, at), :]] + values

    odd = lax.rem(lax.axis_index("dev"), 2) == 1
    for k in range(strips):
        lanes = slice(k * BLK, (k + 1) * BLK)
        tops = edge_values(k, 0, 1)
        lows = edge_values(k, layers - 1, layers - 2)
        row = 0
        for top, low in zip(tops, lows):
            rows = slice(row, row + top.shape[0])
            edge_a[rows, lanes] = jnp.where(odd, top, low)
            edge_b[rows, lanes] = jnp.where(odd, low, top)
            row = rows.stop


def flux_kernel(
    held,
    old,
    mobile,
    pres,
    perm,
    lam,
    scale,
    csum,
    vap,
    resid_hbm,
    step_hbm,
    vap_hbm,
    top_aux,
    low_aux,
    resid,
    first,
    row_sum,
    diag,
    weights,
    step,
    vap_flat,
    step_sem,
    vap_sem,
    out_sem,
):
    comps = held.shape[0]
    strips, layers, _ = scale.shape
    groups = layers // SUB
    padded = layers + 2 * SUB

    def lanes_of(k):
        return pl.ds(pl.multiple_of(k * BLK, BLK), BLK)

    def strip_out(k):
        return pltpu.make_async_copy(resid.at[:, k], resid_hbm.at[:, :, lanes_of(k)], out_sem.at[k])

    for k in range(strips):
        vap_flat[:, k * BLK : (k + 1) * BLK] = vap[k]
    vap_copy = pltpu.make_async_copy(vap_flat, vap_hbm, vap_sem)
    vap_copy.start()
    zero_tile = jnp.zeros((SUB, BLK), jnp.float32)
    for k in range(strips + 2):
        for g in range(groups + 2):
            if k in (0, strips + 1) or g in (0, groups + 1):
                first[k, rows_of(g), :] = zero_tile

    lane_index = lax.broadcasted_iota(jnp.int32, (SUB, BLK), 1)
    is_last_lane = lane_index == BLK - 1
    is_first_lane = lane_index == 0

    def around(load, k, g):
        at = SUB * (g + 1)
        here = load(k + 1, slice(at, at + SUB))
        up = load(k + 1, slice(at - 1, at + SUB - 1))
        down = load(k + 1, slice(at + 1, at + SUB + 1))
        before = load(k, slice(at, at + SUB))
        after = load(k + 2, slice(at, at + SUB))
        left = pltpu.roll(jnp.where(is_last_lane, before, here), 1, 1)
        right = pltpu.roll(jnp.where(is_first_lane, after, here), BLK - 1, 1)
        return here, (up, down, left, right)

    def fluxes(k, carry):
        for g in range(groups):
            rows = rows_of(g)
            p_here, p_near = around(lambda s, r: pres[s, r, :], k, g)
            k_here, k_near = around(lambda s, r: perm[s, r, :], k, g)
            l_here, l_near = around(lambda s, r: lam[s, r, :], k, g)
            drives = []
            couplings = []
            for n in range(4):
                transmiss = k_here * k_near[n] * recip(k_here + k_near[n])
                drives.append((TIME_STEP * transmiss) * (p_here - p_near[n]))
                couplings.append(transmiss * (l_here + l_near[n]))
            drive_sum = (drives[0] + drives[1]) + (drives[2] + drives[3])
            content_scale = scale[k, rows, :]
            flat_rows = pl.ds(pl.multiple_of(k * layers + g * SUB, SUB), SUB)
            row_total = zero_tile
            for i in range(comps):
                m_here, m_near = around(
                    lambda s, r, i=i: mobile[i, pl.ds(s * padded + r.start, SUB), :], k, g
                )
                value = held[i, flat_rows, :] * content_scale - old[i, flat_rows, :]
                value = value + drive_sum * m_here
                value = value + (drives[0] * m_near[0] + drives[1] * m_near[1])
                value = value + (drives[2] * m_near[2] + drives[3] * m_near[3])
                resid[i, k, rows, :] = value
                row_total = row_total + value
            diagonal = TIME_STEP * (
                (couplings[0] + couplings[1]) + (couplings[2] + couplings[3])
            ) + csum[k, rows, :] * recip(p_here)
            inv_diag = recip(diagonal)
            row_sum[k, rows, :] = row_total
            diag[k, rows, :] = diagonal
            first[k + 1, SUB * (g + 1) : SUB * (g + 2), :] = -row_total * inv_diag
            gain = (STEP_SCALE * OFF_SCALE) * inv_diag
            for n in range(4):
                weights[n, k, rows, :] = couplings[n] * gain
        strip_out(k).start()
        return carry

    lax.fori_loop(0, strips, fluxes, 0)

    def steps(k, carry):
        for g in range(groups):
            rows = rows_of(g)
            here, near = around(lambda s, r: first[s, r, :], k, g)
            step[rows, lanes_of(k)] = (
                STEP_SCALE * here
                + (weights[0, k, rows, :] * near[0] + weights[1, k, rows, :] * near[1])
                + (weights[2, k, rows, :] * near[2] + weights[3, k, rows, :] * near[3])
            )
        return carry

    lax.fori_loop(0, strips, steps, 0)
    step_copy = pltpu.make_async_copy(step, step_hbm, step_sem)
    step_copy.start()

    resid_rows = resid.reshape(comps * strips * layers, BLK)
    for aux, at, inner, toward, away in (
        (top_aux, 0, 1, 0, 1),
        (low_aux, layers - 1, layers - 2, 1, 0),
    ):
        for k in range(strips):
            lanes = slice(k * BLK, (k + 1) * BLK)
            here = slice(at, at + 1)
            behind = slice(inner, inner + 1)
            from_row = pl.ds(k * layers + at, comps, stride=strips * layers)
            aux[0:comps, lanes] = resid_rows[from_row, :]
            unscale = diag[k, here, :]
            values = [None] * AUX_ROWS
            values[AUX_IN] = weights[away, k, here, :] * unscale
            values[AUX_LEFT] = weights[2, k, here, :] * unscale
            values[AUX_RIGHT] = weights[3, k, here, :] * unscale
            values[AUX_FIRST] = first[k + 1, SUB + inner : SUB + inner + 1, :]
            values[AUX_GAIN] = weights[toward, k, behind, :]
            values[AUX_STEP] = step[behind, lanes]
            values[AUX_ROW] = row_sum[k, here, :]
            values[AUX_DIAG] = unscale
            for n, value in enumerate(values):
                aux[comps + n : comps + n + 1, lanes] = value
    vap_copy.wait()
    step_copy.wait()
    for k in range(strips):
        strip_out(k).wait()


def transmissibility(perm, perm_near):
    both = perm + perm_near
    return perm * perm_near / jnp.where(both == 0.0, 1.0, both)


def edge_kernel(
    edge_a,
    edge_b,
    top_aux,
    low_aux,
    in_even,
    in_odd,
    resid_in,
    step_in,
    resid_hbm,
    step_hbm,
    resid,
    step,
    sem,
):
    comps, layers, face = resid_hbm.shape
    odd = lax.rem(lax.axis_index("dev"), 2) == 1
    top_edge = jnp.where(odd, edge_a[...], edge_b[...])
    low_edge = jnp.where(odd, edge_b[...], edge_a[...])
    from_prev = jnp.where(odd, in_even[...], in_odd[...])
    from_next = jnp.where(odd, in_odd[...], in_even[...])
    copies = []
    for n, (edge, aux, other, at, inner) in enumerate(
        (
            (top_edge, top_aux, from_prev, 0, 1),
            (low_edge, low_aux, from_next, layers - 1, layers - 2),
        )
    ):

        def own(index):
            return edge[comps + index : comps + index + 1, :]

        def far(index):
            return other[comps + index : comps + index + 1, :]

        def near(index):
            return aux[comps + index : comps + index + 1, :]

        pres_far, perm_far, lam_far = far(EDGE_PRES), far(EDGE_PERM), far(EDGE_LAM)
        transmiss = transmissibility(own(EDGE_PERM), perm_far)
        drive = TIME_STEP * transmiss * (own(EDGE_PRES) - pres_far)
        lam_both = own(EDGE_LAM) + lam_far
        coupling = transmiss * lam_both
        row = near(AUX_ROW) + drive * lam_both
        diag = near(AUX_DIAG) + TIME_STEP * coupling
        first = -row / diag
        first_old = -near(AUX_ROW) / near(AUX_DIAG)
        row_far = far(EDGE_CSUM) - far(EDGE_OSUM) - drive * lam_both
        diag_far = coupling
        lane = lax.broadcasted_iota(jnp.int32, (1, face), 1)
        sides = [(far(EDGE_PRES2), far(EDGE_PERM2), far(EDGE_LAM2))]
        for shift, end in ((1, 0), (face - 1, face - 1)):
            pres_n, perm_n, lam_n = (pltpu.roll(x, shift, 1) for x in (pres_far, perm_far, lam_far))
            sides.append((pres_n, jnp.where(lane == end, 0.0, perm_n), lam_n))
        for pres_n, perm_n, lam_n in sides:
            joint = transmissibility(perm_far, perm_n) * (lam_far + lam_n)
            row_far = row_far + TIME_STEP * joint * (pres_far - pres_n)
            diag_far = diag_far + joint
        diag_far = TIME_STEP * diag_far + far(EDGE_CSUM) / jnp.where(pres_far == 0.0, 1.0, pres_far)
        first_far = -row_far / jnp.where(diag_far == 0.0, 1.0, diag_far)
        off = (
            (STEP_SCALE * OFF_SCALE) * coupling * first_far
            + near(AUX_IN) * near(AUX_FIRST)
            + near(AUX_LEFT) * pltpu.roll(first, 1, 1)
            + near(AUX_RIGHT) * pltpu.roll(first, face - 1, 1)
        )
        least = min(at, inner)
        step[n, at - least : at - least + 1, :] = STEP_SCALE * first + off / diag
        step[n, inner - least : inner - least + 1, :] = near(AUX_STEP) + near(AUX_GAIN) * (
            first - first_old
        )
        resid[n] = aux[0:comps, :] + drive * (edge[0:comps, :] + other[0:comps, :])
        for source, target in (
            (resid.at[n], resid_hbm.at[:, at, :]),
            (step.at[n, 0:2, :], step_hbm.at[least : least + 2, :]),
        ):
            copies.append(pltpu.make_async_copy(source, target, sem.at[len(copies)]))
            copies[-1].start()
    for copy in copies:
        copy.wait()


def on_device(
    moles,
    old_content,
    pressure,
    perm,
    labels,
    roots,
    counts,
    block_ids,
    wilson,
    attraction,
    covolume,
):
    comps, layers, face = moles.shape
    f32 = jnp.float32
    strips = face // BLK
    tables = (block_ids, wilson, covolume, attraction)
    rows_in = comps * SUB
    vmem = pl.BlockSpec(memory_space=pltpu.VMEM)
    hbm = pl.BlockSpec(memory_space=pltpu.HBM)
    padded = layers + 2 * SUB
    flat = pltpu.VMEM((layers, face), f32)
    flat_int = pltpu.VMEM((layers, face), jnp.int32)
    cell = pltpu.VMEM((strips, layers, BLK), f32)
    cell_pad = pltpu.VMEM((strips + 2, padded, BLK), f32)
    field = pltpu.VMEM((comps, odd_tiles(strips * layers), BLK), f32)
    field_pad = pltpu.VMEM((comps, odd_tiles((strips + 2) * padded), BLK), f32)
    packed = pltpu.VMEM((comps, odd_tiles(WIDE * SUB), BLK), f32)
    edge_shape = pltpu.VMEM((EDGE_SPAN, face), f32)
    aux_shape = pltpu.VMEM((comps + AUX_ROWS, face), f32)
    field_shape = jax.ShapeDtypeStruct((comps, layers, face), f32)
    cell_shape = jax.ShapeDtypeStruct((layers, face), f32)
    field_out = pltpu.VMEM((comps, strips, layers, BLK), f32)
    held_types = [field, field, field_pad] + [cell_pad] * 3 + [cell] * 3
    edge_a, edge_b, *state = pl.pallas_call(
        cells_kernel,
        out_shape=[edge_shape, edge_shape]
        + held_types,
        in_specs=[pl.BlockSpec(memory_space=pltpu.SMEM)] + [hbm] * 10,
        out_specs=[vmem] * (2 + len(held_types)),
        scratch_shapes=[flat, flat, flat_int, flat_int]
        + [pltpu.VMEM((rows_in + 2 * SUB, 3 * rows_in), jnp.bfloat16)]
        + [pltpu.VMEM((rows_in, 2 * WIDE * BLK), f32)]
        + [packed, pltpu.VMEM((WIDE * SUB, BLK), f32)]
        + [packed] * 3
        + [pltpu.VMEM((3, WIDE * SUB, BLK), f32), pltpu.VMEM((5, WIDE * SUB, BLK), f32)]
        + [pltpu.SMEM(table.shape, table.dtype) for table in tables[:-1]]
        + [pltpu.VMEM(attraction.shape, f32)]
        + [
            pltpu.SemaphoreType.DMA((strips,)),
            pltpu.SemaphoreType.DMA((strips,)),
            pltpu.SemaphoreType.DMA((4,)),
            pltpu.SemaphoreType.DMA((len(tables),)),
        ],
        compiler_params=pltpu.CompilerParams(vmem_limit_bytes=CELLS_VMEM),
        name="cells",
    )(counts, *keep_in(pltpu.HBM, *tables, moles, old_content, pressure, perm, labels, roots))
    count = lax.axis_size("dev")
    arrived = []
    for start, edge in ((0, edge_a), (1, edge_b)):
        pairs = [(i, i + 1) for i in range(start, count - 1, 2)]
        arrived.append(lax.ppermute(edge, "dev", pairs + [pair[::-1] for pair in pairs]))
    residual, step, vapour, top_aux, low_aux = pl.pallas_call(
        flux_kernel,
        out_shape=[field_shape, cell_shape, cell_shape, aux_shape, aux_shape],
        in_specs=[vmem] * len(state),
        out_specs=[hbm] * 3 + [vmem] * 2,
        scratch_shapes=[field_out, cell_pad, cell, cell]
        + [pltpu.VMEM((4, strips, layers, BLK), f32), flat, flat]
        + [pltpu.SemaphoreType.DMA(())] * 2
        + [pltpu.SemaphoreType.DMA((strips,))],
        compiler_params=pltpu.CompilerParams(vmem_limit_bytes=FLUX_VMEM),
        name="flux",
    )(*keep_in(pltpu.VMEM, *state))
    residual, step = pl.pallas_call(
        edge_kernel,
        out_shape=[field_shape, cell_shape],
        in_specs=[vmem] * 6 + [hbm] * 2,
        out_specs=[hbm] * 2,
        input_output_aliases={6: 0, 7: 1},
        scratch_shapes=[
            pltpu.VMEM((2, comps, face), f32),
            pltpu.VMEM((2, SUB, face), f32),
            pltpu.SemaphoreType.DMA((4,)),
        ],
        compiler_params=pltpu.CompilerParams(vmem_limit_bytes=16 * 1024 * 1024),
        name="edges",
    )(edge_a, edge_b, top_aux, low_aux, *arrived, residual, step)
    return (residual, step, vapour)


def solution(mesh):
    in_specs = (
        P(None, "dev", None),
        P(None, "dev", None),
        P("dev", None),
        P("dev", None),
        P("dev", None),
        P("dev", None),
        P("dev"),
        P("dev"),
        P(),
        P(),
        P(),
    )
    out_specs = (P(None, "dev", None), P("dev", None), P("dev", None))
    return jax.shard_map(
        on_device, mesh=mesh, in_specs=in_specs, out_specs=out_specs, check_vma=False
    )
```

```python
import math

import jax
import jax.numpy as jnp
from jax import lax
from jax.experimental import pallas as pl
from jax.experimental.pallas import tpu as pltpu
from jax.sharding import PartitionSpec as P

BLK = 128
SUB = 8
SS_ITERS = 3
RR_ITERS = 3
Z_ITERS = 5
WIDE = 8
TOGETHER = 2
LOG2E = math.log2(math.e)
CELLS_VMEM = 32 * 1024 * 1024
FLUX_VMEM = 32 * 1024 * 1024

SQRT_TWO = math.sqrt(2.0)
TIME_STEP = 0.5
RELAX = 0.7
STEP_SCALE = 10.0
OFF_SCALE = RELAX * TIME_STEP

EDGE_PRES, EDGE_PERM, EDGE_LAM, EDGE_CSUM, EDGE_OSUM = range(5)
EDGE_PRES2, EDGE_PERM2, EDGE_LAM2 = range(5, 8)
EDGE_ROWS = 8
EDGE_SPAN = 32
AUX_IN, AUX_LEFT, AUX_RIGHT, AUX_FIRST, AUX_GAIN, AUX_STEP, AUX_ROW, AUX_DIAG = range(8)
AUX_ROWS = 8


def keep_in(space, *arrays):
    return [pltpu.with_memory_space_constraint(x, space) for x in arrays]


def recip(value):
    return pltpu.reciprocal(value, approx=True)


def odd_tiles(rows):
    return rows + SUB if (rows // SUB) % 2 == 0 else rows


def split_halves(value):
    high = value.astype(jnp.bfloat16)
    low = (value - high.astype(jnp.float32)).astype(jnp.bfloat16)
    return high, low


def widen(wide, attraction, covolume, comps):
    cols = 3 * comps * SUB
    span = 2 * SUB

    def column(rows):
        at = lax.broadcasted_iota(jnp.int32, (rows, cols), 1)
        pair = at // (3 * span)
        within = at - pair * (3 * span)
        part = within // span
        within = within - part * span
        return 2 * pair + within // SUB, part, lax.rem(within, SUB)

    comp, _, _ = column(comps)
    spread = jnp.where(comp == lax.broadcasted_iota(jnp.int32, (comps, cols), 0), 1.0, 0.0)
    table = attraction[...]
    coefficients = 0.5 * (
        lax.dot_general(table, spread, (((1,), (0,)), ((), ())), precision=lax.Precision.HIGHEST)
        + lax.dot_general(table, spread, (((0,), (0,)), ((), ())), precision=lax.Precision.HIGHEST)
    )
    comp, part, sub = column(SUB)
    diagonal = sub == lax.broadcasted_iota(jnp.int32, (SUB, cols), 0)
    zero = jnp.zeros((SUB, cols), jnp.float32)
    of_cov = zero
    for j in range(comps):
        of_cov = jnp.where(comp == j, covolume[j], of_cov)
    blocks = [coefficients[i : i + 1, :] for i in range(comps)] + [of_cov, zero + 1.0]
    for pair in range(len(blocks) // 2):
        rows = []
        for i in (2 * pair, 2 * pair + 1):
            value = jnp.where(diagonal, blocks[i], zero)
            high = value.astype(jnp.bfloat16).astype(jnp.float32)
            rows.append(jnp.where(part == 1, value - high, high))
        wide[span * pair : span * (pair + 1), :] = jnp.concatenate(rows, 0).astype(jnp.bfloat16)


def rows_of(g):
    return slice(g * SUB, (g + 1) * SUB)


def cubic(big_a, big_b, vapour_flag):
    two_b = 2.0 * big_b
    two_b_square = two_b * big_b
    least = two_b + 0.01
    most = big_b + 2.0
    if vapour_flag is True:
        start, shift, factor = 1.0 + big_b, big_b + 0.5, -0.5 * big_a
    elif vapour_flag is False:
        start, shift, factor = 3.0 * big_b, big_b, 0.5 * recip(big_a)
    else:
        start = jnp.where(vapour_flag, 1.0 + big_b, 3.0 * big_b)
        shift = jnp.where(vapour_flag, big_b + 0.5, big_b)
        factor = jnp.where(vapour_flag, -0.5 * big_a, -0.5 * recip(big_a))
        base = jnp.where(vapour_flag, two_b, 1.0 + two_b)

    def step(w):
        spread = w * w - two_b_square
        if vapour_flag is True:
            part = factor * (w - two_b) * recip(spread)
        elif vapour_flag is False:
            part = spread * ((1.0 + two_b) - w) * factor
        else:
            part = factor * (w - base) * jnp.where(vapour_flag, recip(spread), spread)
        return jnp.minimum(jnp.maximum((0.5 * w + shift) + part, least), most)

    return start, step


def roots_of(*equations):
    steps = [cubic(*equation) for equation in equations]
    found = [start for start, _ in steps]
    for _ in range(Z_ITERS):
        found = [step(w) for w, (_, step) in zip(found, steps)]
    return [w - big_b for w, (_, big_b, _) in zip(found, equations)]


def cells_kernel(
    counts,
    block_ids_hbm,
    wilson_hbm,
    covolume_hbm,
    attraction_hbm,
    moles_hbm,
    old_hbm,
    pres_hbm,
    perm_hbm,
    labels_hbm,
    roots_hbm,
    edge_a,
    edge_b,
    held,
    old,
    mobile,
    pres,
    perm,
    lam,
    scale,
    csum,
    vap,
    pres_flat,
    perm_flat,
    labels,
    roots,
    w_wide,
    sums,
    pack,
    pack_pres,
    inv_excess,
    liquid,
    vapour,
    out_cell,
    found,
    block_ids,
    wilson,
    covolume,
    attraction,
    in_sem,
    old_sem,
    cell_sem,
    table_sem,
):
    comps, layers, face = moles_hbm.shape
    strips = face // BLK
    groups = layers // SUB
    padded = layers + 2 * SUB
    inside = slice(SUB, SUB + layers)

    def lanes_of(k):
        return pl.ds(pl.multiple_of(k * BLK, BLK), BLK)

    def strip_of(k):
        return pl.ds(pl.multiple_of(k * layers, SUB), layers)

    def strip_in(source, target, sem, k):
        return pltpu.make_async_copy(
            source.at[:, :, lanes_of(k)], target.at[:, strip_of(k), :], sem.at[k]
        )

    cell_copies = [
        pltpu.make_async_copy(pres_hbm, pres_flat, cell_sem.at[0]),
        pltpu.make_async_copy(roots_hbm, roots, cell_sem.at[1]),
        pltpu.make_async_copy(labels_hbm, labels, cell_sem.at[2]),
        pltpu.make_async_copy(perm_hbm, perm_flat, cell_sem.at[3]),
    ]
    table_copies = [
        pltpu.make_async_copy(source, target, table_sem.at[n])
        for n, (source, target) in enumerate(
            (
                (attraction_hbm, attraction),
                (covolume_hbm, covolume),
                (wilson_hbm, wilson),
                (block_ids_hbm, block_ids),
            )
        )
    ]
    for copy in table_copies + cell_copies:
        copy.start()
    for k in range(strips):
        strip_in(moles_hbm, held, in_sem, k).start()

    zero_tile = jnp.zeros((SUB, BLK), jnp.float32)
    zero_strip = jnp.zeros((padded, BLK), jnp.float32)

    for ref in (pres, perm, lam):
        for k in (0, strips + 1):
            ref[k] = zero_strip
        for k in range(1, strips + 1):
            ref[k, 0:SUB] = zero_tile
            ref[k, SUB + layers : padded] = zero_tile

    def clear(i, carry):
        for k in (0, strips + 1):
            mobile[i, k * padded : (k + 1) * padded, :] = zero_strip
        for k in range(1, strips + 1):
            mobile[i, k * padded : k * padded + SUB, :] = zero_tile
            mobile[i, (k + 1) * padded - SUB : (k + 1) * padded, :] = zero_tile
        return carry

    lax.fori_loop(0, comps, clear, 0)
    for copy in table_copies:
        copy.wait()
    widen(w_wide, attraction, covolume, comps)

    cols = comps * SUB

    def mixture(tile, count, keep=None):
        parts = ([], [], [])
        for g in range(0, count, 2):
            halves = []
            for j in range(comps // 2):
                both = [
                    jnp.concatenate([tile(2 * j, at), tile(2 * j + 1, at)], 0) for at in (g, g + 1)
                ]
                high, low = split_halves(jnp.concatenate(both, 1))
                halves += [high, high, low]
            result = jnp.dot(
                w_wide[...],
                jnp.concatenate(halves, 0),
                preferred_element_type=jnp.float32,
            )
            if keep is not None:
                sums[:, (keep + g) * BLK : (keep + g + 2) * BLK] = result[0:cols]
            for n, at in enumerate((g, g + 1)):
                lanes = slice(n * BLK, (n + 1) * BLK)
                quad = tile(0, at) * result[0:SUB, lanes]
                for i in range(1, comps):
                    quad = quad + tile(i, at) * result[i * SUB : (i + 1) * SUB, lanes]
                parts[0].append(result[cols + SUB : cols + 2 * SUB, lanes])
                parts[1].append(result[cols : cols + SUB, lanes])
                parts[2].append(quad)
        return [jnp.concatenate(part, 0) for part in parts]

    def total(at, start, count):
        rows = slice(at * SUB, (at + 1) * SUB)
        return jnp.concatenate(
            [sums[rows, g * BLK : (g + 1) * BLK] for g in range(start, start + count)], 0
        )

    for copy in cell_copies:
        copy.wait()
    for k in range(strips):
        pres[k + 1, inside, :] = pres_flat[:, k * BLK : (k + 1) * BLK]
        perm[k + 1, inside, :] = perm_flat[:, k * BLK : (k + 1) * BLK]

    def padded_of(k):
        return pl.ds(pl.multiple_of((k + 1) * padded + SUB, SUB), layers)

    def single(k, carry):
        strip_in(moles_hbm, held, in_sem, k).wait()
        strip_in(old_hbm, old, old_sem, k).start()
        amount, b_sum, quad = mixture(
            lambda i, g: held[i, pl.ds(pl.multiple_of(k * layers + g * SUB, SUB), SUB), :], groups
        )
        pressure = pres[k + 1, inside, :]
        inv_amount = recip(amount)
        big_a = pressure * quad * inv_amount * inv_amount
        big_b = pressure * b_sum * inv_amount
        is_vapour = roots[:, lanes_of(k)] == 1
        (z_factor,) = roots_of((big_a, big_b, is_vapour))
        rho = pressure * recip(z_factor)
        part = labels[:, lanes_of(k)].astype(jnp.float32)
        move = ((1.0 - part) * (1.0 - part) + 4.0 * part * part) * rho
        vap[k] = part
        scale[k] = rho
        csum[k] = amount * rho
        lam[k + 1, inside, :] = amount * move
        for i in range(comps):
            mobile[i, padded_of(k), :] = held[i, strip_of(k), :] * move
        return carry

    lax.fori_loop(0, strips, single, 0)

    batch = WIDE * SUB
    own_count = counts[0]
    held_stride, mobile_stride, pack_stride = (ref.shape[1] for ref in (held, mobile, pack))
    held_rows = held.reshape(comps * held_stride, BLK)
    mobile_rows = mobile.reshape(comps * mobile_stride, BLK)
    pack_rows = pack.reshape(comps * pack_stride, BLK)
    liquid_rows = liquid.reshape(comps * pack_stride, BLK)
    vapour_rows = vapour.reshape(comps * pack_stride, BLK)
    bits = strips.bit_length() - 1

    def place(slot):
        block = block_ids[jnp.minimum(slot, own_count - 1)]
        layer = lax.shift_right_logical(block, bits)
        return block - lax.shift_left(layer, bits), layer

    def field_at(k, layer):
        return pl.ds(k * layers + layer, comps, stride=held_stride)

    def mobile_at(k, layer):
        return pl.ds((k + 1) * padded + layer + SUB, comps, stride=mobile_stride)

    def flash(number, carry):
        base = number * batch

        def gather(group, inner):
            for n in range(SUB):
                r = group * SUB + n
                k, layer = place(base + r)
                pack_rows[pl.ds(r, comps, stride=pack_stride), :] = held_rows[field_at(k, layer), :]
                pack_pres[pl.ds(r, 1), :] = pres[k + 1, pl.ds(layer + SUB, 1), :]
            return inner

        lax.fori_loop(0, WIDE, gather, 0)
        slots = slice(0, batch)
        pressure = pack_pres[...]
        amount = pack[0, slots, :]
        for i in range(1, comps):
            amount = amount + pack[i, slots, :]
        inv_amount = recip(amount)
        for i in range(comps):
            pack[i, slots, :] = pack[i, slots, :] * inv_amount

        def keep_k(i, log2_k):
            inv_excess[i, slots, :] = recip(jnp.exp2(log2_k) - 1.0)

        log2_pres = jnp.log(pressure) * LOG2E
        for i in range(comps):
            keep_k(i, wilson[i] * LOG2E - log2_pres)

        def newton(_, part):
            value = jnp.zeros((batch, BLK), jnp.float32)
            slope = jnp.full((batch, BLK), 0.05, jnp.float32)
            for i in range(comps):
                ratio = recip(inv_excess[i, slots, :] + part)
                term = pack[i, slots, :] * ratio
                value = value + term
                slope = slope + term * ratio
            return jnp.minimum(jnp.maximum(part + value * recip(slope), 0.0), 1.0)

        def sweep(number_of_sweep, inner):
            half = jnp.full((batch, BLK), 0.5, jnp.float32)
            part = lax.fori_loop(0, RR_ITERS, newton, half)
            for i in range(comps):
                fraction = pack[i, slots, :]
                term = fraction * recip(inv_excess[i, slots, :] + part)
                liq = fraction - part * term
                liquid[i, slots, :] = liq
                vapour[i, slots, :] = liq + term
            phases = []
            equations = []
            for n, (ref, flag) in enumerate(((liquid, False), (vapour, True))):
                whole, b_sum, quad = mixture(lambda i, g: ref[i, rows_of(g), :], WIDE, n * WIDE)
                inv_whole = recip(whole)
                b_mix = b_sum * inv_whole
                a_mix = quad * inv_whole * inv_whole
                big_b = pressure * b_mix
                equations.append((pressure * a_mix, big_b, flag))
                phases.append((quad, whole, inv_whole, a_mix, b_mix, big_b))
            factors = roots_of(*equations)
            found[0] = part
            for n in range(2):
                found[1 + n] = factors[n]
                found[3 + n] = phases[n][2]

            @pl.when(number_of_sweep + 1 < SS_ITERS)
            def _():
                parts = []
                for (quad, whole, _, a_mix, b_mix, big_b), z_factor in zip(phases, factors):
                    log_arg = (z_factor + (1.0 + SQRT_TWO) * big_b) * recip(
                        z_factor + (1.0 - SQRT_TWO) * big_b
                    )
                    inv_b = recip(b_mix)
                    depart = a_mix * inv_b * (1.0 / (2.0 * SQRT_TWO)) * jnp.log(log_arg)
                    of_cov = (LOG2E * inv_b) * (z_factor - 1.0 + depart)
                    of_sum = (2.0 * LOG2E) * depart * whole * recip(quad)
                    parts.append((of_cov, LOG2E * jnp.log(z_factor - big_b), of_sum))
                cov_gap = parts[0][0] - parts[1][0]
                log_gap = parts[0][1] - parts[1][1]
                for i in range(comps):
                    log2_k = (covolume[i] * cov_gap - log_gap) - (
                        parts[0][2] * total(i, 0, WIDE) - parts[1][2] * total(i, WIDE, WIDE)
                    )
                    keep_k(i, jnp.minimum(jnp.maximum(log2_k, -3.0 * LOG2E), 3.0 * LOG2E))
            return inner

        lax.fori_loop(0, SS_ITERS, sweep, 0)
        part = found[0]
        rho_liq = amount * pressure * recip(found[1])
        rho_vap = amount * pressure * recip(found[2])
        rest = 1.0 - part
        move_liq = rest * rest * rho_liq
        move_vap = 4.0 * part * part * rho_vap
        hold_liq = rest * rho_liq
        hold_vap = part * rho_vap
        out_cell[0] = part
        out_cell[1] = move_liq + move_vap
        out_cell[2] = hold_liq + hold_vap
        inv_liq, inv_vap = found[3], found[4]
        move_liq = move_liq * inv_liq
        move_vap = move_vap * inv_vap
        hold_liq = hold_liq * inv_liq
        hold_vap = hold_vap * inv_vap
        for i in range(comps):
            liq, gas = liquid[i, slots, :], vapour[i, slots, :]
            liquid[i, slots, :] = move_liq * liq + move_vap * gas
            vapour[i, slots, :] = hold_liq * liq + hold_vap * gas
        one_row = jnp.ones((1, BLK), jnp.float32)

        def scatter(group, inner):
            for n in range(SUB):
                r = group * SUB + n
                k, layer = place(base + r)
                of = pl.ds(r, comps, stride=pack_stride)
                mobile_rows[mobile_at(k, layer), :] = liquid_rows[of, :]
                held_rows[field_at(k, layer), :] = vapour_rows[of, :]
                one = pl.ds(r, 1)
                row = pl.ds(layer, 1)
                vap[k, row, :] = out_cell[0, one, :]
                lam[k + 1, pl.ds(layer + SUB, 1), :] = out_cell[1, one, :]
                csum[k, row, :] = out_cell[2, one, :]
                scale[k, row, :] = one_row
            return inner

        lax.fori_loop(0, WIDE, scatter, 0)
        return carry

    lax.fori_loop(0, (own_count + batch - 1) // batch, flash, 0)
    for k in range(strips):
        strip_in(old_hbm, old, old_sem, k).wait()
    old_rows = old.reshape(comps * old.shape[1], BLK)

    def edge_values(k, at, inner):
        here = slice(at, at + 1)
        pad_here = slice(SUB + at, SUB + at + 1)
        pad_inner = slice(SUB + inner, SUB + inner + 1)
        values = [None] * EDGE_ROWS
        values[EDGE_PRES] = pres[k + 1, pad_here, :]
        values[EDGE_PERM] = perm[k + 1, pad_here, :]
        values[EDGE_LAM] = lam[k + 1, pad_here, :]
        values[EDGE_CSUM] = csum[k, here, :]
        values[EDGE_OSUM] = jnp.sum(old_rows[field_at(k, at), :], 0, keepdims=True)
        values[EDGE_PRES2] = pres[k + 1, pad_inner, :]
        values[EDGE_PERM2] = perm[k + 1, pad_inner, :]
        values[EDGE_LAM2] = lam[k + 1, pad_inner, :]
        return [mobile_rows[mobile_at(k, at), :]] + values

    odd = lax.rem(lax.axis_index("dev"), 2) == 1
    for k in range(strips):
        lanes = slice(k * BLK, (k + 1) * BLK)
        tops = edge_values(k, 0, 1)
        lows = edge_values(k, layers - 1, layers - 2)
        row = 0
        for top, low in zip(tops, lows):
            rows = slice(row, row + top.shape[0])
            edge_a[rows, lanes] = jnp.where(odd, top, low)
            edge_b[rows, lanes] = jnp.where(odd, low, top)
            row = rows.stop


def flux_kernel(
    held,
    old,
    mobile,
    pres,
    perm,
    lam,
    scale,
    csum,
    vap,
    resid_hbm,
    step_hbm,
    vap_hbm,
    top_aux,
    low_aux,
    resid,
    first,
    row_sum,
    diag,
    weights,
    step,
    vap_flat,
    step_sem,
    vap_sem,
    out_sem,
):
    comps = held.shape[0]
    strips, layers, _ = scale.shape
    groups = layers // SUB
    padded = layers + 2 * SUB

    def lanes_of(k):
        return pl.ds(pl.multiple_of(k * BLK, BLK), BLK)

    def strip_out(k):
        return pltpu.make_async_copy(resid.at[:, k], resid_hbm.at[:, :, lanes_of(k)], out_sem.at[k])

    for k in range(strips):
        vap_flat[:, k * BLK : (k + 1) * BLK] = vap[k]
    vap_copy = pltpu.make_async_copy(vap_flat, vap_hbm, vap_sem)
    vap_copy.start()
    zero_tile = jnp.zeros((SUB, BLK), jnp.float32)
    for k in range(strips + 2):
        for g in range(groups + 2):
            if k in (0, strips + 1) or g in (0, groups + 1):
                first[k, rows_of(g), :] = zero_tile

    lane_index = lax.broadcasted_iota(jnp.int32, (SUB, BLK), 1)
    is_last_lane = lane_index == BLK - 1
    is_first_lane = lane_index == 0

    def around(load, k, g, count):
        at = SUB * (g + 1)
        tiles = [load(k + n, slice(at, at + SUB)) for n in range(count + 2)]
        found = []
        for n in range(1, count + 1):
            here = tiles[n]
            up = load(k + n, slice(at - 1, at + SUB - 1))
            down = load(k + n, slice(at + 1, at + SUB + 1))
            left = pltpu.roll(jnp.where(is_last_lane, tiles[n - 1], here), 1, 1)
            right = pltpu.roll(jnp.where(is_first_lane, tiles[n + 1], here), BLK - 1, 1)
            found.append((here, (up, down, left, right)))
        return found

    def fluxes(number, carry):
        first_strip = number * TOGETHER
        for g in range(groups):
            rows = rows_of(g)
            states = []
            for k, pressures, perms, lams in zip(
                range(TOGETHER),
                *(
                    around(lambda s, r: ref[s, r, :], first_strip, g, TOGETHER)
                    for ref in (pres, perm, lam)
                ),
            ):
                (p_here, p_near), (k_here, k_near), (l_here, l_near) = pressures, perms, lams
                drives = []
                couplings = []
                for n in range(4):
                    transmiss = k_here * k_near[n] * recip(k_here + k_near[n])
                    drives.append((TIME_STEP * transmiss) * (p_here - p_near[n]))
                    couplings.append(transmiss * (l_here + l_near[n]))
                drive_sum = (drives[0] + drives[1]) + (drives[2] + drives[3])
                diagonal = TIME_STEP * (
                    (couplings[0] + couplings[1]) + (couplings[2] + couplings[3])
                ) + csum[first_strip + k, rows, :] * recip(p_here)
                inv_diag = recip(diagonal)
                diag[first_strip + k, rows, :] = diagonal
                gain = (STEP_SCALE * OFF_SCALE) * inv_diag
                for n in range(4):
                    weights[n, first_strip + k, rows, :] = couplings[n] * gain
                states.append((drives, drive_sum, inv_diag, scale[first_strip + k, rows, :]))
            row_totals = [zero_tile] * TOGETHER
            for i in range(comps):
                found = around(
                    lambda s, r: mobile[i, pl.ds(s * padded + r.start, SUB), :],
                    first_strip,
                    g,
                    TOGETHER,
                )
                for k, (m_here, m_near) in enumerate(found):
                    drives, drive_sum, _, content_scale = states[k]
                    strip = first_strip + k
                    flat_rows = pl.ds(pl.multiple_of(strip * layers + g * SUB, SUB), SUB)
                    value = held[i, flat_rows, :] * content_scale - old[i, flat_rows, :]
                    value = value + drive_sum * m_here
                    value = value + (drives[0] * m_near[0] + drives[1] * m_near[1])
                    value = value + (drives[2] * m_near[2] + drives[3] * m_near[3])
                    resid[i, strip, rows, :] = value
                    row_totals[k] = row_totals[k] + value
            for k in range(TOGETHER):
                row_sum[first_strip + k, rows, :] = row_totals[k]
                first[first_strip + k + 1, SUB * (g + 1) : SUB * (g + 2), :] = (
                    -row_totals[k] * states[k][2]
                )
        for k in range(TOGETHER):
            strip_out(first_strip + k).start()
        return carry

    lax.fori_loop(0, strips // TOGETHER, fluxes, 0)

    def steps(k, carry):
        for g in range(groups):
            rows = rows_of(g)
            ((here, near),) = around(lambda s, r: first[s, r, :], k, g, 1)
            step[rows, lanes_of(k)] = (
                STEP_SCALE * here
                + (weights[0, k, rows, :] * near[0] + weights[1, k, rows, :] * near[1])
                + (weights[2, k, rows, :] * near[2] + weights[3, k, rows, :] * near[3])
            )
        return carry

    lax.fori_loop(0, strips, steps, 0)
    step_copy = pltpu.make_async_copy(step, step_hbm, step_sem)
    step_copy.start()

    resid_rows = resid.reshape(comps * strips * layers, BLK)
    for aux, at, inner, toward, away in (
        (top_aux, 0, 1, 0, 1),
        (low_aux, layers - 1, layers - 2, 1, 0),
    ):
        for k in range(strips):
            lanes = slice(k * BLK, (k + 1) * BLK)
            here = slice(at, at + 1)
            behind = slice(inner, inner + 1)
            from_row = pl.ds(k * layers + at, comps, stride=strips * layers)
            aux[0:comps, lanes] = resid_rows[from_row, :]
            unscale = diag[k, here, :]
            values = [None] * AUX_ROWS
            values[AUX_IN] = weights[away, k, here, :] * unscale
            values[AUX_LEFT] = weights[2, k, here, :] * unscale
            values[AUX_RIGHT] = weights[3, k, here, :] * unscale
            values[AUX_FIRST] = first[k + 1, SUB + inner : SUB + inner + 1, :]
            values[AUX_GAIN] = weights[toward, k, behind, :]
            values[AUX_STEP] = step[behind, lanes]
            values[AUX_ROW] = row_sum[k, here, :]
            values[AUX_DIAG] = unscale
            for n, value in enumerate(values):
                aux[comps + n : comps + n + 1, lanes] = value
    vap_copy.wait()
    step_copy.wait()
    for k in range(strips):
        strip_out(k).wait()


def transmissibility(perm, perm_near):
    both = perm + perm_near
    return perm * perm_near / jnp.where(both == 0.0, 1.0, both)


def edge_kernel(
    edge_a,
    edge_b,
    top_aux,
    low_aux,
    in_even,
    in_odd,
    resid_in,
    step_in,
    resid_hbm,
    step_hbm,
    resid,
    step,
    sem,
):
    comps, layers, face = resid_hbm.shape
    odd = lax.rem(lax.axis_index("dev"), 2) == 1
    top_edge = jnp.where(odd, edge_a[...], edge_b[...])
    low_edge = jnp.where(odd, edge_b[...], edge_a[...])
    from_prev = jnp.where(odd, in_even[...], in_odd[...])
    from_next = jnp.where(odd, in_odd[...], in_even[...])
    copies = []
    for n, (edge, aux, other, at, inner) in enumerate(
        (
            (top_edge, top_aux, from_prev, 0, 1),
            (low_edge, low_aux, from_next, layers - 1, layers - 2),
        )
    ):

        def own(index):
            return edge[comps + index : comps + index + 1, :]

        def far(index):
            return other[comps + index : comps + index + 1, :]

        def near(index):
            return aux[comps + index : comps + index + 1, :]

        pres_far, perm_far, lam_far = far(EDGE_PRES), far(EDGE_PERM), far(EDGE_LAM)
        transmiss = transmissibility(own(EDGE_PERM), perm_far)
        drive = TIME_STEP * transmiss * (own(EDGE_PRES) - pres_far)
        lam_both = own(EDGE_LAM) + lam_far
        coupling = transmiss * lam_both
        row = near(AUX_ROW) + drive * lam_both
        diag = near(AUX_DIAG) + TIME_STEP * coupling
        first = -row / diag
        first_old = -near(AUX_ROW) / near(AUX_DIAG)
        row_far = far(EDGE_CSUM) - far(EDGE_OSUM) - drive * lam_both
        diag_far = coupling
        lane = lax.broadcasted_iota(jnp.int32, (1, face), 1)
        sides = [(far(EDGE_PRES2), far(EDGE_PERM2), far(EDGE_LAM2))]
        for shift, end in ((1, 0), (face - 1, face - 1)):
            pres_n, perm_n, lam_n = (pltpu.roll(x, shift, 1) for x in (pres_far, perm_far, lam_far))
            sides.append((pres_n, jnp.where(lane == end, 0.0, perm_n), lam_n))
        for pres_n, perm_n, lam_n in sides:
            joint = transmissibility(perm_far, perm_n) * (lam_far + lam_n)
            row_far = row_far + TIME_STEP * joint * (pres_far - pres_n)
            diag_far = diag_far + joint
        diag_far = TIME_STEP * diag_far + far(EDGE_CSUM) / jnp.where(pres_far == 0.0, 1.0, pres_far)
        first_far = -row_far / jnp.where(diag_far == 0.0, 1.0, diag_far)
        off = (
            (STEP_SCALE * OFF_SCALE) * coupling * first_far
            + near(AUX_IN) * near(AUX_FIRST)
            + near(AUX_LEFT) * pltpu.roll(first, 1, 1)
            + near(AUX_RIGHT) * pltpu.roll(first, face - 1, 1)
        )
        least = min(at, inner)
        step[n, at - least : at - least + 1, :] = STEP_SCALE * first + off / diag
        step[n, inner - least : inner - least + 1, :] = near(AUX_STEP) + near(AUX_GAIN) * (
            first - first_old
        )
        resid[n] = aux[0:comps, :] + drive * (edge[0:comps, :] + other[0:comps, :])
        for source, target in (
            (resid.at[n], resid_hbm.at[:, at, :]),
            (step.at[n, 0:2, :], step_hbm.at[least : least + 2, :]),
        ):
            copies.append(pltpu.make_async_copy(source, target, sem.at[len(copies)]))
            copies[-1].start()
    for copy in copies:
        copy.wait()


def on_device(
    moles,
    old_content,
    pressure,
    perm,
    labels,
    roots,
    counts,
    block_ids,
    wilson,
    attraction,
    covolume,
):
    comps, layers, face = moles.shape
    f32 = jnp.float32
    strips = face // BLK
    tables = (block_ids, wilson, covolume, attraction)
    rows_in = comps * SUB
    vmem = pl.BlockSpec(memory_space=pltpu.VMEM)
    hbm = pl.BlockSpec(memory_space=pltpu.HBM)
    padded = layers + 2 * SUB
    flat = pltpu.VMEM((layers, face), f32)
    flat_int = pltpu.VMEM((layers, face), jnp.int32)
    cell = pltpu.VMEM((strips, layers, BLK), f32)
    cell_pad = pltpu.VMEM((strips + 2, padded, BLK), f32)
    field = pltpu.VMEM((comps, odd_tiles(strips * layers), BLK), f32)
    field_pad = pltpu.VMEM((comps, odd_tiles((strips + 2) * padded), BLK), f32)
    packed = pltpu.VMEM((comps, odd_tiles(WIDE * SUB), BLK), f32)
    edge_shape = pltpu.VMEM((EDGE_SPAN, face), f32)
    aux_shape = pltpu.VMEM((comps + AUX_ROWS, face), f32)
    field_shape = jax.ShapeDtypeStruct((comps, layers, face), f32)
    cell_shape = jax.ShapeDtypeStruct((layers, face), f32)
    field_out = pltpu.VMEM((comps, strips, layers, BLK), f32)
    held_types = [field, field, field_pad] + [cell_pad] * 3 + [cell] * 3
    edge_a, edge_b, *state = pl.pallas_call(
        cells_kernel,
        out_shape=[edge_shape, edge_shape]
        + held_types,
        in_specs=[pl.BlockSpec(memory_space=pltpu.SMEM)] + [hbm] * 10,
        out_specs=[vmem] * (2 + len(held_types)),
        scratch_shapes=[flat, flat, flat_int, flat_int]
        + [pltpu.VMEM((rows_in + 2 * SUB, 3 * rows_in), jnp.bfloat16)]
        + [pltpu.VMEM((rows_in, 2 * WIDE * BLK), f32)]
        + [packed, pltpu.VMEM((WIDE * SUB, BLK), f32)]
        + [packed] * 3
        + [pltpu.VMEM((3, WIDE * SUB, BLK), f32), pltpu.VMEM((5, WIDE * SUB, BLK), f32)]
        + [pltpu.SMEM(table.shape, table.dtype) for table in tables[:-1]]
        + [pltpu.VMEM(attraction.shape, f32)]
        + [
            pltpu.SemaphoreType.DMA((strips,)),
            pltpu.SemaphoreType.DMA((strips,)),
            pltpu.SemaphoreType.DMA((4,)),
            pltpu.SemaphoreType.DMA((len(tables),)),
        ],
        compiler_params=pltpu.CompilerParams(vmem_limit_bytes=CELLS_VMEM),
        name="cells",
    )(counts, *keep_in(pltpu.HBM, *tables, moles, old_content, pressure, perm, labels, roots))
    count = lax.axis_size("dev")
    arrived = []
    for start, edge in ((0, edge_a), (1, edge_b)):
        pairs = [(i, i + 1) for i in range(start, count - 1, 2)]
        arrived.append(lax.ppermute(edge, "dev", pairs + [pair[::-1] for pair in pairs]))
    residual, step, vapour, top_aux, low_aux = pl.pallas_call(
        flux_kernel,
        out_shape=[field_shape, cell_shape, cell_shape, aux_shape, aux_shape],
        in_specs=[vmem] * len(state),
        out_specs=[hbm] * 3 + [vmem] * 2,
        scratch_shapes=[field_out, cell_pad, cell, cell]
        + [pltpu.VMEM((4, strips, layers, BLK), f32), flat, flat]
        + [pltpu.SemaphoreType.DMA(())] * 2
        + [pltpu.SemaphoreType.DMA((strips,))],
        compiler_params=pltpu.CompilerParams(vmem_limit_bytes=FLUX_VMEM),
        name="flux",
    )(*keep_in(pltpu.VMEM, *state))
    residual, step = pl.pallas_call(
        edge_kernel,
        out_shape=[field_shape, cell_shape],
        in_specs=[vmem] * 6 + [hbm] * 2,
        out_specs=[hbm] * 2,
        input_output_aliases={6: 0, 7: 1},
        scratch_shapes=[
            pltpu.VMEM((2, comps, face), f32),
            pltpu.VMEM((2, SUB, face), f32),
            pltpu.SemaphoreType.DMA((4,)),
        ],
        compiler_params=pltpu.CompilerParams(vmem_limit_bytes=16 * 1024 * 1024),
        name="edges",
    )(edge_a, edge_b, top_aux, low_aux, *arrived, residual, step)
    return (residual, step, vapour)


def solution(mesh):
    in_specs = (
        P(None, "dev", None),
        P(None, "dev", None),
        P("dev", None),
        P("dev", None),
        P("dev", None),
        P("dev", None),
        P("dev"),
        P("dev"),
        P(),
        P(),
        P(),
    )
    out_specs = (P(None, "dev", None), P("dev", None), P("dev", None))
    return jax.shard_map(
        on_device, mesh=mesh, in_specs=in_specs, out_specs=out_specs, check_vma=False
    )
```

```python
import math

import jax
import jax.numpy as jnp
from jax import lax
from jax.experimental import pallas as pl
from jax.experimental.pallas import tpu as pltpu
from jax.sharding import PartitionSpec as P

BLK = 128
SUB = 8
SS_ITERS = 3
RR_ITERS = 3
Z_ITERS = 5
WIDE = 8
TOGETHER = 1
LOG2E = math.log2(math.e)
CELLS_VMEM = 32 * 1024 * 1024
FLUX_VMEM = 32 * 1024 * 1024

SQRT_TWO = math.sqrt(2.0)
TIME_STEP = 0.5
RELAX = 0.7
STEP_SCALE = 10.0
OFF_SCALE = RELAX * TIME_STEP

EDGE_PRES, EDGE_PERM, EDGE_LAM, EDGE_CSUM, EDGE_OSUM = range(5)
EDGE_PRES2, EDGE_PERM2, EDGE_LAM2 = range(5, 8)
EDGE_ROWS = 8
EDGE_SPAN = 32
AUX_IN, AUX_LEFT, AUX_RIGHT, AUX_FIRST, AUX_GAIN, AUX_STEP, AUX_ROW, AUX_DIAG = range(8)
AUX_ROWS = 8


def keep_in(space, *arrays):
    return [pltpu.with_memory_space_constraint(x, space) for x in arrays]


def recip(value):
    return pltpu.reciprocal(value, approx=True)


def odd_tiles(rows):
    return rows + SUB if (rows // SUB) % 2 == 0 else rows


def split_halves(value):
    high = value.astype(jnp.bfloat16)
    low = (value - high.astype(jnp.float32)).astype(jnp.bfloat16)
    return high, low


def widen(wide, attraction, covolume, comps):
    cols = 3 * comps * SUB
    span = 2 * SUB

    def column(rows):
        at = lax.broadcasted_iota(jnp.int32, (rows, cols), 1)
        pair = at // (3 * span)
        within = at - pair * (3 * span)
        part = within // span
        within = within - part * span
        return 2 * pair + within // SUB, part, lax.rem(within, SUB)

    comp, _, _ = column(comps)
    spread = jnp.where(comp == lax.broadcasted_iota(jnp.int32, (comps, cols), 0), 1.0, 0.0)
    table = attraction[...]
    coefficients = 0.5 * (
        lax.dot_general(table, spread, (((1,), (0,)), ((), ())), precision=lax.Precision.HIGHEST)
        + lax.dot_general(table, spread, (((0,), (0,)), ((), ())), precision=lax.Precision.HIGHEST)
    )
    comp, part, sub = column(SUB)
    diagonal = sub == lax.broadcasted_iota(jnp.int32, (SUB, cols), 0)
    zero = jnp.zeros((SUB, cols), jnp.float32)
    of_cov = zero
    for j in range(comps):
        of_cov = jnp.where(comp == j, covolume[j], of_cov)
    blocks = [coefficients[i : i + 1, :] for i in range(comps)] + [of_cov, zero + 1.0]
    for pair in range(len(blocks) // 2):
        rows = []
        for i in (2 * pair, 2 * pair + 1):
            value = jnp.where(diagonal, blocks[i], zero)
            high = value.astype(jnp.bfloat16).astype(jnp.float32)
            rows.append(jnp.where(part == 1, value - high, high))
        wide[span * pair : span * (pair + 1), :] = jnp.concatenate(rows, 0).astype(jnp.bfloat16)


def rows_of(g):
    return slice(g * SUB, (g + 1) * SUB)


def cubic(big_a, big_b, vapour_flag):
    two_b = 2.0 * big_b
    two_b_square = two_b * big_b
    least = two_b + 0.01
    most = big_b + 2.0
    if vapour_flag is True:
        start, shift, factor = 1.0 + big_b, big_b + 0.5, -0.5 * big_a
    elif vapour_flag is False:
        start, shift, factor = 3.0 * big_b, big_b, 0.5 * recip(big_a)
    else:
        start = jnp.where(vapour_flag, 1.0 + big_b, 3.0 * big_b)
        shift = jnp.where(vapour_flag, big_b + 0.5, big_b)
        factor = jnp.where(vapour_flag, -0.5 * big_a, -0.5 * recip(big_a))
        base = jnp.where(vapour_flag, two_b, 1.0 + two_b)

    def step(w):
        spread = w * w - two_b_square
        if vapour_flag is True:
            part = factor * (w - two_b) * recip(spread)
        elif vapour_flag is False:
            part = spread * ((1.0 + two_b) - w) * factor
        else:
            part = factor * (w - base) * jnp.where(vapour_flag, recip(spread), spread)
        return jnp.minimum(jnp.maximum((0.5 * w + shift) + part, least), most)

    return start, step


def roots_of(*equations):
    steps = [cubic(*equation) for equation in equations]
    found = [start for start, _ in steps]
    for _ in range(Z_ITERS):
        found = [step(w) for w, (_, step) in zip(found, steps)]
    return [w - big_b for w, (_, big_b, _) in zip(found, equations)]


def mixture(tile, count, comps, w_wide, sums=None, keep=0):
    cols = comps * SUB
    parts = ([], [], [])
    for g in range(0, count, 2):
        halves = []
        for j in range(comps // 2):
            both = [
                jnp.concatenate([tile(2 * j, at), tile(2 * j + 1, at)], 0) for at in (g, g + 1)
            ]
            high, low = split_halves(jnp.concatenate(both, 1))
            halves += [high, high, low]
        result = jnp.dot(
            w_wide[...],
            jnp.concatenate(halves, 0),
            preferred_element_type=jnp.float32,
        )
        if sums is not None:
            sums[:, (keep + g) * BLK : (keep + g + 2) * BLK] = result[0:cols]
        for n, at in enumerate((g, g + 1)):
            lanes = slice(n * BLK, (n + 1) * BLK)
            quad = tile(0, at) * result[0:SUB, lanes]
            for i in range(1, comps):
                quad = quad + tile(i, at) * result[i * SUB : (i + 1) * SUB, lanes]
            parts[0].append(result[cols + SUB : cols + 2 * SUB, lanes])
            parts[1].append(result[cols : cols + SUB, lanes])
            parts[2].append(quad)
    return [jnp.concatenate(part, 0) for part in parts]


def inverse_excess(log2_k):
    return recip(jnp.exp2(log2_k) - 1.0)


def flash(at, refs, pack, inv_excess, pack_pres, pack_amount, cov_tiles, w_wide):
    sums, liquid, vapour, out_cell, found = refs
    comps, batch, _ = liquid.shape
    slots = pl.ds(pl.multiple_of(at, SUB), batch)
    pressure = pack_pres[slots, :]
    amount = pack_amount[slots, :]

    def total(i, start, count):
        rows = slice(i * SUB, (i + 1) * SUB)
        return jnp.concatenate(
            [sums[rows, g * BLK : (g + 1) * BLK] for g in range(start, start + count)], 0
        )

    def cov_of(i):
        return jnp.concatenate([cov_tiles[i]] * WIDE, 0)

    def newton(_, part):
        value = jnp.zeros((batch, BLK), jnp.float32)
        slope = jnp.full((batch, BLK), 0.05, jnp.float32)
        for i in range(comps):
            ratio = recip(inv_excess[i, slots, :] + part)
            term = pack[i, slots, :] * ratio
            value = value + term
            slope = slope + term * ratio
        return jnp.minimum(jnp.maximum(part + value * recip(slope), 0.0), 1.0)

    def sweep(number_of_sweep, inner):
        half = jnp.full((batch, BLK), 0.5, jnp.float32)
        part = lax.fori_loop(0, RR_ITERS, newton, half)
        for i in range(comps):
            fraction = pack[i, slots, :]
            term = fraction * recip(inv_excess[i, slots, :] + part)
            liq = fraction - part * term
            liquid[i] = liq
            vapour[i] = liq + term
        phases = []
        equations = []
        for n, (ref, flag) in enumerate(((liquid, False), (vapour, True))):
            whole, b_sum, quad = mixture(
                    lambda i, g: ref[i, rows_of(g), :], WIDE, comps, w_wide, sums, n * WIDE
                )
            inv_whole = recip(whole)
            b_mix = b_sum * inv_whole
            a_mix = quad * inv_whole * inv_whole
            big_b = pressure * b_mix
            equations.append((pressure * a_mix, big_b, flag))
            phases.append((quad, whole, inv_whole, a_mix, b_mix, big_b))
        factors = roots_of(*equations)
        found[0] = part
        for n in range(2):
            found[1 + n] = factors[n]
            found[3 + n] = phases[n][2]

        @pl.when(number_of_sweep + 1 < SS_ITERS)
        def _():
            parts = []
            for (quad, whole, _, a_mix, b_mix, big_b), z_factor in zip(phases, factors):
                log_arg = (z_factor + (1.0 + SQRT_TWO) * big_b) * recip(
                    z_factor + (1.0 - SQRT_TWO) * big_b
                )
                inv_b = recip(b_mix)
                depart = a_mix * inv_b * (1.0 / (2.0 * SQRT_TWO)) * jnp.log(log_arg)
                of_cov = (LOG2E * inv_b) * (z_factor - 1.0 + depart)
                of_sum = (2.0 * LOG2E) * depart * whole * recip(quad)
                parts.append((of_cov, LOG2E * jnp.log(z_factor - big_b), of_sum))
            cov_gap = parts[0][0] - parts[1][0]
            log_gap = parts[0][1] - parts[1][1]
            for i in range(comps):
                log2_k = (cov_of(i) * cov_gap - log_gap) - (
                    parts[0][2] * total(i, 0, WIDE) - parts[1][2] * total(i, WIDE, WIDE)
                )
                inv_excess[i, slots, :] = inverse_excess(jnp.minimum(jnp.maximum(log2_k, -3.0 * LOG2E), 3.0 * LOG2E))
        return inner

    lax.fori_loop(0, SS_ITERS, sweep, 0)
    part = found[0]
    rho_liq = amount * pressure * recip(found[1])
    rho_vap = amount * pressure * recip(found[2])
    rest = 1.0 - part
    move_liq = rest * rest * rho_liq
    move_vap = 4.0 * part * part * rho_vap
    hold_liq = rest * rho_liq
    hold_vap = part * rho_vap
    out_cell[0] = part
    out_cell[1] = move_liq + move_vap
    out_cell[2] = hold_liq + hold_vap
    inv_liq, inv_vap = found[3], found[4]
    move_liq = move_liq * inv_liq
    move_vap = move_vap * inv_vap
    hold_liq = hold_liq * inv_liq
    hold_vap = hold_vap * inv_vap
    for i in range(comps):
        liq, gas = liquid[i], vapour[i]
        liquid[i] = move_liq * liq + move_vap * gas
        vapour[i] = hold_liq * liq + hold_vap * gas


def scatter(at, own_count, order, refs, held, mobile, lam, csum, scale, vap):
    _, liquid, vapour, out_cell, _ = refs
    comps, batch, _ = liquid.shape
    strips, layers, _ = scale.shape
    padded = layers + 2 * SUB
    held_rows, mobile_rows, liquid_rows, vapour_rows = (
        ref.reshape(comps * ref.shape[1], BLK) for ref in (held, mobile, liquid, vapour)
    )
    one_row = jnp.ones((1, BLK), jnp.float32)

    def store(group, inner):
        for n in range(SUB):
            r = group * SUB + n
            k, layer = place(at + r, own_count, order, strips)
            of = pl.ds(r, comps, stride=batch)
            mobile_at = pl.ds((k + 1) * padded + layer + SUB, comps, stride=mobile.shape[1])
            held_at = pl.ds(k * layers + layer, comps, stride=held.shape[1])
            mobile_rows[mobile_at, :] = liquid_rows[of, :]
            held_rows[held_at, :] = vapour_rows[of, :]
            one = pl.ds(r, 1)
            row = pl.ds(layer, 1)
            vap[k, row, :] = out_cell[0, one, :]
            lam[k + 1, pl.ds(layer + SUB, 1), :] = out_cell[1, one, :]
            csum[k, row, :] = out_cell[2, one, :]
            scale[k, row, :] = one_row
        return inner

    lax.fori_loop(0, batch // SUB, store, 0)


def place(slot, own_count, order, strips):
    bits = strips.bit_length() - 1
    block = order[jnp.minimum(slot, own_count - 1)]
    layer = lax.shift_right_logical(block, bits)
    return block - lax.shift_left(layer, bits), layer


def cells_kernel(
    counts,
    block_ids_hbm,
    wilson_hbm,
    covolume_hbm,
    attraction_hbm,
    moles_hbm,
    old_hbm,
    pres_hbm,
    perm_hbm,
    labels_hbm,
    roots_hbm,
    edge_a,
    edge_b,
    held,
    old,
    mobile,
    pres,
    perm,
    lam,
    scale,
    csum,
    vap,
    pack,
    inv_excess,
    pack_pres,
    pack_amount,
    cov_tiles,
    w_wide,
    order_hbm,
    pres_flat,
    perm_flat,
    labels,
    roots,
    sums,
    liquid,
    vapour,
    out_cell,
    found,
    order,
    block_ids,
    wilson,
    covolume,
    attraction,
    in_sem,
    old_sem,
    cell_sem,
    table_sem,
    order_sem,
):
    comps, layers, face = moles_hbm.shape
    strips = face // BLK
    groups = layers // SUB
    padded = layers + 2 * SUB
    inside = slice(SUB, SUB + layers)

    def lanes_of(k):
        return pl.ds(pl.multiple_of(k * BLK, BLK), BLK)

    def strip_of(k):
        return pl.ds(pl.multiple_of(k * layers, SUB), layers)

    def strip_in(source, target, sem, k):
        return pltpu.make_async_copy(
            source.at[:, :, lanes_of(k)], target.at[:, strip_of(k), :], sem.at[k]
        )

    cell_copies = [
        pltpu.make_async_copy(pres_hbm, pres_flat, cell_sem.at[0]),
        pltpu.make_async_copy(roots_hbm, roots, cell_sem.at[1]),
        pltpu.make_async_copy(labels_hbm, labels, cell_sem.at[2]),
        pltpu.make_async_copy(perm_hbm, perm_flat, cell_sem.at[3]),
    ]
    table_copies = [
        pltpu.make_async_copy(source, target, table_sem.at[n])
        for n, (source, target) in enumerate(
            (
                (attraction_hbm, attraction),
                (covolume_hbm, covolume),
                (wilson_hbm, wilson),
                (block_ids_hbm, block_ids),
            )
        )
    ]
    for copy in table_copies + cell_copies:
        copy.start()
    for k in range(strips):
        strip_in(moles_hbm, held, in_sem, k).start()

    zero_tile = jnp.zeros((SUB, BLK), jnp.float32)
    zero_strip = jnp.zeros((padded, BLK), jnp.float32)

    for ref in (pres, perm, lam):
        for k in (0, strips + 1):
            ref[k] = zero_strip
        for k in range(1, strips + 1):
            ref[k, 0:SUB] = zero_tile
            ref[k, SUB + layers : padded] = zero_tile

    def clear(i, carry):
        for k in (0, strips + 1):
            mobile[i, k * padded : (k + 1) * padded, :] = zero_strip
        for k in range(1, strips + 1):
            mobile[i, k * padded : k * padded + SUB, :] = zero_tile
            mobile[i, (k + 1) * padded - SUB : (k + 1) * padded, :] = zero_tile
        return carry

    lax.fori_loop(0, comps, clear, 0)
    for copy in table_copies:
        copy.wait()
    widen(w_wide, attraction, covolume, comps)
    for i in range(comps):
        cov_tiles[i] = jnp.full((SUB, BLK), covolume[i], jnp.float32)

    cols = comps * SUB

    for copy in cell_copies:
        copy.wait()
    for k in range(strips):
        pres[k + 1, inside, :] = pres_flat[:, k * BLK : (k + 1) * BLK]
        perm[k + 1, inside, :] = perm_flat[:, k * BLK : (k + 1) * BLK]

    def padded_of(k):
        return pl.ds(pl.multiple_of((k + 1) * padded + SUB, SUB), layers)

    own_count = counts[0]
    most = block_ids.shape[0]
    each = -(-most // strips)
    bits = strips.bit_length() - 1

    def sort_slots(k, front, back):
        for n in range(each):
            r = k * each + n
            block = block_ids[jnp.minimum(r, most - 1)]
            layer = lax.shift_right_logical(block, bits)
            live = r < own_count
            outer = jnp.logical_or(layer < 2, layer >= layers - 2)
            to_front = jnp.logical_and(live, outer)
            to_back = jnp.logical_and(live, jnp.logical_not(outer))
            order[jnp.where(to_front, front, jnp.where(to_back, back, most))] = block
            front = front + to_front.astype(jnp.int32)
            back = back - to_back.astype(jnp.int32)
        return front, back

    def single(k, carry):
        strip_in(moles_hbm, held, in_sem, k).wait()
        strip_in(old_hbm, old, old_sem, k).start()
        amount, b_sum, quad = mixture(
            lambda i, g: held[i, pl.ds(pl.multiple_of(k * layers + g * SUB, SUB), SUB), :],
            groups,
            comps,
            w_wide,
        )
        pressure = pres[k + 1, inside, :]
        inv_amount = recip(amount)
        big_a = pressure * quad * inv_amount * inv_amount
        big_b = pressure * b_sum * inv_amount
        is_vapour = roots[:, lanes_of(k)] == 1
        (z_factor,) = roots_of((big_a, big_b, is_vapour))
        rho = pressure * recip(z_factor)
        part = labels[:, lanes_of(k)].astype(jnp.float32)
        move = ((1.0 - part) * (1.0 - part) + 4.0 * part * part) * rho
        vap[k] = part
        scale[k] = rho
        csum[k] = amount * rho
        lam[k + 1, inside, :] = amount * move
        for i in range(comps):
            mobile[i, padded_of(k), :] = held[i, strip_of(k), :] * move
        return sort_slots(k, *carry)

    lax.fori_loop(0, strips, single, (jnp.int32(0), own_count - 1))
    order_copy = pltpu.make_async_copy(order, order_hbm, order_sem)
    order_copy.start()

    held_stride, mobile_stride, pack_stride = (ref.shape[1] for ref in (held, mobile, pack))
    held_rows = held.reshape(comps * held_stride, BLK)
    mobile_rows = mobile.reshape(comps * mobile_stride, BLK)
    pack_rows = pack.reshape(comps * pack_stride, BLK)
    batch = WIDE * SUB

    def field_at(k, layer):
        return pl.ds(k * layers + layer, comps, stride=held_stride)

    def mobile_at(k, layer):
        return pl.ds((k + 1) * padded + layer + SUB, comps, stride=mobile_stride)

    def gather(group, inner):
        for n in range(SUB):
            r = group * SUB + n
            k, layer = place(r, own_count, order, strips)
            pack_rows[pl.ds(r, comps, stride=pack_stride), :] = held_rows[field_at(k, layer), :]
            pack_pres[pl.ds(r, 1), :] = pres[k + 1, pl.ds(layer + SUB, 1), :]
        return inner

    def prepare(number, inner):
        slots = pl.ds(pl.multiple_of(number * batch, batch), batch)
        amount = pack[0, slots, :]
        for i in range(1, comps):
            amount = amount + pack[i, slots, :]
        pack_amount[slots, :] = amount
        inv_amount = recip(amount)
        log2_pres = jnp.log(pack_pres[slots, :]) * LOG2E
        for i in range(comps):
            pack[i, slots, :] = pack[i, slots, :] * inv_amount
            inv_excess[i, slots, :] = inverse_excess(wilson[i] * LOG2E - log2_pres)
        return inner

    batches = (own_count + batch - 1) // batch
    lax.fori_loop(0, batches * WIDE, gather, 0)
    lax.fori_loop(0, batches, prepare, 0)
    refs = (sums, liquid, vapour, out_cell, found)
    flash(0, refs, pack, inv_excess, pack_pres, pack_amount, cov_tiles, w_wide)
    scatter(0, own_count, order, refs, held, mobile, lam, csum, scale, vap)

    for k in range(strips):
        strip_in(old_hbm, old, old_sem, k).wait()
    old_rows = old.reshape(comps * old.shape[1], BLK)

    def edge_values(k, at, inner):
        here = slice(at, at + 1)
        pad_here = slice(SUB + at, SUB + at + 1)
        pad_inner = slice(SUB + inner, SUB + inner + 1)
        values = [None] * EDGE_ROWS
        values[EDGE_PRES] = pres[k + 1, pad_here, :]
        values[EDGE_PERM] = perm[k + 1, pad_here, :]
        values[EDGE_LAM] = lam[k + 1, pad_here, :]
        values[EDGE_CSUM] = csum[k, here, :]
        values[EDGE_OSUM] = jnp.sum(old_rows[field_at(k, at), :], 0, keepdims=True)
        values[EDGE_PRES2] = pres[k + 1, pad_inner, :]
        values[EDGE_PERM2] = perm[k + 1, pad_inner, :]
        values[EDGE_LAM2] = lam[k + 1, pad_inner, :]
        return [mobile_rows[mobile_at(k, at), :]] + values

    odd = lax.rem(lax.axis_index("dev"), 2) == 1
    for k in range(strips):
        lanes = slice(k * BLK, (k + 1) * BLK)
        tops = edge_values(k, 0, 1)
        lows = edge_values(k, layers - 1, layers - 2)
        row = 0
        for top, low in zip(tops, lows):
            rows = slice(row, row + top.shape[0])
            edge_a[rows, lanes] = jnp.where(odd, top, low)
            edge_b[rows, lanes] = jnp.where(odd, low, top)
            row = rows.stop
    order_copy.wait()


def flux_kernel(
    counts,
    order_hbm,
    held_in,
    mobile_in,
    lam_in,
    scale_in,
    csum_in,
    vap_in,
    old,
    pres,
    perm,
    pack,
    inv_excess,
    pack_pres,
    pack_amount,
    cov_tiles,
    w_wide,
    held,
    mobile,
    lam,
    scale,
    csum,
    vap,
    resid_hbm,
    step_hbm,
    vap_hbm,
    top_aux,
    low_aux,
    sums,
    liquid,
    vapour,
    out_cell,
    found,
    order,
    resid,
    first,
    row_sum,
    diag,
    weights,
    step,
    vap_flat,
    step_sem,
    vap_sem,
    order_sem,
    out_sem,
):
    comps = held.shape[0]
    strips, layers, _ = scale.shape
    groups = layers // SUB
    padded = layers + 2 * SUB

    def lanes_of(k):
        return pl.ds(pl.multiple_of(k * BLK, BLK), BLK)

    def strip_out(k):
        return pltpu.make_async_copy(resid.at[:, k], resid_hbm.at[:, :, lanes_of(k)], out_sem.at[k])

    order_copy = pltpu.make_async_copy(order_hbm, order, order_sem)
    order_copy.start()
    own_count = counts[0]
    batch = WIDE * SUB
    refs = (sums, liquid, vapour, out_cell, found)

    @pl.when(own_count <= batch)
    def _():
        order_copy.wait()

    def rest(number, carry):
        flash(number * batch, refs, pack, inv_excess, pack_pres, pack_amount, cov_tiles, w_wide)

        @pl.when(number == 1)
        def _():
            order_copy.wait()

        scatter(number * batch, own_count, order, refs, held, mobile, lam, csum, scale, vap)
        return carry

    lax.fori_loop(1, (own_count + batch - 1) // batch, rest, 0)
    for k in range(strips):
        vap_flat[:, k * BLK : (k + 1) * BLK] = vap[k]
    vap_copy = pltpu.make_async_copy(vap_flat, vap_hbm, vap_sem)
    vap_copy.start()
    zero_tile = jnp.zeros((SUB, BLK), jnp.float32)
    for k in range(strips + 2):
        for g in range(groups + 2):
            if k in (0, strips + 1) or g in (0, groups + 1):
                first[k, rows_of(g), :] = zero_tile

    lane_index = lax.broadcasted_iota(jnp.int32, (SUB, BLK), 1)
    is_last_lane = lane_index == BLK - 1
    is_first_lane = lane_index == 0

    def around(load, k, g, count):
        at = SUB * (g + 1)
        tiles = [load(k + n, slice(at, at + SUB)) for n in range(count + 2)]
        found = []
        for n in range(1, count + 1):
            here = tiles[n]
            up = load(k + n, slice(at - 1, at + SUB - 1))
            down = load(k + n, slice(at + 1, at + SUB + 1))
            left = pltpu.roll(jnp.where(is_last_lane, tiles[n - 1], here), 1, 1)
            right = pltpu.roll(jnp.where(is_first_lane, tiles[n + 1], here), BLK - 1, 1)
            found.append((here, (up, down, left, right)))
        return found

    def fluxes(number, carry):
        first_strip = number * TOGETHER
        for g in range(groups):
            rows = rows_of(g)
            states = []
            for k, pressures, perms, lams in zip(
                range(TOGETHER),
                *(
                    around(lambda s, r: ref[s, r, :], first_strip, g, TOGETHER)
                    for ref in (pres, perm, lam)
                ),
            ):
                (p_here, p_near), (k_here, k_near), (l_here, l_near) = pressures, perms, lams
                drives = []
                couplings = []
                for n in range(4):
                    transmiss = k_here * k_near[n] * recip(k_here + k_near[n])
                    drives.append((TIME_STEP * transmiss) * (p_here - p_near[n]))
                    couplings.append(transmiss * (l_here + l_near[n]))
                drive_sum = (drives[0] + drives[1]) + (drives[2] + drives[3])
                diagonal = TIME_STEP * (
                    (couplings[0] + couplings[1]) + (couplings[2] + couplings[3])
                ) + csum[first_strip + k, rows, :] * recip(p_here)
                inv_diag = recip(diagonal)
                diag[first_strip + k, rows, :] = diagonal
                gain = (STEP_SCALE * OFF_SCALE) * inv_diag
                for n in range(4):
                    weights[n, first_strip + k, rows, :] = couplings[n] * gain
                states.append((drives, drive_sum, inv_diag, scale[first_strip + k, rows, :]))
            row_totals = [zero_tile] * TOGETHER
            for i in range(comps):
                found = around(
                    lambda s, r: mobile[i, pl.ds(s * padded + r.start, SUB), :],
                    first_strip,
                    g,
                    TOGETHER,
                )
                for k, (m_here, m_near) in enumerate(found):
                    drives, drive_sum, _, content_scale = states[k]
                    strip = first_strip + k
                    flat_rows = pl.ds(pl.multiple_of(strip * layers + g * SUB, SUB), SUB)
                    value = held[i, flat_rows, :] * content_scale - old[i, flat_rows, :]
                    value = value + drive_sum * m_here
                    value = value + (drives[0] * m_near[0] + drives[1] * m_near[1])
                    value = value + (drives[2] * m_near[2] + drives[3] * m_near[3])
                    resid[i, strip, rows, :] = value
                    row_totals[k] = row_totals[k] + value
            for k in range(TOGETHER):
                row_sum[first_strip + k, rows, :] = row_totals[k]
                first[first_strip + k + 1, SUB * (g + 1) : SUB * (g + 2), :] = (
                    -row_totals[k] * states[k][2]
                )
        for k in range(TOGETHER):
            strip_out(first_strip + k).start()
        return carry

    lax.fori_loop(0, strips // TOGETHER, fluxes, 0)

    def steps(k, carry):
        for g in range(groups):
            rows = rows_of(g)
            ((here, near),) = around(lambda s, r: first[s, r, :], k, g, 1)
            step[rows, lanes_of(k)] = (
                STEP_SCALE * here
                + (weights[0, k, rows, :] * near[0] + weights[1, k, rows, :] * near[1])
                + (weights[2, k, rows, :] * near[2] + weights[3, k, rows, :] * near[3])
            )
        return carry

    lax.fori_loop(0, strips, steps, 0)
    step_copy = pltpu.make_async_copy(step, step_hbm, step_sem)
    step_copy.start()

    resid_rows = resid.reshape(comps * strips * layers, BLK)
    for aux, at, inner, toward, away in (
        (top_aux, 0, 1, 0, 1),
        (low_aux, layers - 1, layers - 2, 1, 0),
    ):
        for k in range(strips):
            lanes = slice(k * BLK, (k + 1) * BLK)
            here = slice(at, at + 1)
            behind = slice(inner, inner + 1)
            from_row = pl.ds(k * layers + at, comps, stride=strips * layers)
            aux[0:comps, lanes] = resid_rows[from_row, :]
            unscale = diag[k, here, :]
            values = [None] * AUX_ROWS
            values[AUX_IN] = weights[away, k, here, :] * unscale
            values[AUX_LEFT] = weights[2, k, here, :] * unscale
            values[AUX_RIGHT] = weights[3, k, here, :] * unscale
            values[AUX_FIRST] = first[k + 1, SUB + inner : SUB + inner + 1, :]
            values[AUX_GAIN] = weights[toward, k, behind, :]
            values[AUX_STEP] = step[behind, lanes]
            values[AUX_ROW] = row_sum[k, here, :]
            values[AUX_DIAG] = unscale
            for n, value in enumerate(values):
                aux[comps + n : comps + n + 1, lanes] = value
    vap_copy.wait()
    step_copy.wait()
    for k in range(strips):
        strip_out(k).wait()


def transmissibility(perm, perm_near):
    both = perm + perm_near
    return perm * perm_near / jnp.where(both == 0.0, 1.0, both)


def edge_kernel(
    edge_a,
    edge_b,
    top_aux,
    low_aux,
    in_even,
    in_odd,
    resid_in,
    step_in,
    resid_hbm,
    step_hbm,
    resid,
    step,
    sem,
):
    comps, layers, face = resid_hbm.shape
    odd = lax.rem(lax.axis_index("dev"), 2) == 1
    top_edge = jnp.where(odd, edge_a[...], edge_b[...])
    low_edge = jnp.where(odd, edge_b[...], edge_a[...])
    from_prev = jnp.where(odd, in_even[...], in_odd[...])
    from_next = jnp.where(odd, in_odd[...], in_even[...])
    copies = []
    for n, (edge, aux, other, at, inner) in enumerate(
        (
            (top_edge, top_aux, from_prev, 0, 1),
            (low_edge, low_aux, from_next, layers - 1, layers - 2),
        )
    ):

        def own(index):
            return edge[comps + index : comps + index + 1, :]

        def far(index):
            return other[comps + index : comps + index + 1, :]

        def near(index):
            return aux[comps + index : comps + index + 1, :]

        pres_far, perm_far, lam_far = far(EDGE_PRES), far(EDGE_PERM), far(EDGE_LAM)
        transmiss = transmissibility(own(EDGE_PERM), perm_far)
        drive = TIME_STEP * transmiss * (own(EDGE_PRES) - pres_far)
        lam_both = own(EDGE_LAM) + lam_far
        coupling = transmiss * lam_both
        row = near(AUX_ROW) + drive * lam_both
        diag = near(AUX_DIAG) + TIME_STEP * coupling
        first = -row / diag
        first_old = -near(AUX_ROW) / near(AUX_DIAG)
        row_far = far(EDGE_CSUM) - far(EDGE_OSUM) - drive * lam_both
        diag_far = coupling
        lane = lax.broadcasted_iota(jnp.int32, (1, face), 1)
        sides = [(far(EDGE_PRES2), far(EDGE_PERM2), far(EDGE_LAM2))]
        for shift, end in ((1, 0), (face - 1, face - 1)):
            pres_n, perm_n, lam_n = (pltpu.roll(x, shift, 1) for x in (pres_far, perm_far, lam_far))
            sides.append((pres_n, jnp.where(lane == end, 0.0, perm_n), lam_n))
        for pres_n, perm_n, lam_n in sides:
            joint = transmissibility(perm_far, perm_n) * (lam_far + lam_n)
            row_far = row_far + TIME_STEP * joint * (pres_far - pres_n)
            diag_far = diag_far + joint
        diag_far = TIME_STEP * diag_far + far(EDGE_CSUM) / jnp.where(pres_far == 0.0, 1.0, pres_far)
        first_far = -row_far / jnp.where(diag_far == 0.0, 1.0, diag_far)
        off = (
            (STEP_SCALE * OFF_SCALE) * coupling * first_far
            + near(AUX_IN) * near(AUX_FIRST)
            + near(AUX_LEFT) * pltpu.roll(first, 1, 1)
            + near(AUX_RIGHT) * pltpu.roll(first, face - 1, 1)
        )
        least = min(at, inner)
        step[n, at - least : at - least + 1, :] = STEP_SCALE * first + off / diag
        step[n, inner - least : inner - least + 1, :] = near(AUX_STEP) + near(AUX_GAIN) * (
            first - first_old
        )
        resid[n] = aux[0:comps, :] + drive * (edge[0:comps, :] + other[0:comps, :])
        for source, target in (
            (resid.at[n], resid_hbm.at[:, at, :]),
            (step.at[n, 0:2, :], step_hbm.at[least : least + 2, :]),
        ):
            copies.append(pltpu.make_async_copy(source, target, sem.at[len(copies)]))
            copies[-1].start()
    for copy in copies:
        copy.wait()


def on_device(
    moles,
    old_content,
    pressure,
    perm,
    labels,
    roots,
    counts,
    block_ids,
    wilson,
    attraction,
    covolume,
):
    comps, layers, face = moles.shape
    f32 = jnp.float32
    strips = face // BLK
    tables = (block_ids, wilson, covolume, attraction)
    rows_in = comps * SUB
    vmem = pl.BlockSpec(memory_space=pltpu.VMEM)
    hbm = pl.BlockSpec(memory_space=pltpu.HBM)
    padded = layers + 2 * SUB
    flat = pltpu.VMEM((layers, face), f32)
    flat_int = pltpu.VMEM((layers, face), jnp.int32)
    cell = pltpu.VMEM((strips, layers, BLK), f32)
    cell_pad = pltpu.VMEM((strips + 2, padded, BLK), f32)
    batch = WIDE * SUB
    slots = -(-block_ids.shape[0] // batch) * batch
    field = pltpu.VMEM((comps, odd_tiles(strips * layers), BLK), f32)
    field_pad = pltpu.VMEM((comps, odd_tiles((strips + 2) * padded), BLK), f32)
    packed = pltpu.VMEM((comps, odd_tiles(slots), BLK), f32)
    results = pltpu.VMEM((comps, batch, BLK), f32)
    flash_types = [pltpu.VMEM((rows_in, 2 * WIDE * BLK), f32), results, results]
    flash_types += [pltpu.VMEM((n, batch, BLK), f32) for n in (3, 5)]
    order_type = ((block_ids.shape[0] + BLK) // BLK * BLK, jnp.int32)
    edge_shape = pltpu.VMEM((EDGE_SPAN, face), f32)
    aux_shape = pltpu.VMEM((comps + AUX_ROWS, face), f32)
    field_shape = jax.ShapeDtypeStruct((comps, layers, face), f32)
    cell_shape = jax.ShapeDtypeStruct((layers, face), f32)
    field_out = pltpu.VMEM((comps, strips, layers, BLK), f32)
    changed = [field, field_pad, cell_pad, cell, cell, cell]
    held_types = [field, field, field_pad] + [cell_pad] * 3 + [cell] * 3
    slot_types = [packed, packed] + [pltpu.VMEM((slots, BLK), f32)] * 2
    slot_types += [pltpu.VMEM((comps, SUB, BLK), f32)]
    slot_types += [pltpu.VMEM((rows_in + 2 * SUB, 3 * rows_in), jnp.bfloat16)]
    smem = pl.BlockSpec(memory_space=pltpu.SMEM)
    edge_a, edge_b, *state, order = pl.pallas_call(
        cells_kernel,
        out_shape=[edge_shape, edge_shape]
        + held_types
        + slot_types
        + [pltpu.HBM((order_type[0],), order_type[1])],
        in_specs=[smem] + [hbm] * 10,
        out_specs=[vmem] * (2 + len(held_types) + len(slot_types)) + [hbm],
        scratch_shapes=[flat, flat, flat_int, flat_int]
        + flash_types
        + [pltpu.SMEM((order_type[0],), order_type[1])]
        + [pltpu.SMEM(table.shape, table.dtype) for table in tables[:-1]]
        + [pltpu.VMEM(attraction.shape, f32)]
        + [
            pltpu.SemaphoreType.DMA((strips,)),
            pltpu.SemaphoreType.DMA((strips,)),
            pltpu.SemaphoreType.DMA((4,)),
            pltpu.SemaphoreType.DMA((len(tables),)),
            pltpu.SemaphoreType.DMA(()),
        ],
        compiler_params=pltpu.CompilerParams(vmem_limit_bytes=CELLS_VMEM),
        name="cells",
    )(counts, *keep_in(pltpu.HBM, *tables, moles, old_content, pressure, perm, labels, roots))
    held, old, mobile, pres, perms, lam, scale, csum, vap, *slot_state = state
    count = lax.axis_size("dev")
    arrived = []
    for start, edge in ((0, edge_a), (1, edge_b)):
        pairs = [(i, i + 1) for i in range(start, count - 1, 2)]
        arrived.append(lax.ppermute(edge, "dev", pairs + [pair[::-1] for pair in pairs]))
    *_, residual, step, vapour, top_aux, low_aux = pl.pallas_call(
        flux_kernel,
        out_shape=changed + [field_shape, cell_shape, cell_shape, aux_shape, aux_shape],
        in_specs=[smem, hbm] + [vmem] * (len(changed) + 3 + len(slot_types)),
        out_specs=[vmem] * len(changed) + [hbm] * 3 + [vmem] * 2,
        input_output_aliases={2 + n: n for n in range(len(changed))},
        scratch_shapes=flash_types
        + [pltpu.SMEM((order_type[0],), order_type[1])]
        + [field_out, cell_pad, cell, cell]
        + [pltpu.VMEM((4, strips, layers, BLK), f32), flat, flat]
        + [pltpu.SemaphoreType.DMA(())] * 3
        + [pltpu.SemaphoreType.DMA((strips,))],
        compiler_params=pltpu.CompilerParams(vmem_limit_bytes=FLUX_VMEM),
        name="flux",
    )(
        counts,
        *keep_in(pltpu.HBM, order),
        *keep_in(pltpu.VMEM, held, mobile, lam, scale, csum, vap),
        *keep_in(pltpu.VMEM, old, pres, perms, *slot_state),
    )
    residual, step = pl.pallas_call(
        edge_kernel,
        out_shape=[field_shape, cell_shape],
        in_specs=[vmem] * 6 + [hbm] * 2,
        out_specs=[hbm] * 2,
        input_output_aliases={6: 0, 7: 1},
        scratch_shapes=[
            pltpu.VMEM((2, comps, face), f32),
            pltpu.VMEM((2, SUB, face), f32),
            pltpu.SemaphoreType.DMA((4,)),
        ],
        compiler_params=pltpu.CompilerParams(vmem_limit_bytes=16 * 1024 * 1024),
        name="edges",
    )(edge_a, edge_b, top_aux, low_aux, *arrived, residual, step)
    return (residual, step, vapour)


def solution(mesh):
    in_specs = (
        P(None, "dev", None),
        P(None, "dev", None),
        P("dev", None),
        P("dev", None),
        P("dev", None),
        P("dev", None),
        P("dev"),
        P("dev"),
        P(),
        P(),
        P(),
    )
    out_specs = (P(None, "dev", None), P("dev", None), P("dev", None))
    return jax.shard_map(
        on_device, mesh=mesh, in_specs=in_specs, out_specs=out_specs, check_vma=False
    )
```

```python
import math

import jax
import jax.numpy as jnp
from jax import lax
from jax.experimental import pallas as pl
from jax.experimental.pallas import tpu as pltpu
from jax.sharding import PartitionSpec as P

BLK = 128
SUB = 8
SS_ITERS = 3
RR_ITERS = 3
Z_ITERS = 5
WIDE = 8
LOG2E = math.log2(math.e)
CELLS_VMEM = 32 * 1024 * 1024
FLUX_VMEM = 32 * 1024 * 1024

SQRT_TWO = math.sqrt(2.0)
TIME_STEP = 0.5
RELAX = 0.7
STEP_SCALE = 10.0
OFF_SCALE = RELAX * TIME_STEP

EDGE_PRES, EDGE_PERM, EDGE_LAM, EDGE_CSUM, EDGE_OSUM = range(5)
EDGE_PRES2, EDGE_PERM2, EDGE_LAM2 = range(5, 8)
EDGE_ROWS = 8
EDGE_SPAN = 32
AUX_IN, AUX_LEFT, AUX_RIGHT, AUX_FIRST, AUX_GAIN, AUX_STEP, AUX_ROW, AUX_DIAG = range(8)
AUX_ROWS = 8


def keep_in(space, *arrays):
    return [pltpu.with_memory_space_constraint(x, space) for x in arrays]


def recip(value):
    return pltpu.reciprocal(value, approx=True)


def odd_tiles(rows):
    return rows + SUB if (rows // SUB) % 2 == 0 else rows


def split_halves(value):
    high = value.astype(jnp.bfloat16)
    low = (value - high.astype(jnp.float32)).astype(jnp.bfloat16)
    return high, low


def widen(wide, attraction, covolume, comps):
    cols = 3 * comps * SUB
    span = 2 * SUB

    def column(rows):
        at = lax.broadcasted_iota(jnp.int32, (rows, cols), 1)
        pair = at // (3 * span)
        within = at - pair * (3 * span)
        part = within // span
        within = within - part * span
        return 2 * pair + within // SUB, part, lax.rem(within, SUB)

    comp, _, _ = column(comps)
    spread = jnp.where(comp == lax.broadcasted_iota(jnp.int32, (comps, cols), 0), 1.0, 0.0)
    table = attraction[...]
    coefficients = 0.5 * (
        lax.dot_general(table, spread, (((1,), (0,)), ((), ())), precision=lax.Precision.HIGHEST)
        + lax.dot_general(table, spread, (((0,), (0,)), ((), ())), precision=lax.Precision.HIGHEST)
    )
    comp, part, sub = column(SUB)
    diagonal = sub == lax.broadcasted_iota(jnp.int32, (SUB, cols), 0)
    zero = jnp.zeros((SUB, cols), jnp.float32)
    of_cov = zero
    for j in range(comps):
        of_cov = jnp.where(comp == j, covolume[j], of_cov)
    blocks = [coefficients[i : i + 1, :] for i in range(comps)] + [of_cov, zero + 1.0]
    for pair in range(len(blocks) // 2):
        rows = []
        for i in (2 * pair, 2 * pair + 1):
            value = jnp.where(diagonal, blocks[i], zero)
            high = value.astype(jnp.bfloat16).astype(jnp.float32)
            rows.append(jnp.where(part == 1, value - high, high))
        wide[span * pair : span * (pair + 1), :] = jnp.concatenate(rows, 0).astype(jnp.bfloat16)


def rows_of(g):
    return slice(g * SUB, (g + 1) * SUB)


def cubic(big_a, big_b, vapour_flag):
    two_b = 2.0 * big_b
    two_b_square = two_b * big_b
    least = two_b + 0.01
    most = big_b + 2.0
    if vapour_flag is True:
        start, shift, factor = 1.0 + big_b, big_b + 0.5, -0.5 * big_a
    elif vapour_flag is False:
        start, shift, factor = 3.0 * big_b, big_b, 0.5 * recip(big_a)
    else:
        start = jnp.where(vapour_flag, 1.0 + big_b, 3.0 * big_b)
        shift = jnp.where(vapour_flag, big_b + 0.5, big_b)
        factor = jnp.where(vapour_flag, -0.5 * big_a, -0.5 * recip(big_a))
        base = jnp.where(vapour_flag, two_b, 1.0 + two_b)

    def step(w):
        spread = w * w - two_b_square
        if vapour_flag is True:
            part = factor * (w - two_b) * recip(spread)
        elif vapour_flag is False:
            part = spread * ((1.0 + two_b) - w) * factor
        else:
            part = factor * (w - base) * jnp.where(vapour_flag, recip(spread), spread)
        return jnp.minimum(jnp.maximum((0.5 * w + shift) + part, least), most)

    return start, step


def roots_of(*equations):
    steps = [cubic(*equation) for equation in equations]
    found = [start for start, _ in steps]
    for _ in range(Z_ITERS):
        found = [step(w) for w, (_, step) in zip(found, steps)]
    return [w - big_b for w, (_, big_b, _) in zip(found, equations)]


def cells_kernel(
    counts,
    block_ids_hbm,
    wilson_hbm,
    covolume_hbm,
    attraction_hbm,
    moles_hbm,
    old_hbm,
    pres_hbm,
    perm_hbm,
    labels_hbm,
    roots_hbm,
    edge_a,
    edge_b,
    held,
    old,
    mobile,
    pres,
    perm,
    lam,
    scale,
    csum,
    vap,
    pres_flat,
    perm_flat,
    labels,
    roots,
    w_wide,
    sums,
    pack,
    pack_pres,
    inv_excess,
    liquid,
    vapour,
    out_cell,
    found,
    mix,
    block_ids,
    wilson,
    covolume,
    attraction,
    in_sem,
    old_sem,
    cell_sem,
    table_sem,
):
    comps, layers, face = moles_hbm.shape
    strips = face // BLK
    groups = layers // SUB
    padded = layers + 2 * SUB
    inside = slice(SUB, SUB + layers)

    def lanes_of(k):
        return pl.ds(pl.multiple_of(k * BLK, BLK), BLK)

    def strip_of(k):
        return pl.ds(pl.multiple_of(k * layers, SUB), layers)

    def strip_in(source, target, sem, k):
        return pltpu.make_async_copy(
            source.at[:, :, lanes_of(k)], target.at[:, strip_of(k), :], sem.at[k]
        )

    cell_copies = [
        pltpu.make_async_copy(pres_hbm, pres_flat, cell_sem.at[0]),
        pltpu.make_async_copy(roots_hbm, roots, cell_sem.at[1]),
        pltpu.make_async_copy(labels_hbm, labels, cell_sem.at[2]),
        pltpu.make_async_copy(perm_hbm, perm_flat, cell_sem.at[3]),
    ]
    table_copies = [
        pltpu.make_async_copy(source, target, table_sem.at[n])
        for n, (source, target) in enumerate(
            (
                (attraction_hbm, attraction),
                (covolume_hbm, covolume),
                (wilson_hbm, wilson),
                (block_ids_hbm, block_ids),
            )
        )
    ]
    for copy in table_copies + cell_copies:
        copy.start()
    for k in range(strips):
        strip_in(moles_hbm, held, in_sem, k).start()

    zero_tile = jnp.zeros((SUB, BLK), jnp.float32)
    zero_strip = jnp.zeros((padded, BLK), jnp.float32)

    for ref in (pres, perm, lam):
        for k in (0, strips + 1):
            ref[k] = zero_strip
        for k in range(1, strips + 1):
            ref[k, 0:SUB] = zero_tile
            ref[k, SUB + layers : padded] = zero_tile

    def clear(i, carry):
        for k in (0, strips + 1):
            mobile[i, k * padded : (k + 1) * padded, :] = zero_strip
        for k in range(1, strips + 1):
            mobile[i, k * padded : k * padded + SUB, :] = zero_tile
            mobile[i, (k + 1) * padded - SUB : (k + 1) * padded, :] = zero_tile
        return carry

    lax.fori_loop(0, comps, clear, 0)
    for copy in table_copies:
        copy.wait()
    widen(w_wide, attraction, covolume, comps)

    cols = comps * SUB

    def mixture(tile, count, keep=None, between=None):
        parts = ([], [], [])
        for g in range(0, count, 2):
            if between is not None:
                between()
            halves = []
            for j in range(comps // 2):
                both = [
                    jnp.concatenate([tile(2 * j, at), tile(2 * j + 1, at)], 0) for at in (g, g + 1)
                ]
                high, low = split_halves(jnp.concatenate(both, 1))
                halves += [high, high, low]
            result = jnp.dot(
                w_wide[...],
                jnp.concatenate(halves, 0),
                preferred_element_type=jnp.float32,
            )
            if keep is not None:
                sums[:, (keep + g) * BLK : (keep + g + 2) * BLK] = result[0:cols]
            for n, at in enumerate((g, g + 1)):
                lanes = slice(n * BLK, (n + 1) * BLK)
                quad = tile(0, at) * result[0:SUB, lanes]
                for i in range(1, comps):
                    quad = quad + tile(i, at) * result[i * SUB : (i + 1) * SUB, lanes]
                parts[0].append(result[cols + SUB : cols + 2 * SUB, lanes])
                parts[1].append(result[cols : cols + SUB, lanes])
                parts[2].append(quad)
        return [jnp.concatenate(part, 0) for part in parts]

    def total(at, start, count):
        rows = slice(at * SUB, (at + 1) * SUB)
        return jnp.concatenate(
            [sums[rows, g * BLK : (g + 1) * BLK] for g in range(start, start + count)], 0
        )

    for copy in cell_copies:
        copy.wait()
    for k in range(strips):
        pres[k + 1, inside, :] = pres_flat[:, k * BLK : (k + 1) * BLK]
        perm[k + 1, inside, :] = perm_flat[:, k * BLK : (k + 1) * BLK]

    def padded_of(k):
        return pl.ds(pl.multiple_of((k + 1) * padded + SUB, SUB), layers)

    def products(k, between=None):
        strip_in(moles_hbm, held, in_sem, k).wait()
        strip_in(old_hbm, old, old_sem, k).start()
        return mixture(
            lambda i, g: held[i, pl.ds(pl.multiple_of(k * layers + g * SUB, SUB), SUB), :],
            groups,
            between=between,
        )

    class Roots:
        def __init__(self, k, amount, b_sum, quad):
            self.pressure = pres[k + 1, inside, :]
            self.amount = amount
            inv_amount = recip(amount)
            big_a = self.pressure * quad * inv_amount * inv_amount
            self.big_b = self.pressure * b_sum * inv_amount
            self.found, self.step = cubic(big_a, self.big_b, roots[:, lanes_of(k)] == 1)
            self.steps = 0

        def advance(self):
            if self.steps < Z_ITERS:
                self.found = self.step(self.found)
                self.steps += 1

    def fields(k, it):
        while it.steps < Z_ITERS:
            it.advance()
        rho = it.pressure * recip(it.found - it.big_b)
        part = labels[:, lanes_of(k)].astype(jnp.float32)
        move = ((1.0 - part) * (1.0 - part) + 4.0 * part * part) * rho
        vap[k] = part
        scale[k] = rho
        csum[k] = it.amount * rho
        lam[k + 1, inside, :] = it.amount * move
        for i in range(comps):
            mobile[i, padded_of(k), :] = held[i, strip_of(k), :] * move

    def keep_mix(values):
        for n, value in enumerate(values):
            mix[n] = value

    def single(k, carry):
        it = Roots(k - 1, *(mix[n] for n in range(3)))
        now = products(k, it.advance)
        fields(k - 1, it)
        keep_mix(now)
        return carry

    keep_mix(products(0))
    lax.fori_loop(1, strips, single, 0)
    fields(strips - 1, Roots(strips - 1, *(mix[n] for n in range(3))))

    batch = WIDE * SUB
    own_count = counts[0]
    held_stride, mobile_stride, pack_stride = (ref.shape[1] for ref in (held, mobile, pack))
    held_rows = held.reshape(comps * held_stride, BLK)
    mobile_rows = mobile.reshape(comps * mobile_stride, BLK)
    pack_rows = pack.reshape(comps * pack_stride, BLK)
    liquid_rows = liquid.reshape(comps * pack_stride, BLK)
    vapour_rows = vapour.reshape(comps * pack_stride, BLK)
    bits = strips.bit_length() - 1

    def place(slot):
        block = block_ids[jnp.minimum(slot, own_count - 1)]
        layer = lax.shift_right_logical(block, bits)
        return block - lax.shift_left(layer, bits), layer

    def field_at(k, layer):
        return pl.ds(k * layers + layer, comps, stride=held_stride)

    def mobile_at(k, layer):
        return pl.ds((k + 1) * padded + layer + SUB, comps, stride=mobile_stride)

    def flash(number, carry):
        base = number * batch

        def gather(group, inner):
            for n in range(SUB):
                r = group * SUB + n
                k, layer = place(base + r)
                pack_rows[pl.ds(r, comps, stride=pack_stride), :] = held_rows[field_at(k, layer), :]
                pack_pres[pl.ds(r, 1), :] = pres[k + 1, pl.ds(layer + SUB, 1), :]
            return inner

        lax.fori_loop(0, WIDE, gather, 0)
        slots = slice(0, batch)
        pressure = pack_pres[...]
        amount = pack[0, slots, :]
        for i in range(1, comps):
            amount = amount + pack[i, slots, :]
        inv_amount = recip(amount)
        for i in range(comps):
            pack[i, slots, :] = pack[i, slots, :] * inv_amount

        def keep_k(i, log2_k):
            inv_excess[i, slots, :] = recip(jnp.exp2(log2_k) - 1.0)

        log2_pres = jnp.log(pressure) * LOG2E
        for i in range(comps):
            keep_k(i, wilson[i] * LOG2E - log2_pres)

        def newton(_, part):
            value = jnp.zeros((batch, BLK), jnp.float32)
            slope = jnp.full((batch, BLK), 0.05, jnp.float32)
            for i in range(comps):
                ratio = recip(inv_excess[i, slots, :] + part)
                term = pack[i, slots, :] * ratio
                value = value + term
                slope = slope + term * ratio
            return jnp.minimum(jnp.maximum(part + value * recip(slope), 0.0), 1.0)

        def sweep(number_of_sweep, inner):
            half = jnp.full((batch, BLK), 0.5, jnp.float32)
            part = lax.fori_loop(0, RR_ITERS, newton, half)
            for i in range(comps):
                fraction = pack[i, slots, :]
                term = fraction * recip(inv_excess[i, slots, :] + part)
                liq = fraction - part * term
                liquid[i, slots, :] = liq
                vapour[i, slots, :] = liq + term
            phases = []
            equations = []
            for n, (ref, flag) in enumerate(((liquid, False), (vapour, True))):
                whole, b_sum, quad = mixture(lambda i, g: ref[i, rows_of(g), :], WIDE, n * WIDE)
                inv_whole = recip(whole)
                b_mix = b_sum * inv_whole
                a_mix = quad * inv_whole * inv_whole
                big_b = pressure * b_mix
                equations.append((pressure * a_mix, big_b, flag))
                phases.append((quad, whole, inv_whole, a_mix, b_mix, big_b))
            factors = roots_of(*equations)
            found[0] = part
            for n in range(2):
                found[1 + n] = factors[n]
                found[3 + n] = phases[n][2]

            @pl.when(number_of_sweep + 1 < SS_ITERS)
            def _():
                parts = []
                for (quad, whole, _, a_mix, b_mix, big_b), z_factor in zip(phases, factors):
                    log_arg = (z_factor + (1.0 + SQRT_TWO) * big_b) * recip(
                        z_factor + (1.0 - SQRT_TWO) * big_b
                    )
                    inv_b = recip(b_mix)
                    depart = a_mix * inv_b * (1.0 / (2.0 * SQRT_TWO)) * jnp.log(log_arg)
                    of_cov = (LOG2E * inv_b) * (z_factor - 1.0 + depart)
                    of_sum = (2.0 * LOG2E) * depart * whole * recip(quad)
                    parts.append((of_cov, LOG2E * jnp.log(z_factor - big_b), of_sum))
                cov_gap = parts[0][0] - parts[1][0]
                log_gap = parts[0][1] - parts[1][1]
                for i in range(comps):
                    log2_k = (covolume[i] * cov_gap - log_gap) - (
                        parts[0][2] * total(i, 0, WIDE) - parts[1][2] * total(i, WIDE, WIDE)
                    )
                    keep_k(i, jnp.minimum(jnp.maximum(log2_k, -3.0 * LOG2E), 3.0 * LOG2E))
            return inner

        lax.fori_loop(0, SS_ITERS, sweep, 0)
        part = found[0]
        rho_liq = amount * pressure * recip(found[1])
        rho_vap = amount * pressure * recip(found[2])
        rest = 1.0 - part
        move_liq = rest * rest * rho_liq
        move_vap = 4.0 * part * part * rho_vap
        hold_liq = rest * rho_liq
        hold_vap = part * rho_vap
        out_cell[0] = part
        out_cell[1] = move_liq + move_vap
        out_cell[2] = hold_liq + hold_vap
        inv_liq, inv_vap = found[3], found[4]
        move_liq = move_liq * inv_liq
        move_vap = move_vap * inv_vap
        hold_liq = hold_liq * inv_liq
        hold_vap = hold_vap * inv_vap
        for i in range(comps):
            liq, gas = liquid[i, slots, :], vapour[i, slots, :]
            liquid[i, slots, :] = move_liq * liq + move_vap * gas
            vapour[i, slots, :] = hold_liq * liq + hold_vap * gas
        one_row = jnp.ones((1, BLK), jnp.float32)

        def scatter(group, inner):
            for n in range(SUB):
                r = group * SUB + n
                k, layer = place(base + r)
                of = pl.ds(r, comps, stride=pack_stride)
                mobile_rows[mobile_at(k, layer), :] = liquid_rows[of, :]
                held_rows[field_at(k, layer), :] = vapour_rows[of, :]
                one = pl.ds(r, 1)
                row = pl.ds(layer, 1)
                vap[k, row, :] = out_cell[0, one, :]
                lam[k + 1, pl.ds(layer + SUB, 1), :] = out_cell[1, one, :]
                csum[k, row, :] = out_cell[2, one, :]
                scale[k, row, :] = one_row
            return inner

        lax.fori_loop(0, WIDE, scatter, 0)
        return carry

    lax.fori_loop(0, (own_count + batch - 1) // batch, flash, 0)
    for k in range(strips):
        strip_in(old_hbm, old, old_sem, k).wait()
    old_rows = old.reshape(comps * old.shape[1], BLK)

    def edge_values(k, at, inner):
        here = slice(at, at + 1)
        pad_here = slice(SUB + at, SUB + at + 1)
        pad_inner = slice(SUB + inner, SUB + inner + 1)
        values = [None] * EDGE_ROWS
        values[EDGE_PRES] = pres[k + 1, pad_here, :]
        values[EDGE_PERM] = perm[k + 1, pad_here, :]
        values[EDGE_LAM] = lam[k + 1, pad_here, :]
        values[EDGE_CSUM] = csum[k, here, :]
        values[EDGE_OSUM] = jnp.sum(old_rows[field_at(k, at), :], 0, keepdims=True)
        values[EDGE_PRES2] = pres[k + 1, pad_inner, :]
        values[EDGE_PERM2] = perm[k + 1, pad_inner, :]
        values[EDGE_LAM2] = lam[k + 1, pad_inner, :]
        return [mobile_rows[mobile_at(k, at), :]] + values

    odd = lax.rem(lax.axis_index("dev"), 2) == 1
    for k in range(strips):
        lanes = slice(k * BLK, (k + 1) * BLK)
        tops = edge_values(k, 0, 1)
        lows = edge_values(k, layers - 1, layers - 2)
        row = 0
        for top, low in zip(tops, lows):
            rows = slice(row, row + top.shape[0])
            edge_a[rows, lanes] = jnp.where(odd, top, low)
            edge_b[rows, lanes] = jnp.where(odd, low, top)
            row = rows.stop


def flux_kernel(
    held,
    old,
    mobile,
    pres,
    perm,
    lam,
    scale,
    csum,
    vap,
    resid_hbm,
    step_hbm,
    vap_hbm,
    top_aux,
    low_aux,
    resid,
    first,
    row_sum,
    diag,
    weights,
    step,
    vap_flat,
    step_sem,
    vap_sem,
    out_sem,
):
    comps = held.shape[0]
    strips, layers, _ = scale.shape
    groups = layers // SUB
    padded = layers + 2 * SUB

    def lanes_of(k):
        return pl.ds(pl.multiple_of(k * BLK, BLK), BLK)

    def strip_out(k):
        return pltpu.make_async_copy(resid.at[:, k], resid_hbm.at[:, :, lanes_of(k)], out_sem.at[k])

    for k in range(strips):
        vap_flat[:, k * BLK : (k + 1) * BLK] = vap[k]
    vap_copy = pltpu.make_async_copy(vap_flat, vap_hbm, vap_sem)
    vap_copy.start()
    zero_tile = jnp.zeros((SUB, BLK), jnp.float32)
    for k in range(strips + 2):
        for g in range(groups + 2):
            if k in (0, strips + 1) or g in (0, groups + 1):
                first[k, rows_of(g), :] = zero_tile

    lane_index = lax.broadcasted_iota(jnp.int32, (SUB, BLK), 1)
    is_last_lane = lane_index == BLK - 1
    is_first_lane = lane_index == 0

    def around(load, k, g):
        at = SUB * (g + 1)
        here = load(k + 1, slice(at, at + SUB))
        up = load(k + 1, slice(at - 1, at + SUB - 1))
        down = load(k + 1, slice(at + 1, at + SUB + 1))
        before = load(k, slice(at, at + SUB))
        after = load(k + 2, slice(at, at + SUB))
        left = pltpu.roll(jnp.where(is_last_lane, before, here), 1, 1)
        right = pltpu.roll(jnp.where(is_first_lane, after, here), BLK - 1, 1)
        return here, (up, down, left, right)

    def fluxes(k, carry):
        for g in range(groups):
            rows = rows_of(g)
            p_here, p_near = around(lambda s, r: pres[s, r, :], k, g)
            k_here, k_near = around(lambda s, r: perm[s, r, :], k, g)
            l_here, l_near = around(lambda s, r: lam[s, r, :], k, g)
            drives = []
            couplings = []
            for n in range(4):
                transmiss = k_here * k_near[n] * recip(k_here + k_near[n])
                drives.append((TIME_STEP * transmiss) * (p_here - p_near[n]))
                couplings.append(transmiss * (l_here + l_near[n]))
            drive_sum = (drives[0] + drives[1]) + (drives[2] + drives[3])
            content_scale = scale[k, rows, :]
            flat_rows = pl.ds(pl.multiple_of(k * layers + g * SUB, SUB), SUB)
            row_total = zero_tile
            for i in range(comps):
                m_here, m_near = around(
                    lambda s, r, i=i: mobile[i, pl.ds(s * padded + r.start, SUB), :], k, g
                )
                value = held[i, flat_rows, :] * content_scale - old[i, flat_rows, :]
                value = value + drive_sum * m_here
                value = value + (drives[0] * m_near[0] + drives[1] * m_near[1])
                value = value + (drives[2] * m_near[2] + drives[3] * m_near[3])
                resid[i, k, rows, :] = value
                row_total = row_total + value
            diagonal = TIME_STEP * (
                (couplings[0] + couplings[1]) + (couplings[2] + couplings[3])
            ) + csum[k, rows, :] * recip(p_here)
            inv_diag = recip(diagonal)
            row_sum[k, rows, :] = row_total
            diag[k, rows, :] = diagonal
            first[k + 1, SUB * (g + 1) : SUB * (g + 2), :] = -row_total * inv_diag
            gain = (STEP_SCALE * OFF_SCALE) * inv_diag
            for n in range(4):
                weights[n, k, rows, :] = couplings[n] * gain
        strip_out(k).start()
        return carry

    lax.fori_loop(0, strips, fluxes, 0)

    def steps(k, carry):
        for g in range(groups):
            rows = rows_of(g)
            here, near = around(lambda s, r: first[s, r, :], k, g)
            step[rows, lanes_of(k)] = (
                STEP_SCALE * here
                + (weights[0, k, rows, :] * near[0] + weights[1, k, rows, :] * near[1])
                + (weights[2, k, rows, :] * near[2] + weights[3, k, rows, :] * near[3])
            )
        return carry

    lax.fori_loop(0, strips, steps, 0)
    step_copy = pltpu.make_async_copy(step, step_hbm, step_sem)
    step_copy.start()

    resid_rows = resid.reshape(comps * strips * layers, BLK)
    for aux, at, inner, toward, away in (
        (top_aux, 0, 1, 0, 1),
        (low_aux, layers - 1, layers - 2, 1, 0),
    ):
        for k in range(strips):
            lanes = slice(k * BLK, (k + 1) * BLK)
            here = slice(at, at + 1)
            behind = slice(inner, inner + 1)
            from_row = pl.ds(k * layers + at, comps, stride=strips * layers)
            aux[0:comps, lanes] = resid_rows[from_row, :]
            unscale = diag[k, here, :]
            values = [None] * AUX_ROWS
            values[AUX_IN] = weights[away, k, here, :] * unscale
            values[AUX_LEFT] = weights[2, k, here, :] * unscale
            values[AUX_RIGHT] = weights[3, k, here, :] * unscale
            values[AUX_FIRST] = first[k + 1, SUB + inner : SUB + inner + 1, :]
            values[AUX_GAIN] = weights[toward, k, behind, :]
            values[AUX_STEP] = step[behind, lanes]
            values[AUX_ROW] = row_sum[k, here, :]
            values[AUX_DIAG] = unscale
            for n, value in enumerate(values):
                aux[comps + n : comps + n + 1, lanes] = value
    vap_copy.wait()
    step_copy.wait()
    for k in range(strips):
        strip_out(k).wait()


def transmissibility(perm, perm_near):
    both = perm + perm_near
    return perm * perm_near / jnp.where(both == 0.0, 1.0, both)


def edge_kernel(
    edge_a,
    edge_b,
    top_aux,
    low_aux,
    in_even,
    in_odd,
    resid_in,
    step_in,
    resid_hbm,
    step_hbm,
    resid,
    step,
    sem,
):
    comps, layers, face = resid_hbm.shape
    odd = lax.rem(lax.axis_index("dev"), 2) == 1
    top_edge = jnp.where(odd, edge_a[...], edge_b[...])
    low_edge = jnp.where(odd, edge_b[...], edge_a[...])
    from_prev = jnp.where(odd, in_even[...], in_odd[...])
    from_next = jnp.where(odd, in_odd[...], in_even[...])
    copies = []
    for n, (edge, aux, other, at, inner) in enumerate(
        (
            (top_edge, top_aux, from_prev, 0, 1),
            (low_edge, low_aux, from_next, layers - 1, layers - 2),
        )
    ):

        def own(index):
            return edge[comps + index : comps + index + 1, :]

        def far(index):
            return other[comps + index : comps + index + 1, :]

        def near(index):
            return aux[comps + index : comps + index + 1, :]

        pres_far, perm_far, lam_far = far(EDGE_PRES), far(EDGE_PERM), far(EDGE_LAM)
        transmiss = transmissibility(own(EDGE_PERM), perm_far)
        drive = TIME_STEP * transmiss * (own(EDGE_PRES) - pres_far)
        lam_both = own(EDGE_LAM) + lam_far
        coupling = transmiss * lam_both
        row = near(AUX_ROW) + drive * lam_both
        diag = near(AUX_DIAG) + TIME_STEP * coupling
        first = -row / diag
        first_old = -near(AUX_ROW) / near(AUX_DIAG)
        row_far = far(EDGE_CSUM) - far(EDGE_OSUM) - drive * lam_both
        diag_far = coupling
        lane = lax.broadcasted_iota(jnp.int32, (1, face), 1)
        sides = [(far(EDGE_PRES2), far(EDGE_PERM2), far(EDGE_LAM2))]
        for shift, end in ((1, 0), (face - 1, face - 1)):
            pres_n, perm_n, lam_n = (pltpu.roll(x, shift, 1) for x in (pres_far, perm_far, lam_far))
            sides.append((pres_n, jnp.where(lane == end, 0.0, perm_n), lam_n))
        for pres_n, perm_n, lam_n in sides:
            joint = transmissibility(perm_far, perm_n) * (lam_far + lam_n)
            row_far = row_far + TIME_STEP * joint * (pres_far - pres_n)
            diag_far = diag_far + joint
        diag_far = TIME_STEP * diag_far + far(EDGE_CSUM) / jnp.where(pres_far == 0.0, 1.0, pres_far)
        first_far = -row_far / jnp.where(diag_far == 0.0, 1.0, diag_far)
        off = (
            (STEP_SCALE * OFF_SCALE) * coupling * first_far
            + near(AUX_IN) * near(AUX_FIRST)
            + near(AUX_LEFT) * pltpu.roll(first, 1, 1)
            + near(AUX_RIGHT) * pltpu.roll(first, face - 1, 1)
        )
        least = min(at, inner)
        step[n, at - least : at - least + 1, :] = STEP_SCALE * first + off / diag
        step[n, inner - least : inner - least + 1, :] = near(AUX_STEP) + near(AUX_GAIN) * (
            first - first_old
        )
        resid[n] = aux[0:comps, :] + drive * (edge[0:comps, :] + other[0:comps, :])
        for source, target in (
            (resid.at[n], resid_hbm.at[:, at, :]),
            (step.at[n, 0:2, :], step_hbm.at[least : least + 2, :]),
        ):
            copies.append(pltpu.make_async_copy(source, target, sem.at[len(copies)]))
            copies[-1].start()
    for copy in copies:
        copy.wait()


def on_device(
    moles,
    old_content,
    pressure,
    perm,
    labels,
    roots,
    counts,
    block_ids,
    wilson,
    attraction,
    covolume,
):
    comps, layers, face = moles.shape
    f32 = jnp.float32
    strips = face // BLK
    tables = (block_ids, wilson, covolume, attraction)
    rows_in = comps * SUB
    vmem = pl.BlockSpec(memory_space=pltpu.VMEM)
    hbm = pl.BlockSpec(memory_space=pltpu.HBM)
    padded = layers + 2 * SUB
    flat = pltpu.VMEM((layers, face), f32)
    flat_int = pltpu.VMEM((layers, face), jnp.int32)
    cell = pltpu.VMEM((strips, layers, BLK), f32)
    cell_pad = pltpu.VMEM((strips + 2, padded, BLK), f32)
    field = pltpu.VMEM((comps, odd_tiles(strips * layers), BLK), f32)
    field_pad = pltpu.VMEM((comps, odd_tiles((strips + 2) * padded), BLK), f32)
    packed = pltpu.VMEM((comps, odd_tiles(WIDE * SUB), BLK), f32)
    edge_shape = pltpu.VMEM((EDGE_SPAN, face), f32)
    aux_shape = pltpu.VMEM((comps + AUX_ROWS, face), f32)
    field_shape = jax.ShapeDtypeStruct((comps, layers, face), f32)
    cell_shape = jax.ShapeDtypeStruct((layers, face), f32)
    field_out = pltpu.VMEM((comps, strips, layers, BLK), f32)
    held_types = [field, field, field_pad] + [cell_pad] * 3 + [cell] * 3
    edge_a, edge_b, *state = pl.pallas_call(
        cells_kernel,
        out_shape=[edge_shape, edge_shape]
        + held_types,
        in_specs=[pl.BlockSpec(memory_space=pltpu.SMEM)] + [hbm] * 10,
        out_specs=[vmem] * (2 + len(held_types)),
        scratch_shapes=[flat, flat, flat_int, flat_int]
        + [pltpu.VMEM((rows_in + 2 * SUB, 3 * rows_in), jnp.bfloat16)]
        + [pltpu.VMEM((rows_in, 2 * WIDE * BLK), f32)]
        + [packed, pltpu.VMEM((WIDE * SUB, BLK), f32)]
        + [packed] * 3
        + [pltpu.VMEM((3, WIDE * SUB, BLK), f32), pltpu.VMEM((5, WIDE * SUB, BLK), f32)]
        + [pltpu.VMEM((3, layers, BLK), f32)]
        + [pltpu.SMEM(table.shape, table.dtype) for table in tables[:-1]]
        + [pltpu.VMEM(attraction.shape, f32)]
        + [
            pltpu.SemaphoreType.DMA((strips,)),
            pltpu.SemaphoreType.DMA((strips,)),
            pltpu.SemaphoreType.DMA((4,)),
            pltpu.SemaphoreType.DMA((len(tables),)),
        ],
        compiler_params=pltpu.CompilerParams(vmem_limit_bytes=CELLS_VMEM),
        name="cells",
    )(counts, *keep_in(pltpu.HBM, *tables, moles, old_content, pressure, perm, labels, roots))
    count = lax.axis_size("dev")
    arrived = []
    for start, edge in ((0, edge_a), (1, edge_b)):
        pairs = [(i, i + 1) for i in range(start, count - 1, 2)]
        arrived.append(lax.ppermute(edge, "dev", pairs + [pair[::-1] for pair in pairs]))
    residual, step, vapour, top_aux, low_aux = pl.pallas_call(
        flux_kernel,
        out_shape=[field_shape, cell_shape, cell_shape, aux_shape, aux_shape],
        in_specs=[vmem] * len(state),
        out_specs=[hbm] * 3 + [vmem] * 2,
        scratch_shapes=[field_out, cell_pad, cell, cell]
        + [pltpu.VMEM((4, strips, layers, BLK), f32), flat, flat]
        + [pltpu.SemaphoreType.DMA(())] * 2
        + [pltpu.SemaphoreType.DMA((strips,))],
        compiler_params=pltpu.CompilerParams(vmem_limit_bytes=FLUX_VMEM),
        name="flux",
    )(*keep_in(pltpu.VMEM, *state))
    residual, step = pl.pallas_call(
        edge_kernel,
        out_shape=[field_shape, cell_shape],
        in_specs=[vmem] * 6 + [hbm] * 2,
        out_specs=[hbm] * 2,
        input_output_aliases={6: 0, 7: 1},
        scratch_shapes=[
            pltpu.VMEM((2, comps, face), f32),
            pltpu.VMEM((2, SUB, face), f32),
            pltpu.SemaphoreType.DMA((4,)),
        ],
        compiler_params=pltpu.CompilerParams(vmem_limit_bytes=16 * 1024 * 1024),
        name="edges",
    )(edge_a, edge_b, top_aux, low_aux, *arrived, residual, step)
    return (residual, step, vapour)


def solution(mesh):
    in_specs = (
        P(None, "dev", None),
        P(None, "dev", None),
        P("dev", None),
        P("dev", None),
        P("dev", None),
        P("dev", None),
        P("dev"),
        P("dev"),
        P(),
        P(),
        P(),
    )
    out_specs = (P(None, "dev", None), P("dev", None), P("dev", None))
    return jax.shard_map(
        on_device, mesh=mesh, in_specs=in_specs, out_specs=out_specs, check_vma=False
    )
```

```python
import math

import jax
import jax.numpy as jnp
from jax import lax
from jax.experimental import pallas as pl
from jax.experimental.pallas import tpu as pltpu
from jax.sharding import PartitionSpec as P

BLK = 128
SUB = 8
SS_ITERS = 3
RR_ITERS = 3
Z_ITERS = 5
WIDE = 8
AHEAD = 3
LOG2E = math.log2(math.e)
CELLS_VMEM = 32 * 1024 * 1024
FLUX_VMEM = 32 * 1024 * 1024

SQRT_TWO = math.sqrt(2.0)
TIME_STEP = 0.5
RELAX = 0.7
STEP_SCALE = 10.0
OFF_SCALE = RELAX * TIME_STEP

EDGE_PRES, EDGE_PERM, EDGE_LAM, EDGE_CSUM, EDGE_OSUM = range(5)
EDGE_PRES2, EDGE_PERM2, EDGE_LAM2 = range(5, 8)
EDGE_ROWS = 8
EDGE_SPAN = 32
AUX_IN, AUX_LEFT, AUX_RIGHT, AUX_FIRST, AUX_GAIN, AUX_STEP, AUX_ROW, AUX_DIAG = range(8)
AUX_ROWS = 8


def keep_in(space, *arrays):
    return [pltpu.with_memory_space_constraint(x, space) for x in arrays]


def recip(value):
    return pltpu.reciprocal(value, approx=True)


def odd_tiles(rows):
    return rows + SUB if (rows // SUB) % 2 == 0 else rows


def split_halves(value):
    high = value.astype(jnp.bfloat16)
    low = (value - high.astype(jnp.float32)).astype(jnp.bfloat16)
    return high, low


def widen(wide, attraction, covolume, comps):
    cols = 3 * comps * SUB
    span = 2 * SUB

    def column(rows):
        at = lax.broadcasted_iota(jnp.int32, (rows, cols), 1)
        pair = at // (3 * span)
        within = at - pair * (3 * span)
        part = within // span
        within = within - part * span
        return 2 * pair + within // SUB, part, lax.rem(within, SUB)

    comp, _, _ = column(comps)
    spread = jnp.where(comp == lax.broadcasted_iota(jnp.int32, (comps, cols), 0), 1.0, 0.0)
    table = attraction[...]
    coefficients = 0.5 * (
        lax.dot_general(table, spread, (((1,), (0,)), ((), ())), precision=lax.Precision.HIGHEST)
        + lax.dot_general(table, spread, (((0,), (0,)), ((), ())), precision=lax.Precision.HIGHEST)
    )
    comp, part, sub = column(SUB)
    diagonal = sub == lax.broadcasted_iota(jnp.int32, (SUB, cols), 0)
    zero = jnp.zeros((SUB, cols), jnp.float32)
    of_cov = zero
    for j in range(comps):
        of_cov = jnp.where(comp == j, covolume[j], of_cov)
    blocks = [coefficients[i : i + 1, :] for i in range(comps)] + [of_cov, zero + 1.0]
    for pair in range(len(blocks) // 2):
        rows = []
        for i in (2 * pair, 2 * pair + 1):
            value = jnp.where(diagonal, blocks[i], zero)
            high = value.astype(jnp.bfloat16).astype(jnp.float32)
            rows.append(jnp.where(part == 1, value - high, high))
        wide[span * pair : span * (pair + 1), :] = jnp.concatenate(rows, 0).astype(jnp.bfloat16)


def rows_of(g):
    return slice(g * SUB, (g + 1) * SUB)


def cubic(big_a, big_b, vapour_flag):
    two_b = 2.0 * big_b
    two_b_square = two_b * big_b
    least = two_b + 0.01
    most = big_b + 2.0
    if vapour_flag is True:
        start, shift, factor = 1.0 + big_b, big_b + 0.5, -0.5 * big_a
    elif vapour_flag is False:
        start, shift, factor = 3.0 * big_b, big_b, 0.5 * recip(big_a)
    else:
        start = jnp.where(vapour_flag, 1.0 + big_b, 3.0 * big_b)
        shift = jnp.where(vapour_flag, big_b + 0.5, big_b)
        factor = jnp.where(vapour_flag, -0.5 * big_a, -0.5 * recip(big_a))
        base = jnp.where(vapour_flag, two_b, 1.0 + two_b)

    def step(w):
        spread = w * w - two_b_square
        if vapour_flag is True:
            part = factor * (w - two_b) * recip(spread)
        elif vapour_flag is False:
            part = spread * ((1.0 + two_b) - w) * factor
        else:
            part = factor * (w - base) * jnp.where(vapour_flag, recip(spread), spread)
        return jnp.minimum(jnp.maximum((0.5 * w + shift) + part, least), most)

    return start, step


def roots_of(*equations):
    steps = [cubic(*equation) for equation in equations]
    found = [start for start, _ in steps]
    for _ in range(Z_ITERS):
        found = [step(w) for w, (_, step) in zip(found, steps)]
    return [w - big_b for w, (_, big_b, _) in zip(found, equations)]


def cells_kernel(
    counts,
    block_ids_hbm,
    wilson_hbm,
    covolume_hbm,
    attraction_hbm,
    moles_hbm,
    old_hbm,
    pres_hbm,
    perm_hbm,
    labels_hbm,
    roots_hbm,
    edge_a,
    edge_b,
    held,
    old,
    mobile,
    pres,
    perm,
    lam,
    scale,
    csum,
    vap,
    pres_flat,
    perm_flat,
    labels,
    roots,
    w_wide,
    sums,
    pack,
    pack_pres,
    inv_excess,
    liquid,
    vapour,
    out_cell,
    found,
    mix,
    block_ids,
    wilson,
    covolume,
    attraction,
    in_sem,
    old_sem,
    cell_sem,
    table_sem,
):
    comps, layers, face = moles_hbm.shape
    strips = face // BLK
    groups = layers // SUB
    padded = layers + 2 * SUB
    inside = slice(SUB, SUB + layers)

    def lanes_of(k):
        return pl.ds(pl.multiple_of(k * BLK, BLK), BLK)

    def strip_of(k):
        return pl.ds(pl.multiple_of(k * layers, SUB), layers)

    def strip_in(source, target, sem, k):
        return pltpu.make_async_copy(
            source.at[:, :, lanes_of(k)], target.at[:, strip_of(k), :], sem.at[k]
        )

    cell_copies = [
        pltpu.make_async_copy(pres_hbm, pres_flat, cell_sem.at[0]),
        pltpu.make_async_copy(roots_hbm, roots, cell_sem.at[1]),
        pltpu.make_async_copy(labels_hbm, labels, cell_sem.at[2]),
        pltpu.make_async_copy(perm_hbm, perm_flat, cell_sem.at[3]),
    ]
    table_copies = [
        pltpu.make_async_copy(source, target, table_sem.at[n])
        for n, (source, target) in enumerate(
            (
                (attraction_hbm, attraction),
                (covolume_hbm, covolume),
                (wilson_hbm, wilson),
                (block_ids_hbm, block_ids),
            )
        )
    ]
    for copy in table_copies:
        copy.start()
    for k in range(min(AHEAD, strips)):
        strip_in(moles_hbm, held, in_sem, k).start()
    for copy in cell_copies:
        copy.start()

    zero_tile = jnp.zeros((SUB, BLK), jnp.float32)
    zero_strip = jnp.zeros((padded, BLK), jnp.float32)

    for ref in (pres, perm, lam):
        for k in (0, strips + 1):
            ref[k] = zero_strip
        for k in range(1, strips + 1):
            ref[k, 0:SUB] = zero_tile
            ref[k, SUB + layers : padded] = zero_tile

    def clear(i, carry):
        for k in (0, strips + 1):
            mobile[i, k * padded : (k + 1) * padded, :] = zero_strip
        for k in range(1, strips + 1):
            mobile[i, k * padded : k * padded + SUB, :] = zero_tile
            mobile[i, (k + 1) * padded - SUB : (k + 1) * padded, :] = zero_tile
        return carry

    lax.fori_loop(0, comps, clear, 0)
    for copy in table_copies:
        copy.wait()
    widen(w_wide, attraction, covolume, comps)

    cols = comps * SUB

    def mixture(tile, count, keep=None, between=None):
        parts = ([], [], [])
        for g in range(0, count, 2):
            if between is not None:
                between()
            halves = []
            for j in range(comps // 2):
                both = [
                    jnp.concatenate([tile(2 * j, at), tile(2 * j + 1, at)], 0) for at in (g, g + 1)
                ]
                high, low = split_halves(jnp.concatenate(both, 1))
                halves += [high, high, low]
            result = jnp.dot(
                w_wide[...],
                jnp.concatenate(halves, 0),
                preferred_element_type=jnp.float32,
            )
            if keep is not None:
                sums[:, (keep + g) * BLK : (keep + g + 2) * BLK] = result[0:cols]
            for n, at in enumerate((g, g + 1)):
                lanes = slice(n * BLK, (n + 1) * BLK)
                quad = tile(0, at) * result[0:SUB, lanes]
                for i in range(1, comps):
                    quad = quad + tile(i, at) * result[i * SUB : (i + 1) * SUB, lanes]
                parts[0].append(result[cols + SUB : cols + 2 * SUB, lanes])
                parts[1].append(result[cols : cols + SUB, lanes])
                parts[2].append(quad)
        return [jnp.concatenate(part, 0) for part in parts]

    def total(at, start, count):
        rows = slice(at * SUB, (at + 1) * SUB)
        return jnp.concatenate(
            [sums[rows, g * BLK : (g + 1) * BLK] for g in range(start, start + count)], 0
        )


    def padded_of(k):
        return pl.ds(pl.multiple_of((k + 1) * padded + SUB, SUB), layers)

    def products(k, between=None):
        strip_in(moles_hbm, held, in_sem, k).wait()

        @pl.when(k + AHEAD < strips)
        def _():
            strip_in(moles_hbm, held, in_sem, k + AHEAD).start()

        return mixture(
            lambda i, g: held[i, pl.ds(pl.multiple_of(k * layers + g * SUB, SUB), SUB), :],
            groups,
            between=between,
        )

    class Roots:
        def __init__(self, k, amount, b_sum, quad):
            self.pressure = pres[k + 1, inside, :]
            self.amount = amount
            inv_amount = recip(amount)
            big_a = self.pressure * quad * inv_amount * inv_amount
            self.big_b = self.pressure * b_sum * inv_amount
            self.found, self.step = cubic(big_a, self.big_b, roots[:, lanes_of(k)] == 1)
            self.steps = 0

        def advance(self):
            if self.steps < Z_ITERS:
                self.found = self.step(self.found)
                self.steps += 1

    def fields(k, it):
        while it.steps < Z_ITERS:
            it.advance()
        rho = it.pressure * recip(it.found - it.big_b)
        part = labels[:, lanes_of(k)].astype(jnp.float32)
        move = ((1.0 - part) * (1.0 - part) + 4.0 * part * part) * rho
        vap[k] = part
        scale[k] = rho
        csum[k] = it.amount * rho
        lam[k + 1, inside, :] = it.amount * move
        for i in range(comps):
            mobile[i, padded_of(k), :] = held[i, strip_of(k), :] * move

    def keep_mix(values):
        for n, value in enumerate(values):
            mix[n] = value

    def single(k, carry):
        it = Roots(k - 1, *(mix[n] for n in range(3)))
        now = products(k, it.advance)
        fields(k - 1, it)
        keep_mix(now)
        return carry

    keep_mix(products(0))
    for copy in cell_copies:
        copy.wait()
    for k in range(strips):
        pres[k + 1, inside, :] = pres_flat[:, k * BLK : (k + 1) * BLK]
        perm[k + 1, inside, :] = perm_flat[:, k * BLK : (k + 1) * BLK]
    lax.fori_loop(1, strips, single, 0)
    for k in range(strips):
        strip_in(old_hbm, old, old_sem, k).start()
    fields(strips - 1, Roots(strips - 1, *(mix[n] for n in range(3))))

    batch = WIDE * SUB
    own_count = counts[0]
    held_stride, mobile_stride, pack_stride = (ref.shape[1] for ref in (held, mobile, pack))
    held_rows = held.reshape(comps * held_stride, BLK)
    mobile_rows = mobile.reshape(comps * mobile_stride, BLK)
    pack_rows = pack.reshape(comps * pack_stride, BLK)
    liquid_rows = liquid.reshape(comps * pack_stride, BLK)
    vapour_rows = vapour.reshape(comps * pack_stride, BLK)
    bits = strips.bit_length() - 1

    def place(slot):
        block = block_ids[jnp.minimum(slot, own_count - 1)]
        layer = lax.shift_right_logical(block, bits)
        return block - lax.shift_left(layer, bits), layer

    def field_at(k, layer):
        return pl.ds(k * layers + layer, comps, stride=held_stride)

    def mobile_at(k, layer):
        return pl.ds((k + 1) * padded + layer + SUB, comps, stride=mobile_stride)

    def flash(number, carry):
        base = number * batch

        def gather(group, inner):
            for n in range(SUB):
                r = group * SUB + n
                k, layer = place(base + r)
                pack_rows[pl.ds(r, comps, stride=pack_stride), :] = held_rows[field_at(k, layer), :]
                pack_pres[pl.ds(r, 1), :] = pres[k + 1, pl.ds(layer + SUB, 1), :]
            return inner

        lax.fori_loop(0, WIDE, gather, 0)
        slots = slice(0, batch)
        pressure = pack_pres[...]
        amount = pack[0, slots, :]
        for i in range(1, comps):
            amount = amount + pack[i, slots, :]
        inv_amount = recip(amount)
        for i in range(comps):
            pack[i, slots, :] = pack[i, slots, :] * inv_amount

        def keep_k(i, log2_k):
            inv_excess[i, slots, :] = recip(jnp.exp2(log2_k) - 1.0)

        log2_pres = jnp.log(pressure) * LOG2E
        for i in range(comps):
            keep_k(i, wilson[i] * LOG2E - log2_pres)

        def newton(_, part):
            value = jnp.zeros((batch, BLK), jnp.float32)
            slope = jnp.full((batch, BLK), 0.05, jnp.float32)
            for i in range(comps):
                ratio = recip(inv_excess[i, slots, :] + part)
                term = pack[i, slots, :] * ratio
                value = value + term
                slope = slope + term * ratio
            return jnp.minimum(jnp.maximum(part + value * recip(slope), 0.0), 1.0)

        def sweep(number_of_sweep, inner):
            half = jnp.full((batch, BLK), 0.5, jnp.float32)
            part = lax.fori_loop(0, RR_ITERS, newton, half)
            for i in range(comps):
                fraction = pack[i, slots, :]
                term = fraction * recip(inv_excess[i, slots, :] + part)
                liq = fraction - part * term
                liquid[i, slots, :] = liq
                vapour[i, slots, :] = liq + term
            phases = []
            equations = []
            for n, (ref, flag) in enumerate(((liquid, False), (vapour, True))):
                whole, b_sum, quad = mixture(lambda i, g: ref[i, rows_of(g), :], WIDE, n * WIDE)
                inv_whole = recip(whole)
                b_mix = b_sum * inv_whole
                a_mix = quad * inv_whole * inv_whole
                big_b = pressure * b_mix
                equations.append((pressure * a_mix, big_b, flag))
                phases.append((quad, whole, inv_whole, a_mix, b_mix, big_b))
            factors = roots_of(*equations)
            found[0] = part
            for n in range(2):
                found[1 + n] = factors[n]
                found[3 + n] = phases[n][2]

            @pl.when(number_of_sweep + 1 < SS_ITERS)
            def _():
                parts = []
                for (quad, whole, _, a_mix, b_mix, big_b), z_factor in zip(phases, factors):
                    log_arg = (z_factor + (1.0 + SQRT_TWO) * big_b) * recip(
                        z_factor + (1.0 - SQRT_TWO) * big_b
                    )
                    inv_b = recip(b_mix)
                    depart = a_mix * inv_b * (1.0 / (2.0 * SQRT_TWO)) * jnp.log(log_arg)
                    of_cov = (LOG2E * inv_b) * (z_factor - 1.0 + depart)
                    of_sum = (2.0 * LOG2E) * depart * whole * recip(quad)
                    parts.append((of_cov, LOG2E * jnp.log(z_factor - big_b), of_sum))
                cov_gap = parts[0][0] - parts[1][0]
                log_gap = parts[0][1] - parts[1][1]
                for i in range(comps):
                    log2_k = (covolume[i] * cov_gap - log_gap) - (
                        parts[0][2] * total(i, 0, WIDE) - parts[1][2] * total(i, WIDE, WIDE)
                    )
                    keep_k(i, jnp.minimum(jnp.maximum(log2_k, -3.0 * LOG2E), 3.0 * LOG2E))
            return inner

        lax.fori_loop(0, SS_ITERS, sweep, 0)
        part = found[0]
        rho_liq = amount * pressure * recip(found[1])
        rho_vap = amount * pressure * recip(found[2])
        rest = 1.0 - part
        move_liq = rest * rest * rho_liq
        move_vap = 4.0 * part * part * rho_vap
        hold_liq = rest * rho_liq
        hold_vap = part * rho_vap
        out_cell[0] = part
        out_cell[1] = move_liq + move_vap
        out_cell[2] = hold_liq + hold_vap
        inv_liq, inv_vap = found[3], found[4]
        move_liq = move_liq * inv_liq
        move_vap = move_vap * inv_vap
        hold_liq = hold_liq * inv_liq
        hold_vap = hold_vap * inv_vap
        for i in range(comps):
            liq, gas = liquid[i, slots, :], vapour[i, slots, :]
            liquid[i, slots, :] = move_liq * liq + move_vap * gas
            vapour[i, slots, :] = hold_liq * liq + hold_vap * gas
        one_row = jnp.ones((1, BLK), jnp.float32)

        def scatter(group, inner):
            for n in range(SUB):
                r = group * SUB + n
                k, layer = place(base + r)
                of = pl.ds(r, comps, stride=pack_stride)
                mobile_rows[mobile_at(k, layer), :] = liquid_rows[of, :]
                held_rows[field_at(k, layer), :] = vapour_rows[of, :]
                one = pl.ds(r, 1)
                row = pl.ds(layer, 1)
                vap[k, row, :] = out_cell[0, one, :]
                lam[k + 1, pl.ds(layer + SUB, 1), :] = out_cell[1, one, :]
                csum[k, row, :] = out_cell[2, one, :]
                scale[k, row, :] = one_row
            return inner

        lax.fori_loop(0, WIDE, scatter, 0)
        return carry

    lax.fori_loop(0, (own_count + batch - 1) // batch, flash, 0)
    for k in range(strips):
        strip_in(old_hbm, old, old_sem, k).wait()
    old_rows = old.reshape(comps * old.shape[1], BLK)

    def edge_values(k, at, inner):
        here = slice(at, at + 1)
        pad_here = slice(SUB + at, SUB + at + 1)
        pad_inner = slice(SUB + inner, SUB + inner + 1)
        values = [None] * EDGE_ROWS
        values[EDGE_PRES] = pres[k + 1, pad_here, :]
        values[EDGE_PERM] = perm[k + 1, pad_here, :]
        values[EDGE_LAM] = lam[k + 1, pad_here, :]
        values[EDGE_CSUM] = csum[k, here, :]
        values[EDGE_OSUM] = jnp.sum(old_rows[field_at(k, at), :], 0, keepdims=True)
        values[EDGE_PRES2] = pres[k + 1, pad_inner, :]
        values[EDGE_PERM2] = perm[k + 1, pad_inner, :]
        values[EDGE_LAM2] = lam[k + 1, pad_inner, :]
        return [mobile_rows[mobile_at(k, at), :]] + values

    odd = lax.rem(lax.axis_index("dev"), 2) == 1
    for k in range(strips):
        lanes = slice(k * BLK, (k + 1) * BLK)
        tops = edge_values(k, 0, 1)
        lows = edge_values(k, layers - 1, layers - 2)
        row = 0
        for top, low in zip(tops, lows):
            rows = slice(row, row + top.shape[0])
            edge_a[rows, lanes] = jnp.where(odd, top, low)
            edge_b[rows, lanes] = jnp.where(odd, low, top)
            row = rows.stop


def flux_kernel(
    held,
    old,
    mobile,
    pres,
    perm,
    lam,
    scale,
    csum,
    vap,
    resid_hbm,
    step_hbm,
    vap_hbm,
    top_aux,
    low_aux,
    resid,
    first,
    row_sum,
    diag,
    weights,
    step,
    vap_flat,
    step_sem,
    vap_sem,
    out_sem,
):
    comps = held.shape[0]
    strips, layers, _ = scale.shape
    groups = layers // SUB
    padded = layers + 2 * SUB

    def lanes_of(k):
        return pl.ds(pl.multiple_of(k * BLK, BLK), BLK)

    def strip_out(k):
        return pltpu.make_async_copy(resid.at[:, k], resid_hbm.at[:, :, lanes_of(k)], out_sem.at[k])

    for k in range(strips):
        vap_flat[:, k * BLK : (k + 1) * BLK] = vap[k]
    vap_copy = pltpu.make_async_copy(vap_flat, vap_hbm, vap_sem)
    vap_copy.start()
    zero_tile = jnp.zeros((SUB, BLK), jnp.float32)
    for k in range(strips + 2):
        for g in range(groups + 2):
            if k in (0, strips + 1) or g in (0, groups + 1):
                first[k, rows_of(g), :] = zero_tile

    lane_index = lax.broadcasted_iota(jnp.int32, (SUB, BLK), 1)
    is_last_lane = lane_index == BLK - 1
    is_first_lane = lane_index == 0

    def around(load, k, g):
        at = SUB * (g + 1)
        here = load(k + 1, slice(at, at + SUB))
        up = load(k + 1, slice(at - 1, at + SUB - 1))
        down = load(k + 1, slice(at + 1, at + SUB + 1))
        before = load(k, slice(at, at + SUB))
        after = load(k + 2, slice(at, at + SUB))
        left = pltpu.roll(jnp.where(is_last_lane, before, here), 1, 1)
        right = pltpu.roll(jnp.where(is_first_lane, after, here), BLK - 1, 1)
        return here, (up, down, left, right)

    def fluxes(k, carry):
        for g in range(groups):
            rows = rows_of(g)
            p_here, p_near = around(lambda s, r: pres[s, r, :], k, g)
            k_here, k_near = around(lambda s, r: perm[s, r, :], k, g)
            l_here, l_near = around(lambda s, r: lam[s, r, :], k, g)
            drives = []
            couplings = []
            for n in range(4):
                transmiss = k_here * k_near[n] * recip(k_here + k_near[n])
                drives.append((TIME_STEP * transmiss) * (p_here - p_near[n]))
                couplings.append(transmiss * (l_here + l_near[n]))
            drive_sum = (drives[0] + drives[1]) + (drives[2] + drives[3])
            content_scale = scale[k, rows, :]
            flat_rows = pl.ds(pl.multiple_of(k * layers + g * SUB, SUB), SUB)
            row_total = zero_tile
            for i in range(comps):
                m_here, m_near = around(
                    lambda s, r, i=i: mobile[i, pl.ds(s * padded + r.start, SUB), :], k, g
                )
                value = held[i, flat_rows, :] * content_scale - old[i, flat_rows, :]
                value = value + drive_sum * m_here
                value = value + (drives[0] * m_near[0] + drives[1] * m_near[1])
                value = value + (drives[2] * m_near[2] + drives[3] * m_near[3])
                resid[i, k, rows, :] = value
                row_total = row_total + value
            diagonal = TIME_STEP * (
                (couplings[0] + couplings[1]) + (couplings[2] + couplings[3])
            ) + csum[k, rows, :] * recip(p_here)
            inv_diag = recip(diagonal)
            row_sum[k, rows, :] = row_total
            diag[k, rows, :] = diagonal
            first[k + 1, SUB * (g + 1) : SUB * (g + 2), :] = -row_total * inv_diag
            gain = (STEP_SCALE * OFF_SCALE) * inv_diag
            for n in range(4):
                weights[n, k, rows, :] = couplings[n] * gain
        strip_out(k).start()
        return carry

    lax.fori_loop(0, strips, fluxes, 0)

    def steps(k, carry):
        for g in range(groups):
            rows = rows_of(g)
            here, near = around(lambda s, r: first[s, r, :], k, g)
            step[rows, lanes_of(k)] = (
                STEP_SCALE * here
                + (weights[0, k, rows, :] * near[0] + weights[1, k, rows, :] * near[1])
                + (weights[2, k, rows, :] * near[2] + weights[3, k, rows, :] * near[3])
            )
        return carry

    lax.fori_loop(0, strips, steps, 0)
    step_copy = pltpu.make_async_copy(step, step_hbm, step_sem)
    step_copy.start()

    resid_rows = resid.reshape(comps * strips * layers, BLK)
    for aux, at, inner, toward, away in (
        (top_aux, 0, 1, 0, 1),
        (low_aux, layers - 1, layers - 2, 1, 0),
    ):
        for k in range(strips):
            lanes = slice(k * BLK, (k + 1) * BLK)
            here = slice(at, at + 1)
            behind = slice(inner, inner + 1)
            from_row = pl.ds(k * layers + at, comps, stride=strips * layers)
            aux[0:comps, lanes] = resid_rows[from_row, :]
            unscale = diag[k, here, :]
            values = [None] * AUX_ROWS
            values[AUX_IN] = weights[away, k, here, :] * unscale
            values[AUX_LEFT] = weights[2, k, here, :] * unscale
            values[AUX_RIGHT] = weights[3, k, here, :] * unscale
            values[AUX_FIRST] = first[k + 1, SUB + inner : SUB + inner + 1, :]
            values[AUX_GAIN] = weights[toward, k, behind, :]
            values[AUX_STEP] = step[behind, lanes]
            values[AUX_ROW] = row_sum[k, here, :]
            values[AUX_DIAG] = unscale
            for n, value in enumerate(values):
                aux[comps + n : comps + n + 1, lanes] = value
    vap_copy.wait()
    step_copy.wait()
    for k in range(strips):
        strip_out(k).wait()


def transmissibility(perm, perm_near):
    both = perm + perm_near
    return perm * perm_near / jnp.where(both == 0.0, 1.0, both)


def edge_kernel(
    edge_a,
    edge_b,
    top_aux,
    low_aux,
    in_even,
    in_odd,
    resid_in,
    step_in,
    resid_hbm,
    step_hbm,
    resid,
    step,
    sem,
):
    comps, layers, face = resid_hbm.shape
    odd = lax.rem(lax.axis_index("dev"), 2) == 1
    top_edge = jnp.where(odd, edge_a[...], edge_b[...])
    low_edge = jnp.where(odd, edge_b[...], edge_a[...])
    from_prev = jnp.where(odd, in_even[...], in_odd[...])
    from_next = jnp.where(odd, in_odd[...], in_even[...])
    copies = []
    for n, (edge, aux, other, at, inner) in enumerate(
        (
            (top_edge, top_aux, from_prev, 0, 1),
            (low_edge, low_aux, from_next, layers - 1, layers - 2),
        )
    ):

        def own(index):
            return edge[comps + index : comps + index + 1, :]

        def far(index):
            return other[comps + index : comps + index + 1, :]

        def near(index):
            return aux[comps + index : comps + index + 1, :]

        pres_far, perm_far, lam_far = far(EDGE_PRES), far(EDGE_PERM), far(EDGE_LAM)
        transmiss = transmissibility(own(EDGE_PERM), perm_far)
        drive = TIME_STEP * transmiss * (own(EDGE_PRES) - pres_far)
        lam_both = own(EDGE_LAM) + lam_far
        coupling = transmiss * lam_both
        row = near(AUX_ROW) + drive * lam_both
        diag = near(AUX_DIAG) + TIME_STEP * coupling
        first = -row / diag
        first_old = -near(AUX_ROW) / near(AUX_DIAG)
        row_far = far(EDGE_CSUM) - far(EDGE_OSUM) - drive * lam_both
        diag_far = coupling
        lane = lax.broadcasted_iota(jnp.int32, (1, face), 1)
        sides = [(far(EDGE_PRES2), far(EDGE_PERM2), far(EDGE_LAM2))]
        for shift, end in ((1, 0), (face - 1, face - 1)):
            pres_n, perm_n, lam_n = (pltpu.roll(x, shift, 1) for x in (pres_far, perm_far, lam_far))
            sides.append((pres_n, jnp.where(lane == end, 0.0, perm_n), lam_n))
        for pres_n, perm_n, lam_n in sides:
            joint = transmissibility(perm_far, perm_n) * (lam_far + lam_n)
            row_far = row_far + TIME_STEP * joint * (pres_far - pres_n)
            diag_far = diag_far + joint
        diag_far = TIME_STEP * diag_far + far(EDGE_CSUM) / jnp.where(pres_far == 0.0, 1.0, pres_far)
        first_far = -row_far / jnp.where(diag_far == 0.0, 1.0, diag_far)
        off = (
            (STEP_SCALE * OFF_SCALE) * coupling * first_far
            + near(AUX_IN) * near(AUX_FIRST)
            + near(AUX_LEFT) * pltpu.roll(first, 1, 1)
            + near(AUX_RIGHT) * pltpu.roll(first, face - 1, 1)
        )
        least = min(at, inner)
        step[n, at - least : at - least + 1, :] = STEP_SCALE * first + off / diag
        step[n, inner - least : inner - least + 1, :] = near(AUX_STEP) + near(AUX_GAIN) * (
            first - first_old
        )
        resid[n] = aux[0:comps, :] + drive * (edge[0:comps, :] + other[0:comps, :])
        for source, target in (
            (resid.at[n], resid_hbm.at[:, at, :]),
            (step.at[n, 0:2, :], step_hbm.at[least : least + 2, :]),
        ):
            copies.append(pltpu.make_async_copy(source, target, sem.at[len(copies)]))
            copies[-1].start()
    for copy in copies:
        copy.wait()


def on_device(
    moles,
    old_content,
    pressure,
    perm,
    labels,
    roots,
    counts,
    block_ids,
    wilson,
    attraction,
    covolume,
):
    comps, layers, face = moles.shape
    f32 = jnp.float32
    strips = face // BLK
    tables = (block_ids, wilson, covolume, attraction)
    rows_in = comps * SUB
    vmem = pl.BlockSpec(memory_space=pltpu.VMEM)
    hbm = pl.BlockSpec(memory_space=pltpu.HBM)
    padded = layers + 2 * SUB
    flat = pltpu.VMEM((layers, face), f32)
    flat_int = pltpu.VMEM((layers, face), jnp.int32)
    cell = pltpu.VMEM((strips, layers, BLK), f32)
    cell_pad = pltpu.VMEM((strips + 2, padded, BLK), f32)
    field = pltpu.VMEM((comps, odd_tiles(strips * layers), BLK), f32)
    field_pad = pltpu.VMEM((comps, odd_tiles((strips + 2) * padded), BLK), f32)
    packed = pltpu.VMEM((comps, odd_tiles(WIDE * SUB), BLK), f32)
    edge_shape = pltpu.VMEM((EDGE_SPAN, face), f32)
    aux_shape = pltpu.VMEM((comps + AUX_ROWS, face), f32)
    field_shape = jax.ShapeDtypeStruct((comps, layers, face), f32)
    cell_shape = jax.ShapeDtypeStruct((layers, face), f32)
    field_out = pltpu.VMEM((comps, strips, layers, BLK), f32)
    held_types = [field, field, field_pad] + [cell_pad] * 3 + [cell] * 3
    edge_a, edge_b, *state = pl.pallas_call(
        cells_kernel,
        out_shape=[edge_shape, edge_shape]
        + held_types,
        in_specs=[pl.BlockSpec(memory_space=pltpu.SMEM)] + [hbm] * 10,
        out_specs=[vmem] * (2 + len(held_types)),
        scratch_shapes=[flat, flat, flat_int, flat_int]
        + [pltpu.VMEM((rows_in + 2 * SUB, 3 * rows_in), jnp.bfloat16)]
        + [pltpu.VMEM((rows_in, 2 * WIDE * BLK), f32)]
        + [packed, pltpu.VMEM((WIDE * SUB, BLK), f32)]
        + [packed] * 3
        + [pltpu.VMEM((3, WIDE * SUB, BLK), f32), pltpu.VMEM((5, WIDE * SUB, BLK), f32)]
        + [pltpu.VMEM((3, layers, BLK), f32)]
        + [pltpu.SMEM(table.shape, table.dtype) for table in tables[:-1]]
        + [pltpu.VMEM(attraction.shape, f32)]
        + [
            pltpu.SemaphoreType.DMA((strips,)),
            pltpu.SemaphoreType.DMA((strips,)),
            pltpu.SemaphoreType.DMA((4,)),
            pltpu.SemaphoreType.DMA((len(tables),)),
        ],
        compiler_params=pltpu.CompilerParams(vmem_limit_bytes=CELLS_VMEM),
        name="cells",
    )(counts, *keep_in(pltpu.HBM, *tables, moles, old_content, pressure, perm, labels, roots))
    count = lax.axis_size("dev")
    arrived = []
    for start, edge in ((0, edge_a), (1, edge_b)):
        pairs = [(i, i + 1) for i in range(start, count - 1, 2)]
        arrived.append(lax.ppermute(edge, "dev", pairs + [pair[::-1] for pair in pairs]))
    residual, step, vapour, top_aux, low_aux = pl.pallas_call(
        flux_kernel,
        out_shape=[field_shape, cell_shape, cell_shape, aux_shape, aux_shape],
        in_specs=[vmem] * len(state),
        out_specs=[hbm] * 3 + [vmem] * 2,
        scratch_shapes=[field_out, cell_pad, cell, cell]
        + [pltpu.VMEM((4, strips, layers, BLK), f32), flat, flat]
        + [pltpu.SemaphoreType.DMA(())] * 2
        + [pltpu.SemaphoreType.DMA((strips,))],
        compiler_params=pltpu.CompilerParams(vmem_limit_bytes=FLUX_VMEM),
        name="flux",
    )(*keep_in(pltpu.VMEM, *state))
    residual, step = pl.pallas_call(
        edge_kernel,
        out_shape=[field_shape, cell_shape],
        in_specs=[vmem] * 6 + [hbm] * 2,
        out_specs=[hbm] * 2,
        input_output_aliases={6: 0, 7: 1},
        scratch_shapes=[
            pltpu.VMEM((2, comps, face), f32),
            pltpu.VMEM((2, SUB, face), f32),
            pltpu.SemaphoreType.DMA((4,)),
        ],
        compiler_params=pltpu.CompilerParams(vmem_limit_bytes=16 * 1024 * 1024),
        name="edges",
    )(edge_a, edge_b, top_aux, low_aux, *arrived, residual, step)
    return (residual, step, vapour)


def solution(mesh):
    in_specs = (
        P(None, "dev", None),
        P(None, "dev", None),
        P("dev", None),
        P("dev", None),
        P("dev", None),
        P("dev", None),
        P("dev"),
        P("dev"),
        P(),
        P(),
        P(),
    )
    out_specs = (P(None, "dev", None), P("dev", None), P("dev", None))
    return jax.shard_map(
        on_device, mesh=mesh, in_specs=in_specs, out_specs=out_specs, check_vma=False
    )
```

```python
import math

import jax
import jax.numpy as jnp
from jax import lax
from jax.experimental import pallas as pl
from jax.experimental.pallas import tpu as pltpu
from jax.sharding import PartitionSpec as P

BLK = 128
SUB = 8
SS_ITERS = 3
RR_ITERS = 3
Z_ITERS = 5
WIDE = 8
AHEAD = 3
LOG2E = math.log2(math.e)
CELLS_VMEM = 32 * 1024 * 1024
FLUX_VMEM = 32 * 1024 * 1024

SQRT_TWO = math.sqrt(2.0)
TIME_STEP = 0.5
RELAX = 0.7
STEP_SCALE = 10.0
OFF_SCALE = RELAX * TIME_STEP

EDGE_PRES, EDGE_PERM, EDGE_LAM, EDGE_CSUM, EDGE_OSUM = range(5)
EDGE_PRES2, EDGE_PERM2, EDGE_LAM2 = range(5, 8)
EDGE_ROWS = 8
EDGE_SPAN = 32
AUX_IN, AUX_LEFT, AUX_RIGHT, AUX_FIRST, AUX_GAIN, AUX_STEP, AUX_ROW, AUX_DIAG = range(8)
AUX_ROWS = 8


def keep_in(space, *arrays):
    return [pltpu.with_memory_space_constraint(x, space) for x in arrays]


def recip(value):
    return pltpu.reciprocal(value, approx=True)


def odd_tiles(rows):
    return rows + SUB if (rows // SUB) % 2 == 0 else rows


def split_halves(value):
    high = value.astype(jnp.bfloat16)
    low = (value - high.astype(jnp.float32)).astype(jnp.bfloat16)
    return high, low


def widen(wide, attraction, covolume, comps):
    cols = 3 * comps * SUB
    span = 2 * SUB

    def column(rows):
        at = lax.broadcasted_iota(jnp.int32, (rows, cols), 1)
        pair = at // (3 * span)
        within = at - pair * (3 * span)
        part = within // span
        within = within - part * span
        return 2 * pair + within // SUB, part, lax.rem(within, SUB)

    comp, _, _ = column(comps)
    spread = jnp.where(comp == lax.broadcasted_iota(jnp.int32, (comps, cols), 0), 1.0, 0.0)
    spread = spread.astype(jnp.bfloat16)
    table = attraction[...]
    of_high, of_low = (
        jnp.dot(half, spread, preferred_element_type=jnp.float32)
        for half in split_halves(0.5 * (table + table.T))
    )
    comp, part, sub = column(SUB)
    diagonal = sub == lax.broadcasted_iota(jnp.int32, (SUB, cols), 0)
    zero = jnp.zeros((SUB, cols), jnp.float32)
    of_cov = zero
    for j in range(comps):
        of_cov = jnp.where(comp == j, covolume[j], of_cov)
    cov_high = of_cov.astype(jnp.bfloat16).astype(jnp.float32)
    taken = jnp.where(part[0:1, :] == 1, of_low, of_high)
    blocks = [taken[i : i + 1, :] for i in range(comps)]
    blocks += [jnp.where(part == 1, of_cov - cov_high, cov_high), jnp.where(part == 1, 0.0, 1.0)]
    for pair in range(len(blocks) // 2):
        rows = [jnp.where(diagonal, blocks[i], zero) for i in (2 * pair, 2 * pair + 1)]
        wide[span * pair : span * (pair + 1), :] = jnp.concatenate(rows, 0).astype(jnp.bfloat16)


def rows_of(g):
    return slice(g * SUB, (g + 1) * SUB)


def cubic(big_a, big_b, vapour_flag):
    two_b = 2.0 * big_b
    two_b_square = two_b * big_b
    least = two_b + 0.01
    most = big_b + 2.0
    if vapour_flag is True:
        start, shift, factor = 1.0 + big_b, big_b + 0.5, -0.5 * big_a
    elif vapour_flag is False:
        start, shift, factor = 3.0 * big_b, big_b, 0.5 * recip(big_a)
    else:
        start = jnp.where(vapour_flag, 1.0 + big_b, 3.0 * big_b)
        shift = jnp.where(vapour_flag, big_b + 0.5, big_b)
        factor = jnp.where(vapour_flag, -0.5 * big_a, -0.5 * recip(big_a))
        base = jnp.where(vapour_flag, two_b, 1.0 + two_b)

    def step(w):
        spread = w * w - two_b_square
        if vapour_flag is True:
            part = factor * (w - two_b) * recip(spread)
        elif vapour_flag is False:
            part = spread * ((1.0 + two_b) - w) * factor
        else:
            part = factor * (w - base) * jnp.where(vapour_flag, recip(spread), spread)
        return jnp.minimum(jnp.maximum((0.5 * w + shift) + part, least), most)

    return start, step


def roots_of(*equations):
    steps = [cubic(*equation) for equation in equations]
    found = [start for start, _ in steps]
    for _ in range(Z_ITERS):
        found = [step(w) for w, (_, step) in zip(found, steps)]
    return [w - big_b for w, (_, big_b, _) in zip(found, equations)]


def cells_kernel(
    counts,
    block_ids_hbm,
    wilson_hbm,
    covolume_hbm,
    attraction_hbm,
    moles_hbm,
    old_hbm,
    pres_hbm,
    perm_hbm,
    labels_hbm,
    roots_hbm,
    edge_a,
    edge_b,
    held,
    old,
    mobile,
    pres,
    perm,
    lam,
    scale,
    csum,
    vap,
    pres_flat,
    perm_flat,
    labels,
    roots,
    w_wide,
    sums,
    pack,
    pack_pres,
    inv_excess,
    liquid,
    vapour,
    out_cell,
    found,
    mix,
    block_ids,
    wilson,
    covolume,
    attraction,
    in_sem,
    old_sem,
    cell_sem,
    table_sem,
):
    comps, layers, face = moles_hbm.shape
    strips = face // BLK
    groups = layers // SUB
    padded = layers + 2 * SUB
    inside = slice(SUB, SUB + layers)

    def lanes_of(k):
        return pl.ds(pl.multiple_of(k * BLK, BLK), BLK)

    def strip_of(k):
        return pl.ds(pl.multiple_of(k * layers, SUB), layers)

    def strip_in(source, target, sem, k):
        return pltpu.make_async_copy(
            source.at[:, :, lanes_of(k)], target.at[:, strip_of(k), :], sem.at[k]
        )

    cell_copies = [
        pltpu.make_async_copy(pres_hbm, pres_flat, cell_sem.at[0]),
        pltpu.make_async_copy(roots_hbm, roots, cell_sem.at[1]),
        pltpu.make_async_copy(labels_hbm, labels, cell_sem.at[2]),
        pltpu.make_async_copy(perm_hbm, perm_flat, cell_sem.at[3]),
    ]
    table_copies = [
        pltpu.make_async_copy(source, target, table_sem.at[n])
        for n, (source, target) in enumerate(
            (
                (attraction_hbm, attraction),
                (covolume_hbm, covolume),
                (wilson_hbm, wilson),
                (block_ids_hbm, block_ids),
            )
        )
    ]
    for copy in table_copies:
        copy.start()
    for k in range(min(AHEAD, strips)):
        strip_in(moles_hbm, held, in_sem, k).start()
    for copy in cell_copies:
        copy.start()

    zero_tile = jnp.zeros((SUB, BLK), jnp.float32)
    zero_strip = jnp.zeros((padded, BLK), jnp.float32)

    for ref in (pres, perm, lam):
        for k in (0, strips + 1):
            ref[k] = zero_strip
        for k in range(1, strips + 1):
            ref[k, 0:SUB] = zero_tile
            ref[k, SUB + layers : padded] = zero_tile

    def clear(i, carry):
        for k in (0, strips + 1):
            mobile[i, k * padded : (k + 1) * padded, :] = zero_strip
        for k in range(1, strips + 1):
            mobile[i, k * padded : k * padded + SUB, :] = zero_tile
            mobile[i, (k + 1) * padded - SUB : (k + 1) * padded, :] = zero_tile
        return carry

    lax.fori_loop(0, comps, clear, 0)
    for copy in table_copies:
        copy.wait()
    widen(w_wide, attraction, covolume, comps)

    cols = comps * SUB

    def mixture(tile, count, keep=None, between=None):
        parts = ([], [], [])
        for g in range(0, count, 2):
            if between is not None:
                between()
            halves = []
            for j in range(comps // 2):
                both = [
                    jnp.concatenate([tile(2 * j, at), tile(2 * j + 1, at)], 0) for at in (g, g + 1)
                ]
                high, low = split_halves(jnp.concatenate(both, 1))
                halves += [high, high, low]
            result = jnp.dot(
                w_wide[...],
                jnp.concatenate(halves, 0),
                preferred_element_type=jnp.float32,
            )
            if keep is not None:
                sums[:, (keep + g) * BLK : (keep + g + 2) * BLK] = result[0:cols]
            for n, at in enumerate((g, g + 1)):
                lanes = slice(n * BLK, (n + 1) * BLK)
                quad = tile(0, at) * result[0:SUB, lanes]
                for i in range(1, comps):
                    quad = quad + tile(i, at) * result[i * SUB : (i + 1) * SUB, lanes]
                parts[0].append(result[cols + SUB : cols + 2 * SUB, lanes])
                parts[1].append(result[cols : cols + SUB, lanes])
                parts[2].append(quad)
        return [jnp.concatenate(part, 0) for part in parts]

    def total(at, start, count):
        rows = slice(at * SUB, (at + 1) * SUB)
        return jnp.concatenate(
            [sums[rows, g * BLK : (g + 1) * BLK] for g in range(start, start + count)], 0
        )


    def padded_of(k):
        return pl.ds(pl.multiple_of((k + 1) * padded + SUB, SUB), layers)

    def products(k, between=None):
        strip_in(moles_hbm, held, in_sem, k).wait()

        @pl.when(k + AHEAD < strips)
        def _():
            strip_in(moles_hbm, held, in_sem, k + AHEAD).start()

        return mixture(
            lambda i, g: held[i, pl.ds(pl.multiple_of(k * layers + g * SUB, SUB), SUB), :],
            groups,
            between=between,
        )

    class Roots:
        def __init__(self, k, amount, b_sum, quad):
            self.pressure = pres[k + 1, inside, :]
            self.amount = amount
            inv_amount = recip(amount)
            big_a = self.pressure * quad * inv_amount * inv_amount
            self.big_b = self.pressure * b_sum * inv_amount
            self.found, self.step = cubic(big_a, self.big_b, roots[:, lanes_of(k)] == 1)
            self.steps = 0

        def advance(self):
            if self.steps < Z_ITERS:
                self.found = self.step(self.found)
                self.steps += 1

    def fields(k, it):
        while it.steps < Z_ITERS:
            it.advance()
        rho = it.pressure * recip(it.found - it.big_b)
        part = labels[:, lanes_of(k)].astype(jnp.float32)
        move = ((1.0 - part) * (1.0 - part) + 4.0 * part * part) * rho
        vap[k] = part
        scale[k] = rho
        csum[k] = it.amount * rho
        lam[k + 1, inside, :] = it.amount * move
        for i in range(comps):
            mobile[i, padded_of(k), :] = held[i, strip_of(k), :] * move

    def keep_mix(values):
        for n, value in enumerate(values):
            mix[n] = value

    def single(k, carry):
        it = Roots(k - 1, *(mix[n] for n in range(3)))
        now = products(k, it.advance)
        fields(k - 1, it)
        keep_mix(now)
        return carry

    keep_mix(products(0))
    for copy in cell_copies:
        copy.wait()
    for k in range(strips):
        pres[k + 1, inside, :] = pres_flat[:, k * BLK : (k + 1) * BLK]
        perm[k + 1, inside, :] = perm_flat[:, k * BLK : (k + 1) * BLK]
    lax.fori_loop(1, strips, single, 0)
    for k in range(strips):
        strip_in(old_hbm, old, old_sem, k).start()
    fields(strips - 1, Roots(strips - 1, *(mix[n] for n in range(3))))

    batch = WIDE * SUB
    own_count = counts[0]
    held_stride, mobile_stride, pack_stride = (ref.shape[1] for ref in (held, mobile, pack))
    held_rows = held.reshape(comps * held_stride, BLK)
    mobile_rows = mobile.reshape(comps * mobile_stride, BLK)
    pack_rows = pack.reshape(comps * pack_stride, BLK)
    liquid_rows = liquid.reshape(comps * pack_stride, BLK)
    vapour_rows = vapour.reshape(comps * pack_stride, BLK)
    bits = strips.bit_length() - 1

    def place(slot):
        block = block_ids[jnp.minimum(slot, own_count - 1)]
        layer = lax.shift_right_logical(block, bits)
        return block - lax.shift_left(layer, bits), layer

    def field_at(k, layer):
        return pl.ds(k * layers + layer, comps, stride=held_stride)

    def mobile_at(k, layer):
        return pl.ds((k + 1) * padded + layer + SUB, comps, stride=mobile_stride)

    def flash(number, carry):
        base = number * batch

        def gather(group, inner):
            for n in range(SUB):
                r = group * SUB + n
                k, layer = place(base + r)
                pack_rows[pl.ds(r, comps, stride=pack_stride), :] = held_rows[field_at(k, layer), :]
                pack_pres[pl.ds(r, 1), :] = pres[k + 1, pl.ds(layer + SUB, 1), :]
            return inner

        lax.fori_loop(0, WIDE, gather, 0)
        slots = slice(0, batch)
        pressure = pack_pres[...]
        amount = pack[0, slots, :]
        for i in range(1, comps):
            amount = amount + pack[i, slots, :]
        inv_amount = recip(amount)
        for i in range(comps):
            pack[i, slots, :] = pack[i, slots, :] * inv_amount

        def keep_k(i, log2_k):
            inv_excess[i, slots, :] = recip(jnp.exp2(log2_k) - 1.0)

        log2_pres = jnp.log(pressure) * LOG2E
        for i in range(comps):
            keep_k(i, wilson[i] * LOG2E - log2_pres)

        def newton(_, part):
            value = jnp.zeros((batch, BLK), jnp.float32)
            slope = jnp.full((batch, BLK), 0.05, jnp.float32)
            for i in range(comps):
                ratio = recip(inv_excess[i, slots, :] + part)
                term = pack[i, slots, :] * ratio
                value = value + term
                slope = slope + term * ratio
            return jnp.minimum(jnp.maximum(part + value * recip(slope), 0.0), 1.0)

        def sweep(number_of_sweep, inner):
            half = jnp.full((batch, BLK), 0.5, jnp.float32)
            part = lax.fori_loop(0, RR_ITERS, newton, half)
            for i in range(comps):
                fraction = pack[i, slots, :]
                term = fraction * recip(inv_excess[i, slots, :] + part)
                liq = fraction - part * term
                liquid[i, slots, :] = liq
                vapour[i, slots, :] = liq + term
            phases = []
            equations = []
            for n, (ref, flag) in enumerate(((liquid, False), (vapour, True))):
                whole, b_sum, quad = mixture(lambda i, g: ref[i, rows_of(g), :], WIDE, n * WIDE)
                inv_whole = recip(whole)
                b_mix = b_sum * inv_whole
                a_mix = quad * inv_whole * inv_whole
                big_b = pressure * b_mix
                equations.append((pressure * a_mix, big_b, flag))
                phases.append((quad, whole, inv_whole, a_mix, b_mix, big_b))
            factors = roots_of(*equations)
            found[0] = part
            for n in range(2):
                found[1 + n] = factors[n]
                found[3 + n] = phases[n][2]

            @pl.when(number_of_sweep + 1 < SS_ITERS)
            def _():
                parts = []
                for (quad, whole, _, a_mix, b_mix, big_b), z_factor in zip(phases, factors):
                    log_arg = (z_factor + (1.0 + SQRT_TWO) * big_b) * recip(
                        z_factor + (1.0 - SQRT_TWO) * big_b
                    )
                    inv_b = recip(b_mix)
                    depart = a_mix * inv_b * (1.0 / (2.0 * SQRT_TWO)) * jnp.log(log_arg)
                    of_cov = (LOG2E * inv_b) * (z_factor - 1.0 + depart)
                    of_sum = (2.0 * LOG2E) * depart * whole * recip(quad)
                    parts.append((of_cov, z_factor - big_b, of_sum))
                cov_gap = parts[0][0] - parts[1][0]
                log_gap = LOG2E * jnp.log(parts[0][1] * recip(parts[1][1]))
                for i in range(comps):
                    log2_k = (covolume[i] * cov_gap - log_gap) - (
                        parts[0][2] * total(i, 0, WIDE) - parts[1][2] * total(i, WIDE, WIDE)
                    )
                    keep_k(i, jnp.minimum(jnp.maximum(log2_k, -3.0 * LOG2E), 3.0 * LOG2E))
            return inner

        lax.fori_loop(0, SS_ITERS, sweep, 0)
        part = found[0]
        rho_liq = amount * pressure * recip(found[1])
        rho_vap = amount * pressure * recip(found[2])
        rest = 1.0 - part
        move_liq = rest * rest * rho_liq
        move_vap = 4.0 * part * part * rho_vap
        hold_liq = rest * rho_liq
        hold_vap = part * rho_vap
        out_cell[0] = part
        out_cell[1] = move_liq + move_vap
        out_cell[2] = hold_liq + hold_vap
        inv_liq, inv_vap = found[3], found[4]
        move_liq = move_liq * inv_liq
        move_vap = move_vap * inv_vap
        hold_liq = hold_liq * inv_liq
        hold_vap = hold_vap * inv_vap
        for i in range(comps):
            liq, gas = liquid[i, slots, :], vapour[i, slots, :]
            liquid[i, slots, :] = move_liq * liq + move_vap * gas
            vapour[i, slots, :] = hold_liq * liq + hold_vap * gas
        one_row = jnp.ones((1, BLK), jnp.float32)

        def scatter(group, inner):
            for n in range(SUB):
                r = group * SUB + n
                k, layer = place(base + r)
                of = pl.ds(r, comps, stride=pack_stride)
                mobile_rows[mobile_at(k, layer), :] = liquid_rows[of, :]
                held_rows[field_at(k, layer), :] = vapour_rows[of, :]
                one = pl.ds(r, 1)
                row = pl.ds(layer, 1)
                vap[k, row, :] = out_cell[0, one, :]
                lam[k + 1, pl.ds(layer + SUB, 1), :] = out_cell[1, one, :]
                csum[k, row, :] = out_cell[2, one, :]
                scale[k, row, :] = one_row
            return inner

        lax.fori_loop(0, WIDE, scatter, 0)
        return carry

    lax.fori_loop(0, (own_count + batch - 1) // batch, flash, 0)
    for k in range(strips):
        strip_in(old_hbm, old, old_sem, k).wait()
    old_rows = old.reshape(comps * old.shape[1], BLK)

    def edge_values(k, at, inner):
        here = slice(at, at + 1)
        pad_here = slice(SUB + at, SUB + at + 1)
        pad_inner = slice(SUB + inner, SUB + inner + 1)
        values = [None] * EDGE_ROWS
        values[EDGE_PRES] = pres[k + 1, pad_here, :]
        values[EDGE_PERM] = perm[k + 1, pad_here, :]
        values[EDGE_LAM] = lam[k + 1, pad_here, :]
        values[EDGE_CSUM] = csum[k, here, :]
        values[EDGE_OSUM] = jnp.sum(old_rows[field_at(k, at), :], 0, keepdims=True)
        values[EDGE_PRES2] = pres[k + 1, pad_inner, :]
        values[EDGE_PERM2] = perm[k + 1, pad_inner, :]
        values[EDGE_LAM2] = lam[k + 1, pad_inner, :]
        return [mobile_rows[mobile_at(k, at), :]] + values

    odd = lax.rem(lax.axis_index("dev"), 2) == 1
    for k in range(strips):
        lanes = slice(k * BLK, (k + 1) * BLK)
        tops = edge_values(k, 0, 1)
        lows = edge_values(k, layers - 1, layers - 2)
        row = 0
        for top, low in zip(tops, lows):
            rows = slice(row, row + top.shape[0])
            edge_a[rows, lanes] = jnp.where(odd, top, low)
            edge_b[rows, lanes] = jnp.where(odd, low, top)
            row = rows.stop


def flux_kernel(
    held,
    old,
    mobile,
    pres,
    perm,
    lam,
    scale,
    csum,
    vap,
    resid_hbm,
    step_hbm,
    vap_hbm,
    top_aux,
    low_aux,
    resid,
    first,
    row_sum,
    diag,
    weights,
    step,
    vap_flat,
    step_sem,
    vap_sem,
    out_sem,
):
    comps = held.shape[0]
    strips, layers, _ = scale.shape
    groups = layers // SUB
    padded = layers + 2 * SUB

    def lanes_of(k):
        return pl.ds(pl.multiple_of(k * BLK, BLK), BLK)

    def strip_out(k):
        return pltpu.make_async_copy(resid.at[:, k], resid_hbm.at[:, :, lanes_of(k)], out_sem.at[k])

    for k in range(strips):
        vap_flat[:, k * BLK : (k + 1) * BLK] = vap[k]
    vap_copy = pltpu.make_async_copy(vap_flat, vap_hbm, vap_sem)
    vap_copy.start()
    zero_tile = jnp.zeros((SUB, BLK), jnp.float32)
    for k in range(strips + 2):
        for g in range(groups + 2):
            if k in (0, strips + 1) or g in (0, groups + 1):
                first[k, rows_of(g), :] = zero_tile

    lane_index = lax.broadcasted_iota(jnp.int32, (SUB, BLK), 1)
    is_last_lane = lane_index == BLK - 1
    is_first_lane = lane_index == 0

    def around(load, k, g):
        at = SUB * (g + 1)
        here = load(k + 1, slice(at, at + SUB))
        up = load(k + 1, slice(at - 1, at + SUB - 1))
        down = load(k + 1, slice(at + 1, at + SUB + 1))
        before = load(k, slice(at, at + SUB))
        after = load(k + 2, slice(at, at + SUB))
        left = pltpu.roll(jnp.where(is_last_lane, before, here), 1, 1)
        right = pltpu.roll(jnp.where(is_first_lane, after, here), BLK - 1, 1)
        return here, (up, down, left, right)

    def fluxes(k, carry):
        for g in range(groups):
            rows = rows_of(g)
            p_here, p_near = around(lambda s, r: pres[s, r, :], k, g)
            k_here, k_near = around(lambda s, r: perm[s, r, :], k, g)
            l_here, l_near = around(lambda s, r: lam[s, r, :], k, g)
            drives = []
            couplings = []
            for n in range(4):
                transmiss = k_here * k_near[n] * recip(k_here + k_near[n])
                drives.append((TIME_STEP * transmiss) * (p_here - p_near[n]))
                couplings.append(transmiss * (l_here + l_near[n]))
            drive_sum = (drives[0] + drives[1]) + (drives[2] + drives[3])
            content_scale = scale[k, rows, :]
            flat_rows = pl.ds(pl.multiple_of(k * layers + g * SUB, SUB), SUB)
            row_total = zero_tile
            for i in range(comps):
                m_here, m_near = around(
                    lambda s, r, i=i: mobile[i, pl.ds(s * padded + r.start, SUB), :], k, g
                )
                value = held[i, flat_rows, :] * content_scale - old[i, flat_rows, :]
                value = value + drive_sum * m_here
                value = value + (drives[0] * m_near[0] + drives[1] * m_near[1])
                value = value + (drives[2] * m_near[2] + drives[3] * m_near[3])
                resid[i, k, rows, :] = value
                row_total = row_total + value
            diagonal = TIME_STEP * (
                (couplings[0] + couplings[1]) + (couplings[2] + couplings[3])
            ) + csum[k, rows, :] * recip(p_here)
            inv_diag = recip(diagonal)
            row_sum[k, rows, :] = row_total
            diag[k, rows, :] = diagonal
            first[k + 1, SUB * (g + 1) : SUB * (g + 2), :] = -row_total * inv_diag
            gain = (STEP_SCALE * OFF_SCALE) * inv_diag
            for n in range(4):
                weights[n, k, rows, :] = couplings[n] * gain
        strip_out(k).start()
        return carry

    lax.fori_loop(0, strips, fluxes, 0)

    def steps(k, carry):
        for g in range(groups):
            rows = rows_of(g)
            here, near = around(lambda s, r: first[s, r, :], k, g)
            step[rows, lanes_of(k)] = (
                STEP_SCALE * here
                + (weights[0, k, rows, :] * near[0] + weights[1, k, rows, :] * near[1])
                + (weights[2, k, rows, :] * near[2] + weights[3, k, rows, :] * near[3])
            )
        return carry

    lax.fori_loop(0, strips, steps, 0)
    step_copy = pltpu.make_async_copy(step, step_hbm, step_sem)
    step_copy.start()

    resid_rows = resid.reshape(comps * strips * layers, BLK)
    for aux, at, inner, toward, away in (
        (top_aux, 0, 1, 0, 1),
        (low_aux, layers - 1, layers - 2, 1, 0),
    ):
        for k in range(strips):
            lanes = slice(k * BLK, (k + 1) * BLK)
            here = slice(at, at + 1)
            behind = slice(inner, inner + 1)
            from_row = pl.ds(k * layers + at, comps, stride=strips * layers)
            aux[0:comps, lanes] = resid_rows[from_row, :]
            unscale = diag[k, here, :]
            values = [None] * AUX_ROWS
            values[AUX_IN] = weights[away, k, here, :] * unscale
            values[AUX_LEFT] = weights[2, k, here, :] * unscale
            values[AUX_RIGHT] = weights[3, k, here, :] * unscale
            values[AUX_FIRST] = first[k + 1, SUB + inner : SUB + inner + 1, :]
            values[AUX_GAIN] = weights[toward, k, behind, :]
            values[AUX_STEP] = step[behind, lanes]
            values[AUX_ROW] = row_sum[k, here, :]
            values[AUX_DIAG] = unscale
            for n, value in enumerate(values):
                aux[comps + n : comps + n + 1, lanes] = value
    vap_copy.wait()
    step_copy.wait()
    for k in range(strips):
        strip_out(k).wait()


def transmissibility(perm, perm_near):
    both = perm + perm_near
    return perm * perm_near / jnp.where(both == 0.0, 1.0, both)


def edge_kernel(
    edge_a,
    edge_b,
    top_aux,
    low_aux,
    in_even,
    in_odd,
    resid_in,
    step_in,
    resid_hbm,
    step_hbm,
    resid,
    step,
    sem,
):
    comps, layers, face = resid_hbm.shape
    odd = lax.rem(lax.axis_index("dev"), 2) == 1
    top_edge = jnp.where(odd, edge_a[...], edge_b[...])
    low_edge = jnp.where(odd, edge_b[...], edge_a[...])
    from_prev = jnp.where(odd, in_even[...], in_odd[...])
    from_next = jnp.where(odd, in_odd[...], in_even[...])
    copies = []
    for n, (edge, aux, other, at, inner) in enumerate(
        (
            (top_edge, top_aux, from_prev, 0, 1),
            (low_edge, low_aux, from_next, layers - 1, layers - 2),
        )
    ):

        def own(index):
            return edge[comps + index : comps + index + 1, :]

        def far(index):
            return other[comps + index : comps + index + 1, :]

        def near(index):
            return aux[comps + index : comps + index + 1, :]

        pres_far, perm_far, lam_far = far(EDGE_PRES), far(EDGE_PERM), far(EDGE_LAM)
        transmiss = transmissibility(own(EDGE_PERM), perm_far)
        drive = TIME_STEP * transmiss * (own(EDGE_PRES) - pres_far)
        lam_both = own(EDGE_LAM) + lam_far
        coupling = transmiss * lam_both
        row = near(AUX_ROW) + drive * lam_both
        diag = near(AUX_DIAG) + TIME_STEP * coupling
        first = -row / diag
        first_old = -near(AUX_ROW) / near(AUX_DIAG)
        row_far = far(EDGE_CSUM) - far(EDGE_OSUM) - drive * lam_both
        diag_far = coupling
        lane = lax.broadcasted_iota(jnp.int32, (1, face), 1)
        sides = [(far(EDGE_PRES2), far(EDGE_PERM2), far(EDGE_LAM2))]
        for shift, end in ((1, 0), (face - 1, face - 1)):
            pres_n, perm_n, lam_n = (pltpu.roll(x, shift, 1) for x in (pres_far, perm_far, lam_far))
            sides.append((pres_n, jnp.where(lane == end, 0.0, perm_n), lam_n))
        for pres_n, perm_n, lam_n in sides:
            joint = transmissibility(perm_far, perm_n) * (lam_far + lam_n)
            row_far = row_far + TIME_STEP * joint * (pres_far - pres_n)
            diag_far = diag_far + joint
        diag_far = TIME_STEP * diag_far + far(EDGE_CSUM) / jnp.where(pres_far == 0.0, 1.0, pres_far)
        first_far = -row_far / jnp.where(diag_far == 0.0, 1.0, diag_far)
        off = (
            (STEP_SCALE * OFF_SCALE) * coupling * first_far
            + near(AUX_IN) * near(AUX_FIRST)
            + near(AUX_LEFT) * pltpu.roll(first, 1, 1)
            + near(AUX_RIGHT) * pltpu.roll(first, face - 1, 1)
        )
        least = min(at, inner)
        step[n, at - least : at - least + 1, :] = STEP_SCALE * first + off / diag
        step[n, inner - least : inner - least + 1, :] = near(AUX_STEP) + near(AUX_GAIN) * (
            first - first_old
        )
        resid[n] = aux[0:comps, :] + drive * (edge[0:comps, :] + other[0:comps, :])
        for source, target in (
            (resid.at[n], resid_hbm.at[:, at, :]),
            (step.at[n, 0:2, :], step_hbm.at[least : least + 2, :]),
        ):
            copies.append(pltpu.make_async_copy(source, target, sem.at[len(copies)]))
            copies[-1].start()
    for copy in copies:
        copy.wait()


def on_device(
    moles,
    old_content,
    pressure,
    perm,
    labels,
    roots,
    counts,
    block_ids,
    wilson,
    attraction,
    covolume,
):
    comps, layers, face = moles.shape
    f32 = jnp.float32
    strips = face // BLK
    tables = (block_ids, wilson, covolume, attraction)
    rows_in = comps * SUB
    vmem = pl.BlockSpec(memory_space=pltpu.VMEM)
    hbm = pl.BlockSpec(memory_space=pltpu.HBM)
    padded = layers + 2 * SUB
    flat = pltpu.VMEM((layers, face), f32)
    flat_int = pltpu.VMEM((layers, face), jnp.int32)
    cell = pltpu.VMEM((strips, layers, BLK), f32)
    cell_pad = pltpu.VMEM((strips + 2, padded, BLK), f32)
    field = pltpu.VMEM((comps, odd_tiles(strips * layers), BLK), f32)
    field_pad = pltpu.VMEM((comps, odd_tiles((strips + 2) * padded), BLK), f32)
    packed = pltpu.VMEM((comps, odd_tiles(WIDE * SUB), BLK), f32)
    edge_shape = pltpu.VMEM((EDGE_SPAN, face), f32)
    aux_shape = pltpu.VMEM((comps + AUX_ROWS, face), f32)
    field_shape = jax.ShapeDtypeStruct((comps, layers, face), f32)
    cell_shape = jax.ShapeDtypeStruct((layers, face), f32)
    field_out = pltpu.VMEM((comps, strips, layers, BLK), f32)
    held_types = [field, field, field_pad] + [cell_pad] * 3 + [cell] * 3
    edge_a, edge_b, *state = pl.pallas_call(
        cells_kernel,
        out_shape=[edge_shape, edge_shape]
        + held_types,
        in_specs=[pl.BlockSpec(memory_space=pltpu.SMEM)] + [hbm] * 10,
        out_specs=[vmem] * (2 + len(held_types)),
        scratch_shapes=[flat, flat, flat_int, flat_int]
        + [pltpu.VMEM((rows_in + 2 * SUB, 3 * rows_in), jnp.bfloat16)]
        + [pltpu.VMEM((rows_in, 2 * WIDE * BLK), f32)]
        + [packed, pltpu.VMEM((WIDE * SUB, BLK), f32)]
        + [packed] * 3
        + [pltpu.VMEM((3, WIDE * SUB, BLK), f32), pltpu.VMEM((5, WIDE * SUB, BLK), f32)]
        + [pltpu.VMEM((3, layers, BLK), f32)]
        + [pltpu.SMEM(table.shape, table.dtype) for table in tables[:-1]]
        + [pltpu.VMEM(attraction.shape, f32)]
        + [
            pltpu.SemaphoreType.DMA((strips,)),
            pltpu.SemaphoreType.DMA((strips,)),
            pltpu.SemaphoreType.DMA((4,)),
            pltpu.SemaphoreType.DMA((len(tables),)),
        ],
        compiler_params=pltpu.CompilerParams(vmem_limit_bytes=CELLS_VMEM),
        name="cells",
    )(counts, *keep_in(pltpu.HBM, *tables, moles, old_content, pressure, perm, labels, roots))
    count = lax.axis_size("dev")
    arrived = []
    for start, edge in ((0, edge_a), (1, edge_b)):
        pairs = [(i, i + 1) for i in range(start, count - 1, 2)]
        arrived.append(lax.ppermute(edge, "dev", pairs + [pair[::-1] for pair in pairs]))
    residual, step, vapour, top_aux, low_aux = pl.pallas_call(
        flux_kernel,
        out_shape=[field_shape, cell_shape, cell_shape, aux_shape, aux_shape],
        in_specs=[vmem] * len(state),
        out_specs=[hbm] * 3 + [vmem] * 2,
        scratch_shapes=[field_out, cell_pad, cell, cell]
        + [pltpu.VMEM((4, strips, layers, BLK), f32), flat, flat]
        + [pltpu.SemaphoreType.DMA(())] * 2
        + [pltpu.SemaphoreType.DMA((strips,))],
        compiler_params=pltpu.CompilerParams(vmem_limit_bytes=FLUX_VMEM),
        name="flux",
    )(*keep_in(pltpu.VMEM, *state))
    residual, step = pl.pallas_call(
        edge_kernel,
        out_shape=[field_shape, cell_shape],
        in_specs=[vmem] * 6 + [hbm] * 2,
        out_specs=[hbm] * 2,
        input_output_aliases={6: 0, 7: 1},
        scratch_shapes=[
            pltpu.VMEM((2, comps, face), f32),
            pltpu.VMEM((2, SUB, face), f32),
            pltpu.SemaphoreType.DMA((4,)),
        ],
        compiler_params=pltpu.CompilerParams(vmem_limit_bytes=16 * 1024 * 1024),
        name="edges",
    )(edge_a, edge_b, top_aux, low_aux, *arrived, residual, step)
    return (residual, step, vapour)


def solution(mesh):
    in_specs = (
        P(None, "dev", None),
        P(None, "dev", None),
        P("dev", None),
        P("dev", None),
        P("dev", None),
        P("dev", None),
        P("dev"),
        P("dev"),
        P(),
        P(),
        P(),
    )
    out_specs = (P(None, "dev", None), P("dev", None), P("dev", None))
    return jax.shard_map(
        on_device, mesh=mesh, in_specs=in_specs, out_specs=out_specs, check_vma=False
    )
```

```python
import math

import jax
import jax.numpy as jnp
from jax import lax
from jax.experimental import pallas as pl
from jax.experimental.pallas import tpu as pltpu
from jax.sharding import PartitionSpec as P

BLK = 128
SUB = 8
SS_ITERS = 3
RR_ITERS = 3
Z_ITERS = 5
WIDE = 8
AHEAD = 3
LOG2E = math.log2(math.e)
CELLS_VMEM = 32 * 1024 * 1024
FLUX_VMEM = 32 * 1024 * 1024

SQRT_TWO = math.sqrt(2.0)
TIME_STEP = 0.5
RELAX = 0.7
STEP_SCALE = 10.0
OFF_SCALE = RELAX * TIME_STEP

EDGE_PRES, EDGE_PERM, EDGE_LAM, EDGE_CSUM, EDGE_OSUM = range(5)
EDGE_PRES2, EDGE_PERM2, EDGE_LAM2 = range(5, 8)
EDGE_ROWS = 8
EDGE_SPAN = 32
AUX_IN, AUX_LEFT, AUX_RIGHT, AUX_FIRST, AUX_GAIN, AUX_STEP, AUX_ROW, AUX_DIAG = range(8)
AUX_ROWS = 8


def keep_in(space, *arrays):
    return [pltpu.with_memory_space_constraint(x, space) for x in arrays]


def recip(value):
    return pltpu.reciprocal(value, approx=True)


def odd_tiles(rows):
    return rows + SUB if (rows // SUB) % 2 == 0 else rows


def split_halves(value):
    high = value.astype(jnp.bfloat16)
    low = (value - high.astype(jnp.float32)).astype(jnp.bfloat16)
    return high, low


def widen(wide, attraction, covolume, comps):
    cols = 3 * comps * SUB
    span = 2 * SUB

    def column(rows):
        at = lax.broadcasted_iota(jnp.int32, (rows, cols), 1)
        pair = at // (3 * span)
        within = at - pair * (3 * span)
        part = within // span
        within = within - part * span
        return 2 * pair + within // SUB, part, lax.rem(within, SUB)

    comp, _, _ = column(comps)
    spread = jnp.where(comp == lax.broadcasted_iota(jnp.int32, (comps, cols), 0), 1.0, 0.0)
    spread = spread.astype(jnp.bfloat16)
    table = attraction[...]
    of_high, of_low = (
        jnp.dot(half, spread, preferred_element_type=jnp.float32)
        for half in split_halves(0.5 * (table + table.T))
    )
    comp, part, sub = column(SUB)
    diagonal = sub == lax.broadcasted_iota(jnp.int32, (SUB, cols), 0)
    zero = jnp.zeros((SUB, cols), jnp.float32)
    of_cov = zero
    for j in range(comps):
        of_cov = jnp.where(comp == j, covolume[j], of_cov)
    cov_high = of_cov.astype(jnp.bfloat16).astype(jnp.float32)
    taken = jnp.where(part[0:1, :] == 1, of_low, of_high)
    blocks = [taken[i : i + 1, :] for i in range(comps)]
    blocks += [jnp.where(part == 1, of_cov - cov_high, cov_high), jnp.where(part == 1, 0.0, 1.0)]
    for pair in range(len(blocks) // 2):
        rows = [jnp.where(diagonal, blocks[i], zero) for i in (2 * pair, 2 * pair + 1)]
        wide[span * pair : span * (pair + 1), :] = jnp.concatenate(rows, 0).astype(jnp.bfloat16)


def rows_of(g):
    return slice(g * SUB, (g + 1) * SUB)


def cubic(big_a, big_b, vapour_flag):
    two_b = 2.0 * big_b
    two_b_square = two_b * big_b
    least = two_b + 0.01
    most = big_b + 2.0
    if vapour_flag is True:
        start, shift, factor = 1.0 + big_b, big_b + 0.5, -0.5 * big_a
    elif vapour_flag is False:
        start, shift, factor = 3.0 * big_b, big_b, 0.5 * recip(big_a)
    else:
        start = jnp.where(vapour_flag, 1.0 + big_b, 3.0 * big_b)
        shift = jnp.where(vapour_flag, big_b + 0.5, big_b)
        factor = jnp.where(vapour_flag, -0.5 * big_a, -0.5 * recip(big_a))
        base = jnp.where(vapour_flag, two_b, 1.0 + two_b)

    def step(w):
        spread = w * w - two_b_square
        if vapour_flag is True:
            part = factor * (w - two_b) * recip(spread)
        elif vapour_flag is False:
            part = spread * ((1.0 + two_b) - w) * factor
        else:
            part = factor * (w - base) * jnp.where(vapour_flag, recip(spread), spread)
        return jnp.minimum(jnp.maximum((0.5 * w + shift) + part, least), most)

    return start, step


def roots_of(*equations):
    steps = [cubic(*equation) for equation in equations]
    found = [start for start, _ in steps]
    for _ in range(Z_ITERS):
        found = [step(w) for w, (_, step) in zip(found, steps)]
    return [w - big_b for w, (_, big_b, _) in zip(found, equations)]


def cells_kernel(
    counts,
    block_ids_hbm,
    wilson_hbm,
    covolume_hbm,
    attraction_hbm,
    moles_hbm,
    old_hbm,
    pres_hbm,
    perm_hbm,
    labels_hbm,
    roots_hbm,
    edge_a,
    edge_b,
    held,
    old,
    mobile,
    pres,
    perm,
    lam,
    scale,
    csum,
    vap,
    pres_flat,
    perm_flat,
    labels,
    roots,
    w_wide,
    sums,
    pack,
    pack_pres,
    inv_excess,
    liquid,
    vapour,
    out_cell,
    found,
    mix,
    block_ids,
    wilson,
    covolume,
    attraction,
    in_sem,
    old_sem,
    cell_sem,
    table_sem,
):
    comps, layers, face = moles_hbm.shape
    strips = face // BLK
    groups = layers // SUB
    padded = layers + 2 * SUB
    inside = slice(SUB, SUB + layers)

    def lanes_of(k):
        return pl.ds(pl.multiple_of(k * BLK, BLK), BLK)

    def strip_of(k):
        return pl.ds(pl.multiple_of(k * layers, SUB), layers)

    def strip_in(source, target, sem, k):
        return pltpu.make_async_copy(
            source.at[:, :, lanes_of(k)], target.at[:, strip_of(k), :], sem.at[k]
        )

    cell_copies = [
        pltpu.make_async_copy(pres_hbm, pres_flat, cell_sem.at[0]),
        pltpu.make_async_copy(roots_hbm, roots, cell_sem.at[1]),
        pltpu.make_async_copy(labels_hbm, labels, cell_sem.at[2]),
        pltpu.make_async_copy(perm_hbm, perm_flat, cell_sem.at[3]),
    ]
    table_copies = [
        pltpu.make_async_copy(source, target, table_sem.at[n])
        for n, (source, target) in enumerate(
            (
                (attraction_hbm, attraction),
                (covolume_hbm, covolume),
                (wilson_hbm, wilson),
                (block_ids_hbm, block_ids),
            )
        )
    ]
    for copy in table_copies:
        copy.start()
    for k in range(min(AHEAD, strips)):
        strip_in(moles_hbm, held, in_sem, k).start()
    for copy in cell_copies:
        copy.start()

    zero_tile = jnp.zeros((SUB, BLK), jnp.float32)
    zero_strip = jnp.zeros((padded, BLK), jnp.float32)

    for ref in (pres, perm, lam):
        for k in (0, strips + 1):
            ref[k] = zero_strip
        for k in range(1, strips + 1):
            ref[k, 0:SUB] = zero_tile
            ref[k, SUB + layers : padded] = zero_tile

    def clear(i, carry):
        for k in (0, strips + 1):
            mobile[i, k * padded : (k + 1) * padded, :] = zero_strip
        for k in range(1, strips + 1):
            mobile[i, k * padded : k * padded + SUB, :] = zero_tile
            mobile[i, (k + 1) * padded - SUB : (k + 1) * padded, :] = zero_tile
        return carry

    lax.fori_loop(0, comps, clear, 0)
    for copy in table_copies:
        copy.wait()
    widen(w_wide, attraction, covolume, comps)

    cols = comps * SUB

    def mixture(tile, count, keep=None, between=None):
        parts = ([], [], [])
        for g in range(0, count, 2):
            if between is not None:
                between()
            halves = []
            for j in range(comps // 2):
                both = [
                    jnp.concatenate([tile(2 * j, at), tile(2 * j + 1, at)], 0) for at in (g, g + 1)
                ]
                high, low = split_halves(jnp.concatenate(both, 1))
                halves += [high, high, low]
            result = jnp.dot(
                w_wide[...],
                jnp.concatenate(halves, 0),
                preferred_element_type=jnp.float32,
            )
            if keep is not None:
                sums[:, (keep + g) * BLK : (keep + g + 2) * BLK] = result[0:cols]
            for n, at in enumerate((g, g + 1)):
                lanes = slice(n * BLK, (n + 1) * BLK)
                quad = tile(0, at) * result[0:SUB, lanes]
                for i in range(1, comps):
                    quad = quad + tile(i, at) * result[i * SUB : (i + 1) * SUB, lanes]
                parts[0].append(result[cols + SUB : cols + 2 * SUB, lanes])
                parts[1].append(result[cols : cols + SUB, lanes])
                parts[2].append(quad)
        return [jnp.concatenate(part, 0) for part in parts]

    def total(at, start, count):
        rows = slice(at * SUB, (at + 1) * SUB)
        return jnp.concatenate(
            [sums[rows, g * BLK : (g + 1) * BLK] for g in range(start, start + count)], 0
        )


    def padded_of(k):
        return pl.ds(pl.multiple_of((k + 1) * padded + SUB, SUB), layers)

    def products(k, between=None):
        strip_in(moles_hbm, held, in_sem, k).wait()

        @pl.when(k + AHEAD < strips)
        def _():
            strip_in(moles_hbm, held, in_sem, k + AHEAD).start()

        return mixture(
            lambda i, g: held[i, pl.ds(pl.multiple_of(k * layers + g * SUB, SUB), SUB), :],
            groups,
            between=between,
        )

    class Roots:
        def __init__(self, k, amount, b_sum, quad):
            self.pressure = pres[k + 1, inside, :]
            self.amount = amount
            inv_amount = recip(amount)
            big_a = self.pressure * quad * inv_amount * inv_amount
            self.big_b = self.pressure * b_sum * inv_amount
            self.found, self.step = cubic(big_a, self.big_b, roots[:, lanes_of(k)] == 1)
            self.steps = 0

        def advance(self):
            if self.steps < Z_ITERS:
                self.found = self.step(self.found)
                self.steps += 1

    def fields(k, it):
        while it.steps < Z_ITERS:
            it.advance()
        rho = it.pressure * recip(it.found - it.big_b)
        part = labels[:, lanes_of(k)].astype(jnp.float32)
        move = ((1.0 - part) * (1.0 - part) + 4.0 * part * part) * rho
        vap[k] = part
        scale[k] = rho
        csum[k] = it.amount * rho
        lam[k + 1, inside, :] = it.amount * move
        for i in range(comps):
            mobile[i, padded_of(k), :] = held[i, strip_of(k), :] * move

    def keep_mix(values):
        for n, value in enumerate(values):
            mix[n] = value

    def single(k, carry):
        it = Roots(k - 1, *(mix[n] for n in range(3)))
        now = products(k, it.advance)
        fields(k - 1, it)
        keep_mix(now)
        return carry

    keep_mix(products(0))
    for copy in cell_copies:
        copy.wait()
    for k in range(strips):
        pres[k + 1, inside, :] = pres_flat[:, k * BLK : (k + 1) * BLK]
        perm[k + 1, inside, :] = perm_flat[:, k * BLK : (k + 1) * BLK]
    lax.fori_loop(1, strips, single, 0)
    for k in range(strips):
        strip_in(old_hbm, old, old_sem, k).start()
    fields(strips - 1, Roots(strips - 1, *(mix[n] for n in range(3))))

    batch = WIDE * SUB
    own_count = counts[0]
    held_stride, mobile_stride, pack_stride = (ref.shape[1] for ref in (held, mobile, pack))
    held_rows = held.reshape(comps * held_stride, BLK)
    mobile_rows = mobile.reshape(comps * mobile_stride, BLK)
    pack_rows = pack.reshape(comps * pack_stride, BLK)
    liquid_rows = liquid.reshape(comps * pack_stride, BLK)
    vapour_rows = vapour.reshape(comps * pack_stride, BLK)
    bits = strips.bit_length() - 1

    def place(slot):
        block = block_ids[jnp.minimum(slot, own_count - 1)]
        layer = lax.shift_right_logical(block, bits)
        return block - lax.shift_left(layer, bits), layer

    def field_at(k, layer):
        return pl.ds(k * layers + layer, comps, stride=held_stride)

    def mobile_at(k, layer):
        return pl.ds((k + 1) * padded + layer + SUB, comps, stride=mobile_stride)

    def flash(number, carry):
        base = number * batch

        def gather(group, inner):
            for n in range(SUB):
                r = group * SUB + n
                k, layer = place(base + r)
                pack_rows[pl.ds(r, comps, stride=pack_stride), :] = held_rows[field_at(k, layer), :]
                pack_pres[pl.ds(r, 1), :] = pres[k + 1, pl.ds(layer + SUB, 1), :]
            return inner

        lax.fori_loop(0, WIDE, gather, 0)
        slots = slice(0, batch)
        pressure = pack_pres[...]
        amount = pack[0, slots, :]
        for i in range(1, comps):
            amount = amount + pack[i, slots, :]
        inv_amount = recip(amount)
        for i in range(comps):
            pack[i, slots, :] = pack[i, slots, :] * inv_amount

        def keep_k(i, log2_k):
            inv_excess[i, slots, :] = recip(jnp.exp2(log2_k) - 1.0)

        log2_pres = jnp.log(pressure) * LOG2E
        for i in range(comps):
            keep_k(i, wilson[i] * LOG2E - log2_pres)

        def newton(part):
            value = jnp.zeros((batch, BLK), jnp.float32)
            slope = jnp.full((batch, BLK), 0.05, jnp.float32)
            for i in range(comps):
                ratio = recip(inv_excess[i, slots, :] + part)
                term = pack[i, slots, :] * ratio
                value = value + term
                slope = slope + term * ratio
            return jnp.minimum(jnp.maximum(part + value * recip(slope), 0.0), 1.0)

        def sweep(is_last):
            half = jnp.full((batch, BLK), 0.5, jnp.float32)
            part = half
            for _ in range(RR_ITERS):
                part = newton(part)
            for i in range(comps):
                fraction = pack[i, slots, :]
                term = fraction * recip(inv_excess[i, slots, :] + part)
                liq = fraction - part * term
                liquid[i, slots, :] = liq
                vapour[i, slots, :] = liq + term
            phases = []
            equations = []
            for n, (ref, flag) in enumerate(((liquid, False), (vapour, True))):
                whole, b_sum, quad = mixture(lambda i, g: ref[i, rows_of(g), :], WIDE, None if is_last else n * WIDE)
                inv_whole = recip(whole)
                b_mix = b_sum * inv_whole
                a_mix = quad * inv_whole * inv_whole
                big_b = pressure * b_mix
                equations.append((pressure * a_mix, big_b, flag))
                phases.append((quad, whole, inv_whole, a_mix, b_mix, big_b))
            factors = roots_of(*equations)
            found[0] = part
            for n in range(2):
                found[1 + n] = factors[n]
                found[3 + n] = phases[n][2]

            if not is_last:
                parts = []
                for (quad, whole, _, a_mix, b_mix, big_b), z_factor in zip(phases, factors):
                    log_arg = (z_factor + (1.0 + SQRT_TWO) * big_b) * recip(
                        z_factor + (1.0 - SQRT_TWO) * big_b
                    )
                    inv_b = recip(b_mix)
                    depart = a_mix * inv_b * (1.0 / (2.0 * SQRT_TWO)) * jnp.log(log_arg)
                    of_cov = (LOG2E * inv_b) * (z_factor - 1.0 + depart)
                    of_sum = (2.0 * LOG2E) * depart * whole * recip(quad)
                    parts.append((of_cov, z_factor - big_b, of_sum))
                cov_gap = parts[0][0] - parts[1][0]
                log_gap = LOG2E * jnp.log(parts[0][1] * recip(parts[1][1]))
                for i in range(comps):
                    log2_k = (covolume[i] * cov_gap - log_gap) - (
                        parts[0][2] * total(i, 0, WIDE) - parts[1][2] * total(i, WIDE, WIDE)
                    )
                    keep_k(i, jnp.minimum(jnp.maximum(log2_k, -3.0 * LOG2E), 3.0 * LOG2E))

        for number_of_sweep in range(SS_ITERS):
            sweep(number_of_sweep + 1 == SS_ITERS)
        part = found[0]
        rho_liq = amount * pressure * recip(found[1])
        rho_vap = amount * pressure * recip(found[2])
        rest = 1.0 - part
        move_liq = rest * rest * rho_liq
        move_vap = 4.0 * part * part * rho_vap
        hold_liq = rest * rho_liq
        hold_vap = part * rho_vap
        out_cell[0] = part
        out_cell[1] = move_liq + move_vap
        out_cell[2] = hold_liq + hold_vap
        inv_liq, inv_vap = found[3], found[4]
        move_liq = move_liq * inv_liq
        move_vap = move_vap * inv_vap
        hold_liq = hold_liq * inv_liq
        hold_vap = hold_vap * inv_vap
        for i in range(comps):
            liq, gas = liquid[i, slots, :], vapour[i, slots, :]
            liquid[i, slots, :] = move_liq * liq + move_vap * gas
            vapour[i, slots, :] = hold_liq * liq + hold_vap * gas
        one_row = jnp.ones((1, BLK), jnp.float32)

        def scatter(group, inner):
            for n in range(SUB):
                r = group * SUB + n
                k, layer = place(base + r)
                of = pl.ds(r, comps, stride=pack_stride)
                mobile_rows[mobile_at(k, layer), :] = liquid_rows[of, :]
                held_rows[field_at(k, layer), :] = vapour_rows[of, :]
                one = pl.ds(r, 1)
                row = pl.ds(layer, 1)
                vap[k, row, :] = out_cell[0, one, :]
                lam[k + 1, pl.ds(layer + SUB, 1), :] = out_cell[1, one, :]
                csum[k, row, :] = out_cell[2, one, :]
                scale[k, row, :] = one_row
            return inner

        lax.fori_loop(0, WIDE, scatter, 0)
        return carry

    lax.fori_loop(0, (own_count + batch - 1) // batch, flash, 0)
    for k in range(strips):
        strip_in(old_hbm, old, old_sem, k).wait()
    old_rows = old.reshape(comps * old.shape[1], BLK)

    def edge_values(k, at, inner):
        here = slice(at, at + 1)
        pad_here = slice(SUB + at, SUB + at + 1)
        pad_inner = slice(SUB + inner, SUB + inner + 1)
        values = [None] * EDGE_ROWS
        values[EDGE_PRES] = pres[k + 1, pad_here, :]
        values[EDGE_PERM] = perm[k + 1, pad_here, :]
        values[EDGE_LAM] = lam[k + 1, pad_here, :]
        values[EDGE_CSUM] = csum[k, here, :]
        values[EDGE_OSUM] = jnp.sum(old_rows[field_at(k, at), :], 0, keepdims=True)
        values[EDGE_PRES2] = pres[k + 1, pad_inner, :]
        values[EDGE_PERM2] = perm[k + 1, pad_inner, :]
        values[EDGE_LAM2] = lam[k + 1, pad_inner, :]
        return [mobile_rows[mobile_at(k, at), :]] + values

    odd = lax.rem(lax.axis_index("dev"), 2) == 1
    for k in range(strips):
        lanes = slice(k * BLK, (k + 1) * BLK)
        tops = edge_values(k, 0, 1)
        lows = edge_values(k, layers - 1, layers - 2)
        row = 0
        for top, low in zip(tops, lows):
            rows = slice(row, row + top.shape[0])
            edge_a[rows, lanes] = jnp.where(odd, top, low)
            edge_b[rows, lanes] = jnp.where(odd, low, top)
            row = rows.stop


def flux_kernel(
    held,
    old,
    mobile,
    pres,
    perm,
    lam,
    scale,
    csum,
    vap,
    resid_hbm,
    step_hbm,
    vap_hbm,
    top_aux,
    low_aux,
    resid,
    first,
    row_sum,
    diag,
    weights,
    step,
    vap_flat,
    step_sem,
    vap_sem,
    out_sem,
):
    comps = held.shape[0]
    strips, layers, _ = scale.shape
    groups = layers // SUB
    padded = layers + 2 * SUB

    def lanes_of(k):
        return pl.ds(pl.multiple_of(k * BLK, BLK), BLK)

    def strip_out(k):
        return pltpu.make_async_copy(resid.at[:, k], resid_hbm.at[:, :, lanes_of(k)], out_sem.at[k])

    for k in range(strips):
        vap_flat[:, k * BLK : (k + 1) * BLK] = vap[k]
    vap_copy = pltpu.make_async_copy(vap_flat, vap_hbm, vap_sem)
    vap_copy.start()
    zero_tile = jnp.zeros((SUB, BLK), jnp.float32)
    for k in range(strips + 2):
        for g in range(groups + 2):
            if k in (0, strips + 1) or g in (0, groups + 1):
                first[k, rows_of(g), :] = zero_tile

    lane_index = lax.broadcasted_iota(jnp.int32, (SUB, BLK), 1)
    is_last_lane = lane_index == BLK - 1
    is_first_lane = lane_index == 0

    def around(load, k, g):
        at = SUB * (g + 1)
        here = load(k + 1, slice(at, at + SUB))
        up = load(k + 1, slice(at - 1, at + SUB - 1))
        down = load(k + 1, slice(at + 1, at + SUB + 1))
        before = load(k, slice(at, at + SUB))
        after = load(k + 2, slice(at, at + SUB))
        left = pltpu.roll(jnp.where(is_last_lane, before, here), 1, 1)
        right = pltpu.roll(jnp.where(is_first_lane, after, here), BLK - 1, 1)
        return here, (up, down, left, right)

    def fluxes(k, carry):
        for g in range(groups):
            rows = rows_of(g)
            p_here, p_near = around(lambda s, r: pres[s, r, :], k, g)
            k_here, k_near = around(lambda s, r: perm[s, r, :], k, g)
            l_here, l_near = around(lambda s, r: lam[s, r, :], k, g)
            drives = []
            couplings = []
            for n in range(4):
                transmiss = k_here * k_near[n] * recip(k_here + k_near[n])
                drives.append((TIME_STEP * transmiss) * (p_here - p_near[n]))
                couplings.append(transmiss * (l_here + l_near[n]))
            drive_sum = (drives[0] + drives[1]) + (drives[2] + drives[3])
            content_scale = scale[k, rows, :]
            flat_rows = pl.ds(pl.multiple_of(k * layers + g * SUB, SUB), SUB)
            row_total = zero_tile
            for i in range(comps):
                m_here, m_near = around(
                    lambda s, r, i=i: mobile[i, pl.ds(s * padded + r.start, SUB), :], k, g
                )
                value = held[i, flat_rows, :] * content_scale - old[i, flat_rows, :]
                value = value + drive_sum * m_here
                value = value + (drives[0] * m_near[0] + drives[1] * m_near[1])
                value = value + (drives[2] * m_near[2] + drives[3] * m_near[3])
                resid[i, k, rows, :] = value
                row_total = row_total + value
            diagonal = TIME_STEP * (
                (couplings[0] + couplings[1]) + (couplings[2] + couplings[3])
            ) + csum[k, rows, :] * recip(p_here)
            inv_diag = recip(diagonal)
            row_sum[k, rows, :] = row_total
            diag[k, rows, :] = diagonal
            first[k + 1, SUB * (g + 1) : SUB * (g + 2), :] = -row_total * inv_diag
            gain = (STEP_SCALE * OFF_SCALE) * inv_diag
            for n in range(4):
                weights[n, k, rows, :] = couplings[n] * gain
        strip_out(k).start()
        return carry

    lax.fori_loop(0, strips, fluxes, 0)

    def steps(k, carry):
        for g in range(groups):
            rows = rows_of(g)
            here, near = around(lambda s, r: first[s, r, :], k, g)
            step[rows, lanes_of(k)] = (
                STEP_SCALE * here
                + (weights[0, k, rows, :] * near[0] + weights[1, k, rows, :] * near[1])
                + (weights[2, k, rows, :] * near[2] + weights[3, k, rows, :] * near[3])
            )
        return carry

    lax.fori_loop(0, strips, steps, 0)
    step_copy = pltpu.make_async_copy(step, step_hbm, step_sem)
    step_copy.start()

    resid_rows = resid.reshape(comps * strips * layers, BLK)
    for aux, at, inner, toward, away in (
        (top_aux, 0, 1, 0, 1),
        (low_aux, layers - 1, layers - 2, 1, 0),
    ):
        for k in range(strips):
            lanes = slice(k * BLK, (k + 1) * BLK)
            here = slice(at, at + 1)
            behind = slice(inner, inner + 1)
            from_row = pl.ds(k * layers + at, comps, stride=strips * layers)
            aux[0:comps, lanes] = resid_rows[from_row, :]
            unscale = diag[k, here, :]
            values = [None] * AUX_ROWS
            values[AUX_IN] = weights[away, k, here, :] * unscale
            values[AUX_LEFT] = weights[2, k, here, :] * unscale
            values[AUX_RIGHT] = weights[3, k, here, :] * unscale
            values[AUX_FIRST] = first[k + 1, SUB + inner : SUB + inner + 1, :]
            values[AUX_GAIN] = weights[toward, k, behind, :]
            values[AUX_STEP] = step[behind, lanes]
            values[AUX_ROW] = row_sum[k, here, :]
            values[AUX_DIAG] = unscale
            for n, value in enumerate(values):
                aux[comps + n : comps + n + 1, lanes] = value
    vap_copy.wait()
    step_copy.wait()
    for k in range(strips):
        strip_out(k).wait()


def transmissibility(perm, perm_near):
    both = perm + perm_near
    return perm * perm_near / jnp.where(both == 0.0, 1.0, both)


def edge_kernel(
    edge_a,
    edge_b,
    top_aux,
    low_aux,
    in_even,
    in_odd,
    resid_in,
    step_in,
    resid_hbm,
    step_hbm,
    resid,
    step,
    sem,
):
    comps, layers, face = resid_hbm.shape
    odd = lax.rem(lax.axis_index("dev"), 2) == 1
    top_edge = jnp.where(odd, edge_a[...], edge_b[...])
    low_edge = jnp.where(odd, edge_b[...], edge_a[...])
    from_prev = jnp.where(odd, in_even[...], in_odd[...])
    from_next = jnp.where(odd, in_odd[...], in_even[...])
    copies = []
    for n, (edge, aux, other, at, inner) in enumerate(
        (
            (top_edge, top_aux, from_prev, 0, 1),
            (low_edge, low_aux, from_next, layers - 1, layers - 2),
        )
    ):

        def own(index):
            return edge[comps + index : comps + index + 1, :]

        def far(index):
            return other[comps + index : comps + index + 1, :]

        def near(index):
            return aux[comps + index : comps + index + 1, :]

        pres_far, perm_far, lam_far = far(EDGE_PRES), far(EDGE_PERM), far(EDGE_LAM)
        transmiss = transmissibility(own(EDGE_PERM), perm_far)
        drive = TIME_STEP * transmiss * (own(EDGE_PRES) - pres_far)
        lam_both = own(EDGE_LAM) + lam_far
        coupling = transmiss * lam_both
        row = near(AUX_ROW) + drive * lam_both
        diag = near(AUX_DIAG) + TIME_STEP * coupling
        first = -row / diag
        first_old = -near(AUX_ROW) / near(AUX_DIAG)
        row_far = far(EDGE_CSUM) - far(EDGE_OSUM) - drive * lam_both
        diag_far = coupling
        lane = lax.broadcasted_iota(jnp.int32, (1, face), 1)
        sides = [(far(EDGE_PRES2), far(EDGE_PERM2), far(EDGE_LAM2))]
        for shift, end in ((1, 0), (face - 1, face - 1)):
            pres_n, perm_n, lam_n = (pltpu.roll(x, shift, 1) for x in (pres_far, perm_far, lam_far))
            sides.append((pres_n, jnp.where(lane == end, 0.0, perm_n), lam_n))
        for pres_n, perm_n, lam_n in sides:
            joint = transmissibility(perm_far, perm_n) * (lam_far + lam_n)
            row_far = row_far + TIME_STEP * joint * (pres_far - pres_n)
            diag_far = diag_far + joint
        diag_far = TIME_STEP * diag_far + far(EDGE_CSUM) / jnp.where(pres_far == 0.0, 1.0, pres_far)
        first_far = -row_far / jnp.where(diag_far == 0.0, 1.0, diag_far)
        off = (
            (STEP_SCALE * OFF_SCALE) * coupling * first_far
            + near(AUX_IN) * near(AUX_FIRST)
            + near(AUX_LEFT) * pltpu.roll(first, 1, 1)
            + near(AUX_RIGHT) * pltpu.roll(first, face - 1, 1)
        )
        least = min(at, inner)
        step[n, at - least : at - least + 1, :] = STEP_SCALE * first + off / diag
        step[n, inner - least : inner - least + 1, :] = near(AUX_STEP) + near(AUX_GAIN) * (
            first - first_old
        )
        resid[n] = aux[0:comps, :] + drive * (edge[0:comps, :] + other[0:comps, :])
        for source, target in (
            (resid.at[n], resid_hbm.at[:, at, :]),
            (step.at[n, 0:2, :], step_hbm.at[least : least + 2, :]),
        ):
            copies.append(pltpu.make_async_copy(source, target, sem.at[len(copies)]))
            copies[-1].start()
    for copy in copies:
        copy.wait()


def on_device(
    moles,
    old_content,
    pressure,
    perm,
    labels,
    roots,
    counts,
    block_ids,
    wilson,
    attraction,
    covolume,
):
    comps, layers, face = moles.shape
    f32 = jnp.float32
    strips = face // BLK
    tables = (block_ids, wilson, covolume, attraction)
    rows_in = comps * SUB
    vmem = pl.BlockSpec(memory_space=pltpu.VMEM)
    hbm = pl.BlockSpec(memory_space=pltpu.HBM)
    padded = layers + 2 * SUB
    flat = pltpu.VMEM((layers, face), f32)
    flat_int = pltpu.VMEM((layers, face), jnp.int32)
    cell = pltpu.VMEM((strips, layers, BLK), f32)
    cell_pad = pltpu.VMEM((strips + 2, padded, BLK), f32)
    field = pltpu.VMEM((comps, odd_tiles(strips * layers), BLK), f32)
    field_pad = pltpu.VMEM((comps, odd_tiles((strips + 2) * padded), BLK), f32)
    packed = pltpu.VMEM((comps, odd_tiles(WIDE * SUB), BLK), f32)
    edge_shape = pltpu.VMEM((EDGE_SPAN, face), f32)
    aux_shape = pltpu.VMEM((comps + AUX_ROWS, face), f32)
    field_shape = jax.ShapeDtypeStruct((comps, layers, face), f32)
    cell_shape = jax.ShapeDtypeStruct((layers, face), f32)
    field_out = pltpu.VMEM((comps, strips, layers, BLK), f32)
    held_types = [field, field, field_pad] + [cell_pad] * 3 + [cell] * 3
    edge_a, edge_b, *state = pl.pallas_call(
        cells_kernel,
        out_shape=[edge_shape, edge_shape]
        + held_types,
        in_specs=[pl.BlockSpec(memory_space=pltpu.SMEM)] + [hbm] * 10,
        out_specs=[vmem] * (2 + len(held_types)),
        scratch_shapes=[flat, flat, flat_int, flat_int]
        + [pltpu.VMEM((rows_in + 2 * SUB, 3 * rows_in), jnp.bfloat16)]
        + [pltpu.VMEM((rows_in, 2 * WIDE * BLK), f32)]
        + [packed, pltpu.VMEM((WIDE * SUB, BLK), f32)]
        + [packed] * 3
        + [pltpu.VMEM((3, WIDE * SUB, BLK), f32), pltpu.VMEM((5, WIDE * SUB, BLK), f32)]
        + [pltpu.VMEM((3, layers, BLK), f32)]
        + [pltpu.SMEM(table.shape, table.dtype) for table in tables[:-1]]
        + [pltpu.VMEM(attraction.shape, f32)]
        + [
            pltpu.SemaphoreType.DMA((strips,)),
            pltpu.SemaphoreType.DMA((strips,)),
            pltpu.SemaphoreType.DMA((4,)),
            pltpu.SemaphoreType.DMA((len(tables),)),
        ],
        compiler_params=pltpu.CompilerParams(vmem_limit_bytes=CELLS_VMEM),
        name="cells",
    )(counts, *keep_in(pltpu.HBM, *tables, moles, old_content, pressure, perm, labels, roots))
    count = lax.axis_size("dev")
    arrived = []
    for start, edge in ((0, edge_a), (1, edge_b)):
        pairs = [(i, i + 1) for i in range(start, count - 1, 2)]
        arrived.append(lax.ppermute(edge, "dev", pairs + [pair[::-1] for pair in pairs]))
    residual, step, vapour, top_aux, low_aux = pl.pallas_call(
        flux_kernel,
        out_shape=[field_shape, cell_shape, cell_shape, aux_shape, aux_shape],
        in_specs=[vmem] * len(state),
        out_specs=[hbm] * 3 + [vmem] * 2,
        scratch_shapes=[field_out, cell_pad, cell, cell]
        + [pltpu.VMEM((4, strips, layers, BLK), f32), flat, flat]
        + [pltpu.SemaphoreType.DMA(())] * 2
        + [pltpu.SemaphoreType.DMA((strips,))],
        compiler_params=pltpu.CompilerParams(vmem_limit_bytes=FLUX_VMEM),
        name="flux",
    )(*keep_in(pltpu.VMEM, *state))
    residual, step = pl.pallas_call(
        edge_kernel,
        out_shape=[field_shape, cell_shape],
        in_specs=[vmem] * 6 + [hbm] * 2,
        out_specs=[hbm] * 2,
        input_output_aliases={6: 0, 7: 1},
        scratch_shapes=[
            pltpu.VMEM((2, comps, face), f32),
            pltpu.VMEM((2, SUB, face), f32),
            pltpu.SemaphoreType.DMA((4,)),
        ],
        compiler_params=pltpu.CompilerParams(vmem_limit_bytes=16 * 1024 * 1024),
        name="edges",
    )(edge_a, edge_b, top_aux, low_aux, *arrived, residual, step)
    return (residual, step, vapour)


def solution(mesh):
    in_specs = (
        P(None, "dev", None),
        P(None, "dev", None),
        P("dev", None),
        P("dev", None),
        P("dev", None),
        P("dev", None),
        P("dev"),
        P("dev"),
        P(),
        P(),
        P(),
    )
    out_specs = (P(None, "dev", None), P("dev", None), P("dev", None))
    return jax.shard_map(
        on_device, mesh=mesh, in_specs=in_specs, out_specs=out_specs, check_vma=False
    )
```
